32 devices in a mesh: gz: 4 (over y, core), xy: 8 (over z, x).
Axes of the slice: x: 2, y: 2, z: 4, core: 2. Of those that a mesh axis runs over, the one named last changes fastest.
Arguments:
- fine: bfloat16 [1024, 64, 512], P(('gz', 'xy')), may hold values from -6 to 6
- fine_mask: int32 [1024, 512], P(('gz', 'xy')), may hold values 0 or 1
- slot_source: int32 [1024], P(('gz', 'xy')), may hold values from -1 to 31, as said below
- w_down: bfloat16 [512, 128], replicated, may hold values from -0.25 to 0.25
- w_first: bfloat16 [27, 128, 128], replicated, may hold values from -0.109375 to 0.109375
- w_second: bfloat16 [27, 128, 128], replicated, may hold values from -0.109375 to 0.109375
- w_up: bfloat16 [128, 512], replicated, may hold values from -0.5 to 0.5
Outputs:
- fine_out: bfloat16 [1024, 64, 512], P(('gz', 'xy'))
- coarse: bfloat16 [64, 128, 8, 128], P('gz', 'xy')
The draws below stay inside these ranges and needn't reach their ends.
Inputs may be any that keep to these rules, and one draw needn't show every extreme that they name: `slot_source`: slot entries of device (g, o): a value m names row m of device (g, (o - m // 4) mod 8); on each device every value appears at most once, and between 4 // 2 (at least 1) and 4 of the rows m // 4 = j are named for each j below 8. Rows that no slot names are inactive.
All inputs are finite; a program needn't handle non-finite values. No bound on the sum of `fine_mask` on one device may be relied on, other than what follows from the above.
Results may differ from the reference program's by a relative error of at most 0.0052.
Values may be sent and summed in bfloat16 or wider, within the bound.
No kernel may reach another device: no remote copies, remote signals or barrier semaphores. Data moves between devices by JAX's collectives and lax.ppermute only.
A program may use at most 64 MiB of HBM per device.

```python
import jax
import jax.numpy as jnp
from jax import lax

C_IN = 64
C_MID = 128
BC = 1
CAP = 4
K = 8
SLOTS = 32
FB = 32
BRICKS = 1024
GD = 64
GR = 128
GC = 8
N_GZ = 4
N_XY = 8


def draw_slot_source(key, part):
    key = jax.random.fold_in(key, 11)
    count_key, ranking_key = jax.random.split(key)
    least_count = max(CAP // 2, 1)
    counts = jax.random.randint(count_key, (N_GZ, N_XY, K), least_count, CAP + 1)
    owners = jnp.arange(N_XY, dtype=jnp.int32)[None, :, None]
    offsets = jnp.arange(K, dtype=jnp.int32)[None, None, :]
    counts = jnp.where((offsets == 0) | (owners == 0), CAP, counts)
    position = jnp.arange(SLOTS, dtype=jnp.int32)
    within = position % CAP
    grouping = jnp.minimum(position // CAP, K - 1)
    inside = position < K * CAP
    chosen = jnp.take_along_axis(counts, jnp.broadcast_to(grouping[None, None, :], (N_GZ, N_XY, SLOTS)), axis=2)
    values = jnp.where(inside[None, None, :] & (within[None, None, :] < chosen), position[None, None, :], -1)
    scores = jax.random.randint(ranking_key, (N_GZ, N_XY, SLOTS), 0, 2 ** 20) * SLOTS + position[None, None, :]
    ranking = jnp.argsort(scores, axis=2)
    shuffled = jnp.take_along_axis(values, ranking, axis=2)
    return shuffled.reshape(-1).astype(jnp.int32)


def touch_ends(values, key, low, largest):
    index_at = [jax.random.randint(jax.random.fold_in(key, axis), (), 0, length) for axis, length in enumerate(values.shape)]
    main_axis = values.shape.index(max(values.shape))
    neighbour = index_at[:main_axis] + [(index_at[main_axis] + 1) % values.shape[main_axis]] + index_at[main_axis + 1:]
    return values.at[tuple(index_at)].set(low).at[tuple(neighbour)].set(largest)


def block_levels(stream_key, extent, cuts, low, top_value):
    def one(axis_at, blocks):
        draws = jax.random.uniform(jax.random.fold_in(jax.random.fold_in(stream_key, 6), axis_at), (blocks,), jnp.float32, low / len(cuts), top_value / len(cuts))
        return jnp.repeat(jnp.exp(draws), extent[axis_at] // blocks).reshape((-1,) + (1,) * (len(extent) - axis_at - 1))

    gain = one(*cuts[0])
    for cut in cuts[1:]:
        gain = gain * one(*cut)
    return gain


def bell_draw(own_key, dims, spread, limit, cuts=(), kind=jnp.bfloat16):
    factor_of = block_levels(own_key, dims, cuts, -0.22, 0.18) if cuts else 1.0
    drawn = jax.random.normal(own_key, dims, jnp.float32) * spread * factor_of
    return jnp.minimum(jnp.maximum(drawn, -limit), limit).astype(kind)


def setup_inputs(seed: int = 0) -> dict:
    key_of = jax.random.split(jax.random.key(seed), 8)
    return {
        "fine": bell_draw(key_of[0], (BRICKS, 64, 8 * C_IN), 1.0, 6.0, ((0, 32),)),
        "fine_mask": touch_ends((jax.random.randint(key_of[1], (BRICKS, 512), 0, 4) < 3).astype(jnp.int32), jax.random.fold_in(key_of[1], 1), 0, 1),
        "slot_source": draw_slot_source(jax.random.fold_in(key_of[7], 71), 0),
        "w_down": bell_draw(key_of[3], (8 * C_IN, C_MID), (8 * C_IN) ** -0.5, 0.25),
        "w_first": bell_draw(key_of[4], (27, C_MID, C_MID), (27 * C_MID) ** -0.5, 0.109375),
        "w_second": bell_draw(key_of[5], (27, C_MID, C_MID), (27 * C_MID) ** -0.5, 0.109375),
        "w_up": bell_draw(key_of[6], (C_MID, 8 * C_IN), C_MID ** -0.5, 0.5),
    }


def convolve_block(padded, weights):
    depth = padded.shape[0] - 2
    rowcount = padded.shape[1] - 2
    colcount = padded.shape[2] - 2
    channels = padded.shape[3]
    summed = jnp.zeros((depth * rowcount * colcount, weights.shape[2]), jnp.float32)
    for step_d in range(3):
        for step_r in range(3):
            for step_c in range(3):
                window = padded[step_d:step_d + depth, step_r:step_r + rowcount, step_c:step_c + colcount]
                summed = summed + jnp.dot(window.reshape(-1, channels), weights[9 * step_d + 3 * step_r + step_c], preferred_element_type=jnp.float32)
    return summed.reshape(depth, rowcount, colcount, weights.shape[2])


def grid_conv(grid, weights, finish):
    padded = jnp.pad(grid, ((1, 1), (1, 1), (1, 1), (0, 0)))

    def one_block(block_index):
        start = block_index * 16
        piece = lax.dynamic_slice_in_dim(padded, start, 18, 0)
        return finish(convolve_block(piece, weights), start)

    blocks = lax.map(one_block, jnp.arange(GD // 16, dtype=jnp.int32))
    return blocks.reshape(GD, GR, GC, grid.shape[3])


def reference(fine, fine_mask, slot_source, w_down, w_first, w_second, w_up):
    voxel_mask = fine_mask.reshape(BRICKS, 64, 8, 1)
    fine_in = (fine.reshape(BRICKS, 64, 8, C_IN) * voxel_mask.astype(jnp.bfloat16)).reshape(BRICKS, 64, 8 * C_IN)
    reduced = jnp.dot(fine_in.reshape(-1, 8 * C_IN), w_down, preferred_element_type=jnp.float32).astype(jnp.bfloat16)
    reduced = reduced.reshape(BRICKS, 64, C_MID)
    slot_grid = slot_source.reshape(N_GZ, N_XY, SLOTS)
    present = slot_grid >= 0
    owners = jnp.arange(N_XY, dtype=jnp.int32)[None, :, None]
    groups = jnp.arange(N_GZ, dtype=jnp.int32)[:, None, None]
    sources = (owners - slot_grid // CAP) % N_XY
    brick_rows = (groups * N_XY + sources) * FB + jnp.where(present, slot_grid, 0)
    gathered = jnp.take(reduced, brick_rows.reshape(-1), axis=0).reshape(N_GZ, N_XY, SLOTS, 64, C_MID)
    gathered = gathered * present[..., None, None].astype(jnp.bfloat16)
    coarse_in = gathered.reshape(N_GZ, N_XY, 2, 2, BC, 2, 2, 2, 4, 4, 4, C_MID)
    coarse_in = coarse_in.transpose(0, 2, 5, 8, 1, 3, 6, 9, 4, 7, 10, 11).reshape(GD, GR, GC, C_MID)
    filled = jnp.broadcast_to(present[..., None].astype(jnp.float32), (N_GZ, N_XY, SLOTS, 64))
    occupancy = filled.reshape(N_GZ, N_XY, 2, 2, BC, 2, 2, 2, 4, 4, 4)
    occupancy = occupancy.transpose(0, 2, 5, 8, 1, 3, 6, 9, 4, 7, 10).reshape(GD, GR, GC)

    def finish_first(result, start):
        local_mask = lax.dynamic_slice_in_dim(occupancy, start, 16, 0)
        return (jax.nn.silu(result) * local_mask[..., None]).astype(jnp.bfloat16)

    hidden = grid_conv(coarse_in, w_first, finish_first)

    def finish_second(result, start):
        local_mask = lax.dynamic_slice_in_dim(occupancy, start, 16, 0)
        local_input = lax.dynamic_slice_in_dim(coarse_in, start, 16, 0)
        return ((local_input.astype(jnp.float32) + result) * local_mask[..., None]).astype(jnp.bfloat16)

    coarse = grid_conv(hidden, w_second, finish_second)
    back_slots = coarse.reshape(N_GZ, 2, 2, 4, N_XY, 2, 2, 4, BC, 2, 4, C_MID)
    back_slots = back_slots.transpose(0, 4, 1, 5, 8, 2, 6, 9, 3, 7, 10, 11).reshape(N_GZ * N_XY * SLOTS, 64, C_MID)
    slot_numbers = jnp.broadcast_to(jnp.arange(SLOTS, dtype=jnp.int32)[None, None, :], (N_GZ, N_XY, SLOTS))
    group_index = jnp.broadcast_to(groups, (N_GZ, N_XY, SLOTS))
    owner_index = jnp.broadcast_to(owners, (N_GZ, N_XY, SLOTS))
    target = jnp.where(present, slot_grid, FB)
    inverse = jnp.zeros((N_GZ, N_XY, FB + 1), jnp.int32).at[group_index, owner_index, target].set(slot_numbers)
    named = jnp.zeros((N_GZ, N_XY, FB + 1), jnp.int32).at[group_index, owner_index, target].set(1)
    row_ids = jnp.arange(BRICKS, dtype=jnp.int32)
    row_group = row_ids // (N_XY * FB)
    row_source = (row_ids // FB) % N_XY
    row_local = row_ids % FB
    row_owner = (row_source + row_local // CAP) % N_XY
    row_slot = inverse[row_group, row_owner, row_local]
    row_named = named[row_group, row_owner, row_local]
    octant = jnp.take(back_slots, (row_group * N_XY + row_owner) * SLOTS + row_slot, axis=0)
    octant = octant * row_named[:, None, None].astype(jnp.bfloat16)
    upward = jnp.dot(octant.reshape(-1, C_MID), w_up, preferred_element_type=jnp.float32).reshape(BRICKS, 64, 8, C_IN)
    mask_float = voxel_mask.astype(jnp.float32)
    fine_out = ((fine_in.reshape(BRICKS, 64, 8, C_IN).astype(jnp.float32) + upward) * mask_float).astype(jnp.bfloat16)
    return fine_out.reshape(BRICKS, 64, 8 * C_IN), coarse
```

```python
import functools

import jax
import jax.numpy as jnp
from jax import lax
from jax.experimental import pallas as pl
from jax.experimental.pallas import tpu as pltpu
from jax.sharding import PartitionSpec as P

CAP = 4
K = 8
CELLS = 64
SIDE = 16
COLS = 8
WIDE = SIDE + 4
HID = SIDE + 2
VMEM_LIMIT = 56 * 1024 * 1024


def place_of(base, j, sign, rotated):
    if not rotated:
        return j
    return lax.rem(base + sign * j + K, K)


def expand_mask(mask):
    bricks = mask.shape[0]
    values = mask.astype(jnp.float32)
    cell = lax.broadcasted_iota(jnp.int32, (16, 128), 0)
    lane = lax.broadcasted_iota(jnp.int32, (16, 128), 1)
    chosen = (cell == lane // 8).astype(jnp.float32)
    parts = [
        values[:, t * 128 : (t + 1) * 128].reshape(bricks, 1, 128) * chosen[None] for t in range(4)
    ]
    spread = jnp.concatenate(parts, axis=1).reshape(bricks * CELLS, 128).astype(jnp.bfloat16)
    source = lax.broadcasted_iota(jnp.int32, (128, 512), 0)
    target = lax.broadcasted_iota(jnp.int32, (128, 512), 1)
    widen = ((source & 7) == (target >> 6)).astype(jnp.bfloat16)
    return jnp.dot(spread, widen, preferred_element_type=jnp.float32)


def down_kernel(rotated, base_ref, fine_ref, mask_ref, w_ref, out_ref):
    step = pl.program_id(0)
    bricks = fine_ref.shape[0]
    mask = expand_mask(mask_ref[...]).astype(jnp.bfloat16)
    x = fine_ref[...].reshape(bricks * CELLS, -1) * mask
    y = jnp.dot(x, w_ref[...], preferred_element_type=jnp.float32).astype(jnp.bfloat16)
    rows = CAP * CELLS
    for part in range(bricks // CAP):
        j = step * (bricks // CAP) + part
        out_ref[place_of(base_ref[0], j, 1, rotated)] = y[part * rows : (part + 1) * rows]


def down_call(base, fine, mask, w, rotated):
    bricks, cells, width = fine.shape
    mid = w.shape[1]
    step = 8
    return pl.pallas_call(
        functools.partial(down_kernel, rotated),
        grid=(bricks // step,),
        in_specs=[
            pl.BlockSpec(memory_space=pltpu.SMEM),
            pl.BlockSpec((step, cells, width), lambda i: (i, 0, 0)),
            pl.BlockSpec((step, width), lambda i: (i, 0)),
            pl.BlockSpec((width, mid), lambda i: (0, 0)),
        ],
        out_specs=pl.BlockSpec((K, CAP * cells, mid), lambda i: (0, 0, 0)),
        out_shape=jax.ShapeDtypeStruct((K, CAP * cells, mid), jnp.bfloat16),
        compiler_params=pltpu.CompilerParams(vmem_limit_bytes=VMEM_LIMIT),
        name="down",
    )(base, fine, mask, w)


def up_kernel(rotated, base_ref, fine_ref, mask_ref, w_ref, octant_ref, out_ref):
    step = pl.program_id(0)
    bricks, cells, width = fine_ref.shape
    mask = expand_mask(mask_ref[...])
    count = bricks // CAP
    parts = [
        octant_ref[place_of(base_ref[0], step * count + part, 1, rotated)] for part in range(count)
    ]
    octant = jnp.concatenate(parts, axis=0)
    up = jnp.dot(octant, w_ref[...], preferred_element_type=jnp.float32)
    fine = fine_ref[...].reshape(bricks * cells, width).astype(jnp.float32)
    out = jnp.where(mask > 0.5, fine + up, 0.0).astype(jnp.bfloat16)
    out_ref[...] = out.reshape(bricks, cells, width)


def up_call(base, fine, mask, w, octant, rotated):
    bricks, cells, width = fine.shape
    mid = w.shape[0]
    step = 8
    return pl.pallas_call(
        functools.partial(up_kernel, rotated),
        grid=(bricks // step,),
        in_specs=[
            pl.BlockSpec(memory_space=pltpu.SMEM),
            pl.BlockSpec((step, cells, width), lambda i: (i, 0, 0)),
            pl.BlockSpec((step, width), lambda i: (i, 0)),
            pl.BlockSpec((mid, width), lambda i: (0, 0)),
            pl.BlockSpec((K, CAP * cells, mid), lambda i: (0, 0, 0)),
        ],
        out_specs=pl.BlockSpec((step, cells, width), lambda i: (i, 0, 0)),
        out_shape=jax.ShapeDtypeStruct(fine.shape, jnp.bfloat16),
        compiler_params=pltpu.CompilerParams(vmem_limit_bytes=VMEM_LIMIT),
        name="up",
    )(base, fine, mask, w, octant)


def low_half(shape):
    return lax.broadcasted_iota(jnp.int32, shape, len(shape) - 2) < 4


def slot_flags(source_ref, first):
    pair = [jnp.where(source_ref[first + k] >= 0, 1.0, 0.0).astype(jnp.float32) for k in range(2)]
    return jnp.where(low_half((8, 128)), pair[0], pair[1])


def slot_index(depth_brick, row_brick):
    pd, qd = divmod(depth_brick, 2)
    pr, qr = divmod(row_brick, 2)
    return (pd * 2 + pr) * 8 + qd * 4 + qr * 2


def brick_place(rotated, base_ref, value):
    j = value // CAP
    return place_of(base_ref[0], j, -1, rotated), pl.multiple_of((value % CAP) * CELLS, CELLS)


def take_brick(rotated, base_ref, source_ref, arrived_ref, slot):
    value = source_ref[slot]
    place, first = brick_place(rotated, base_ref, jnp.maximum(value, 0))
    brick = arrived_ref[place, pl.ds(first, CELLS), :].astype(jnp.float32)
    return jnp.where(value >= 0, brick, 0.0).reshape(8, 8, 128)


def place_kernel(rotated, base_ref, source_ref, arrived_ref, block_ref, low_ref, high_ref):
    half = low_half((8, 8, 128))
    for depth_brick in range(4):
        for row_brick in range(4):
            slot = slot_index(depth_brick, row_brick)
            b0 = take_brick(rotated, base_ref, source_ref, arrived_ref, slot)
            b1 = take_brick(rotated, base_ref, source_ref, arrived_ref, slot + 1)
            even = jnp.where(half, b0, pltpu.roll(b1, 4, 1))
            odd = jnp.where(half, pltpu.roll(b0, 4, 1), b1)
            both = jnp.stack([even, odd], axis=1).reshape(4, 32, 128).astype(jnp.bfloat16)
            for vd in range(4):
                row = ((depth_brick * 4 + vd) * SIDE + row_brick * 4) * COLS
                block_ref[row : row + 32] = both[vd]
                place = (depth_brick * 4 + vd) * 16
                if row_brick == 0:
                    low_ref[place : place + 16] = both[vd, :16]
                if row_brick == 3:
                    high_ref[place : place + 16] = both[vd, 16:]
    for row_brick, ref in ((0, low_ref), (3, high_ref)):
        flags = [slot_flags(source_ref, slot_index(d, row_brick)) for d in range(4)]
        ref[256:288] = jnp.concatenate(flags, axis=0).astype(jnp.bfloat16)


def place_call(base, source, arrived, rotated):
    mid = arrived.shape[2]
    smem = pl.BlockSpec(memory_space=pltpu.SMEM)
    vmem = pl.BlockSpec(memory_space=pltpu.VMEM)
    return pl.pallas_call(
        functools.partial(place_kernel, rotated),
        in_specs=[smem, smem, vmem],
        out_specs=[vmem] * 3,
        out_shape=[
            jax.ShapeDtypeStruct((rows, mid), jnp.bfloat16)
            for rows in (SIDE * SIDE * COLS, 288, 288)
        ],
        compiler_params=pltpu.CompilerParams(vmem_limit_bytes=VMEM_LIMIT),
        name="place",
    )(base, source, arrived)


def edge_kernel(source_ref, block_ref, before_ref, after_ref, low_ref, high_ref):
    for ref, planes, brick in ((low_ref, (0, 1), 0), (high_ref, (SIDE - 2, SIDE - 1), 3)):
        for k, plane in enumerate(planes):
            start = k * WIDE * COLS
            ref[start : start + 16] = before_ref[plane * 16 : plane * 16 + 16]
            ref[start + 16 : start + 144] = block_ref[plane * 128 : plane * 128 + 128]
            ref[start + 144 : start + 160] = after_ref[plane * 16 : plane * 16 + 16]
        first = 256 + brick * 8
        flags = [before_ref[256:288].astype(jnp.float32)[brick * 8 : brick * 8 + 8]]
        flags += [slot_flags(source_ref, slot_index(brick, r)) for r in range(4)]
        flags += [after_ref[256:288].astype(jnp.float32)[brick * 8 : brick * 8 + 8]]
        ref[320:368] = jnp.concatenate(flags, axis=0).astype(jnp.bfloat16)


def edge_call(source, block, before, after):
    smem = pl.BlockSpec(memory_space=pltpu.SMEM)
    vmem = pl.BlockSpec(memory_space=pltpu.VMEM)
    return pl.pallas_call(
        edge_kernel,
        in_specs=[smem, vmem, vmem, vmem],
        out_specs=[vmem] * 2,
        out_shape=[jax.ShapeDtypeStruct((368, block.shape[1]), jnp.bfloat16)] * 2,
        compiler_params=pltpu.CompilerParams(vmem_limit_bytes=VMEM_LIMIT),
        name="edge",
    )(source, block, before, after)


def column_taps(plane):
    column = lax.broadcasted_iota(jnp.int32, plane.shape, 1)
    left = jnp.where(column == 0, 0.0, pltpu.roll(plane, 1, 1))
    right = jnp.where(column == COLS - 1, 0.0, pltpu.roll(plane, COLS - 1, 1))
    return left, plane, right


def store_taps(here_ref, next_ref, index, plane):
    rows = plane.shape[0]
    width = plane.shape[2]
    empty = jnp.zeros((1, COLS, width), jnp.float32)
    for k, tap in enumerate(column_taps(plane)):
        lanes = slice(k * width, (k + 1) * width)
        here_ref[index, :, lanes] = tap.reshape(rows * COLS, width).astype(jnp.bfloat16)
        moved = jnp.concatenate([tap[1:], empty], axis=0)
        next_ref[index, :, lanes] = moved.reshape(rows * COLS, width).astype(jnp.bfloat16)


def conv_planes(here_ref, next_ref, w_ref, first, planes, rows):
    total = None
    for dd in range(3):
        span = pl.ds(first + dd, planes)
        taps = [
            here_ref[span, 0:rows, :],
            next_ref[span, 0:rows, :],
            here_ref[span, 16 : rows + 16, :],
        ]
        lhs = jnp.concatenate(taps, axis=2)
        lhs = lhs.reshape(planes * rows, lhs.shape[2])
        part = jnp.dot(lhs, w_ref[dd], preferred_element_type=jnp.float32)
        total = part if total is None else total + part
    return total


def as_planes(value):
    value = value.astype(jnp.float32)
    return value.reshape(value.shape[0] // COLS, COLS, value.shape[1])


def conv_kernel(
    rotated,
    base_ref,
    source_ref,
    block_ref,
    before_ref,
    after_ref,
    under_ref,
    over_ref,
    w1_ref,
    w2_ref,
    coarse_ref,
    back_ref,
    x_here,
    x_next,
    h_here,
    h_next,
    flag_ref,
):
    width = block_ref.shape[1]
    for ref, brick in ((under_ref, 0), (over_ref, 5)):
        flags = as_planes(ref[320:368])
        flag_ref[brick] = flags
        for k in range(2):
            plane = as_planes(ref[k * 160 : (k + 1) * 160])
            store_taps(x_here, x_next, (0 if brick == 0 else WIDE - 2) + k, plane)
    flags_before = as_planes(before_ref[256:288])
    flags_after = as_planes(after_ref[256:288])
    for d in range(4):
        flag_ref[d + 1, 0] = flags_before[d]
        for r in range(4):
            flag_ref[d + 1, r + 1] = slot_flags(source_ref, slot_index(d, r))
        flag_ref[d + 1, 5] = flags_after[d]

    @pl.loop(0, SIDE)
    def _(d):
        edge = pl.ds(pl.multiple_of(d * 16, 16), 16)
        own = pl.ds(pl.multiple_of(d * 128, 128), 128)
        plane = jnp.concatenate(
            [as_planes(before_ref[edge]), as_planes(block_ref[own]), as_planes(after_ref[edge])],
            axis=0,
        )
        store_taps(x_here, x_next, d + 2, plane)

    @pl.loop(0, HID // 3)
    def _(group):
        value = conv_planes(x_here, x_next, w1_ref, group * 3, 3, HID * COLS)
        value = (value / (1.0 + jnp.exp(-value))).reshape(3, HID, COLS, width)
        for k in range(3):
            index = group * 3 + k
            flags = flag_ref[(index + 3) // 4]
            spread = jnp.concatenate(
                [flags[0:1]]
                + [jnp.broadcast_to(flags[r : r + 1], (4, COLS, width)) for r in range(1, 5)]
                + [flags[5:6]],
                axis=0,
            )
            store_taps(h_here, h_next, index, value[k] * spread)

    back_ref[...] = jnp.zeros(back_ref.shape, jnp.bfloat16)

    @pl.loop(0, 4)
    def _(depth_brick):
        value = conv_planes(h_here, h_next, w2_ref, depth_brick * 4, 4, SIDE * COLS)
        value = value.reshape(4, SIDE, COLS, width)
        rows = pl.ds(pl.multiple_of(depth_brick * 512, 512), 512)
        own = block_ref[rows].astype(jnp.float32).reshape(4, SIDE, COLS, width)
        flags = flag_ref[depth_brick + 1]
        spread = jnp.concatenate(
            [jnp.broadcast_to(flags[r : r + 1], (4, COLS, width)) for r in range(1, 5)], axis=0
        )
        value = (value + own) * spread[None]
        coarse_ref[rows] = value.reshape(4 * SIDE * COLS, width).astype(jnp.bfloat16)
        half = low_half((4, 2, COLS, width))
        for r in range(4):
            part = value[:, r * 4 : (r + 1) * 4].reshape(4, 2, 2, COLS, width)
            even, odd = part[:, :, 0], part[:, :, 1]
            b0 = jnp.where(half, even, pltpu.roll(odd, 4, 2))
            b1 = jnp.where(half, pltpu.roll(even, 4, 2), odd)
            slot = ((depth_brick // 2) * 2 + r // 2) * 8 + (depth_brick % 2) * 4 + (r % 2) * 2
            for k, brick in enumerate((b0, b1)):
                source = source_ref[slot + k]

                @pl.when(source >= 0)
                def _():
                    place, first = brick_place(rotated, base_ref, source)
                    back_ref[place, pl.ds(first, CELLS), :] = brick.reshape(CELLS, width).astype(
                        jnp.bfloat16
                    )


def conv_call(base, source, block, before, after, under, over, w_first, w_second, rotated):
    mid = block.shape[1]
    smem = pl.BlockSpec(memory_space=pltpu.SMEM)
    vmem = pl.BlockSpec(memory_space=pltpu.VMEM)
    return pl.pallas_call(
        functools.partial(conv_kernel, rotated),
        in_specs=[smem, smem] + [vmem] * 7,
        out_specs=[vmem] * 2,
        out_shape=[
            jax.ShapeDtypeStruct(block.shape, jnp.bfloat16),
            jax.ShapeDtypeStruct((K, CAP * CELLS, mid), jnp.bfloat16),
        ],
        scratch_shapes=[
            pltpu.VMEM((WIDE, WIDE * COLS, 3 * mid), jnp.bfloat16),
            pltpu.VMEM((WIDE, WIDE * COLS, 3 * mid), jnp.bfloat16),
            pltpu.VMEM((HID, HID * COLS, 3 * mid), jnp.bfloat16),
            pltpu.VMEM((HID, HID * COLS, 3 * mid), jnp.bfloat16),
            pltpu.VMEM((6, 6, COLS, mid), jnp.float32),
        ],
        compiler_params=pltpu.CompilerParams(vmem_limit_bytes=VMEM_LIMIT),
        name="conv",
    )(base, source, block, before, after, under, over, w_first, w_second)


def from_behind(value, axis, steps):
    count = lax.axis_size(axis)
    pairs = [(source, (source + steps) % count) for source in range(count)]
    return lax.ppermute(value, axis, pairs)


def exchange(value, rotated, sign):
    if rotated:
        return lax.all_to_all(value, "xy", 0, 0, tiled=True)
    return jnp.stack([from_behind(value[j], "xy", sign * j) for j in range(K)])


def neighbours(low, high, axis):
    count = lax.axis_size(axis)
    forward = [(i, i + 1) for i in range(count - 1)]
    backward = [(target, source) for source, target in forward]
    return lax.ppermute(high, axis, forward), lax.ppermute(low, axis, backward)


def shards(fine, fine_mask, slot_source, w_down, w_first, w_second, w_up):
    rotated = lax.axis_size("xy") == K
    mid = w_down.shape[1]
    base = lax.axis_index("xy").astype(jnp.int32).reshape(1)
    sent = down_call(base, fine, fine_mask, w_down, rotated)
    arrived = exchange(sent, rotated, 1)
    block, low, high = place_call(base, slot_source, arrived, rotated)
    before, after = neighbours(low, high, "xy")
    under_send, over_send = edge_call(slot_source, block, before, after)
    under, over = neighbours(under_send, over_send, "gz")
    coarse, back = conv_call(
        base,
        slot_source,
        block,
        before,
        after,
        under,
        over,
        w_first.reshape(3, 9 * mid, mid),
        w_second.reshape(3, 9 * mid, mid),
        rotated,
    )
    octant = exchange(back, rotated, -1)
    fine_out = up_call(base, fine, fine_mask, w_up, octant, rotated)
    return fine_out, coarse.reshape(SIDE, SIDE, COLS, mid)


def solution(mesh):
    placed = (
        P(("gz", "xy"), None, None),
        P(("gz", "xy"), None),
        P(("gz", "xy")),
        P(),
        P(),
        P(),
        P(),
    )
    return jax.shard_map(
        shards,
        mesh=mesh,
        in_specs=placed,
        out_specs=(P(("gz", "xy"), None, None), P("gz", "xy", None, None)),
        check_vma=False,
    )
```

```python
import functools

import jax
import jax.numpy as jnp
from jax import lax
from jax.experimental import pallas as pl
from jax.experimental.pallas import tpu as pltpu
from jax.sharding import PartitionSpec as P

CAP = 4
K = 8
CELLS = 64
SIDE = 16
COLS = 8
WIDE = SIDE + 4
HID = SIDE + 2
VMEM_LIMIT = 24 * 1024 * 1024


def place_of(base, j, sign, rotated):
    if not rotated:
        return j
    return lax.rem(base + sign * j + K, K)


def expand_mask(mask):
    bricks = mask.shape[0]
    values = mask.astype(jnp.float32)
    cell = lax.broadcasted_iota(jnp.int32, (16, 128), 0)
    lane = lax.broadcasted_iota(jnp.int32, (16, 128), 1)
    chosen = (cell == lane // 8).astype(jnp.float32)
    parts = [
        values[:, t * 128 : (t + 1) * 128].reshape(bricks, 1, 128) * chosen[None] for t in range(4)
    ]
    spread = jnp.concatenate(parts, axis=1).reshape(bricks * CELLS, 128).astype(jnp.bfloat16)
    source = lax.broadcasted_iota(jnp.int32, (128, 512), 0)
    target = lax.broadcasted_iota(jnp.int32, (128, 512), 1)
    widen = ((source & 7) == (target >> 6)).astype(jnp.bfloat16)
    return jnp.dot(spread, widen, preferred_element_type=jnp.float32)


def down_kernel(rotated, base_ref, fine_ref, mask_ref, w_ref, out_ref):
    step = pl.program_id(0)
    bricks = fine_ref.shape[0]
    mask = expand_mask(mask_ref[...]).astype(jnp.bfloat16)
    x = fine_ref[...].reshape(bricks * CELLS, -1) * mask
    y = jnp.dot(x, w_ref[...], preferred_element_type=jnp.float32).astype(jnp.bfloat16)
    rows = CAP * CELLS
    for part in range(bricks // CAP):
        j = step * (bricks // CAP) + part
        out_ref[place_of(base_ref[0], j, 1, rotated)] = y[part * rows : (part + 1) * rows]


def down_call(base, fine, mask, w, rotated):
    bricks, cells, width = fine.shape
    mid = w.shape[1]
    step = 8
    return pl.pallas_call(
        functools.partial(down_kernel, rotated),
        grid=(bricks // step,),
        in_specs=[
            pl.BlockSpec(memory_space=pltpu.SMEM),
            pl.BlockSpec((step, cells, width), lambda i: (i, 0, 0)),
            pl.BlockSpec((step, width), lambda i: (i, 0)),
            pl.BlockSpec((width, mid), lambda i: (0, 0)),
        ],
        out_specs=pl.BlockSpec((K, CAP * cells, mid), lambda i: (0, 0, 0)),
        out_shape=jax.ShapeDtypeStruct((K, CAP * cells, mid), jnp.bfloat16),
        compiler_params=pltpu.CompilerParams(vmem_limit_bytes=VMEM_LIMIT),
        name="down",
    )(base, fine, mask, w)


def up_kernel(rotated, base_ref, fine_ref, mask_ref, w_ref, octant_ref, out_ref):
    step = pl.program_id(0)
    bricks, cells, width = fine_ref.shape
    mask = expand_mask(mask_ref[...])
    count = bricks // CAP
    parts = [
        octant_ref[place_of(base_ref[0], step * count + part, 1, rotated)] for part in range(count)
    ]
    octant = jnp.concatenate(parts, axis=0)
    up = jnp.dot(octant, w_ref[...], preferred_element_type=jnp.float32)
    fine = fine_ref[...].reshape(bricks * cells, width).astype(jnp.float32)
    out = jnp.where(mask > 0.5, fine + up, 0.0).astype(jnp.bfloat16)
    out_ref[...] = out.reshape(bricks, cells, width)


def up_call(base, fine, mask, w, octant, rotated):
    bricks, cells, width = fine.shape
    mid = w.shape[0]
    step = 8
    return pl.pallas_call(
        functools.partial(up_kernel, rotated),
        grid=(bricks // step,),
        in_specs=[
            pl.BlockSpec(memory_space=pltpu.SMEM),
            pl.BlockSpec((step, cells, width), lambda i: (i, 0, 0)),
            pl.BlockSpec((step, width), lambda i: (i, 0)),
            pl.BlockSpec((mid, width), lambda i: (0, 0)),
            pl.BlockSpec((K, CAP * cells, mid), lambda i: (0, 0, 0)),
        ],
        out_specs=pl.BlockSpec((step, cells, width), lambda i: (i, 0, 0)),
        out_shape=jax.ShapeDtypeStruct(fine.shape, jnp.bfloat16),
        compiler_params=pltpu.CompilerParams(vmem_limit_bytes=VMEM_LIMIT),
        name="up",
    )(base, fine, mask, w, octant)


def low_half(shape):
    return lax.broadcasted_iota(jnp.int32, shape, len(shape) - 2) < 4


def slot_flags(source_ref, first):
    pair = [jnp.where(source_ref[first + k] >= 0, 1.0, 0.0).astype(jnp.float32) for k in range(2)]
    return jnp.where(low_half((8, 128)), pair[0], pair[1])


def slot_index(depth_brick, row_brick):
    pd, qd = divmod(depth_brick, 2)
    pr, qr = divmod(row_brick, 2)
    return (pd * 2 + pr) * 8 + qd * 4 + qr * 2


def brick_place(rotated, base_ref, value):
    j = value // CAP
    return place_of(base_ref[0], j, -1, rotated), pl.multiple_of((value % CAP) * CELLS, CELLS)


def take_brick(rotated, base_ref, source_ref, arrived_ref, slot):
    value = source_ref[slot]
    place, first = brick_place(rotated, base_ref, jnp.maximum(value, 0))
    brick = arrived_ref[place, pl.ds(first, CELLS), :].astype(jnp.float32)
    return jnp.where(value >= 0, brick, 0.0).reshape(8, 8, 128)


def place_kernel(rotated, base_ref, source_ref, arrived_ref, block_ref, low_ref, high_ref):
    half = low_half((8, 8, 128))
    for depth_brick in range(4):
        for row_brick in range(4):
            slot = slot_index(depth_brick, row_brick)
            b0 = take_brick(rotated, base_ref, source_ref, arrived_ref, slot)
            b1 = take_brick(rotated, base_ref, source_ref, arrived_ref, slot + 1)
            even = jnp.where(half, b0, pltpu.roll(b1, 4, 1))
            odd = jnp.where(half, pltpu.roll(b0, 4, 1), b1)
            both = jnp.stack([even, odd], axis=1).reshape(4, 32, 128).astype(jnp.bfloat16)
            for vd in range(4):
                row = ((depth_brick * 4 + vd) * SIDE + row_brick * 4) * COLS
                block_ref[row : row + 32] = both[vd]
                place = (depth_brick * 4 + vd) * 16
                if row_brick == 0:
                    low_ref[place : place + 16] = both[vd, :16]
                if row_brick == 3:
                    high_ref[place : place + 16] = both[vd, 16:]
    for row_brick, ref in ((0, low_ref), (3, high_ref)):
        flags = [slot_flags(source_ref, slot_index(d, row_brick)) for d in range(4)]
        ref[256:288] = jnp.concatenate(flags, axis=0).astype(jnp.bfloat16)


def place_call(base, source, arrived, rotated):
    mid = arrived.shape[2]
    smem = pl.BlockSpec(memory_space=pltpu.SMEM)
    vmem = pl.BlockSpec(memory_space=pltpu.VMEM)
    return pl.pallas_call(
        functools.partial(place_kernel, rotated),
        in_specs=[smem, smem, vmem],
        out_specs=[vmem] * 3,
        out_shape=[
            jax.ShapeDtypeStruct((rows, mid), jnp.bfloat16)
            for rows in (SIDE * SIDE * COLS, 288, 288)
        ],
        compiler_params=pltpu.CompilerParams(vmem_limit_bytes=VMEM_LIMIT),
        name="place",
    )(base, source, arrived)


def edge_kernel(source_ref, block_ref, before_ref, after_ref, low_ref, high_ref):
    for ref, planes, brick in ((low_ref, (0, 1), 0), (high_ref, (SIDE - 2, SIDE - 1), 3)):
        for k, plane in enumerate(planes):
            start = k * WIDE * COLS
            ref[start : start + 16] = before_ref[plane * 16 : plane * 16 + 16]
            ref[start + 16 : start + 144] = block_ref[plane * 128 : plane * 128 + 128]
            ref[start + 144 : start + 160] = after_ref[plane * 16 : plane * 16 + 16]
        first = 256 + brick * 8
        flags = [before_ref[256:288].astype(jnp.float32)[brick * 8 : brick * 8 + 8]]
        flags += [slot_flags(source_ref, slot_index(brick, r)) for r in range(4)]
        flags += [after_ref[256:288].astype(jnp.float32)[brick * 8 : brick * 8 + 8]]
        ref[320:368] = jnp.concatenate(flags, axis=0).astype(jnp.bfloat16)


def edge_call(source, block, before, after):
    smem = pl.BlockSpec(memory_space=pltpu.SMEM)
    vmem = pl.BlockSpec(memory_space=pltpu.VMEM)
    return pl.pallas_call(
        edge_kernel,
        in_specs=[smem, vmem, vmem, vmem],
        out_specs=[vmem] * 2,
        out_shape=[jax.ShapeDtypeStruct((368, block.shape[1]), jnp.bfloat16)] * 2,
        compiler_params=pltpu.CompilerParams(vmem_limit_bytes=VMEM_LIMIT),
        name="edge",
    )(source, block, before, after)


def store_rows(here_ref, next_ref, index, plane):
    rows = plane.shape[0]
    width = plane.shape[2]
    here_ref[index] = plane.reshape(rows * COLS, width).astype(jnp.bfloat16)
    empty = jnp.zeros((1, COLS, width), jnp.float32)
    moved = jnp.concatenate([plane[1:], empty], axis=0)
    next_ref[index] = moved.reshape(rows * COLS, width).astype(jnp.bfloat16)


def gather_weights(w_ref, wide_ref):
    width = w_ref.shape[2]
    for tap in range(9):
        for column in range(3):
            wide_ref[tap * width : (tap + 1) * width, column * width : (column + 1) * width] = (
                w_ref[tap * 3 + column]
            )


def conv_planes(here_ref, next_ref, wide_ref, first, planes, rows):
    width = here_ref.shape[2]
    taps = []
    for dd in range(3):
        span = pl.ds(first + dd, planes)
        taps += [
            here_ref[span, 0:rows, :],
            next_ref[span, 0:rows, :],
            here_ref[span, 16 : rows + 16, :],
        ]
    lhs = jnp.concatenate(taps, axis=2).reshape(planes * rows, 9 * width)
    wide = jnp.dot(lhs, wide_ref[...], preferred_element_type=jnp.float32)
    wide = wide.reshape(planes * rows // COLS, COLS, 3 * width)
    column = lax.broadcasted_iota(jnp.int32, (planes * rows // COLS, COLS, width), 1)
    left = jnp.where(column == 0, 0.0, pltpu.roll(wide[:, :, :width], 1, 1))
    right = jnp.where(column == COLS - 1, 0.0, pltpu.roll(wide[:, :, 2 * width :], COLS - 1, 1))
    return left + wide[:, :, width : 2 * width] + right


def as_planes(value):
    value = value.astype(jnp.float32)
    return value.reshape(value.shape[0] // COLS, COLS, value.shape[1])


def conv_kernel(
    rotated,
    base_ref,
    source_ref,
    block_ref,
    before_ref,
    after_ref,
    under_ref,
    over_ref,
    w1_ref,
    w2_ref,
    coarse_ref,
    back_ref,
    x_here,
    x_next,
    h_here,
    h_next,
    flag_ref,
    wide1_ref,
    wide2_ref,
):
    width = block_ref.shape[1]
    gather_weights(w1_ref, wide1_ref)
    gather_weights(w2_ref, wide2_ref)
    for ref, brick in ((under_ref, 0), (over_ref, 5)):
        flags = as_planes(ref[320:368])
        flag_ref[brick] = flags
        for k in range(2):
            plane = as_planes(ref[k * 160 : (k + 1) * 160])
            store_rows(x_here, x_next, (0 if brick == 0 else WIDE - 2) + k, plane)
    flags_before = as_planes(before_ref[256:288])
    flags_after = as_planes(after_ref[256:288])
    for d in range(4):
        flag_ref[d + 1, 0] = flags_before[d]
        for r in range(4):
            flag_ref[d + 1, r + 1] = slot_flags(source_ref, slot_index(d, r))
        flag_ref[d + 1, 5] = flags_after[d]

    @pl.loop(0, SIDE)
    def _(d):
        edge = pl.ds(pl.multiple_of(d * 16, 16), 16)
        own = pl.ds(pl.multiple_of(d * 128, 128), 128)
        plane = jnp.concatenate(
            [as_planes(before_ref[edge]), as_planes(block_ref[own]), as_planes(after_ref[edge])],
            axis=0,
        )
        store_rows(x_here, x_next, d + 2, plane)

    @pl.loop(0, HID // 3)
    def _(group):
        value = conv_planes(x_here, x_next, wide1_ref, group * 3, 3, HID * COLS)
        value = (value / (1.0 + jnp.exp(-value))).reshape(3, HID, COLS, width)
        for k in range(3):
            index = group * 3 + k
            flags = flag_ref[(index + 3) // 4]
            spread = jnp.concatenate(
                [flags[0:1]]
                + [jnp.broadcast_to(flags[r : r + 1], (4, COLS, width)) for r in range(1, 5)]
                + [flags[5:6]],
                axis=0,
            )
            store_rows(h_here, h_next, index, value[k] * spread)

    back_ref[...] = jnp.zeros(back_ref.shape, jnp.bfloat16)

    @pl.loop(0, 4)
    def _(depth_brick):
        value = conv_planes(h_here, h_next, wide2_ref, depth_brick * 4, 4, SIDE * COLS)
        value = value.reshape(4, SIDE, COLS, width)
        rows = pl.ds(pl.multiple_of(depth_brick * 512, 512), 512)
        own = block_ref[rows].astype(jnp.float32).reshape(4, SIDE, COLS, width)
        flags = flag_ref[depth_brick + 1]
        spread = jnp.concatenate(
            [jnp.broadcast_to(flags[r : r + 1], (4, COLS, width)) for r in range(1, 5)], axis=0
        )
        value = (value + own) * spread[None]
        coarse_ref[rows] = value.reshape(4 * SIDE * COLS, width).astype(jnp.bfloat16)
        half = low_half((4, 2, COLS, width))
        for r in range(4):
            part = value[:, r * 4 : (r + 1) * 4].reshape(4, 2, 2, COLS, width)
            even, odd = part[:, :, 0], part[:, :, 1]
            b0 = jnp.where(half, even, pltpu.roll(odd, 4, 2))
            b1 = jnp.where(half, pltpu.roll(even, 4, 2), odd)
            slot = ((depth_brick // 2) * 2 + r // 2) * 8 + (depth_brick % 2) * 4 + (r % 2) * 2
            for k, brick in enumerate((b0, b1)):
                source = source_ref[slot + k]

                @pl.when(source >= 0)
                def _():
                    place, first = brick_place(rotated, base_ref, source)
                    back_ref[place, pl.ds(first, CELLS), :] = brick.reshape(CELLS, width).astype(
                        jnp.bfloat16
                    )


def conv_call(base, source, block, before, after, under, over, w_first, w_second, rotated):
    mid = block.shape[1]
    smem = pl.BlockSpec(memory_space=pltpu.SMEM)
    vmem = pl.BlockSpec(memory_space=pltpu.VMEM)
    return pl.pallas_call(
        functools.partial(conv_kernel, rotated),
        in_specs=[smem, smem] + [vmem] * 7,
        out_specs=[vmem] * 2,
        out_shape=[
            jax.ShapeDtypeStruct(block.shape, jnp.bfloat16),
            jax.ShapeDtypeStruct((K, CAP * CELLS, mid), jnp.bfloat16),
        ],
        scratch_shapes=[
            pltpu.VMEM((WIDE, WIDE * COLS, mid), jnp.bfloat16),
            pltpu.VMEM((WIDE, WIDE * COLS, mid), jnp.bfloat16),
            pltpu.VMEM((HID, HID * COLS, mid), jnp.bfloat16),
            pltpu.VMEM((HID, HID * COLS, mid), jnp.bfloat16),
            pltpu.VMEM((6, 6, COLS, mid), jnp.float32),
            pltpu.VMEM((9 * mid, 3 * mid), jnp.bfloat16),
            pltpu.VMEM((9 * mid, 3 * mid), jnp.bfloat16),
        ],
        compiler_params=pltpu.CompilerParams(vmem_limit_bytes=VMEM_LIMIT),
        name="conv",
    )(base, source, block, before, after, under, over, w_first, w_second)


def from_behind(value, axis, steps):
    count = lax.axis_size(axis)
    pairs = [(source, (source + steps) % count) for source in range(count)]
    return lax.ppermute(value, axis, pairs)


def exchange(value, rotated, sign):
    if rotated:
        return lax.all_to_all(value, "xy", 0, 0, tiled=True)
    return jnp.stack([from_behind(value[j], "xy", sign * j) for j in range(K)])


def neighbours(low, high, axis):
    count = lax.axis_size(axis)
    forward = [(i, i + 1) for i in range(count - 1)]
    backward = [(target, source) for source, target in forward]
    return lax.ppermute(high, axis, forward), lax.ppermute(low, axis, backward)


def shards(fine, fine_mask, slot_source, w_down, w_first, w_second, w_up):
    rotated = lax.axis_size("xy") == K
    mid = w_down.shape[1]
    base = lax.axis_index("xy").astype(jnp.int32).reshape(1)
    sent = down_call(base, fine, fine_mask, w_down, rotated)
    arrived = exchange(sent, rotated, 1)
    block, low, high = place_call(base, slot_source, arrived, rotated)
    before, after = neighbours(low, high, "xy")
    under_send, over_send = edge_call(slot_source, block, before, after)
    under, over = neighbours(under_send, over_send, "gz")
    coarse, back = conv_call(
        base,
        slot_source,
        block,
        before,
        after,
        under,
        over,
        w_first,
        w_second,
        rotated,
    )
    octant = exchange(back, rotated, -1)
    fine_out = up_call(base, fine, fine_mask, w_up, octant, rotated)
    return fine_out, coarse.reshape(SIDE, SIDE, COLS, mid)


def solution(mesh):
    placed = (
        P(("gz", "xy"), None, None),
        P(("gz", "xy"), None),
        P(("gz", "xy")),
        P(),
        P(),
        P(),
        P(),
    )
    return jax.shard_map(
        shards,
        mesh=mesh,
        in_specs=placed,
        out_specs=(P(("gz", "xy"), None, None), P("gz", "xy", None, None)),
        check_vma=False,
    )
```

```python
import functools

import jax
import jax.numpy as jnp
from jax import lax
from jax.experimental import pallas as pl
from jax.experimental.pallas import tpu as pltpu
from jax.sharding import PartitionSpec as P

CAP = 4
K = 8
CELLS = 64
SIDE = 16
COLS = 8
WIDE = SIDE + 4
HID = SIDE + 2
EARLY = ((1, 3), (4, 4), (8, 4))
LATE = ((12, 3),)
EARLY_PLANES = 11
LATE_PLANES = 3
DOWN_LIMIT = 62 * 1024 * 1024
VMEM_LIMIT = 24 * 1024 * 1024


def place_of(base, j, sign, rotated):
    if not rotated:
        return j
    return lax.rem(base + sign * j + K, K)


def expand_mask(mask):
    bricks = mask.shape[0]
    values = mask.astype(jnp.float32)
    cell = lax.broadcasted_iota(jnp.int32, (16, 128), 0)
    lane = lax.broadcasted_iota(jnp.int32, (16, 128), 1)
    chosen = (cell == lane // 8).astype(jnp.float32)
    parts = [
        values[:, t * 128 : (t + 1) * 128].reshape(bricks, 1, 128) * chosen[None] for t in range(4)
    ]
    spread = jnp.concatenate(parts, axis=1).reshape(bricks * CELLS, 128).astype(jnp.bfloat16)
    source = lax.broadcasted_iota(jnp.int32, (128, 512), 0)
    target = lax.broadcasted_iota(jnp.int32, (128, 512), 1)
    widen = ((source & 7) == (target >> 6)).astype(jnp.bfloat16)
    return jnp.dot(spread, widen, preferred_element_type=jnp.float32)


def down_kernel(rotated, base_ref, fine_hbm, mask_hbm, w_hbm, out_ref, fine_ref, mask_ref, w_ref, sems):
    parts = sems.shape[0] - 2
    step = fine_hbm.shape[0] // parts
    rows = CAP * CELLS
    first = [
        pltpu.make_async_copy(mask_hbm, mask_ref, sems.at[parts]),
        pltpu.make_async_copy(w_hbm, w_ref, sems.at[parts + 1]),
    ]
    chunks = [
        pltpu.make_async_copy(
            fine_hbm.at[pl.ds(part * step, step)], fine_ref.at[pl.ds(part * step, step)], sems.at[part]
        )
        for part in range(parts)
    ]
    for copy in first + chunks:
        copy.start()
    for copy in first:
        copy.wait()
    for part in range(parts):
        bricks = slice(part * step, (part + 1) * step)
        mask = expand_mask(mask_ref[bricks]).astype(jnp.bfloat16)
        chunks[part].wait()
        x = fine_ref[bricks].reshape(step * CELLS, -1) * mask
        y = jnp.dot(x, w_ref[...], preferred_element_type=jnp.float32).astype(jnp.bfloat16)
        for inner in range(step // CAP):
            j = part * (step // CAP) + inner
            out_ref[place_of(base_ref[0], j, 1, rotated)] = y[inner * rows : (inner + 1) * rows]


def down_call(base, fine, mask, w, rotated):
    bricks, cells, width = fine.shape
    mid = w.shape[1]
    parts = 4
    hbm = pl.BlockSpec(memory_space=pltpu.HBM)
    return pl.pallas_call(
        functools.partial(down_kernel, rotated),
        in_specs=[pl.BlockSpec(memory_space=pltpu.SMEM), hbm, hbm, hbm],
        out_specs=pl.BlockSpec(memory_space=pltpu.VMEM),
        out_shape=jax.ShapeDtypeStruct((K, CAP * cells, mid), jnp.bfloat16),
        scratch_shapes=[
            pltpu.VMEM(fine.shape, fine.dtype),
            pltpu.VMEM(mask.shape, mask.dtype),
            pltpu.VMEM(w.shape, w.dtype),
            pltpu.SemaphoreType.DMA((parts + 2,)),
        ],
        compiler_params=pltpu.CompilerParams(vmem_limit_bytes=DOWN_LIMIT),
        name="down",
    )(base, fine, mask, w)


def up_kernel(rotated, base_ref, fine_ref, mask_ref, w_ref, octant_ref, out_ref):
    step = pl.program_id(0)
    bricks, cells, width = fine_ref.shape
    mask = expand_mask(mask_ref[...])
    count = bricks // CAP
    parts = [
        octant_ref[place_of(base_ref[0], step * count + part, 1, rotated)] for part in range(count)
    ]
    octant = jnp.concatenate(parts, axis=0)
    up = jnp.dot(octant, w_ref[...], preferred_element_type=jnp.float32)
    fine = fine_ref[...].reshape(bricks * cells, width).astype(jnp.float32)
    out = jnp.where(mask > 0.5, fine + up, 0.0).astype(jnp.bfloat16)
    out_ref[...] = out.reshape(bricks, cells, width)


def up_call(base, fine, mask, w, octant, rotated):
    bricks, cells, width = fine.shape
    mid = w.shape[0]
    step = 8
    return pl.pallas_call(
        functools.partial(up_kernel, rotated),
        grid=(bricks // step,),
        in_specs=[
            pl.BlockSpec(memory_space=pltpu.SMEM),
            pl.BlockSpec((step, cells, width), lambda i: (i, 0, 0)),
            pl.BlockSpec((step, width), lambda i: (i, 0)),
            pl.BlockSpec((mid, width), lambda i: (0, 0)),
            pl.BlockSpec((K, CAP * cells, mid), lambda i: (0, 0, 0)),
        ],
        out_specs=pl.BlockSpec((step, cells, width), lambda i: (i, 0, 0)),
        out_shape=jax.ShapeDtypeStruct(fine.shape, jnp.bfloat16),
        compiler_params=pltpu.CompilerParams(vmem_limit_bytes=VMEM_LIMIT),
        name="up",
    )(base, fine, mask, w, octant)


def low_half(shape):
    return lax.broadcasted_iota(jnp.int32, shape, len(shape) - 2) < 4


def slot_flags(source_ref, first):
    pair = [jnp.where(source_ref[first + k] >= 0, 1.0, 0.0).astype(jnp.float32) for k in range(2)]
    return jnp.where(low_half((8, 128)), pair[0], pair[1])


def slot_index(depth_brick, row_brick):
    pd, qd = divmod(depth_brick, 2)
    pr, qr = divmod(row_brick, 2)
    return (pd * 2 + pr) * 8 + qd * 4 + qr * 2


def brick_place(rotated, base_ref, value):
    j = value // CAP
    return place_of(base_ref[0], j, -1, rotated), pl.multiple_of((value % CAP) * CELLS, CELLS)


def take_brick(rotated, base_ref, source_ref, arrived_ref, slot):
    value = source_ref[slot]
    place, first = brick_place(rotated, base_ref, jnp.maximum(value, 0))
    brick = arrived_ref[place, pl.ds(first, CELLS), :].astype(jnp.float32)
    return jnp.where(value >= 0, brick, 0.0).reshape(8, 8, 128)


def place_kernel(rotated, base_ref, source_ref, arrived_ref, block_ref, low_ref, high_ref):
    half = low_half((8, 8, 128))
    for depth_brick in range(4):
        for row_brick in range(4):
            slot = slot_index(depth_brick, row_brick)
            b0 = take_brick(rotated, base_ref, source_ref, arrived_ref, slot)
            b1 = take_brick(rotated, base_ref, source_ref, arrived_ref, slot + 1)
            even = jnp.where(half, b0, pltpu.roll(b1, 4, 1))
            odd = jnp.where(half, pltpu.roll(b0, 4, 1), b1)
            both = jnp.stack([even, odd], axis=1).reshape(4, 32, 128).astype(jnp.bfloat16)
            for vd in range(4):
                row = ((depth_brick * 4 + vd) * SIDE + row_brick * 4) * COLS
                block_ref[row : row + 32] = both[vd]
                place = (depth_brick * 4 + vd) * 16
                if row_brick == 0:
                    low_ref[place : place + 16] = both[vd, :16]
                if row_brick == 3:
                    high_ref[place : place + 16] = both[vd, 16:]
    for row_brick, ref in ((0, low_ref), (3, high_ref)):
        flags = [slot_flags(source_ref, slot_index(d, row_brick)) for d in range(4)]
        ref[256:288] = jnp.concatenate(flags, axis=0).astype(jnp.bfloat16)


def place_call(base, source, arrived, rotated):
    mid = arrived.shape[2]
    smem = pl.BlockSpec(memory_space=pltpu.SMEM)
    vmem = pl.BlockSpec(memory_space=pltpu.VMEM)
    return pl.pallas_call(
        functools.partial(place_kernel, rotated),
        in_specs=[smem, smem, vmem],
        out_specs=[vmem] * 3,
        out_shape=[
            jax.ShapeDtypeStruct((rows, mid), jnp.bfloat16)
            for rows in (SIDE * SIDE * COLS, 288, 288)
        ],
        compiler_params=pltpu.CompilerParams(vmem_limit_bytes=VMEM_LIMIT),
        name="place",
    )(base, source, arrived)


def edge_kernel(source_ref, block_ref, before_ref, after_ref, low_ref, high_ref):
    for ref, planes, brick in ((low_ref, (0, 1), 0), (high_ref, (SIDE - 2, SIDE - 1), 3)):
        for k, plane in enumerate(planes):
            start = k * WIDE * COLS
            ref[start : start + 16] = before_ref[plane * 16 : plane * 16 + 16]
            ref[start + 16 : start + 144] = block_ref[plane * 128 : plane * 128 + 128]
            ref[start + 144 : start + 160] = after_ref[plane * 16 : plane * 16 + 16]
        first = 256 + brick * 8
        flags = [before_ref[256:288].astype(jnp.float32)[brick * 8 : brick * 8 + 8]]
        flags += [slot_flags(source_ref, slot_index(brick, r)) for r in range(4)]
        flags += [after_ref[256:288].astype(jnp.float32)[brick * 8 : brick * 8 + 8]]
        ref[320:368] = jnp.concatenate(flags, axis=0).astype(jnp.bfloat16)


def edge_call(source, block, before, after):
    smem = pl.BlockSpec(memory_space=pltpu.SMEM)
    vmem = pl.BlockSpec(memory_space=pltpu.VMEM)
    return pl.pallas_call(
        edge_kernel,
        in_specs=[smem, vmem, vmem, vmem],
        out_specs=[vmem] * 2,
        out_shape=[jax.ShapeDtypeStruct((368, block.shape[1]), jnp.bfloat16)] * 2,
        compiler_params=pltpu.CompilerParams(vmem_limit_bytes=VMEM_LIMIT),
        name="edge",
    )(source, block, before, after)


def gather_weights(w_ref, wide_ref):
    width = w_ref.shape[2]
    for tap in range(9):
        for column in range(3):
            wide_ref[tap * width : (tap + 1) * width, column * width : (column + 1) * width] = (
                w_ref[tap * 3 + column]
            )


def as_rows(value):
    value = value.astype(jnp.float32)
    return value.reshape(value.shape[0] // COLS, COLS, value.shape[1])


def moved_rows(rows):
    empty = jnp.zeros((1,) + rows.shape[1:], jnp.float32)
    return jnp.concatenate([rows[1:], empty], axis=0)


def as_tiles(rows):
    return rows.reshape(rows.shape[0] * COLS, rows.shape[2]).astype(jnp.bfloat16)


def multiply_taps(lhs, wide_ref):
    width = wide_ref.shape[1] // 3
    wide = jnp.dot(lhs, wide_ref[...], preferred_element_type=jnp.float32)
    wide = wide.reshape(lhs.shape[0] // COLS, COLS, 3 * width)
    column = lax.broadcasted_iota(jnp.int32, (lhs.shape[0] // COLS, COLS, width), 1)
    left = jnp.where(column == 0, 0.0, pltpu.roll(wide[:, :, :width], 1, 1))
    right = jnp.where(column == COLS - 1, 0.0, pltpu.roll(wide[:, :, 2 * width :], COLS - 1, 1))
    return left + wide[:, :, width : 2 * width] + right


def conv_planes(here_ref, next_ref, wide_ref, first, planes, rows):
    taps = []
    for dd in range(3):
        span = slice(first + dd, first + dd + planes)
        taps += [
            here_ref[span, 0:rows, :],
            next_ref[span, 0:rows, :],
            here_ref[span, 16 : rows + 16, :],
        ]
    lhs = jnp.concatenate(taps, axis=2)
    return multiply_taps(lhs.reshape(planes * rows, lhs.shape[2]), wide_ref)


def activate(value, flags):
    return value / (1.0 + jnp.exp(-value)) * flags


def spread_flags(flags, repeats):
    return jnp.concatenate(
        [jnp.broadcast_to(flag[None], (count,) + flag.shape) for flag, count in zip(flags, repeats)],
        axis=0,
    )


def inner_planes(source_ref, block_ref, wide1_ref, hidden_ref, here, moved, groups):
    width = block_ref.shape[1]
    base = groups[0][0] - 1
    for d in range(base, groups[-1][0] + groups[-1][1] + 1):
        plane = block_ref[d * 128 : (d + 1) * 128]
        here[d - base] = plane
        moved[d - base] = as_tiles(moved_rows(as_rows(plane)))
    inner = SIDE - 2
    rows = inner * COLS
    for first, planes in groups:
        value = conv_planes(here, moved, wide1_ref, first - 1 - base, planes, rows)
        value = value.reshape(planes, inner, COLS, width)
        flags = [slot_flags(source_ref, slot_index(first // 4, r)) for r in range(4)]
        value = activate(value, spread_flags(flags, (3, 4, 4, 3))[None])
        hidden_ref[first - 1 - base : first - 1 - base + planes] = value.reshape(
            planes, rows, width
        ).astype(jnp.bfloat16)


def inner_kernel(source_ref, block_ref, w1_ref, hidden_ref, wide1_ref, here, moved):
    gather_weights(w1_ref, wide1_ref)
    inner_planes(source_ref, block_ref, wide1_ref, hidden_ref, here, moved, EARLY)


def conv_cost(rows, width):
    return pl.CostEstimate(
        flops=2 * rows * 27 * width * width, bytes_accessed=27 * width * width * 4, transcendentals=0
    )


def inner_call(source, block, w_first):
    mid = block.shape[1]
    smem = pl.BlockSpec(memory_space=pltpu.SMEM)
    vmem = pl.BlockSpec(memory_space=pltpu.VMEM)
    rows = (SIDE - 2) * COLS
    return pl.pallas_call(
        inner_kernel,
        in_specs=[smem, vmem, vmem],
        out_specs=[vmem] * 2,
        out_shape=[
            jax.ShapeDtypeStruct((EARLY_PLANES, rows, mid), jnp.bfloat16),
            jax.ShapeDtypeStruct((9 * mid, 3 * mid), jnp.bfloat16),
        ],
        scratch_shapes=[pltpu.VMEM((EARLY_PLANES + 2, SIDE * COLS, mid), jnp.bfloat16)] * 2,
        compiler_params=pltpu.CompilerParams(vmem_limit_bytes=VMEM_LIMIT),
        cost_estimate=conv_cost(EARLY_PLANES * rows, mid),
        name="inner",
    )(source, block, w_first)


def side_kernel(
    source_ref,
    block_ref,
    before_ref,
    after_ref,
    wide1_ref,
    w2_ref,
    hidden_ref,
    late_ref,
    wide2_ref,
    mixed,
    here,
    moved,
):
    gather_weights(w2_ref, wide2_ref)
    inner_planes(source_ref, block_ref, wide1_ref, late_ref, here, moved, LATE)
    width = block_ref.shape[1]
    for d in range(SIDE):
        edge = slice(d * 16, (d + 1) * 16)
        low = as_rows(block_ref[d * 128 : d * 128 + 16])
        high = as_rows(block_ref[d * 128 + 112 : d * 128 + 128])
        before = as_rows(before_ref[edge])
        after = as_rows(after_ref[edge])
        mixed[0, edge] = as_tiles(jnp.concatenate([before[1:], low[:1]], axis=0))
        mixed[1, edge] = as_tiles(jnp.concatenate([high[1:], after[:1]], axis=0))
    inner = SIDE - 2
    taps = []
    for dd in range(3):
        span = slice(dd * 16, (dd + inner) * 16)
        low = [block_ref[(d + dd) * 128 : (d + dd) * 128 + 16] for d in range(inner)]
        high = [block_ref[(d + dd) * 128 + 112 : (d + dd) * 128 + 128] for d in range(inner)]
        taps.append(jnp.concatenate([before_ref[span]] + high, axis=0))
        taps.append(jnp.concatenate([mixed[0, span], mixed[1, span]], axis=0))
        taps.append(jnp.concatenate(low + [after_ref[span]], axis=0))
    value = multiply_taps(jnp.concatenate(taps, axis=1), wide1_ref)
    depths = (3, 4, 4, 3)
    edge_flags = (as_rows(before_ref[256:288]), as_rows(after_ref[256:288]))
    flags = []
    for side, row_brick in ((0, 0), (1, 3)):
        own = [slot_flags(source_ref, slot_index(d, row_brick)) for d in range(4)]
        pairs = [jnp.stack([edge_flags[side][d], own[d]][:: 1 - 2 * side], axis=0) for d in range(4)]
        flags.append(spread_flags(pairs, depths))
    flags = jnp.stack(flags, axis=0)
    value = activate(value.reshape(2, inner, 2, COLS, width), flags)
    hidden_ref[...] = value.reshape(2, inner, 16, width).astype(jnp.bfloat16)


def side_call(source, block, before, after, wide1, w_second):
    mid = block.shape[1]
    smem = pl.BlockSpec(memory_space=pltpu.SMEM)
    vmem = pl.BlockSpec(memory_space=pltpu.VMEM)
    inner = SIDE - 2
    return pl.pallas_call(
        side_kernel,
        in_specs=[smem] + [vmem] * 5,
        out_specs=[vmem] * 3,
        out_shape=[
            jax.ShapeDtypeStruct((2, inner, 16, mid), jnp.bfloat16),
            jax.ShapeDtypeStruct((LATE_PLANES, inner * COLS, mid), jnp.bfloat16),
            jax.ShapeDtypeStruct((9 * mid, 3 * mid), jnp.bfloat16),
        ],
        scratch_shapes=[
            pltpu.VMEM((2, SIDE * 16, mid), jnp.bfloat16),
            pltpu.VMEM((LATE_PLANES + 2, SIDE * COLS, mid), jnp.bfloat16),
            pltpu.VMEM((LATE_PLANES + 2, SIDE * COLS, mid), jnp.bfloat16),
        ],
        compiler_params=pltpu.CompilerParams(vmem_limit_bytes=VMEM_LIMIT),
        cost_estimate=conv_cost(inner * (4 + LATE_PLANES) * COLS, mid),
        name="side",
    )(source, block, before, after, wide1, w_second)


def final_kernel(
    rotated,
    base_ref,
    source_ref,
    block_ref,
    before_ref,
    after_ref,
    under_ref,
    over_ref,
    early_ref,
    late_ref,
    side_ref,
    wide1_ref,
    wide2_ref,
    coarse_ref,
    back_ref,
    x_here,
    x_next,
    h_here,
    h_next,
    stage,
):
    width = block_ref.shape[1]
    flags_before = as_rows(before_ref[256:288])
    flags_after = as_rows(after_ref[256:288])
    for end, ref in ((0, under_ref), (1, over_ref)):
        planes = []
        own = [0, 1] if end == 0 else [SIDE - 2, SIDE - 1]
        for d in own:
            edge = slice(d * 16, (d + 1) * 16)
            planes.append(
                jnp.concatenate(
                    [before_ref[edge], block_ref[d * 128 : (d + 1) * 128], after_ref[edge]], axis=0
                )
            )
        far = [ref[k * 160 : (k + 1) * 160] for k in range(2)]
        for index, plane in enumerate(far + planes if end == 0 else planes + far):
            x_here[index] = plane
            x_next[index] = as_tiles(moved_rows(as_rows(plane)))
        value = conv_planes(x_here, x_next, wide1_ref, 0, 2, HID * COLS)
        value = value.reshape(2, HID, COLS, width)
        far_flags = as_rows(ref[320:368])
        brick = 0 if end == 0 else 3
        own_flags = [flags_before[brick]]
        own_flags += [slot_flags(source_ref, slot_index(brick, r)) for r in range(4)]
        own_flags += [flags_after[brick]]
        spread = [
            spread_flags([far_flags[r] for r in range(6)], (1, 4, 4, 4, 4, 1)),
            spread_flags(own_flags, (1, 4, 4, 4, 4, 1)),
        ]
        for k in range(2):
            flags = spread[k if end == 0 else 1 - k]
            rows = activate(value[k], flags)
            index = k if end == 0 else HID - 2 + k
            h_here[index] = as_tiles(rows)
            h_next[index] = as_tiles(moved_rows(rows))
    for d in range(SIDE - 2):
        middle = early_ref[d] if d < EARLY_PLANES else late_ref[d - EARLY_PLANES]
        plane = jnp.concatenate([side_ref[0, d], middle, side_ref[1, d]], axis=0)
        h_here[d + 2] = plane
        h_next[d + 2] = as_tiles(moved_rows(as_rows(plane)))

    stage[...] = jnp.zeros(stage.shape, jnp.bfloat16)
    for depth_brick in range(4):
        value = conv_planes(h_here, h_next, wide2_ref, depth_brick * 4, 4, SIDE * COLS)
        value = value.reshape(4, SIDE, COLS, width)
        rows = slice(depth_brick * 512, (depth_brick + 1) * 512)
        own = block_ref[rows].astype(jnp.float32).reshape(4, SIDE, COLS, width)
        flags = [slot_flags(source_ref, slot_index(depth_brick, r)) for r in range(4)]
        value = (value + own) * spread_flags(flags, (4, 4, 4, 4))[None]
        coarse_ref[rows] = value.reshape(4 * SIDE * COLS, width).astype(jnp.bfloat16)
        half = low_half((4, 2, COLS, width))
        for r in range(4):
            part = value[:, r * 4 : (r + 1) * 4].reshape(4, 2, 2, COLS, width)
            even, odd = part[:, :, 0], part[:, :, 1]
            b0 = jnp.where(half, even, pltpu.roll(odd, 4, 2))
            b1 = jnp.where(half, pltpu.roll(even, 4, 2), odd)
            slot = slot_index(depth_brick, r)
            for k, brick in enumerate((b0, b1)):
                source = source_ref[slot + k]
                place, first = brick_place(rotated, base_ref, jnp.maximum(source, 0))
                row = jnp.where(source >= 0, place * CAP * CELLS + first, K * CAP * CELLS)
                row = pl.multiple_of(row, CELLS)
                stage[pl.ds(row, CELLS), :] = brick.reshape(CELLS, width).astype(jnp.bfloat16)
    for place in range(K):
        back_ref[place] = stage[place * CAP * CELLS : (place + 1) * CAP * CELLS]


def final_call(base, source, block, halo, hidden, wide1, wide2, rotated):
    mid = block.shape[1]
    smem = pl.BlockSpec(memory_space=pltpu.SMEM)
    vmem = pl.BlockSpec(memory_space=pltpu.VMEM)
    return pl.pallas_call(
        functools.partial(final_kernel, rotated),
        in_specs=[smem, smem] + [vmem] * 10,
        out_specs=[vmem] * 2,
        out_shape=[
            jax.ShapeDtypeStruct(block.shape, jnp.bfloat16),
            jax.ShapeDtypeStruct((K, CAP * CELLS, mid), jnp.bfloat16),
        ],
        scratch_shapes=[
            pltpu.VMEM((4, WIDE * COLS, mid), jnp.bfloat16),
            pltpu.VMEM((4, WIDE * COLS, mid), jnp.bfloat16),
            pltpu.VMEM((HID, HID * COLS, mid), jnp.bfloat16),
            pltpu.VMEM((HID, HID * COLS, mid), jnp.bfloat16),
            pltpu.VMEM(((K * CAP + 1) * CELLS, mid), jnp.bfloat16),
        ],
        compiler_params=pltpu.CompilerParams(vmem_limit_bytes=VMEM_LIMIT),
        cost_estimate=conv_cost(SIDE * SIDE * COLS, mid),
        name="final",
    )(base, source, block, *halo, *hidden, wide1, wide2)


def from_behind(value, axis, steps):
    count = lax.axis_size(axis)
    pairs = [(source, (source + steps) % count) for source in range(count)]
    return lax.ppermute(value, axis, pairs)


def exchange(value, rotated, sign):
    if rotated:
        return lax.all_to_all(value, "xy", 0, 0, tiled=True)
    return jnp.stack([from_behind(value[j], "xy", sign * j) for j in range(K)])


def neighbours(low, high, axis):
    count = lax.axis_size(axis)
    forward = [(i, i + 1) for i in range(count - 1)]
    backward = [(target, source) for source, target in forward]
    return lax.ppermute(high, axis, forward), lax.ppermute(low, axis, backward)


def shards(fine, fine_mask, slot_source, w_down, w_first, w_second, w_up):
    rotated = lax.axis_size("xy") == K
    mid = w_down.shape[1]
    base = lax.axis_index("xy").astype(jnp.int32).reshape(1)
    sent = down_call(base, fine, fine_mask, w_down, rotated)
    arrived = exchange(sent, rotated, 1)
    block, low, high = place_call(base, slot_source, arrived, rotated)
    before, after = neighbours(low, high, "xy")
    early, wide1 = inner_call(slot_source, block, w_first)
    before, after, early, wide1 = lax.optimization_barrier((before, after, early, wide1))
    under_send, over_send = edge_call(slot_source, block, before, after)
    under, over = neighbours(under_send, over_send, "gz")
    side, late, wide2 = side_call(slot_source, block, before, after, wide1, w_second)
    coarse, back = final_call(
        base,
        slot_source,
        block,
        (before, after, under, over),
        (early, late, side),
        wide1,
        wide2,
        rotated,
    )
    octant = exchange(back, rotated, -1)
    fine_out = up_call(base, fine, fine_mask, w_up, octant, rotated)
    return fine_out, coarse.reshape(SIDE, SIDE, COLS, mid)


def solution(mesh):
    placed = (
        P(("gz", "xy"), None, None),
        P(("gz", "xy"), None),
        P(("gz", "xy")),
        P(),
        P(),
        P(),
        P(),
    )
    return jax.shard_map(
        shards,
        mesh=mesh,
        in_specs=placed,
        out_specs=(P(("gz", "xy"), None, None), P("gz", "xy", None, None)),
        check_vma=False,
    )
```

```python
import functools

import jax
import jax.numpy as jnp
from jax import lax
from jax.experimental import pallas as pl
from jax.experimental.pallas import tpu as pltpu
from jax.sharding import PartitionSpec as P

CAP = 4
K = 8
CELLS = 64
SIDE = 16
COLS = 8
WIDE = SIDE + 4
HID = SIDE + 2
EARLY = ((1, 3), (4, 4), (8, 4))
LATE = ((12, 3),)
EARLY_PLANES = 11
LATE_PLANES = 3
DOWN_LIMIT = 62 * 1024 * 1024
VMEM_LIMIT = 24 * 1024 * 1024


def place_of(base, j, sign, rotated):
    if not rotated:
        return j
    return lax.rem(base + sign * j + K, K)


def expand_mask(mask):
    bricks = mask.shape[0]
    values = mask.astype(jnp.float32)
    cell = lax.broadcasted_iota(jnp.int32, (16, 128), 0)
    lane = lax.broadcasted_iota(jnp.int32, (16, 128), 1)
    chosen = (cell == lane // 8).astype(jnp.float32)
    parts = [
        values[:, t * 128 : (t + 1) * 128].reshape(bricks, 1, 128) * chosen[None] for t in range(4)
    ]
    spread = jnp.concatenate(parts, axis=1).reshape(bricks * CELLS, 128).astype(jnp.bfloat16)
    source = lax.broadcasted_iota(jnp.int32, (128, 512), 0)
    target = lax.broadcasted_iota(jnp.int32, (128, 512), 1)
    widen = ((source & 7) == (target >> 6)).astype(jnp.bfloat16)
    return jnp.dot(spread, widen, preferred_element_type=jnp.float32)


def down_kernel(rotated, base_ref, fine_hbm, mask_hbm, w_hbm, out_ref, fine_ref, mask_ref, w_ref, sems):
    parts = sems.shape[0] - 2
    step = fine_hbm.shape[0] // parts
    rows = CAP * CELLS
    first = [
        pltpu.make_async_copy(mask_hbm, mask_ref, sems.at[parts]),
        pltpu.make_async_copy(w_hbm, w_ref, sems.at[parts + 1]),
    ]
    chunks = [
        pltpu.make_async_copy(
            fine_hbm.at[pl.ds(part * step, step)], fine_ref.at[pl.ds(part * step, step)], sems.at[part]
        )
        for part in range(parts)
    ]
    for copy in first + chunks:
        copy.start()
    for copy in first:
        copy.wait()
    for part in range(parts):
        bricks = slice(part * step, (part + 1) * step)
        mask = expand_mask(mask_ref[bricks]).astype(jnp.bfloat16)
        chunks[part].wait()
        x = fine_ref[bricks].reshape(step * CELLS, -1) * mask
        y = jnp.dot(x, w_ref[...], preferred_element_type=jnp.float32).astype(jnp.bfloat16)
        for inner in range(step // CAP):
            j = part * (step // CAP) + inner
            out_ref[place_of(base_ref[0], j, 1, rotated)] = y[inner * rows : (inner + 1) * rows]


def down_call(base, fine, mask, w, rotated):
    bricks, cells, width = fine.shape
    mid = w.shape[1]
    parts = 4
    hbm = pl.BlockSpec(memory_space=pltpu.HBM)
    return pl.pallas_call(
        functools.partial(down_kernel, rotated),
        in_specs=[pl.BlockSpec(memory_space=pltpu.SMEM), hbm, hbm, hbm],
        out_specs=pl.BlockSpec(memory_space=pltpu.VMEM),
        out_shape=jax.ShapeDtypeStruct((K, CAP * cells, mid), jnp.bfloat16),
        scratch_shapes=[
            pltpu.VMEM(fine.shape, fine.dtype),
            pltpu.VMEM(mask.shape, mask.dtype),
            pltpu.VMEM(w.shape, w.dtype),
            pltpu.SemaphoreType.DMA((parts + 2,)),
        ],
        compiler_params=pltpu.CompilerParams(vmem_limit_bytes=DOWN_LIMIT),
        name="down",
    )(base, fine, mask, w)


def up_kernel(rotated, base_ref, fine_ref, mask_ref, w_ref, octant_ref, out_ref):
    step = pl.program_id(0)
    bricks, cells, width = fine_ref.shape
    mask = expand_mask(mask_ref[...])
    count = bricks // CAP
    parts = [
        octant_ref[place_of(base_ref[0], step * count + part, 1, rotated)] for part in range(count)
    ]
    octant = jnp.concatenate(parts, axis=0)
    up = jnp.dot(octant, w_ref[...], preferred_element_type=jnp.float32)
    fine = fine_ref[...].reshape(bricks * cells, width).astype(jnp.float32)
    out = jnp.where(mask > 0.5, fine + up, 0.0).astype(jnp.bfloat16)
    out_ref[...] = out.reshape(bricks, cells, width)


def up_call(base, fine, mask, w, octant, rotated):
    bricks, cells, width = fine.shape
    mid = w.shape[0]
    step = 8
    return pl.pallas_call(
        functools.partial(up_kernel, rotated),
        grid=(bricks // step,),
        in_specs=[
            pl.BlockSpec(memory_space=pltpu.SMEM),
            pl.BlockSpec((step, cells, width), lambda i: (i, 0, 0)),
            pl.BlockSpec((step, width), lambda i: (i, 0)),
            pl.BlockSpec((mid, width), lambda i: (0, 0)),
            pl.BlockSpec((K, CAP * cells, mid), lambda i: (0, 0, 0)),
        ],
        out_specs=pl.BlockSpec((step, cells, width), lambda i: (i, 0, 0)),
        out_shape=jax.ShapeDtypeStruct(fine.shape, jnp.bfloat16),
        compiler_params=pltpu.CompilerParams(vmem_limit_bytes=VMEM_LIMIT),
        name="up",
    )(base, fine, mask, w, octant)


def low_half(shape):
    return lax.broadcasted_iota(jnp.int32, shape, len(shape) - 2) < 4


def slot_flags(source_ref, first):
    pair = [jnp.where(source_ref[first + k] >= 0, 1.0, 0.0).astype(jnp.float32) for k in range(2)]
    return jnp.where(low_half((8, 128)), pair[0], pair[1])


def slot_index(depth_brick, row_brick):
    pd, qd = divmod(depth_brick, 2)
    pr, qr = divmod(row_brick, 2)
    return (pd * 2 + pr) * 8 + qd * 4 + qr * 2


def brick_place(rotated, base_ref, value):
    j = value // CAP
    return place_of(base_ref[0], j, -1, rotated), pl.multiple_of((value % CAP) * CELLS, CELLS)


def take_brick(rotated, base_ref, source_ref, arrived_ref, slot):
    value = source_ref[slot]
    place, first = brick_place(rotated, base_ref, jnp.maximum(value, 0))
    brick = arrived_ref[place, pl.ds(first, CELLS), :].astype(jnp.float32)
    return jnp.where(value >= 0, brick, 0.0).reshape(8, 8, 128)


def place_kernel(
    rotated, base_ref, source_ref, arrived_ref, block_ref, even_ref, odd_ref, low_ref, high_ref
):
    half = low_half((8, 8, 128))
    for depth_brick in range(4):
        for row_brick in range(4):
            slot = slot_index(depth_brick, row_brick)
            b0 = take_brick(rotated, base_ref, source_ref, arrived_ref, slot)
            b1 = take_brick(rotated, base_ref, source_ref, arrived_ref, slot + 1)
            even = jnp.where(half, b0, pltpu.roll(b1, 4, 1))
            odd = jnp.where(half, pltpu.roll(b0, 4, 1), b1)
            both = jnp.stack([even, odd], axis=1).reshape(4, 32, 128).astype(jnp.bfloat16)
            for vd in range(4):
                row = ((depth_brick * 4 + vd) * SIDE + row_brick * 4) * COLS
                block_ref[row : row + 32] = both[vd]
                place = (depth_brick * 4 + vd) * 16
                if row_brick == 0:
                    low_ref[place : place + 16] = both[vd, :16]
                if row_brick == 3:
                    high_ref[place : place + 16] = both[vd, 16:]
    for row_brick, ref in ((0, low_ref), (3, high_ref)):
        flags = [slot_flags(source_ref, slot_index(d, row_brick)) for d in range(4)]
        ref[256:288] = jnp.concatenate(flags, axis=0).astype(jnp.bfloat16)
    face_out(base_ref[0], low_ref, high_ref, even_ref, odd_ref)


def face_out(index, low_ref, high_ref, even_ref, odd_ref):
    is_even = index % 2 == 0

    @pl.when(is_even)
    def _():
        even_ref[...] = high_ref[...]
        odd_ref[...] = low_ref[...]

    @pl.when(jnp.logical_not(is_even))
    def _():
        even_ref[...] = low_ref[...]
        odd_ref[...] = high_ref[...]


def face_in(index, count, even_ref, odd_ref, low_ref, high_ref):
    is_even = index % 2 == 0

    @pl.when(is_even)
    def _():
        low_ref[...] = odd_ref[0]
        high_ref[...] = even_ref[1]

    @pl.when(jnp.logical_not(is_even))
    def _():
        low_ref[...] = even_ref[0]
        high_ref[...] = odd_ref[1]

    @pl.when(index == 0)
    def _():
        low_ref[...] = jnp.zeros(low_ref.shape, low_ref.dtype)

    @pl.when(index == count - 1)
    def _():
        high_ref[...] = jnp.zeros(high_ref.shape, high_ref.dtype)


def place_call(base, source, arrived, rotated):
    mid = arrived.shape[2]
    smem = pl.BlockSpec(memory_space=pltpu.SMEM)
    vmem = pl.BlockSpec(memory_space=pltpu.VMEM)
    return pl.pallas_call(
        functools.partial(place_kernel, rotated),
        in_specs=[smem, smem, vmem],
        out_specs=[vmem] * 3,
        out_shape=[
            jax.ShapeDtypeStruct((rows, mid), jnp.bfloat16)
            for rows in (SIDE * SIDE * COLS, 288, 288)
        ],
        scratch_shapes=[pltpu.VMEM((288, mid), jnp.bfloat16)] * 2,
        compiler_params=pltpu.CompilerParams(vmem_limit_bytes=VMEM_LIMIT),
        name="place",
    )(base, source, arrived)


def edge_kernel(
    counts,
    base_ref,
    source_ref,
    block_ref,
    even_ref,
    odd_ref,
    before_ref,
    after_ref,
    even_out,
    odd_out,
    low_ref,
    high_ref,
):
    face_in(base_ref[0], counts[1], even_ref, odd_ref, before_ref, after_ref)
    for ref, planes, brick in ((low_ref, (0, 1), 0), (high_ref, (SIDE - 2, SIDE - 1), 3)):
        for k, plane in enumerate(planes):
            start = k * WIDE * COLS
            ref[start : start + 16] = before_ref[plane * 16 : plane * 16 + 16]
            ref[start + 16 : start + 144] = block_ref[plane * 128 : plane * 128 + 128]
            ref[start + 144 : start + 160] = after_ref[plane * 16 : plane * 16 + 16]
        flags = [before_ref[256:288].astype(jnp.float32)[brick * 8 : brick * 8 + 8]]
        flags += [slot_flags(source_ref, slot_index(brick, r)) for r in range(4)]
        flags += [after_ref[256:288].astype(jnp.float32)[brick * 8 : brick * 8 + 8]]
        ref[320:368] = jnp.concatenate(flags, axis=0).astype(jnp.bfloat16)
    face_out(base_ref[1], low_ref, high_ref, even_out, odd_out)


def edge_call(counts, base, source, block, even, odd):
    smem = pl.BlockSpec(memory_space=pltpu.SMEM)
    vmem = pl.BlockSpec(memory_space=pltpu.VMEM)
    mid = block.shape[1]
    return pl.pallas_call(
        functools.partial(edge_kernel, counts),
        in_specs=[smem, smem, vmem, vmem, vmem],
        out_specs=[vmem] * 4,
        out_shape=[
            jax.ShapeDtypeStruct((rows, mid), jnp.bfloat16) for rows in (288, 288, 368, 368)
        ],
        scratch_shapes=[pltpu.VMEM((368, mid), jnp.bfloat16)] * 2,
        compiler_params=pltpu.CompilerParams(vmem_limit_bytes=VMEM_LIMIT),
        name="edge",
    )(base, source, block, even, odd)


def gather_weights(w_ref, wide_ref):
    width = w_ref.shape[2]
    for tap in range(9):
        for column in range(3):
            wide_ref[tap * width : (tap + 1) * width, column * width : (column + 1) * width] = (
                w_ref[tap * 3 + column]
            )


def as_rows(value):
    value = value.astype(jnp.float32)
    return value.reshape(value.shape[0] // COLS, COLS, value.shape[1])


def moved_rows(rows):
    empty = jnp.zeros((1,) + rows.shape[1:], jnp.float32)
    return jnp.concatenate([rows[1:], empty], axis=0)


def as_tiles(rows):
    return rows.reshape(rows.shape[0] * COLS, rows.shape[2]).astype(jnp.bfloat16)


def multiply_taps(lhs, wide_ref):
    width = wide_ref.shape[1] // 3
    wide = jnp.dot(lhs, wide_ref[...], preferred_element_type=jnp.float32)
    wide = wide.reshape(lhs.shape[0] // COLS, COLS, 3 * width)
    column = lax.broadcasted_iota(jnp.int32, (lhs.shape[0] // COLS, COLS, width), 1)
    left = jnp.where(column == 0, 0.0, pltpu.roll(wide[:, :, :width], 1, 1))
    right = jnp.where(column == COLS - 1, 0.0, pltpu.roll(wide[:, :, 2 * width :], COLS - 1, 1))
    return left + wide[:, :, width : 2 * width] + right


def conv_planes(here_ref, next_ref, wide_ref, first, planes, rows):
    taps = []
    for dd in range(3):
        span = slice(first + dd, first + dd + planes)
        taps += [
            here_ref[span, 0:rows, :],
            next_ref[span, 0:rows, :],
            here_ref[span, 16 : rows + 16, :],
        ]
    lhs = jnp.concatenate(taps, axis=2)
    return multiply_taps(lhs.reshape(planes * rows, lhs.shape[2]), wide_ref)


def activate(value, flags):
    return value / (1.0 + jnp.exp(-value)) * flags


def spread_flags(flags, repeats):
    return jnp.concatenate(
        [jnp.broadcast_to(flag[None], (count,) + flag.shape) for flag, count in zip(flags, repeats)],
        axis=0,
    )


def inner_planes(source_ref, block_ref, wide1_ref, hidden_ref, here, moved, groups):
    width = block_ref.shape[1]
    base = groups[0][0] - 1
    for d in range(base, groups[-1][0] + groups[-1][1] + 1):
        plane = block_ref[d * 128 : (d + 1) * 128]
        here[d - base] = plane
        moved[d - base] = as_tiles(moved_rows(as_rows(plane)))
    inner = SIDE - 2
    rows = inner * COLS
    for first, planes in groups:
        value = conv_planes(here, moved, wide1_ref, first - 1 - base, planes, rows)
        value = value.reshape(planes, inner, COLS, width)
        flags = [slot_flags(source_ref, slot_index(first // 4, r)) for r in range(4)]
        value = activate(value, spread_flags(flags, (3, 4, 4, 3))[None])
        hidden_ref[first - 1 - base : first - 1 - base + planes] = value.reshape(
            planes, rows, width
        ).astype(jnp.bfloat16)


def inner_kernel(source_ref, block_ref, w1_ref, hidden_ref, wide1_ref, here, moved):
    gather_weights(w1_ref, wide1_ref)
    inner_planes(source_ref, block_ref, wide1_ref, hidden_ref, here, moved, EARLY)


def conv_cost(rows, width):
    return pl.CostEstimate(
        flops=2 * rows * 27 * width * width, bytes_accessed=27 * width * width * 4, transcendentals=0
    )


def inner_call(source, block, w_first):
    mid = block.shape[1]
    smem = pl.BlockSpec(memory_space=pltpu.SMEM)
    vmem = pl.BlockSpec(memory_space=pltpu.VMEM)
    rows = (SIDE - 2) * COLS
    return pl.pallas_call(
        inner_kernel,
        in_specs=[smem, vmem, vmem],
        out_specs=[vmem] * 2,
        out_shape=[
            jax.ShapeDtypeStruct((EARLY_PLANES, rows, mid), jnp.bfloat16),
            jax.ShapeDtypeStruct((9 * mid, 3 * mid), jnp.bfloat16),
        ],
        scratch_shapes=[pltpu.VMEM((EARLY_PLANES + 2, SIDE * COLS, mid), jnp.bfloat16)] * 2,
        compiler_params=pltpu.CompilerParams(vmem_limit_bytes=VMEM_LIMIT),
        cost_estimate=conv_cost(EARLY_PLANES * rows, mid),
        name="inner",
    )(source, block, w_first)


def side_kernel(
    source_ref,
    block_ref,
    before_ref,
    after_ref,
    wide1_ref,
    w2_ref,
    hidden_ref,
    late_ref,
    wide2_ref,
    mixed,
    here,
    moved,
):
    gather_weights(w2_ref, wide2_ref)
    inner_planes(source_ref, block_ref, wide1_ref, late_ref, here, moved, LATE)
    width = block_ref.shape[1]
    for d in range(SIDE):
        edge = slice(d * 16, (d + 1) * 16)
        low = as_rows(block_ref[d * 128 : d * 128 + 16])
        high = as_rows(block_ref[d * 128 + 112 : d * 128 + 128])
        before = as_rows(before_ref[edge])
        after = as_rows(after_ref[edge])
        mixed[0, edge] = as_tiles(jnp.concatenate([before[1:], low[:1]], axis=0))
        mixed[1, edge] = as_tiles(jnp.concatenate([high[1:], after[:1]], axis=0))
    inner = SIDE - 2
    taps = []
    for dd in range(3):
        span = slice(dd * 16, (dd + inner) * 16)
        low = [block_ref[(d + dd) * 128 : (d + dd) * 128 + 16] for d in range(inner)]
        high = [block_ref[(d + dd) * 128 + 112 : (d + dd) * 128 + 128] for d in range(inner)]
        taps.append(jnp.concatenate([before_ref[span]] + high, axis=0))
        taps.append(jnp.concatenate([mixed[0, span], mixed[1, span]], axis=0))
        taps.append(jnp.concatenate(low + [after_ref[span]], axis=0))
    value = multiply_taps(jnp.concatenate(taps, axis=1), wide1_ref)
    depths = (3, 4, 4, 3)
    edge_flags = (as_rows(before_ref[256:288]), as_rows(after_ref[256:288]))
    flags = []
    for side, row_brick in ((0, 0), (1, 3)):
        own = [slot_flags(source_ref, slot_index(d, row_brick)) for d in range(4)]
        pairs = [jnp.stack([edge_flags[side][d], own[d]][:: 1 - 2 * side], axis=0) for d in range(4)]
        flags.append(spread_flags(pairs, depths))
    flags = jnp.stack(flags, axis=0)
    value = activate(value.reshape(2, inner, 2, COLS, width), flags)
    hidden_ref[...] = value.reshape(2, inner, 16, width).astype(jnp.bfloat16)


def side_call(source, block, before, after, wide1, w_second):
    mid = block.shape[1]
    smem = pl.BlockSpec(memory_space=pltpu.SMEM)
    vmem = pl.BlockSpec(memory_space=pltpu.VMEM)
    inner = SIDE - 2
    return pl.pallas_call(
        side_kernel,
        in_specs=[smem] + [vmem] * 5,
        out_specs=[vmem] * 3,
        out_shape=[
            jax.ShapeDtypeStruct((2, inner, 16, mid), jnp.bfloat16),
            jax.ShapeDtypeStruct((LATE_PLANES, inner * COLS, mid), jnp.bfloat16),
            jax.ShapeDtypeStruct((9 * mid, 3 * mid), jnp.bfloat16),
        ],
        scratch_shapes=[
            pltpu.VMEM((2, SIDE * 16, mid), jnp.bfloat16),
            pltpu.VMEM((LATE_PLANES + 2, SIDE * COLS, mid), jnp.bfloat16),
            pltpu.VMEM((LATE_PLANES + 2, SIDE * COLS, mid), jnp.bfloat16),
        ],
        compiler_params=pltpu.CompilerParams(vmem_limit_bytes=VMEM_LIMIT),
        cost_estimate=conv_cost(inner * (4 + LATE_PLANES) * COLS, mid),
        name="side",
    )(source, block, before, after, wide1, w_second)


def final_kernel(
    rotated,
    counts,
    base_ref,
    source_ref,
    block_ref,
    before_ref,
    after_ref,
    even_ref,
    odd_ref,
    early_ref,
    late_ref,
    side_ref,
    wide1_ref,
    wide2_ref,
    coarse_ref,
    back_ref,
    x_here,
    x_next,
    h_here,
    h_next,
    stage,
    under_ref,
    over_ref,
):
    width = block_ref.shape[1]
    face_in(base_ref[1], counts[0], even_ref, odd_ref, under_ref, over_ref)
    flags_before = as_rows(before_ref[256:288])
    flags_after = as_rows(after_ref[256:288])
    for end, ref in ((0, under_ref), (1, over_ref)):
        planes = []
        own = [0, 1] if end == 0 else [SIDE - 2, SIDE - 1]
        for d in own:
            edge = slice(d * 16, (d + 1) * 16)
            planes.append(
                jnp.concatenate(
                    [before_ref[edge], block_ref[d * 128 : (d + 1) * 128], after_ref[edge]], axis=0
                )
            )
        far = [ref[k * 160 : (k + 1) * 160] for k in range(2)]
        for index, plane in enumerate(far + planes if end == 0 else planes + far):
            x_here[index] = plane
            x_next[index] = as_tiles(moved_rows(as_rows(plane)))
        value = conv_planes(x_here, x_next, wide1_ref, 0, 2, HID * COLS)
        value = value.reshape(2, HID, COLS, width)
        far_flags = as_rows(ref[320:368])
        brick = 0 if end == 0 else 3
        own_flags = [flags_before[brick]]
        own_flags += [slot_flags(source_ref, slot_index(brick, r)) for r in range(4)]
        own_flags += [flags_after[brick]]
        spread = [
            spread_flags([far_flags[r] for r in range(6)], (1, 4, 4, 4, 4, 1)),
            spread_flags(own_flags, (1, 4, 4, 4, 4, 1)),
        ]
        for k in range(2):
            flags = spread[k if end == 0 else 1 - k]
            rows = activate(value[k], flags)
            index = k if end == 0 else HID - 2 + k
            h_here[index] = as_tiles(rows)
            h_next[index] = as_tiles(moved_rows(rows))
    for d in range(SIDE - 2):
        middle = early_ref[d] if d < EARLY_PLANES else late_ref[d - EARLY_PLANES]
        plane = jnp.concatenate([side_ref[0, d], middle, side_ref[1, d]], axis=0)
        h_here[d + 2] = plane
        h_next[d + 2] = as_tiles(moved_rows(as_rows(plane)))

    stage[...] = jnp.zeros(stage.shape, jnp.bfloat16)
    for depth_brick in range(4):
        value = conv_planes(h_here, h_next, wide2_ref, depth_brick * 4, 4, SIDE * COLS)
        value = value.reshape(4, SIDE, COLS, width)
        rows = slice(depth_brick * 512, (depth_brick + 1) * 512)
        own = block_ref[rows].astype(jnp.float32).reshape(4, SIDE, COLS, width)
        flags = [slot_flags(source_ref, slot_index(depth_brick, r)) for r in range(4)]
        value = (value + own) * spread_flags(flags, (4, 4, 4, 4))[None]
        coarse_ref[rows] = value.reshape(4 * SIDE * COLS, width).astype(jnp.bfloat16)
        half = low_half((4, 2, COLS, width))
        for r in range(4):
            part = value[:, r * 4 : (r + 1) * 4].reshape(4, 2, 2, COLS, width)
            even, odd = part[:, :, 0], part[:, :, 1]
            b0 = jnp.where(half, even, pltpu.roll(odd, 4, 2))
            b1 = jnp.where(half, pltpu.roll(even, 4, 2), odd)
            slot = slot_index(depth_brick, r)
            for k, brick in enumerate((b0, b1)):
                source = source_ref[slot + k]
                place, first = brick_place(rotated, base_ref, jnp.maximum(source, 0))
                row = jnp.where(source >= 0, place * CAP * CELLS + first, K * CAP * CELLS)
                row = pl.multiple_of(row, CELLS)
                stage[pl.ds(row, CELLS), :] = brick.reshape(CELLS, width).astype(jnp.bfloat16)
    for place in range(K):
        back_ref[place] = stage[place * CAP * CELLS : (place + 1) * CAP * CELLS]


def final_call(counts, base, source, block, halo, hidden, wide1, wide2, rotated):
    mid = block.shape[1]
    smem = pl.BlockSpec(memory_space=pltpu.SMEM)
    vmem = pl.BlockSpec(memory_space=pltpu.VMEM)
    return pl.pallas_call(
        functools.partial(final_kernel, rotated, counts),
        in_specs=[smem, smem] + [vmem] * 10,
        out_specs=[vmem] * 2,
        out_shape=[
            jax.ShapeDtypeStruct(block.shape, jnp.bfloat16),
            jax.ShapeDtypeStruct((K, CAP * CELLS, mid), jnp.bfloat16),
        ],
        scratch_shapes=[
            pltpu.VMEM((4, WIDE * COLS, mid), jnp.bfloat16),
            pltpu.VMEM((4, WIDE * COLS, mid), jnp.bfloat16),
            pltpu.VMEM((HID, HID * COLS, mid), jnp.bfloat16),
            pltpu.VMEM((HID, HID * COLS, mid), jnp.bfloat16),
            pltpu.VMEM(((K * CAP + 1) * CELLS, mid), jnp.bfloat16),
            pltpu.VMEM((368, mid), jnp.bfloat16),
            pltpu.VMEM((368, mid), jnp.bfloat16),
        ],
        compiler_params=pltpu.CompilerParams(vmem_limit_bytes=VMEM_LIMIT),
        cost_estimate=conv_cost(SIDE * SIDE * COLS, mid),
        name="final",
    )(base, source, block, *halo, *hidden, wide1, wide2)


def from_behind(value, axis, steps):
    count = lax.axis_size(axis)
    pairs = [(source, (source + steps) % count) for source in range(count)]
    return lax.ppermute(value, axis, pairs)


def exchange(value, rotated, sign):
    if rotated:
        return lax.all_to_all(value, "xy", 0, 0, tiled=True)
    return jnp.stack([from_behind(value[j], "xy", sign * j) for j in range(K)])


def pair_faces(even, odd, axis):
    count = lax.axis_size(axis)
    firsts = [[i, i + 1] for i in range(0, count, 2)]
    seconds = [[i, (i + 1) % count] for i in range(1, count, 2)]
    return (
        lax.all_gather(even, axis, axis_index_groups=firsts),
        lax.all_gather(odd, axis, axis_index_groups=seconds),
    )


def shards(fine, fine_mask, slot_source, w_down, w_first, w_second, w_up):
    rotated = lax.axis_size("xy") == K
    mid = w_down.shape[1]
    base = jnp.stack([lax.axis_index("xy"), lax.axis_index("gz")]).astype(jnp.int32)
    counts = (lax.axis_size("gz"), lax.axis_size("xy"))
    sent = down_call(base, fine, fine_mask, w_down, rotated)
    arrived = exchange(sent, rotated, 1)
    block, even, odd = place_call(base, slot_source, arrived, rotated)
    even, odd = pair_faces(even, odd, "xy")
    early, wide1 = inner_call(slot_source, block, w_first)
    even, odd, early, wide1 = lax.optimization_barrier((even, odd, early, wide1))
    before, after, even, odd = edge_call(counts, base, slot_source, block, even, odd)
    even, odd = pair_faces(even, odd, "gz")
    side, late, wide2 = side_call(slot_source, block, before, after, wide1, w_second)
    coarse, back = final_call(
        counts,
        base,
        slot_source,
        block,
        (before, after, even, odd),
        (early, late, side),
        wide1,
        wide2,
        rotated,
    )
    octant = exchange(back, rotated, -1)
    fine_out = up_call(base, fine, fine_mask, w_up, octant, rotated)
    return fine_out, coarse.reshape(SIDE, SIDE, COLS, mid)


def solution(mesh):
    placed = (
        P(("gz", "xy"), None, None),
        P(("gz", "xy"), None),
        P(("gz", "xy")),
        P(),
        P(),
        P(),
        P(),
    )
    return jax.shard_map(
        shards,
        mesh=mesh,
        in_specs=placed,
        out_specs=(P(("gz", "xy"), None, None), P("gz", "xy", None, None)),
        check_vma=False,
    )
```

```python
import functools

import jax
import jax.numpy as jnp
from jax import lax
from jax.experimental import pallas as pl
from jax.experimental.pallas import tpu as pltpu
from jax.sharding import PartitionSpec as P

CAP = 4
K = 8
CELLS = 64
SIDE = 16
COLS = 8
WIDE = SIDE + 4
HID = SIDE + 2
EARLY = ((1, 3), (4, 4), (8, 4))
LATE = ((12, 3),)
EARLY_PLANES = 11
LATE_PLANES = 3
FIRST_SENT = (4, 3, 5)
LAST_SENT = (2, 6, 1, 7, 0)
UP_OFFSETS = 4
DOWN_LIMIT = 62 * 1024 * 1024
VMEM_LIMIT = 24 * 1024 * 1024


def expand_mask(mask):
    bricks = mask.shape[0]
    values = mask.astype(jnp.float32)
    cell = lax.broadcasted_iota(jnp.int32, (16, 128), 0)
    lane = lax.broadcasted_iota(jnp.int32, (16, 128), 1)
    chosen = (cell == lane // 8).astype(jnp.float32)
    parts = [
        values[:, t * 128 : (t + 1) * 128].reshape(bricks, 1, 128) * chosen[None] for t in range(4)
    ]
    spread = jnp.concatenate(parts, axis=1).reshape(bricks * CELLS, 128).astype(jnp.bfloat16)
    source = lax.broadcasted_iota(jnp.int32, (128, 512), 0)
    target = lax.broadcasted_iota(jnp.int32, (128, 512), 1)
    widen = ((source & 7) == (target >> 6)).astype(jnp.bfloat16)
    return jnp.dot(spread, widen, preferred_element_type=jnp.float32)


def down_kernel(offsets, fine_hbm, mask_hbm, w_hbm, *refs):
    outs = refs[: len(offsets)]
    fine_ref, mask_ref, w_ref, sems = refs[len(offsets) :]
    count = len(offsets)
    first = [
        pltpu.make_async_copy(mask_hbm, mask_ref, sems.at[count]),
        pltpu.make_async_copy(w_hbm, w_ref, sems.at[count + 1]),
    ]
    chunks = [
        pltpu.make_async_copy(fine_hbm.at[pl.ds(j * CAP, CAP)], fine_ref.at[k], sems.at[k])
        for k, j in enumerate(offsets)
    ]
    for copy in first + chunks:
        copy.start()
    for copy in first:
        copy.wait()
    for k, j in enumerate(offsets):
        mask = expand_mask(mask_ref[j * CAP : (j + 1) * CAP]).astype(jnp.bfloat16)
        chunks[k].wait()
        x = fine_ref[k].reshape(CAP * CELLS, -1) * mask
        y = jnp.dot(x, w_ref[...], preferred_element_type=jnp.float32)
        outs[k][...] = y.astype(jnp.bfloat16)


def down_call(fine, mask, w, offsets):
    cells, width = fine.shape[1:]
    mid = w.shape[1]
    count = len(offsets)
    hbm = pl.BlockSpec(memory_space=pltpu.HBM)
    rows = count * CAP * cells
    outs = pl.pallas_call(
        functools.partial(down_kernel, offsets),
        in_specs=[hbm, hbm, hbm],
        out_specs=[pl.BlockSpec(memory_space=pltpu.VMEM)] * count,
        out_shape=[jax.ShapeDtypeStruct((CAP * cells, mid), jnp.bfloat16)] * count,
        scratch_shapes=[
            pltpu.VMEM((count, CAP, cells, width), fine.dtype),
            pltpu.VMEM(mask.shape, mask.dtype),
            pltpu.VMEM(w.shape, w.dtype),
            pltpu.SemaphoreType.DMA((count + 2,)),
        ],
        compiler_params=pltpu.CompilerParams(vmem_limit_bytes=DOWN_LIMIT),
        cost_estimate=pl.CostEstimate(
            flops=2 * rows * width * mid, bytes_accessed=rows * width * 2, transcendentals=0
        ),
        name="down",
    )(fine, mask, w)
    return dict(zip(offsets, outs))


def up_kernel(fine_ref, mask_ref, w_ref, *refs):
    out_ref = refs[-1]
    step = pl.program_id(0)
    bricks, cells, width = fine_ref.shape
    mask = expand_mask(mask_ref[...])
    count = bricks // CAP
    steps = UP_OFFSETS // count
    for part in range(count):
        octant = refs[part][...]
        for other in range(1, steps):
            octant = jnp.where(step == other, refs[other * count + part][...], octant)
        rows = slice(part * CAP * cells, (part + 1) * CAP * cells)
        up = jnp.dot(octant, w_ref[...], preferred_element_type=jnp.float32)
        fine = fine_ref[part * CAP : (part + 1) * CAP].reshape(CAP * cells, width)
        out = jnp.where(mask[rows] > 0.5, fine.astype(jnp.float32) + up, 0.0)
        out_ref[part * CAP : (part + 1) * CAP] = out.astype(jnp.bfloat16).reshape(CAP, cells, width)


def up_call(fine, mask, w, octants, first, partial):
    bricks, cells, width = fine.shape
    mid = w.shape[0]
    step = 8
    blocks = bricks // step

    def place(i):
        return (first + i) % blocks

    partials = [] if partial is None else [partial]
    return pl.pallas_call(
        up_kernel,
        grid=(UP_OFFSETS * CAP // step,),
        in_specs=[
            pl.BlockSpec((step, cells, width), lambda i: (place(i), 0, 0)),
            pl.BlockSpec((step, width), lambda i: (place(i), 0)),
            pl.BlockSpec((mid, width), lambda i: (0, 0)),
        ]
        + [pl.BlockSpec((CAP * cells, mid), lambda i: (0, 0))] * UP_OFFSETS
        + [pl.BlockSpec(memory_space=pl.ANY)] * len(partials),
        out_specs=pl.BlockSpec((step, cells, width), lambda i: (place(i), 0, 0)),
        out_shape=jax.ShapeDtypeStruct(fine.shape, jnp.bfloat16),
        input_output_aliases={3 + UP_OFFSETS: 0} if partials else {},
        compiler_params=pltpu.CompilerParams(vmem_limit_bytes=VMEM_LIMIT),
        cost_estimate=pl.CostEstimate(
            flops=bricks * cells * width * mid, bytes_accessed=bricks * cells * width * 2, transcendentals=0
        ),
        name="up",
    )(fine, mask, w, *octants, *partials)


def low_half(shape):
    return lax.broadcasted_iota(jnp.int32, shape, len(shape) - 2) < 4


def slot_flags(source_ref, first):
    pair = [jnp.where(source_ref[first + k] >= 0, 1.0, 0.0).astype(jnp.float32) for k in range(2)]
    return jnp.where(low_half((8, 128)), pair[0], pair[1])


def slot_index(depth_brick, row_brick):
    pd, qd = divmod(depth_brick, 2)
    pr, qr = divmod(row_brick, 2)
    return (pd * 2 + pr) * 8 + qd * 4 + qr * 2


def take_brick(source_ref, arrived, slot):
    value = source_ref[slot]
    first = pl.multiple_of(jnp.maximum(value, 0) * CELLS, CELLS)
    brick = arrived[pl.ds(first, CELLS), :].astype(jnp.float32)
    return jnp.where(value >= 0, brick, 0.0).reshape(8, 8, 128)


def place_kernel(source_ref, *refs):
    block_ref, low_ref, high_ref, arrived = refs[K:]
    for j in range(K):
        arrived[j * CAP * CELLS : (j + 1) * CAP * CELLS] = refs[j][...]
    half = low_half((8, 8, 128))
    for depth_brick in range(4):
        for row_brick in range(4):
            slot = slot_index(depth_brick, row_brick)
            b0 = take_brick(source_ref, arrived, slot)
            b1 = take_brick(source_ref, arrived, slot + 1)
            even = jnp.where(half, b0, pltpu.roll(b1, 4, 1))
            odd = jnp.where(half, pltpu.roll(b0, 4, 1), b1)
            both = jnp.stack([even, odd], axis=1).reshape(4, 32, 128).astype(jnp.bfloat16)
            for vd in range(4):
                row = ((depth_brick * 4 + vd) * SIDE + row_brick * 4) * COLS
                block_ref[row : row + 32] = both[vd]
                place = (depth_brick * 4 + vd) * 16
                if row_brick == 0:
                    low_ref[place : place + 16] = both[vd, :16]
                if row_brick == 3:
                    high_ref[place : place + 16] = both[vd, 16:]
    for row_brick, ref in ((0, low_ref), (3, high_ref)):
        flags = [slot_flags(source_ref, slot_index(d, row_brick)) for d in range(4)]
        ref[256:288] = jnp.concatenate(flags, axis=0).astype(jnp.bfloat16)


def place_call(source, arrived):
    mid = arrived[0].shape[1]
    smem = pl.BlockSpec(memory_space=pltpu.SMEM)
    vmem = pl.BlockSpec(memory_space=pltpu.VMEM)
    return pl.pallas_call(
        place_kernel,
        in_specs=[smem] + [vmem] * K,
        out_specs=[vmem] * 3,
        out_shape=[
            jax.ShapeDtypeStruct((rows, mid), jnp.bfloat16)
            for rows in (SIDE * SIDE * COLS, 288, 288)
        ],
        scratch_shapes=[pltpu.VMEM((K * CAP * CELLS, mid), jnp.bfloat16)],
        compiler_params=pltpu.CompilerParams(vmem_limit_bytes=VMEM_LIMIT),
        name="place",
    )(source, *arrived)


def edge_kernel(source_ref, block_ref, before_ref, after_ref, low_ref, high_ref):
    for ref, planes, brick in ((low_ref, (0, 1), 0), (high_ref, (SIDE - 2, SIDE - 1), 3)):
        for k, plane in enumerate(planes):
            start = k * WIDE * COLS
            ref[start : start + 16] = before_ref[plane * 16 : plane * 16 + 16]
            ref[start + 16 : start + 144] = block_ref[plane * 128 : plane * 128 + 128]
            ref[start + 144 : start + 160] = after_ref[plane * 16 : plane * 16 + 16]
        first = 256 + brick * 8
        flags = [before_ref[256:288].astype(jnp.float32)[brick * 8 : brick * 8 + 8]]
        flags += [slot_flags(source_ref, slot_index(brick, r)) for r in range(4)]
        flags += [after_ref[256:288].astype(jnp.float32)[brick * 8 : brick * 8 + 8]]
        ref[320:368] = jnp.concatenate(flags, axis=0).astype(jnp.bfloat16)


def edge_call(source, block, before, after):
    smem = pl.BlockSpec(memory_space=pltpu.SMEM)
    vmem = pl.BlockSpec(memory_space=pltpu.VMEM)
    return pl.pallas_call(
        edge_kernel,
        in_specs=[smem, vmem, vmem, vmem],
        out_specs=[vmem] * 2,
        out_shape=[jax.ShapeDtypeStruct((368, block.shape[1]), jnp.bfloat16)] * 2,
        compiler_params=pltpu.CompilerParams(vmem_limit_bytes=VMEM_LIMIT),
        name="edge",
    )(source, block, before, after)


def gather_weights(w_ref, wide_ref):
    width = w_ref.shape[2]
    for tap in range(9):
        for column in range(3):
            wide_ref[tap * width : (tap + 1) * width, column * width : (column + 1) * width] = (
                w_ref[tap * 3 + column]
            )


def as_rows(value):
    value = value.astype(jnp.float32)
    return value.reshape(value.shape[0] // COLS, COLS, value.shape[1])


def moved_rows(rows):
    empty = jnp.zeros((1,) + rows.shape[1:], jnp.float32)
    return jnp.concatenate([rows[1:], empty], axis=0)


def as_tiles(rows):
    return rows.reshape(rows.shape[0] * COLS, rows.shape[2]).astype(jnp.bfloat16)


def multiply_taps(lhs, wide_ref):
    width = wide_ref.shape[1] // 3
    wide = jnp.dot(lhs, wide_ref[...], preferred_element_type=jnp.float32)
    wide = wide.reshape(lhs.shape[0] // COLS, COLS, 3 * width)
    column = lax.broadcasted_iota(jnp.int32, (lhs.shape[0] // COLS, COLS, width), 1)
    left = jnp.where(column == 0, 0.0, pltpu.roll(wide[:, :, :width], 1, 1))
    right = jnp.where(column == COLS - 1, 0.0, pltpu.roll(wide[:, :, 2 * width :], COLS - 1, 1))
    return left + wide[:, :, width : 2 * width] + right


def conv_planes(here_ref, next_ref, wide_ref, first, planes, rows):
    taps = []
    for dd in range(3):
        span = slice(first + dd, first + dd + planes)
        taps += [
            here_ref[span, 0:rows, :],
            next_ref[span, 0:rows, :],
            here_ref[span, 16 : rows + 16, :],
        ]
    lhs = jnp.concatenate(taps, axis=2)
    return multiply_taps(lhs.reshape(planes * rows, lhs.shape[2]), wide_ref)


def activate(value, flags):
    return value / (1.0 + jnp.exp(-value)) * flags


def spread_flags(flags, repeats):
    return jnp.concatenate(
        [jnp.broadcast_to(flag[None], (count,) + flag.shape) for flag, count in zip(flags, repeats)],
        axis=0,
    )


def inner_planes(source_ref, block_ref, wide1_ref, hidden_ref, here, moved, groups):
    width = block_ref.shape[1]
    base = groups[0][0] - 1
    for d in range(base, groups[-1][0] + groups[-1][1] + 1):
        plane = block_ref[d * 128 : (d + 1) * 128]
        here[d - base] = plane
        moved[d - base] = as_tiles(moved_rows(as_rows(plane)))
    inner = SIDE - 2
    rows = inner * COLS
    for first, planes in groups:
        value = conv_planes(here, moved, wide1_ref, first - 1 - base, planes, rows)
        value = value.reshape(planes, inner, COLS, width)
        flags = [slot_flags(source_ref, slot_index(first // 4, r)) for r in range(4)]
        value = activate(value, spread_flags(flags, (3, 4, 4, 3))[None])
        hidden_ref[first - 1 - base : first - 1 - base + planes] = value.reshape(
            planes, rows, width
        ).astype(jnp.bfloat16)


def inner_kernel(source_ref, block_ref, w1_ref, hidden_ref, wide1_ref, here, moved):
    gather_weights(w1_ref, wide1_ref)
    inner_planes(source_ref, block_ref, wide1_ref, hidden_ref, here, moved, EARLY)


def conv_cost(rows, width):
    return pl.CostEstimate(
        flops=2 * rows * 27 * width * width, bytes_accessed=27 * width * width * 4, transcendentals=0
    )


def inner_call(source, block, w_first):
    mid = block.shape[1]
    smem = pl.BlockSpec(memory_space=pltpu.SMEM)
    vmem = pl.BlockSpec(memory_space=pltpu.VMEM)
    rows = (SIDE - 2) * COLS
    return pl.pallas_call(
        inner_kernel,
        in_specs=[smem, vmem, vmem],
        out_specs=[vmem] * 2,
        out_shape=[
            jax.ShapeDtypeStruct((EARLY_PLANES, rows, mid), jnp.bfloat16),
            jax.ShapeDtypeStruct((9 * mid, 3 * mid), jnp.bfloat16),
        ],
        scratch_shapes=[pltpu.VMEM((EARLY_PLANES + 2, SIDE * COLS, mid), jnp.bfloat16)] * 2,
        compiler_params=pltpu.CompilerParams(vmem_limit_bytes=VMEM_LIMIT),
        cost_estimate=conv_cost(EARLY_PLANES * rows, mid),
        name="inner",
    )(source, block, w_first)


def side_kernel(
    source_ref,
    block_ref,
    before_ref,
    after_ref,
    wide1_ref,
    w2_ref,
    hidden_ref,
    late_ref,
    wide2_ref,
    mixed,
    here,
    moved,
):
    gather_weights(w2_ref, wide2_ref)
    inner_planes(source_ref, block_ref, wide1_ref, late_ref, here, moved, LATE)
    width = block_ref.shape[1]
    for d in range(SIDE):
        edge = slice(d * 16, (d + 1) * 16)
        low = as_rows(block_ref[d * 128 : d * 128 + 16])
        high = as_rows(block_ref[d * 128 + 112 : d * 128 + 128])
        before = as_rows(before_ref[edge])
        after = as_rows(after_ref[edge])
        mixed[0, edge] = as_tiles(jnp.concatenate([before[1:], low[:1]], axis=0))
        mixed[1, edge] = as_tiles(jnp.concatenate([high[1:], after[:1]], axis=0))
    inner = SIDE - 2
    taps = []
    for dd in range(3):
        span = slice(dd * 16, (dd + inner) * 16)
        low = [block_ref[(d + dd) * 128 : (d + dd) * 128 + 16] for d in range(inner)]
        high = [block_ref[(d + dd) * 128 + 112 : (d + dd) * 128 + 128] for d in range(inner)]
        taps.append(jnp.concatenate([before_ref[span]] + high, axis=0))
        taps.append(jnp.concatenate([mixed[0, span], mixed[1, span]], axis=0))
        taps.append(jnp.concatenate(low + [after_ref[span]], axis=0))
    value = multiply_taps(jnp.concatenate(taps, axis=1), wide1_ref)
    depths = (3, 4, 4, 3)
    edge_flags = (as_rows(before_ref[256:288]), as_rows(after_ref[256:288]))
    flags = []
    for side, row_brick in ((0, 0), (1, 3)):
        own = [slot_flags(source_ref, slot_index(d, row_brick)) for d in range(4)]
        pairs = [jnp.stack([edge_flags[side][d], own[d]][:: 1 - 2 * side], axis=0) for d in range(4)]
        flags.append(spread_flags(pairs, depths))
    flags = jnp.stack(flags, axis=0)
    value = activate(value.reshape(2, inner, 2, COLS, width), flags)
    hidden_ref[...] = value.reshape(2, inner, 16, width).astype(jnp.bfloat16)


def side_call(source, block, before, after, wide1, w_second):
    mid = block.shape[1]
    smem = pl.BlockSpec(memory_space=pltpu.SMEM)
    vmem = pl.BlockSpec(memory_space=pltpu.VMEM)
    inner = SIDE - 2
    return pl.pallas_call(
        side_kernel,
        in_specs=[smem] + [vmem] * 5,
        out_specs=[vmem] * 3,
        out_shape=[
            jax.ShapeDtypeStruct((2, inner, 16, mid), jnp.bfloat16),
            jax.ShapeDtypeStruct((LATE_PLANES, inner * COLS, mid), jnp.bfloat16),
            jax.ShapeDtypeStruct((9 * mid, 3 * mid), jnp.bfloat16),
        ],
        scratch_shapes=[
            pltpu.VMEM((2, SIDE * 16, mid), jnp.bfloat16),
            pltpu.VMEM((LATE_PLANES + 2, SIDE * COLS, mid), jnp.bfloat16),
            pltpu.VMEM((LATE_PLANES + 2, SIDE * COLS, mid), jnp.bfloat16),
        ],
        compiler_params=pltpu.CompilerParams(vmem_limit_bytes=VMEM_LIMIT),
        cost_estimate=conv_cost(inner * (4 + LATE_PLANES) * COLS, mid),
        name="side",
    )(source, block, before, after, wide1, w_second)


def final_kernel(source_ref, *refs):
    block_ref, before_ref, after_ref, under_ref, over_ref = refs[:5]
    early_ref, late_ref, side_ref, wide1_ref, wide2_ref, coarse_ref = refs[5:11]
    backs = refs[11 : 11 + K]
    x_here, x_next, h_here, h_next, stage = refs[11 + K :]
    width = block_ref.shape[1]
    flags_before = as_rows(before_ref[256:288])
    flags_after = as_rows(after_ref[256:288])
    for end, ref in ((0, under_ref), (1, over_ref)):
        planes = []
        own = [0, 1] if end == 0 else [SIDE - 2, SIDE - 1]
        for d in own:
            edge = slice(d * 16, (d + 1) * 16)
            planes.append(
                jnp.concatenate(
                    [before_ref[edge], block_ref[d * 128 : (d + 1) * 128], after_ref[edge]], axis=0
                )
            )
        far = [ref[k * 160 : (k + 1) * 160] for k in range(2)]
        for index, plane in enumerate(far + planes if end == 0 else planes + far):
            x_here[index] = plane
            x_next[index] = as_tiles(moved_rows(as_rows(plane)))
        value = conv_planes(x_here, x_next, wide1_ref, 0, 2, HID * COLS)
        value = value.reshape(2, HID, COLS, width)
        far_flags = as_rows(ref[320:368])
        brick = 0 if end == 0 else 3
        own_flags = [flags_before[brick]]
        own_flags += [slot_flags(source_ref, slot_index(brick, r)) for r in range(4)]
        own_flags += [flags_after[brick]]
        spread = [
            spread_flags([far_flags[r] for r in range(6)], (1, 4, 4, 4, 4, 1)),
            spread_flags(own_flags, (1, 4, 4, 4, 4, 1)),
        ]
        for k in range(2):
            flags = spread[k if end == 0 else 1 - k]
            rows = activate(value[k], flags)
            index = k if end == 0 else HID - 2 + k
            h_here[index] = as_tiles(rows)
            h_next[index] = as_tiles(moved_rows(rows))
    for d in range(SIDE - 2):
        middle = early_ref[d] if d < EARLY_PLANES else late_ref[d - EARLY_PLANES]
        plane = jnp.concatenate([side_ref[0, d], middle, side_ref[1, d]], axis=0)
        h_here[d + 2] = plane
        h_next[d + 2] = as_tiles(moved_rows(as_rows(plane)))

    stage[...] = jnp.zeros(stage.shape, jnp.bfloat16)
    for depth_brick in range(4):
        value = conv_planes(h_here, h_next, wide2_ref, depth_brick * 4, 4, SIDE * COLS)
        value = value.reshape(4, SIDE, COLS, width)
        rows = slice(depth_brick * 512, (depth_brick + 1) * 512)
        own = block_ref[rows].astype(jnp.float32).reshape(4, SIDE, COLS, width)
        flags = [slot_flags(source_ref, slot_index(depth_brick, r)) for r in range(4)]
        value = (value + own) * spread_flags(flags, (4, 4, 4, 4))[None]
        coarse_ref[rows] = value.reshape(4 * SIDE * COLS, width).astype(jnp.bfloat16)
        half = low_half((4, 2, COLS, width))
        for r in range(4):
            part = value[:, r * 4 : (r + 1) * 4].reshape(4, 2, 2, COLS, width)
            even, odd = part[:, :, 0], part[:, :, 1]
            b0 = jnp.where(half, even, pltpu.roll(odd, 4, 2))
            b1 = jnp.where(half, pltpu.roll(even, 4, 2), odd)
            slot = slot_index(depth_brick, r)
            for k, brick in enumerate((b0, b1)):
                source = source_ref[slot + k]
                row = pl.multiple_of(jnp.where(source >= 0, source, K * CAP) * CELLS, CELLS)
                stage[pl.ds(row, CELLS), :] = brick.reshape(CELLS, width).astype(jnp.bfloat16)
    for j in range(K):
        backs[j][...] = stage[j * CAP * CELLS : (j + 1) * CAP * CELLS]


def final_call(source, block, halo, hidden, wide1, wide2):
    mid = block.shape[1]
    smem = pl.BlockSpec(memory_space=pltpu.SMEM)
    vmem = pl.BlockSpec(memory_space=pltpu.VMEM)
    return pl.pallas_call(
        final_kernel,
        in_specs=[smem] + [vmem] * 10,
        out_specs=[vmem] * (1 + K),
        out_shape=[
            jax.ShapeDtypeStruct(block.shape, jnp.bfloat16),
        ]
        + [jax.ShapeDtypeStruct((CAP * CELLS, mid), jnp.bfloat16)] * K,
        scratch_shapes=[
            pltpu.VMEM((4, WIDE * COLS, mid), jnp.bfloat16),
            pltpu.VMEM((4, WIDE * COLS, mid), jnp.bfloat16),
            pltpu.VMEM((HID, HID * COLS, mid), jnp.bfloat16),
            pltpu.VMEM((HID, HID * COLS, mid), jnp.bfloat16),
            pltpu.VMEM(((K * CAP + 1) * CELLS, mid), jnp.bfloat16),
        ],
        compiler_params=pltpu.CompilerParams(vmem_limit_bytes=VMEM_LIMIT),
        cost_estimate=conv_cost(SIDE * SIDE * COLS, mid),
        name="final",
    )(source, block, *halo, *hidden, wide1, wide2)


def from_behind(value, axis, steps):
    count = lax.axis_size(axis)
    pairs = [(source, (source + steps) % count) for source in range(count)]
    return lax.ppermute(value, axis, pairs)


def neighbours(low, high, axis):
    count = lax.axis_size(axis)
    forward = [(i, i + 1) for i in range(count - 1)]
    backward = [(target, source) for source, target in forward]
    return lax.ppermute(high, axis, forward), lax.ppermute(low, axis, backward)


def shards(fine, fine_mask, slot_source, w_down, w_first, w_second, w_up):
    mid = w_down.shape[1]
    sent = down_call(fine, fine_mask, w_down, FIRST_SENT)
    arrived = {j: from_behind(sent[j], "xy", j) for j in FIRST_SENT}
    sent = down_call(fine, fine_mask, w_down, LAST_SENT)
    arrived.update({j: from_behind(sent[j], "xy", j) for j in LAST_SENT if j})
    arrived[0] = sent[0]
    block, low, high = place_call(slot_source, [arrived[j] for j in range(K)])
    before, after = neighbours(low, high, "xy")
    early, wide1 = inner_call(slot_source, block, w_first)
    before, after, early, wide1 = lax.optimization_barrier((before, after, early, wide1))
    under_send, over_send = edge_call(slot_source, block, before, after)
    under, over = neighbours(under_send, over_send, "gz")
    side, late, wide2 = side_call(slot_source, block, before, after, wide1, w_second)
    coarse, *back = final_call(
        slot_source, block, (before, after, under, over), (early, late, side), wide1, wide2
    )
    octant = {j: from_behind(back[j], "xy", -j) for j in FIRST_SENT + LAST_SENT if j}
    octant[0] = back[0]
    fine_out = up_call(fine, fine_mask, w_up, [octant[j] for j in (2, 3, 4, 5)], 1, None)
    fine_out = up_call(fine, fine_mask, w_up, [octant[j] for j in (6, 7, 0, 1)], 3, fine_out)
    return fine_out, coarse.reshape(SIDE, SIDE, COLS, mid)


def solution(mesh):
    placed = (
        P(("gz", "xy"), None, None),
        P(("gz", "xy"), None),
        P(("gz", "xy")),
        P(),
        P(),
        P(),
        P(),
    )
    return jax.shard_map(
        shards,
        mesh=mesh,
        in_specs=placed,
        out_specs=(P(("gz", "xy"), None, None), P("gz", "xy", None, None)),
        check_vma=False,
    )
```

```python
import functools

import jax
import jax.numpy as jnp
from jax import lax
from jax.experimental import pallas as pl
from jax.experimental.pallas import tpu as pltpu
from jax.sharding import PartitionSpec as P

CAP = 4
K = 8
CELLS = 64
SIDE = 16
COLS = 8
WIDE = SIDE + 4
HID = SIDE + 2
EARLY = ((1, 3), (4, 4), (8, 4))
LATE = ((12, 3),)
EARLY_PLANES = 11
LATE_PLANES = 3
SENT = (4, 3, 5, 2, 6, 1, 7, 0)
RETURNED = (1, 7, 6, 4, 2, 3, 5)
UP_OFFSETS = 4
DOWN_LIMIT = 62 * 1024 * 1024
VMEM_LIMIT = 24 * 1024 * 1024


def expand_mask(mask):
    bricks = mask.shape[0]
    values = mask.astype(jnp.float32)
    cell = lax.broadcasted_iota(jnp.int32, (16, 128), 0)
    lane = lax.broadcasted_iota(jnp.int32, (16, 128), 1)
    chosen = (cell == lane // 8).astype(jnp.float32)
    parts = [
        values[:, t * 128 : (t + 1) * 128].reshape(bricks, 1, 128) * chosen[None] for t in range(4)
    ]
    spread = jnp.concatenate(parts, axis=1).reshape(bricks * CELLS, 128).astype(jnp.bfloat16)
    source = lax.broadcasted_iota(jnp.int32, (128, 512), 0)
    target = lax.broadcasted_iota(jnp.int32, (128, 512), 1)
    widen = ((source & 7) == (target >> 6)).astype(jnp.bfloat16)
    return jnp.dot(spread, widen, preferred_element_type=jnp.float32)


def down_kernel(fine_hbm, mask_hbm, w_hbm, *refs):
    outs = refs[:K]
    fine_ref, mask_ref, w_ref, wide_ref, sems = refs[K:]
    first = [
        pltpu.make_async_copy(mask_hbm, mask_ref, sems.at[K]),
        pltpu.make_async_copy(w_hbm, w_ref, sems.at[K + 1]),
    ]
    chunks = {
        j: pltpu.make_async_copy(fine_hbm.at[pl.ds(j * CAP, CAP)], fine_ref.at[j], sems.at[j])
        for j in SENT
    }
    for copy in first + list(chunks.values()):
        copy.start()
    first[0].wait()
    rows = CAP * CELLS
    for part in range(K // 2):
        wide_ref[part * 2 * rows : (part + 1) * 2 * rows] = expand_mask(
            mask_ref[part * 2 * CAP : (part + 1) * 2 * CAP]
        ).astype(jnp.bfloat16)
    first[1].wait()
    for part in range(K // 2):
        pair = SENT[2 * part : 2 * part + 2]
        for j in pair:
            chunks[j].wait()
        x = [
            fine_ref[j].reshape(rows, -1) * wide_ref[j * rows : (j + 1) * rows] for j in pair
        ]
        y = jnp.dot(jnp.concatenate(x, axis=0), w_ref[...], preferred_element_type=jnp.float32)
        y = y.astype(jnp.bfloat16)
        for k, j in enumerate(pair):
            outs[j][...] = y[k * rows : (k + 1) * rows]


def down_call(fine, mask, w):
    bricks, cells, width = fine.shape
    mid = w.shape[1]
    hbm = pl.BlockSpec(memory_space=pltpu.HBM)
    return pl.pallas_call(
        down_kernel,
        in_specs=[hbm, hbm, hbm],
        out_specs=[pl.BlockSpec(memory_space=pltpu.VMEM)] * K,
        out_shape=[jax.ShapeDtypeStruct((CAP * cells, mid), jnp.bfloat16)] * K,
        scratch_shapes=[
            pltpu.VMEM((K, CAP, cells, width), fine.dtype),
            pltpu.VMEM(mask.shape, mask.dtype),
            pltpu.VMEM(w.shape, w.dtype),
            pltpu.VMEM((bricks * cells, width), jnp.bfloat16),
            pltpu.SemaphoreType.DMA((K + 2,)),
        ],
        compiler_params=pltpu.CompilerParams(vmem_limit_bytes=DOWN_LIMIT),
        name="down",
    )(fine, mask, w)


def prepare_kernel(mask_ref, w1_ref, w2_ref, mask_out, wide1_ref, wide2_ref):
    gather_weights(w1_ref, wide1_ref)
    gather_weights(w2_ref, wide2_ref)
    step = 8
    for part in range(mask_ref.shape[0] // step):
        rows = slice(part * step * CELLS, (part + 1) * step * CELLS)
        mask_out[rows] = expand_mask(mask_ref[part * step : (part + 1) * step]).astype(jnp.bfloat16)


def prepare_call(mask, w_first, w_second):
    mid = w_first.shape[1]
    vmem = pl.BlockSpec(memory_space=pltpu.VMEM)
    rows = mask.shape[0] * CELLS
    wide = jax.ShapeDtypeStruct((9 * mid, 3 * mid), jnp.bfloat16)
    return pl.pallas_call(
        prepare_kernel,
        in_specs=[vmem] * 3,
        out_specs=[vmem] * 3,
        out_shape=[jax.ShapeDtypeStruct((rows, mask.shape[1]), jnp.bfloat16), wide, wide],
        compiler_params=pltpu.CompilerParams(vmem_limit_bytes=VMEM_LIMIT),
        cost_estimate=pl.CostEstimate(
            flops=2 * rows * mask.shape[1] * 128, bytes_accessed=rows * mask.shape[1] * 2, transcendentals=0
        ),
        name="prepare",
    )(mask, w_first, w_second)


def up_kernel(fine_ref, mask_ref, w_ref, *refs):
    out_ref = refs[-1]
    step = pl.program_id(0)
    bricks, cells, width = fine_ref.shape
    count = bricks // CAP
    steps = UP_OFFSETS // count
    for part in range(count):
        octant = refs[part][...]
        for other in range(1, steps):
            octant = jnp.where(step == other, refs[other * count + part][...], octant)
        rows = slice(part * CAP * cells, (part + 1) * CAP * cells)
        up = jnp.dot(octant, w_ref[...], preferred_element_type=jnp.float32)
        fine = fine_ref[part * CAP : (part + 1) * CAP].reshape(CAP * cells, width)
        mask = mask_ref[rows].astype(jnp.float32)
        out = jnp.where(mask > 0.5, fine.astype(jnp.float32) + up, 0.0)
        out_ref[part * CAP : (part + 1) * CAP] = out.astype(jnp.bfloat16).reshape(CAP, cells, width)


def up_call(fine, mask, w, octants, first, partial):
    bricks, cells, width = fine.shape
    mid = w.shape[0]
    step = 8
    blocks = bricks // step

    def place(i):
        return (first + i) % blocks

    partials = [] if partial is None else [partial]
    return pl.pallas_call(
        up_kernel,
        grid=(UP_OFFSETS * CAP // step,),
        in_specs=[
            pl.BlockSpec((step, cells, width), lambda i: (place(i), 0, 0)),
            pl.BlockSpec((step * cells, width), lambda i: (place(i), 0)),
            pl.BlockSpec((mid, width), lambda i: (0, 0)),
        ]
        + [pl.BlockSpec((CAP * cells, mid), lambda i: (0, 0))] * UP_OFFSETS
        + [pl.BlockSpec(memory_space=pl.ANY)] * len(partials),
        out_specs=pl.BlockSpec((step, cells, width), lambda i: (place(i), 0, 0)),
        out_shape=jax.ShapeDtypeStruct(fine.shape, jnp.bfloat16),
        input_output_aliases={3 + UP_OFFSETS: 0} if partials else {},
        compiler_params=pltpu.CompilerParams(vmem_limit_bytes=VMEM_LIMIT),
        cost_estimate=pl.CostEstimate(
            flops=bricks * cells * width * mid, bytes_accessed=bricks * cells * width * 2, transcendentals=0
        ),
        name="up",
    )(fine, mask, w, *octants, *partials)


def low_half(shape):
    return lax.broadcasted_iota(jnp.int32, shape, len(shape) - 2) < 4


def slot_flags(source_ref, first):
    pair = [jnp.where(source_ref[first + k] >= 0, 1.0, 0.0).astype(jnp.float32) for k in range(2)]
    return jnp.where(low_half((8, 128)), pair[0], pair[1])


def slot_index(depth_brick, row_brick):
    pd, qd = divmod(depth_brick, 2)
    pr, qr = divmod(row_brick, 2)
    return (pd * 2 + pr) * 8 + qd * 4 + qr * 2


def take_brick(source_ref, arrived, slot):
    value = source_ref[slot]
    first = pl.multiple_of(jnp.maximum(value, 0) * CELLS, CELLS)
    brick = arrived[pl.ds(first, CELLS), :].astype(jnp.float32)
    return jnp.where(value >= 0, brick, 0.0).reshape(8, 8, 128)


def place_kernel(source_ref, *refs):
    block_ref, low_ref, high_ref, arrived = refs[K:]
    for j in range(K):
        arrived[j * CAP * CELLS : (j + 1) * CAP * CELLS] = refs[j][...]
    half = low_half((8, 8, 128))
    for depth_brick in range(4):
        for row_brick in range(4):
            slot = slot_index(depth_brick, row_brick)
            b0 = take_brick(source_ref, arrived, slot)
            b1 = take_brick(source_ref, arrived, slot + 1)
            even = jnp.where(half, b0, pltpu.roll(b1, 4, 1))
            odd = jnp.where(half, pltpu.roll(b0, 4, 1), b1)
            both = jnp.stack([even, odd], axis=1).reshape(4, 32, 128).astype(jnp.bfloat16)
            for vd in range(4):
                row = ((depth_brick * 4 + vd) * SIDE + row_brick * 4) * COLS
                block_ref[row : row + 32] = both[vd]
                place = (depth_brick * 4 + vd) * 16
                if row_brick == 0:
                    low_ref[place : place + 16] = both[vd, :16]
                if row_brick == 3:
                    high_ref[place : place + 16] = both[vd, 16:]
    for row_brick, ref in ((0, low_ref), (3, high_ref)):
        flags = [slot_flags(source_ref, slot_index(d, row_brick)) for d in range(4)]
        ref[256:288] = jnp.concatenate(flags, axis=0).astype(jnp.bfloat16)


def place_call(source, arrived):
    mid = arrived[0].shape[1]
    smem = pl.BlockSpec(memory_space=pltpu.SMEM)
    vmem = pl.BlockSpec(memory_space=pltpu.VMEM)
    return pl.pallas_call(
        place_kernel,
        in_specs=[smem] + [vmem] * K,
        out_specs=[vmem] * 3,
        out_shape=[
            jax.ShapeDtypeStruct((rows, mid), jnp.bfloat16)
            for rows in (SIDE * SIDE * COLS, 288, 288)
        ],
        scratch_shapes=[pltpu.VMEM((K * CAP * CELLS, mid), jnp.bfloat16)],
        compiler_params=pltpu.CompilerParams(vmem_limit_bytes=VMEM_LIMIT),
        name="place",
    )(source, *arrived)


def edge_kernel(source_ref, block_ref, before_ref, after_ref, low_ref, high_ref):
    for ref, planes, brick in ((low_ref, (0, 1), 0), (high_ref, (SIDE - 2, SIDE - 1), 3)):
        for k, plane in enumerate(planes):
            start = k * WIDE * COLS
            ref[start : start + 16] = before_ref[plane * 16 : plane * 16 + 16]
            ref[start + 16 : start + 144] = block_ref[plane * 128 : plane * 128 + 128]
            ref[start + 144 : start + 160] = after_ref[plane * 16 : plane * 16 + 16]
        first = 256 + brick * 8
        flags = [before_ref[256:288].astype(jnp.float32)[brick * 8 : brick * 8 + 8]]
        flags += [slot_flags(source_ref, slot_index(brick, r)) for r in range(4)]
        flags += [after_ref[256:288].astype(jnp.float32)[brick * 8 : brick * 8 + 8]]
        ref[320:368] = jnp.concatenate(flags, axis=0).astype(jnp.bfloat16)


def edge_call(source, block, before, after):
    smem = pl.BlockSpec(memory_space=pltpu.SMEM)
    vmem = pl.BlockSpec(memory_space=pltpu.VMEM)
    return pl.pallas_call(
        edge_kernel,
        in_specs=[smem, vmem, vmem, vmem],
        out_specs=[vmem] * 2,
        out_shape=[jax.ShapeDtypeStruct((368, block.shape[1]), jnp.bfloat16)] * 2,
        compiler_params=pltpu.CompilerParams(vmem_limit_bytes=VMEM_LIMIT),
        name="edge",
    )(source, block, before, after)


def gather_weights(w_ref, wide_ref):
    width = w_ref.shape[2]
    for tap in range(9):
        for column in range(3):
            wide_ref[tap * width : (tap + 1) * width, column * width : (column + 1) * width] = (
                w_ref[tap * 3 + column]
            )


def as_rows(value):
    value = value.astype(jnp.float32)
    return value.reshape(value.shape[0] // COLS, COLS, value.shape[1])


def moved_rows(rows):
    empty = jnp.zeros((1,) + rows.shape[1:], jnp.float32)
    return jnp.concatenate([rows[1:], empty], axis=0)


def as_tiles(rows):
    return rows.reshape(rows.shape[0] * COLS, rows.shape[2]).astype(jnp.bfloat16)


def multiply_taps(lhs, wide_ref):
    width = wide_ref.shape[1] // 3
    wide = jnp.dot(lhs, wide_ref[...], preferred_element_type=jnp.float32)
    wide = wide.reshape(lhs.shape[0] // COLS, COLS, 3 * width)
    column = lax.broadcasted_iota(jnp.int32, (lhs.shape[0] // COLS, COLS, width), 1)
    left = jnp.where(column == 0, 0.0, pltpu.roll(wide[:, :, :width], 1, 1))
    right = jnp.where(column == COLS - 1, 0.0, pltpu.roll(wide[:, :, 2 * width :], COLS - 1, 1))
    return left + wide[:, :, width : 2 * width] + right


def conv_planes(here_ref, next_ref, wide_ref, first, planes, rows):
    taps = []
    for dd in range(3):
        span = slice(first + dd, first + dd + planes)
        taps += [
            here_ref[span, 0:rows, :],
            next_ref[span, 0:rows, :],
            here_ref[span, 16 : rows + 16, :],
        ]
    lhs = jnp.concatenate(taps, axis=2)
    return multiply_taps(lhs.reshape(planes * rows, lhs.shape[2]), wide_ref)


def activate(value, flags):
    return value / (1.0 + jnp.exp(-value)) * flags


def spread_flags(flags, repeats):
    return jnp.concatenate(
        [jnp.broadcast_to(flag[None], (count,) + flag.shape) for flag, count in zip(flags, repeats)],
        axis=0,
    )


def inner_planes(source_ref, block_ref, wide1_ref, hidden_ref, here, moved, groups):
    width = block_ref.shape[1]
    base = groups[0][0] - 1
    for d in range(base, groups[-1][0] + groups[-1][1] + 1):
        plane = block_ref[d * 128 : (d + 1) * 128]
        here[d - base] = plane
        moved[d - base] = as_tiles(moved_rows(as_rows(plane)))
    inner = SIDE - 2
    rows = inner * COLS
    for first, planes in groups:
        value = conv_planes(here, moved, wide1_ref, first - 1 - base, planes, rows)
        value = value.reshape(planes, inner, COLS, width)
        flags = [slot_flags(source_ref, slot_index(first // 4, r)) for r in range(4)]
        value = activate(value, spread_flags(flags, (3, 4, 4, 3))[None])
        hidden_ref[first - 1 - base : first - 1 - base + planes] = value.reshape(
            planes, rows, width
        ).astype(jnp.bfloat16)


def inner_kernel(source_ref, block_ref, wide1_ref, hidden_ref, here, moved):
    inner_planes(source_ref, block_ref, wide1_ref, hidden_ref, here, moved, EARLY)


def conv_cost(rows, width):
    return pl.CostEstimate(
        flops=2 * rows * 27 * width * width, bytes_accessed=27 * width * width * 4, transcendentals=0
    )


def inner_call(source, block, wide1):
    mid = block.shape[1]
    smem = pl.BlockSpec(memory_space=pltpu.SMEM)
    vmem = pl.BlockSpec(memory_space=pltpu.VMEM)
    rows = (SIDE - 2) * COLS
    return pl.pallas_call(
        inner_kernel,
        in_specs=[smem, vmem, vmem],
        out_specs=vmem,
        out_shape=jax.ShapeDtypeStruct((EARLY_PLANES, rows, mid), jnp.bfloat16),
        scratch_shapes=[pltpu.VMEM((EARLY_PLANES + 2, SIDE * COLS, mid), jnp.bfloat16)] * 2,
        compiler_params=pltpu.CompilerParams(vmem_limit_bytes=VMEM_LIMIT),
        cost_estimate=conv_cost(EARLY_PLANES * rows, mid),
        name="inner",
    )(source, block, wide1)


def side_kernel(
    source_ref,
    block_ref,
    before_ref,
    after_ref,
    wide1_ref,
    hidden_ref,
    late_ref,
    mixed,
    here,
    moved,
):
    inner_planes(source_ref, block_ref, wide1_ref, late_ref, here, moved, LATE)
    width = block_ref.shape[1]
    for d in range(SIDE):
        edge = slice(d * 16, (d + 1) * 16)
        low = as_rows(block_ref[d * 128 : d * 128 + 16])
        high = as_rows(block_ref[d * 128 + 112 : d * 128 + 128])
        before = as_rows(before_ref[edge])
        after = as_rows(after_ref[edge])
        mixed[0, edge] = as_tiles(jnp.concatenate([before[1:], low[:1]], axis=0))
        mixed[1, edge] = as_tiles(jnp.concatenate([high[1:], after[:1]], axis=0))
    inner = SIDE - 2
    taps = []
    for dd in range(3):
        span = slice(dd * 16, (dd + inner) * 16)
        low = [block_ref[(d + dd) * 128 : (d + dd) * 128 + 16] for d in range(inner)]
        high = [block_ref[(d + dd) * 128 + 112 : (d + dd) * 128 + 128] for d in range(inner)]
        taps.append(jnp.concatenate([before_ref[span]] + high, axis=0))
        taps.append(jnp.concatenate([mixed[0, span], mixed[1, span]], axis=0))
        taps.append(jnp.concatenate(low + [after_ref[span]], axis=0))
    value = multiply_taps(jnp.concatenate(taps, axis=1), wide1_ref)
    depths = (3, 4, 4, 3)
    edge_flags = (as_rows(before_ref[256:288]), as_rows(after_ref[256:288]))
    flags = []
    for side, row_brick in ((0, 0), (1, 3)):
        own = [slot_flags(source_ref, slot_index(d, row_brick)) for d in range(4)]
        pairs = [jnp.stack([edge_flags[side][d], own[d]][:: 1 - 2 * side], axis=0) for d in range(4)]
        flags.append(spread_flags(pairs, depths))
    flags = jnp.stack(flags, axis=0)
    value = activate(value.reshape(2, inner, 2, COLS, width), flags)
    hidden_ref[...] = value.reshape(2, inner, 16, width).astype(jnp.bfloat16)


def side_call(source, block, before, after, wide1):
    mid = block.shape[1]
    smem = pl.BlockSpec(memory_space=pltpu.SMEM)
    vmem = pl.BlockSpec(memory_space=pltpu.VMEM)
    inner = SIDE - 2
    return pl.pallas_call(
        side_kernel,
        in_specs=[smem] + [vmem] * 4,
        out_specs=[vmem] * 2,
        out_shape=[
            jax.ShapeDtypeStruct((2, inner, 16, mid), jnp.bfloat16),
            jax.ShapeDtypeStruct((LATE_PLANES, inner * COLS, mid), jnp.bfloat16),
        ],
        scratch_shapes=[
            pltpu.VMEM((2, SIDE * 16, mid), jnp.bfloat16),
            pltpu.VMEM((LATE_PLANES + 2, SIDE * COLS, mid), jnp.bfloat16),
            pltpu.VMEM((LATE_PLANES + 2, SIDE * COLS, mid), jnp.bfloat16),
        ],
        compiler_params=pltpu.CompilerParams(vmem_limit_bytes=VMEM_LIMIT),
        cost_estimate=conv_cost(inner * (4 + LATE_PLANES) * COLS, mid),
        name="side",
    )(source, block, before, after, wide1)


def final_kernel(source_ref, *refs):
    block_ref, before_ref, after_ref, under_ref, over_ref = refs[:5]
    early_ref, late_ref, side_ref, wide1_ref, wide2_ref, coarse_ref = refs[5:11]
    backs = refs[11 : 11 + K]
    x_here, x_next, h_here, h_next, stage = refs[11 + K :]
    width = block_ref.shape[1]
    flags_before = as_rows(before_ref[256:288])
    flags_after = as_rows(after_ref[256:288])
    for end, ref in ((0, under_ref), (1, over_ref)):
        planes = []
        own = [0, 1] if end == 0 else [SIDE - 2, SIDE - 1]
        for d in own:
            edge = slice(d * 16, (d + 1) * 16)
            planes.append(
                jnp.concatenate(
                    [before_ref[edge], block_ref[d * 128 : (d + 1) * 128], after_ref[edge]], axis=0
                )
            )
        far = [ref[k * 160 : (k + 1) * 160] for k in range(2)]
        for index, plane in enumerate(far + planes if end == 0 else planes + far):
            x_here[index] = plane
            x_next[index] = as_tiles(moved_rows(as_rows(plane)))
        value = conv_planes(x_here, x_next, wide1_ref, 0, 2, HID * COLS)
        value = value.reshape(2, HID, COLS, width)
        far_flags = as_rows(ref[320:368])
        brick = 0 if end == 0 else 3
        own_flags = [flags_before[brick]]
        own_flags += [slot_flags(source_ref, slot_index(brick, r)) for r in range(4)]
        own_flags += [flags_after[brick]]
        spread = [
            spread_flags([far_flags[r] for r in range(6)], (1, 4, 4, 4, 4, 1)),
            spread_flags(own_flags, (1, 4, 4, 4, 4, 1)),
        ]
        for k in range(2):
            flags = spread[k if end == 0 else 1 - k]
            rows = activate(value[k], flags)
            index = k if end == 0 else HID - 2 + k
            h_here[index] = as_tiles(rows)
            h_next[index] = as_tiles(moved_rows(rows))
    for d in range(SIDE - 2):
        middle = early_ref[d] if d < EARLY_PLANES else late_ref[d - EARLY_PLANES]
        plane = jnp.concatenate([side_ref[0, d], middle, side_ref[1, d]], axis=0)
        h_here[d + 2] = plane
        h_next[d + 2] = as_tiles(moved_rows(as_rows(plane)))

    stage[...] = jnp.zeros(stage.shape, jnp.bfloat16)
    for depth_brick in range(4):
        value = conv_planes(h_here, h_next, wide2_ref, depth_brick * 4, 4, SIDE * COLS)
        value = value.reshape(4, SIDE, COLS, width)
        rows = slice(depth_brick * 512, (depth_brick + 1) * 512)
        own = block_ref[rows].astype(jnp.float32).reshape(4, SIDE, COLS, width)
        flags = [slot_flags(source_ref, slot_index(depth_brick, r)) for r in range(4)]
        value = (value + own) * spread_flags(flags, (4, 4, 4, 4))[None]
        coarse_ref[rows] = value.reshape(4 * SIDE * COLS, width).astype(jnp.bfloat16)
        half = low_half((4, 2, COLS, width))
        for r in range(4):
            part = value[:, r * 4 : (r + 1) * 4].reshape(4, 2, 2, COLS, width)
            even, odd = part[:, :, 0], part[:, :, 1]
            b0 = jnp.where(half, even, pltpu.roll(odd, 4, 2))
            b1 = jnp.where(half, pltpu.roll(even, 4, 2), odd)
            slot = slot_index(depth_brick, r)
            for k, brick in enumerate((b0, b1)):
                source = source_ref[slot + k]
                row = pl.multiple_of(jnp.where(source >= 0, source, K * CAP) * CELLS, CELLS)
                stage[pl.ds(row, CELLS), :] = brick.reshape(CELLS, width).astype(jnp.bfloat16)
    for j in range(K):
        backs[j][...] = stage[j * CAP * CELLS : (j + 1) * CAP * CELLS]


def final_call(source, block, halo, hidden, wide1, wide2):
    mid = block.shape[1]
    smem = pl.BlockSpec(memory_space=pltpu.SMEM)
    vmem = pl.BlockSpec(memory_space=pltpu.VMEM)
    return pl.pallas_call(
        final_kernel,
        in_specs=[smem] + [vmem] * 10,
        out_specs=[vmem] * (1 + K),
        out_shape=[
            jax.ShapeDtypeStruct(block.shape, jnp.bfloat16),
        ]
        + [jax.ShapeDtypeStruct((CAP * CELLS, mid), jnp.bfloat16)] * K,
        scratch_shapes=[
            pltpu.VMEM((4, WIDE * COLS, mid), jnp.bfloat16),
            pltpu.VMEM((4, WIDE * COLS, mid), jnp.bfloat16),
            pltpu.VMEM((HID, HID * COLS, mid), jnp.bfloat16),
            pltpu.VMEM((HID, HID * COLS, mid), jnp.bfloat16),
            pltpu.VMEM(((K * CAP + 1) * CELLS, mid), jnp.bfloat16),
        ],
        compiler_params=pltpu.CompilerParams(vmem_limit_bytes=VMEM_LIMIT),
        cost_estimate=conv_cost(SIDE * SIDE * COLS, mid),
        name="final",
    )(source, block, *halo, *hidden, wide1, wide2)


def from_behind(value, axis, steps):
    count = lax.axis_size(axis)
    pairs = [(source, (source + steps) % count) for source in range(count)]
    return lax.ppermute(value, axis, pairs)


def neighbours(low, high, axis):
    count = lax.axis_size(axis)
    forward = [(i, i + 1) for i in range(count - 1)]
    backward = [(target, source) for source, target in forward]
    return lax.ppermute(high, axis, forward), lax.ppermute(low, axis, backward)


def shards(fine, fine_mask, slot_source, w_down, w_first, w_second, w_up):
    mid = w_down.shape[1]
    sent = down_call(fine, fine_mask, w_down)
    arrived = {j: from_behind(sent[j], "xy", j) for j in SENT if j}
    later_mask, own = lax.optimization_barrier((fine_mask, sent[0]))
    mask, wide1, wide2 = prepare_call(later_mask, w_first, w_second)
    own, mask, wide1, wide2 = lax.optimization_barrier((own, mask, wide1, wide2))
    arrived[0] = own
    block, low, high = place_call(slot_source, [arrived[j] for j in range(K)])
    before, after = neighbours(low, high, "xy")
    early = inner_call(slot_source, block, wide1)
    before, after, early = lax.optimization_barrier((before, after, early))
    under_send, over_send = edge_call(slot_source, block, before, after)
    under, over = neighbours(under_send, over_send, "gz")
    side, late = side_call(slot_source, block, before, after, wide1)
    coarse, *back = final_call(
        slot_source, block, (before, after, under, over), (early, late, side), wide1, wide2
    )
    octant = {j: from_behind(back[j], "xy", -j) for j in RETURNED}
    octant[0] = back[0]
    fine_out = up_call(fine, mask, w_up, [octant[j] for j in (6, 7, 0, 1)], 3, None)
    fine_out = up_call(fine, mask, w_up, [octant[j] for j in (2, 3, 4, 5)], 1, fine_out)
    return fine_out, coarse.reshape(SIDE, SIDE, COLS, mid)


def solution(mesh):
    placed = (
        P(("gz", "xy"), None, None),
        P(("gz", "xy"), None),
        P(("gz", "xy")),
        P(),
        P(),
        P(),
        P(),
    )
    return jax.shard_map(
        shards,
        mesh=mesh,
        in_specs=placed,
        out_specs=(P(("gz", "xy"), None, None), P("gz", "xy", None, None)),
        check_vma=False,
    )
```

```python
import functools

import jax
import jax.numpy as jnp
from jax import lax
from jax.experimental import pallas as pl
from jax.experimental.pallas import tpu as pltpu
from jax.sharding import PartitionSpec as P

CAP = 4
K = 8
CELLS = 64
SIDE = 16
COLS = 8
WIDE = SIDE + 4
HID = SIDE + 2
EARLY = ((1, 3), (4, 4), (8, 4))
LATE = ((12, 3),)
EARLY_PLANES = 11
LATE_PLANES = 3
FIRST_SENT = (4,)
LAST_SENT = (3, 5, 2, 6, 1, 7)
RETURNED = (1, 7, 6, 4, 2, 3, 5)
UP_OFFSETS = 4
DOWN_LIMIT = 62 * 1024 * 1024
VMEM_LIMIT = 24 * 1024 * 1024


def expand_mask(mask):
    bricks = mask.shape[0]
    values = mask.astype(jnp.float32)
    cell = lax.broadcasted_iota(jnp.int32, (16, 128), 0)
    lane = lax.broadcasted_iota(jnp.int32, (16, 128), 1)
    chosen = (cell == lane // 8).astype(jnp.float32)
    parts = [
        values[:, t * 128 : (t + 1) * 128].reshape(bricks, 1, 128) * chosen[None] for t in range(4)
    ]
    spread = jnp.concatenate(parts, axis=1).reshape(bricks * CELLS, 128).astype(jnp.bfloat16)
    source = lax.broadcasted_iota(jnp.int32, (128, 512), 0)
    target = lax.broadcasted_iota(jnp.int32, (128, 512), 1)
    widen = ((source & 7) == (target >> 6)).astype(jnp.bfloat16)
    return jnp.dot(spread, widen, preferred_element_type=jnp.float32)


def down_kernel(offsets, fine_hbm, mask_hbm, w_hbm, *refs):
    count = len(offsets)
    outs = refs[:count]
    fine_ref, mask_ref, w_ref, wide_ref, sems = refs[count:]
    first = [
        pltpu.make_async_copy(mask_hbm, mask_ref, sems.at[count]),
        pltpu.make_async_copy(w_hbm, w_ref, sems.at[count + 1]),
    ]
    chunks = [
        pltpu.make_async_copy(fine_hbm.at[pl.ds(j * CAP, CAP)], fine_ref.at[k], sems.at[k])
        for k, j in enumerate(offsets)
    ]
    for copy in first + chunks:
        copy.start()
    first[0].wait()
    rows = CAP * CELLS
    for k, j in enumerate(offsets):
        wide_ref[k * rows : (k + 1) * rows] = expand_mask(
            mask_ref[j * CAP : (j + 1) * CAP]
        ).astype(jnp.bfloat16)
    first[1].wait()
    for start in range(0, count, 2):
        group = range(start, min(start + 2, count))
        for k in group:
            chunks[k].wait()
        x = [
            fine_ref[k].reshape(rows, -1) * wide_ref[k * rows : (k + 1) * rows] for k in group
        ]
        y = jnp.dot(jnp.concatenate(x, axis=0), w_ref[...], preferred_element_type=jnp.float32)
        y = y.astype(jnp.bfloat16)
        for part, k in enumerate(group):
            outs[k][...] = y[part * rows : (part + 1) * rows]


def down_call(fine, mask, w, offsets):
    cells, width = fine.shape[1:]
    mid = w.shape[1]
    count = len(offsets)
    rows = count * CAP * cells
    hbm = pl.BlockSpec(memory_space=pltpu.HBM)
    outs = pl.pallas_call(
        functools.partial(down_kernel, offsets),
        in_specs=[hbm, hbm, hbm],
        out_specs=[pl.BlockSpec(memory_space=pltpu.VMEM)] * count,
        out_shape=[jax.ShapeDtypeStruct((CAP * cells, mid), jnp.bfloat16)] * count,
        scratch_shapes=[
            pltpu.VMEM((count, CAP, cells, width), fine.dtype),
            pltpu.VMEM(mask.shape, mask.dtype),
            pltpu.VMEM(w.shape, w.dtype),
            pltpu.VMEM((rows, width), jnp.bfloat16),
            pltpu.SemaphoreType.DMA((count + 2,)),
        ],
        compiler_params=pltpu.CompilerParams(vmem_limit_bytes=DOWN_LIMIT),
        cost_estimate=pl.CostEstimate(
            flops=2 * rows * width * mid, bytes_accessed=rows * width * 2, transcendentals=0
        ),
        name="down",
    )(fine, mask, w)
    return dict(zip(offsets, outs))


def prepare_kernel(
    fine_ref, mask_ref, w_down_ref, w1_ref, w2_ref, own_ref, mask_out, wide1_ref, wide2_ref
):
    gather_weights(w1_ref, wide1_ref)
    gather_weights(w2_ref, wide2_ref)
    step = 8
    for part in range(mask_ref.shape[0] // step):
        rows = slice(part * step * CELLS, (part + 1) * step * CELLS)
        mask_out[rows] = expand_mask(mask_ref[part * step : (part + 1) * step]).astype(jnp.bfloat16)
    rows = CAP * CELLS
    own = fine_ref[...].reshape(rows, -1) * mask_out[:rows]
    own = jnp.dot(own, w_down_ref[...], preferred_element_type=jnp.float32)
    own_ref[...] = own.astype(jnp.bfloat16)


def prepare_call(fine, mask, w_down, w_first, w_second):
    mid = w_first.shape[1]
    vmem = pl.BlockSpec(memory_space=pltpu.VMEM)
    rows = mask.shape[0] * CELLS
    wide = jax.ShapeDtypeStruct((9 * mid, 3 * mid), jnp.bfloat16)
    return pl.pallas_call(
        prepare_kernel,
        grid=(1,),
        in_specs=[pl.BlockSpec((CAP,) + fine.shape[1:], lambda i: (0, 0, 0))] + [vmem] * 4,
        out_specs=[vmem] * 4,
        out_shape=[
            jax.ShapeDtypeStruct((CAP * CELLS, mid), jnp.bfloat16),
            jax.ShapeDtypeStruct((rows, mask.shape[1]), jnp.bfloat16),
            wide,
            wide,
        ],
        compiler_params=pltpu.CompilerParams(vmem_limit_bytes=VMEM_LIMIT),
        cost_estimate=pl.CostEstimate(
            flops=2 * rows * mask.shape[1] * 128, bytes_accessed=rows * mask.shape[1] * 2, transcendentals=0
        ),
        name="prepare",
    )(fine, mask, w_down, w_first, w_second)


def up_kernel(fine_ref, mask_ref, w_ref, *refs):
    out_ref = refs[-1]
    step = pl.program_id(0)
    bricks, cells, width = fine_ref.shape
    count = bricks // CAP
    steps = UP_OFFSETS // count
    for part in range(count):
        octant = refs[part][...]
        for other in range(1, steps):
            octant = jnp.where(step == other, refs[other * count + part][...], octant)
        rows = slice(part * CAP * cells, (part + 1) * CAP * cells)
        up = jnp.dot(octant, w_ref[...], preferred_element_type=jnp.float32)
        fine = fine_ref[part * CAP : (part + 1) * CAP].reshape(CAP * cells, width)
        mask = mask_ref[rows].astype(jnp.float32)
        out = jnp.where(mask > 0.5, fine.astype(jnp.float32) + up, 0.0)
        out_ref[part * CAP : (part + 1) * CAP] = out.astype(jnp.bfloat16).reshape(CAP, cells, width)


def up_call(fine, mask, w, octants, first, partial):
    bricks, cells, width = fine.shape
    mid = w.shape[0]
    step = 8
    blocks = bricks // step

    def place(i):
        return (first + i) % blocks

    partials = [] if partial is None else [partial]
    return pl.pallas_call(
        up_kernel,
        grid=(UP_OFFSETS * CAP // step,),
        in_specs=[
            pl.BlockSpec((step, cells, width), lambda i: (place(i), 0, 0)),
            pl.BlockSpec((step * cells, width), lambda i: (place(i), 0)),
            pl.BlockSpec((mid, width), lambda i: (0, 0)),
        ]
        + [pl.BlockSpec((CAP * cells, mid), lambda i: (0, 0))] * UP_OFFSETS
        + [pl.BlockSpec(memory_space=pl.ANY)] * len(partials),
        out_specs=pl.BlockSpec((step, cells, width), lambda i: (place(i), 0, 0)),
        out_shape=jax.ShapeDtypeStruct(fine.shape, jnp.bfloat16),
        input_output_aliases={3 + UP_OFFSETS: 0} if partials else {},
        compiler_params=pltpu.CompilerParams(vmem_limit_bytes=VMEM_LIMIT),
        cost_estimate=pl.CostEstimate(
            flops=bricks * cells * width * mid, bytes_accessed=bricks * cells * width * 2, transcendentals=0
        ),
        name="up",
    )(fine, mask, w, *octants, *partials)


def low_half(shape):
    return lax.broadcasted_iota(jnp.int32, shape, len(shape) - 2) < 4


def slot_flags(source_ref, first):
    pair = [jnp.where(source_ref[first + k] >= 0, 1.0, 0.0).astype(jnp.float32) for k in range(2)]
    return jnp.where(low_half((8, 128)), pair[0], pair[1])


def slot_index(depth_brick, row_brick):
    pd, qd = divmod(depth_brick, 2)
    pr, qr = divmod(row_brick, 2)
    return (pd * 2 + pr) * 8 + qd * 4 + qr * 2


def take_brick(source_ref, arrived, slot):
    value = source_ref[slot]
    first = pl.multiple_of(jnp.maximum(value, 0) * CELLS, CELLS)
    brick = arrived[pl.ds(first, CELLS), :].astype(jnp.float32)
    return jnp.where(value >= 0, brick, 0.0).reshape(8, 8, 128)


def place_kernel(base_ref, source_ref, *refs):
    block_ref, even_ref, odd_ref, low_ref, high_ref, arrived = refs[K:]
    for j in range(K):
        arrived[j * CAP * CELLS : (j + 1) * CAP * CELLS] = refs[j][...]
    half = low_half((8, 8, 128))
    for depth_brick in range(4):
        for row_brick in range(4):
            slot = slot_index(depth_brick, row_brick)
            b0 = take_brick(source_ref, arrived, slot)
            b1 = take_brick(source_ref, arrived, slot + 1)
            even = jnp.where(half, b0, pltpu.roll(b1, 4, 1))
            odd = jnp.where(half, pltpu.roll(b0, 4, 1), b1)
            both = jnp.stack([even, odd], axis=1).reshape(4, 32, 128).astype(jnp.bfloat16)
            for vd in range(4):
                row = ((depth_brick * 4 + vd) * SIDE + row_brick * 4) * COLS
                block_ref[row : row + 32] = both[vd]
                place = (depth_brick * 4 + vd) * 16
                if row_brick == 0:
                    low_ref[place : place + 16] = both[vd, :16]
                if row_brick == 3:
                    high_ref[place : place + 16] = both[vd, 16:]
    for row_brick, ref in ((0, low_ref), (3, high_ref)):
        flags = [slot_flags(source_ref, slot_index(d, row_brick)) for d in range(4)]
        ref[256:288] = jnp.concatenate(flags, axis=0).astype(jnp.bfloat16)
    face_out(base_ref[0], low_ref, high_ref, even_ref, odd_ref)


def face_out(index, low_ref, high_ref, even_ref, odd_ref):
    is_even = index % 2 == 0
    even_ref[...] = jnp.where(is_even, high_ref[...], low_ref[...])
    odd_ref[...] = jnp.where(is_even, low_ref[...], high_ref[...])


def face_in(index, count, even_ref, odd_ref, low_ref, high_ref):
    is_even = index % 2 == 0
    empty = jnp.zeros(low_ref.shape, low_ref.dtype)
    low = jnp.where(is_even, odd_ref[...], even_ref[...])
    high = jnp.where(is_even, even_ref[...], odd_ref[...])
    low_ref[...] = jnp.where(index == 0, empty, low)
    high_ref[...] = jnp.where(index == count - 1, empty, high)


def place_call(base, source, arrived):
    mid = arrived[0].shape[1]
    smem = pl.BlockSpec(memory_space=pltpu.SMEM)
    vmem = pl.BlockSpec(memory_space=pltpu.VMEM)
    return pl.pallas_call(
        place_kernel,
        in_specs=[smem, smem] + [vmem] * K,
        out_specs=[vmem] * 3,
        out_shape=[
            jax.ShapeDtypeStruct((rows, mid), jnp.bfloat16)
            for rows in (SIDE * SIDE * COLS, 288, 288)
        ],
        scratch_shapes=[
            pltpu.VMEM((288, mid), jnp.bfloat16),
            pltpu.VMEM((288, mid), jnp.bfloat16),
            pltpu.VMEM((K * CAP * CELLS, mid), jnp.bfloat16),
        ],
        compiler_params=pltpu.CompilerParams(vmem_limit_bytes=VMEM_LIMIT),
        name="place",
    )(base, source, *arrived)


def edge_kernel(
    counts,
    base_ref,
    source_ref,
    block_ref,
    even_ref,
    odd_ref,
    before_ref,
    after_ref,
    even_out,
    odd_out,
    low_ref,
    high_ref,
):
    face_in(base_ref[0], counts[1], even_ref, odd_ref, before_ref, after_ref)
    for ref, planes, brick in ((low_ref, (0, 1), 0), (high_ref, (SIDE - 2, SIDE - 1), 3)):
        for k, plane in enumerate(planes):
            start = k * WIDE * COLS
            ref[start : start + 16] = before_ref[plane * 16 : plane * 16 + 16]
            ref[start + 16 : start + 144] = block_ref[plane * 128 : plane * 128 + 128]
            ref[start + 144 : start + 160] = after_ref[plane * 16 : plane * 16 + 16]
        flags = [before_ref[256:288].astype(jnp.float32)[brick * 8 : brick * 8 + 8]]
        flags += [slot_flags(source_ref, slot_index(brick, r)) for r in range(4)]
        flags += [after_ref[256:288].astype(jnp.float32)[brick * 8 : brick * 8 + 8]]
        ref[320:368] = jnp.concatenate(flags, axis=0).astype(jnp.bfloat16)
    face_out(base_ref[1], low_ref, high_ref, even_out, odd_out)


def edge_call(counts, base, source, block, even, odd):
    smem = pl.BlockSpec(memory_space=pltpu.SMEM)
    vmem = pl.BlockSpec(memory_space=pltpu.VMEM)
    mid = block.shape[1]
    return pl.pallas_call(
        functools.partial(edge_kernel, counts),
        in_specs=[smem, smem, vmem, vmem, vmem],
        out_specs=[vmem] * 4,
        out_shape=[
            jax.ShapeDtypeStruct((rows, mid), jnp.bfloat16) for rows in (288, 288, 368, 368)
        ],
        scratch_shapes=[pltpu.VMEM((368, mid), jnp.bfloat16)] * 2,
        compiler_params=pltpu.CompilerParams(vmem_limit_bytes=VMEM_LIMIT),
        name="edge",
    )(base, source, block, even, odd)


def gather_weights(w_ref, wide_ref):
    width = w_ref.shape[2]
    for tap in range(9):
        for column in range(3):
            wide_ref[tap * width : (tap + 1) * width, column * width : (column + 1) * width] = (
                w_ref[tap * 3 + column]
            )


def as_rows(value):
    value = value.astype(jnp.float32)
    return value.reshape(value.shape[0] // COLS, COLS, value.shape[1])


def moved_rows(rows):
    empty = jnp.zeros((1,) + rows.shape[1:], jnp.float32)
    return jnp.concatenate([rows[1:], empty], axis=0)


def as_tiles(rows):
    return rows.reshape(rows.shape[0] * COLS, rows.shape[2]).astype(jnp.bfloat16)


def multiply_taps(lhs, wide_ref):
    width = wide_ref.shape[1] // 3
    wide = jnp.dot(lhs, wide_ref[...], preferred_element_type=jnp.float32)
    wide = wide.reshape(lhs.shape[0] // COLS, COLS, 3 * width)
    column = lax.broadcasted_iota(jnp.int32, (lhs.shape[0] // COLS, COLS, width), 1)
    left = jnp.where(column == 0, 0.0, pltpu.roll(wide[:, :, :width], 1, 1))
    right = jnp.where(column == COLS - 1, 0.0, pltpu.roll(wide[:, :, 2 * width :], COLS - 1, 1))
    return left + wide[:, :, width : 2 * width] + right


def conv_planes(here_ref, next_ref, wide_ref, first, planes, rows):
    taps = []
    for dd in range(3):
        span = slice(first + dd, first + dd + planes)
        taps += [
            here_ref[span, 0:rows, :],
            next_ref[span, 0:rows, :],
            here_ref[span, 16 : rows + 16, :],
        ]
    lhs = jnp.concatenate(taps, axis=2)
    return multiply_taps(lhs.reshape(planes * rows, lhs.shape[2]), wide_ref)


def activate(value, flags):
    return value / (1.0 + jnp.exp(-value)) * flags


def spread_flags(flags, repeats):
    return jnp.concatenate(
        [jnp.broadcast_to(flag[None], (count,) + flag.shape) for flag, count in zip(flags, repeats)],
        axis=0,
    )


def inner_planes(source_ref, block_ref, wide1_ref, hidden_ref, here, moved, groups):
    width = block_ref.shape[1]
    base = groups[0][0] - 1
    for d in range(base, groups[-1][0] + groups[-1][1] + 1):
        plane = block_ref[d * 128 : (d + 1) * 128]
        here[d - base] = plane
        moved[d - base] = as_tiles(moved_rows(as_rows(plane)))
    inner = SIDE - 2
    rows = inner * COLS
    for first, planes in groups:
        value = conv_planes(here, moved, wide1_ref, first - 1 - base, planes, rows)
        value = value.reshape(planes, inner, COLS, width)
        flags = [slot_flags(source_ref, slot_index(first // 4, r)) for r in range(4)]
        value = activate(value, spread_flags(flags, (3, 4, 4, 3))[None])
        hidden_ref[first - 1 - base : first - 1 - base + planes] = value.reshape(
            planes, rows, width
        ).astype(jnp.bfloat16)


def inner_kernel(source_ref, block_ref, wide1_ref, hidden_ref, here, moved):
    inner_planes(source_ref, block_ref, wide1_ref, hidden_ref, here, moved, EARLY)


def conv_cost(rows, width):
    return pl.CostEstimate(
        flops=2 * rows * 27 * width * width, bytes_accessed=27 * width * width * 4, transcendentals=0
    )


def inner_call(source, block, wide1):
    mid = block.shape[1]
    smem = pl.BlockSpec(memory_space=pltpu.SMEM)
    vmem = pl.BlockSpec(memory_space=pltpu.VMEM)
    rows = (SIDE - 2) * COLS
    return pl.pallas_call(
        inner_kernel,
        in_specs=[smem, vmem, vmem],
        out_specs=vmem,
        out_shape=jax.ShapeDtypeStruct((EARLY_PLANES, rows, mid), jnp.bfloat16),
        scratch_shapes=[pltpu.VMEM((EARLY_PLANES + 2, SIDE * COLS, mid), jnp.bfloat16)] * 2,
        compiler_params=pltpu.CompilerParams(vmem_limit_bytes=VMEM_LIMIT),
        cost_estimate=conv_cost(EARLY_PLANES * rows, mid),
        name="inner",
    )(source, block, wide1)


def side_kernel(
    source_ref,
    block_ref,
    before_ref,
    after_ref,
    wide1_ref,
    hidden_ref,
    late_ref,
    mixed,
    here,
    moved,
):
    inner_planes(source_ref, block_ref, wide1_ref, late_ref, here, moved, LATE)
    width = block_ref.shape[1]
    for d in range(SIDE):
        edge = slice(d * 16, (d + 1) * 16)
        low = as_rows(block_ref[d * 128 : d * 128 + 16])
        high = as_rows(block_ref[d * 128 + 112 : d * 128 + 128])
        before = as_rows(before_ref[edge])
        after = as_rows(after_ref[edge])
        mixed[0, edge] = as_tiles(jnp.concatenate([before[1:], low[:1]], axis=0))
        mixed[1, edge] = as_tiles(jnp.concatenate([high[1:], after[:1]], axis=0))
    inner = SIDE - 2
    taps = []
    for dd in range(3):
        span = slice(dd * 16, (dd + inner) * 16)
        low = [block_ref[(d + dd) * 128 : (d + dd) * 128 + 16] for d in range(inner)]
        high = [block_ref[(d + dd) * 128 + 112 : (d + dd) * 128 + 128] for d in range(inner)]
        taps.append(jnp.concatenate([before_ref[span]] + high, axis=0))
        taps.append(jnp.concatenate([mixed[0, span], mixed[1, span]], axis=0))
        taps.append(jnp.concatenate(low + [after_ref[span]], axis=0))
    value = multiply_taps(jnp.concatenate(taps, axis=1), wide1_ref)
    depths = (3, 4, 4, 3)
    edge_flags = (as_rows(before_ref[256:288]), as_rows(after_ref[256:288]))
    flags = []
    for side, row_brick in ((0, 0), (1, 3)):
        own = [slot_flags(source_ref, slot_index(d, row_brick)) for d in range(4)]
        pairs = [jnp.stack([edge_flags[side][d], own[d]][:: 1 - 2 * side], axis=0) for d in range(4)]
        flags.append(spread_flags(pairs, depths))
    flags = jnp.stack(flags, axis=0)
    value = activate(value.reshape(2, inner, 2, COLS, width), flags)
    hidden_ref[...] = value.reshape(2, inner, 16, width).astype(jnp.bfloat16)


def side_call(source, block, before, after, wide1):
    mid = block.shape[1]
    smem = pl.BlockSpec(memory_space=pltpu.SMEM)
    vmem = pl.BlockSpec(memory_space=pltpu.VMEM)
    inner = SIDE - 2
    return pl.pallas_call(
        side_kernel,
        in_specs=[smem] + [vmem] * 4,
        out_specs=[vmem] * 2,
        out_shape=[
            jax.ShapeDtypeStruct((2, inner, 16, mid), jnp.bfloat16),
            jax.ShapeDtypeStruct((LATE_PLANES, inner * COLS, mid), jnp.bfloat16),
        ],
        scratch_shapes=[
            pltpu.VMEM((2, SIDE * 16, mid), jnp.bfloat16),
            pltpu.VMEM((LATE_PLANES + 2, SIDE * COLS, mid), jnp.bfloat16),
            pltpu.VMEM((LATE_PLANES + 2, SIDE * COLS, mid), jnp.bfloat16),
        ],
        compiler_params=pltpu.CompilerParams(vmem_limit_bytes=VMEM_LIMIT),
        cost_estimate=conv_cost(inner * (4 + LATE_PLANES) * COLS, mid),
        name="side",
    )(source, block, before, after, wide1)


def final_kernel(count, base_ref, source_ref, *refs):
    block_ref, before_ref, after_ref, even_ref, odd_ref = refs[:5]
    early_ref, late_ref, side_ref, wide1_ref, wide2_ref, coarse_ref = refs[5:11]
    backs = refs[11 : 11 + K]
    x_here, x_next, h_here, h_next, stage, under_ref, over_ref = refs[11 + K :]
    face_in(base_ref[1], count, even_ref, odd_ref, under_ref, over_ref)
    width = block_ref.shape[1]
    flags_before = as_rows(before_ref[256:288])
    flags_after = as_rows(after_ref[256:288])
    for end, ref in ((0, under_ref), (1, over_ref)):
        planes = []
        own = [0, 1] if end == 0 else [SIDE - 2, SIDE - 1]
        for d in own:
            edge = slice(d * 16, (d + 1) * 16)
            planes.append(
                jnp.concatenate(
                    [before_ref[edge], block_ref[d * 128 : (d + 1) * 128], after_ref[edge]], axis=0
                )
            )
        far = [ref[k * 160 : (k + 1) * 160] for k in range(2)]
        for index, plane in enumerate(far + planes if end == 0 else planes + far):
            x_here[index] = plane
            x_next[index] = as_tiles(moved_rows(as_rows(plane)))
        value = conv_planes(x_here, x_next, wide1_ref, 0, 2, HID * COLS)
        value = value.reshape(2, HID, COLS, width)
        far_flags = as_rows(ref[320:368])
        brick = 0 if end == 0 else 3
        own_flags = [flags_before[brick]]
        own_flags += [slot_flags(source_ref, slot_index(brick, r)) for r in range(4)]
        own_flags += [flags_after[brick]]
        spread = [
            spread_flags([far_flags[r] for r in range(6)], (1, 4, 4, 4, 4, 1)),
            spread_flags(own_flags, (1, 4, 4, 4, 4, 1)),
        ]
        for k in range(2):
            flags = spread[k if end == 0 else 1 - k]
            rows = activate(value[k], flags)
            index = k if end == 0 else HID - 2 + k
            h_here[index] = as_tiles(rows)
            h_next[index] = as_tiles(moved_rows(rows))
    for d in range(SIDE - 2):
        middle = early_ref[d] if d < EARLY_PLANES else late_ref[d - EARLY_PLANES]
        plane = jnp.concatenate([side_ref[0, d], middle, side_ref[1, d]], axis=0)
        h_here[d + 2] = plane
        h_next[d + 2] = as_tiles(moved_rows(as_rows(plane)))

    stage[...] = jnp.zeros(stage.shape, jnp.bfloat16)
    for depth_brick in range(4):
        value = conv_planes(h_here, h_next, wide2_ref, depth_brick * 4, 4, SIDE * COLS)
        value = value.reshape(4, SIDE, COLS, width)
        rows = slice(depth_brick * 512, (depth_brick + 1) * 512)
        own = block_ref[rows].astype(jnp.float32).reshape(4, SIDE, COLS, width)
        flags = [slot_flags(source_ref, slot_index(depth_brick, r)) for r in range(4)]
        value = (value + own) * spread_flags(flags, (4, 4, 4, 4))[None]
        coarse_ref[rows] = value.reshape(4 * SIDE * COLS, width).astype(jnp.bfloat16)
        half = low_half((4, 2, COLS, width))
        for r in range(4):
            part = value[:, r * 4 : (r + 1) * 4].reshape(4, 2, 2, COLS, width)
            even, odd = part[:, :, 0], part[:, :, 1]
            b0 = jnp.where(half, even, pltpu.roll(odd, 4, 2))
            b1 = jnp.where(half, pltpu.roll(even, 4, 2), odd)
            slot = slot_index(depth_brick, r)
            for k, brick in enumerate((b0, b1)):
                source = source_ref[slot + k]
                row = pl.multiple_of(jnp.where(source >= 0, source, K * CAP) * CELLS, CELLS)
                stage[pl.ds(row, CELLS), :] = brick.reshape(CELLS, width).astype(jnp.bfloat16)
    for j in range(K):
        backs[j][...] = stage[j * CAP * CELLS : (j + 1) * CAP * CELLS]


def final_call(count, base, source, block, halo, hidden, wide1, wide2):
    mid = block.shape[1]
    smem = pl.BlockSpec(memory_space=pltpu.SMEM)
    vmem = pl.BlockSpec(memory_space=pltpu.VMEM)
    return pl.pallas_call(
        functools.partial(final_kernel, count),
        in_specs=[smem, smem] + [vmem] * 10,
        out_specs=[vmem] * (1 + K),
        out_shape=[
            jax.ShapeDtypeStruct(block.shape, jnp.bfloat16),
        ]
        + [jax.ShapeDtypeStruct((CAP * CELLS, mid), jnp.bfloat16)] * K,
        scratch_shapes=[
            pltpu.VMEM((4, WIDE * COLS, mid), jnp.bfloat16),
            pltpu.VMEM((4, WIDE * COLS, mid), jnp.bfloat16),
            pltpu.VMEM((HID, HID * COLS, mid), jnp.bfloat16),
            pltpu.VMEM((HID, HID * COLS, mid), jnp.bfloat16),
            pltpu.VMEM(((K * CAP + 1) * CELLS, mid), jnp.bfloat16),
            pltpu.VMEM((368, mid), jnp.bfloat16),
            pltpu.VMEM((368, mid), jnp.bfloat16),
        ],
        compiler_params=pltpu.CompilerParams(vmem_limit_bytes=VMEM_LIMIT),
        cost_estimate=conv_cost(SIDE * SIDE * COLS, mid),
        name="final",
    )(base, source, block, *halo, *hidden, wide1, wide2)


def from_behind(value, axis, steps):
    count = lax.axis_size(axis)
    pairs = [(source, (source + steps) % count) for source in range(count)]
    return lax.ppermute(value, axis, pairs)


def swap_faces(even, odd, axis):
    count = lax.axis_size(axis)
    swapped = []
    for face, first in ((even, 0), (odd, 1)):
        partner = list(range(count))
        for i in range(first, count - 1, 2):
            partner[i], partner[i + 1] = i + 1, i
        swapped.append(lax.ppermute(face, axis, list(enumerate(partner))))
    return swapped


def shards(fine, fine_mask, slot_source, w_down, w_first, w_second, w_up):
    mid = w_down.shape[1]
    base = jnp.stack([lax.axis_index("xy"), lax.axis_index("gz")]).astype(jnp.int32)
    counts = (lax.axis_size("gz"), lax.axis_size("xy"))
    sent = down_call(fine, fine_mask, w_down, FIRST_SENT)
    arrived = {j: from_behind(sent[j], "xy", j) for j in FIRST_SENT}
    fine_again, sent[FIRST_SENT[0]] = lax.optimization_barrier((fine, sent[FIRST_SENT[0]]))
    sent = down_call(fine_again, fine_mask, w_down, LAST_SENT)
    arrived.update({j: from_behind(sent[j], "xy", j) for j in LAST_SENT})
    middle = LAST_SENT[1]
    later = (arrived[middle], fine, fine_mask, w_down, w_first, w_second)
    arrived[middle], *later = lax.optimization_barrier(later)
    prepared = lax.optimization_barrier(tuple(prepare_call(*later)))
    arrived[0], mask, wide1, wide2 = prepared
    block, even, odd = place_call(base, slot_source, [arrived[j] for j in range(K)])
    even, odd = swap_faces(even, odd, "xy")
    early = inner_call(slot_source, block, wide1)
    even, odd, early = lax.optimization_barrier((even, odd, early))
    before, after, even, odd = edge_call(counts, base, slot_source, block, even, odd)
    even, odd = swap_faces(even, odd, "gz")
    side, late = side_call(slot_source, block, before, after, wide1)
    coarse, *back = final_call(
        counts[0],
        base,
        slot_source,
        block,
        (before, after, even, odd),
        (early, late, side),
        wide1,
        wide2,
    )
    octant = {j: from_behind(back[j], "xy", -j) for j in RETURNED}
    octant[0] = back[0]
    fine_out = up_call(fine, mask, w_up, [octant[j] for j in (6, 7, 0, 1)], 3, None)
    fine_out = up_call(fine, mask, w_up, [octant[j] for j in (2, 3, 4, 5)], 1, fine_out)
    return fine_out, coarse.reshape(SIDE, SIDE, COLS, mid)


def solution(mesh):
    placed = (
        P(("gz", "xy"), None, None),
        P(("gz", "xy"), None),
        P(("gz", "xy")),
        P(),
        P(),
        P(),
        P(),
    )
    return jax.shard_map(
        shards,
        mesh=mesh,
        in_specs=placed,
        out_specs=(P(("gz", "xy"), None, None), P("gz", "xy", None, None)),
        check_vma=False,
    )
```

```python
import functools

import jax
import jax.numpy as jnp
from jax import lax
from jax.experimental import pallas as pl
from jax.experimental.pallas import tpu as pltpu
from jax.sharding import PartitionSpec as P

CAP = 4
K = 8
CELLS = 64
SIDE = 16
COLS = 8
WIDE = SIDE + 4
HID = SIDE + 2
EARLY = ((1, 3), (4, 4), (8, 4))
LATE = ((12, 3),)
EARLY_PLANES = 11
LATE_PLANES = 3
SENT = (4, 3, 5, 2, 6, 1, 7)
UP_GROUPS = ((3, 4, 5, 0), (6, 7, 1, 2))
DOWN_LIMIT = 62 * 1024 * 1024
VMEM_LIMIT = 24 * 1024 * 1024


def expand_mask(mask):
    bricks = mask.shape[0]
    values = mask.astype(jnp.float32)
    cell = lax.broadcasted_iota(jnp.int32, (16, 128), 0)
    lane = lax.broadcasted_iota(jnp.int32, (16, 128), 1)
    chosen = (cell == lane // 8).astype(jnp.float32)
    parts = [
        values[:, t * 128 : (t + 1) * 128].reshape(bricks, 1, 128) * chosen[None] for t in range(4)
    ]
    spread = jnp.concatenate(parts, axis=1).reshape(bricks * CELLS, 128).astype(jnp.bfloat16)
    source = lax.broadcasted_iota(jnp.int32, (128, 512), 0)
    target = lax.broadcasted_iota(jnp.int32, (128, 512), 1)
    widen = ((source & 7) == (target >> 6)).astype(jnp.bfloat16)
    return jnp.dot(spread, widen, preferred_element_type=jnp.float32)


def down_kernel(offsets, fine_hbm, mask_hbm, w_hbm, *refs):
    count = len(offsets)
    outs = refs[:count]
    fine_ref, mask_ref, w_ref, wide_ref, sems = refs[count:]
    first = [
        pltpu.make_async_copy(mask_hbm, mask_ref, sems.at[count]),
        pltpu.make_async_copy(w_hbm, w_ref, sems.at[count + 1]),
    ]
    chunks = [
        pltpu.make_async_copy(fine_hbm.at[pl.ds(j * CAP, CAP)], fine_ref.at[k], sems.at[k])
        for k, j in enumerate(offsets)
    ]
    for copy in first + chunks:
        copy.start()
    first[0].wait()
    rows = CAP * CELLS
    for k, j in enumerate(offsets):
        wide_ref[k * rows : (k + 1) * rows] = expand_mask(
            mask_ref[j * CAP : (j + 1) * CAP]
        ).astype(jnp.bfloat16)
    first[1].wait()
    for start in range(0, count, 2):
        group = range(start, min(start + 2, count))
        for k in group:
            chunks[k].wait()
        x = [
            fine_ref[k].reshape(rows, -1) * wide_ref[k * rows : (k + 1) * rows] for k in group
        ]
        y = jnp.dot(jnp.concatenate(x, axis=0), w_ref[...], preferred_element_type=jnp.float32)
        y = y.astype(jnp.bfloat16)
        for part, k in enumerate(group):
            outs[k][...] = y[part * rows : (part + 1) * rows]


def down_call(fine, mask, w, offsets):
    cells, width = fine.shape[1:]
    mid = w.shape[1]
    count = len(offsets)
    rows = count * CAP * cells
    hbm = pl.BlockSpec(memory_space=pltpu.HBM)
    outs = pl.pallas_call(
        functools.partial(down_kernel, offsets),
        in_specs=[hbm, hbm, hbm],
        out_specs=[pl.BlockSpec(memory_space=pltpu.VMEM)] * count,
        out_shape=[jax.ShapeDtypeStruct((CAP * cells, mid), jnp.bfloat16)] * count,
        scratch_shapes=[
            pltpu.VMEM((count, CAP, cells, width), fine.dtype),
            pltpu.VMEM(mask.shape, mask.dtype),
            pltpu.VMEM(w.shape, w.dtype),
            pltpu.VMEM((rows, width), jnp.bfloat16),
            pltpu.SemaphoreType.DMA((count + 2,)),
        ],
        compiler_params=pltpu.CompilerParams(vmem_limit_bytes=DOWN_LIMIT),
        cost_estimate=pl.CostEstimate(
            flops=2 * rows * width * mid, bytes_accessed=rows * width * 2, transcendentals=0
        ),
        name="down",
    )(fine, mask, w)
    return dict(zip(offsets, outs))


def prepare_kernel(
    fine_ref, mask_ref, w_down_ref, w1_ref, w2_ref, own_ref, mask_out, wide1_ref, wide2_ref
):
    gather_weights(w1_ref, wide1_ref)
    gather_weights(w2_ref, wide2_ref)
    step = 8
    for part in range(mask_ref.shape[0] // step):
        rows = slice(part * step * CELLS, (part + 1) * step * CELLS)
        mask_out[rows] = expand_mask(mask_ref[part * step : (part + 1) * step]).astype(jnp.bfloat16)
    rows = CAP * CELLS
    own = fine_ref[...].reshape(rows, -1) * mask_out[:rows]
    own = jnp.dot(own, w_down_ref[...], preferred_element_type=jnp.float32)
    own_ref[...] = own.astype(jnp.bfloat16)


def prepare_call(fine, mask, w_down, w_first, w_second):
    mid = w_first.shape[1]
    vmem = pl.BlockSpec(memory_space=pltpu.VMEM)
    rows = mask.shape[0] * CELLS
    wide = jax.ShapeDtypeStruct((9 * mid, 3 * mid), jnp.bfloat16)
    return pl.pallas_call(
        prepare_kernel,
        grid=(1,),
        in_specs=[pl.BlockSpec((CAP,) + fine.shape[1:], lambda i: (0, 0, 0))] + [vmem] * 4,
        out_specs=[vmem] * 4,
        out_shape=[
            jax.ShapeDtypeStruct((CAP * CELLS, mid), jnp.bfloat16),
            jax.ShapeDtypeStruct((rows, mask.shape[1]), jnp.bfloat16),
            wide,
            wide,
        ],
        compiler_params=pltpu.CompilerParams(vmem_limit_bytes=VMEM_LIMIT),
        cost_estimate=pl.CostEstimate(
            flops=2 * rows * mask.shape[1] * 128, bytes_accessed=rows * mask.shape[1] * 2, transcendentals=0
        ),
        name="prepare",
    )(fine, mask, w_down, w_first, w_second)


def up_kernel(fine_ref, mask_ref, w_ref, *refs):
    out_ref = refs[-1]
    step = pl.program_id(0)
    bricks, cells, width = fine_ref.shape
    octant = refs[0][...]
    for other in range(1, len(UP_GROUPS[0])):
        octant = jnp.where(step == other, refs[other][...], octant)
    up = jnp.dot(octant, w_ref[...], preferred_element_type=jnp.float32)
    fine = fine_ref[...].reshape(bricks * cells, width)
    mask = mask_ref[...].astype(jnp.float32)
    out = jnp.where(mask > 0.5, fine.astype(jnp.float32) + up, 0.0)
    out_ref[...] = out.astype(jnp.bfloat16).reshape(bricks, cells, width)


def up_call(fine, mask, w, octants, offsets, partial):
    bricks, cells, width = fine.shape
    mid = w.shape[0]
    count = len(offsets)

    def place(i):
        index = offsets[0]
        for k in range(1, count):
            index = jnp.where(i == k, offsets[k], index)
        return index

    partials = [] if partial is None else [partial]
    return pl.pallas_call(
        up_kernel,
        grid=(count,),
        in_specs=[
            pl.BlockSpec((CAP, cells, width), lambda i: (place(i), 0, 0)),
            pl.BlockSpec((CAP * cells, width), lambda i: (place(i), 0)),
            pl.BlockSpec((mid, width), lambda i: (0, 0)),
        ]
        + [pl.BlockSpec((CAP * cells, mid), lambda i: (0, 0))] * count
        + [pl.BlockSpec(memory_space=pl.ANY)] * len(partials),
        out_specs=pl.BlockSpec((CAP, cells, width), lambda i: (place(i), 0, 0)),
        out_shape=jax.ShapeDtypeStruct(fine.shape, jnp.bfloat16),
        input_output_aliases={3 + count: 0} if partials else {},
        compiler_params=pltpu.CompilerParams(vmem_limit_bytes=VMEM_LIMIT),
        cost_estimate=pl.CostEstimate(
            flops=2 * count * CAP * cells * width * mid,
            bytes_accessed=count * CAP * cells * width * 4,
            transcendentals=0,
        ),
        name="up",
    )(fine, mask, w, *octants, *partials)


def low_half(shape):
    return lax.broadcasted_iota(jnp.int32, shape, len(shape) - 2) < 4


def slot_flags(source_ref, first):
    pair = [jnp.where(source_ref[first + k] >= 0, 1.0, 0.0).astype(jnp.float32) for k in range(2)]
    return jnp.where(low_half((8, 128)), pair[0], pair[1])


def slot_index(depth_brick, row_brick):
    pd, qd = divmod(depth_brick, 2)
    pr, qr = divmod(row_brick, 2)
    return (pd * 2 + pr) * 8 + qd * 4 + qr * 2


def take_brick(source_ref, arrived, slot):
    value = source_ref[slot]
    first = pl.multiple_of(jnp.maximum(value, 0) * CELLS, CELLS)
    brick = arrived[pl.ds(first, CELLS), :].astype(jnp.float32)
    return jnp.where(value >= 0, brick, 0.0).reshape(8, 8, 128)


def place_kernel(base_ref, source_ref, *refs):
    block_ref, even_ref, odd_ref, gz_even_ref, gz_odd_ref = refs[K : K + 5]
    low_ref, high_ref, under_ref, over_ref, arrived = refs[K + 5 :]
    for j in range(K):
        arrived[j * CAP * CELLS : (j + 1) * CAP * CELLS] = refs[j][...]
    half = low_half((8, 8, 128))
    for depth_brick in range(4):
        for row_brick in range(4):
            slot = slot_index(depth_brick, row_brick)
            b0 = take_brick(source_ref, arrived, slot)
            b1 = take_brick(source_ref, arrived, slot + 1)
            even = jnp.where(half, b0, pltpu.roll(b1, 4, 1))
            odd = jnp.where(half, pltpu.roll(b0, 4, 1), b1)
            both = jnp.stack([even, odd], axis=1).reshape(4, 32, 128).astype(jnp.bfloat16)
            for vd in range(4):
                row = ((depth_brick * 4 + vd) * SIDE + row_brick * 4) * COLS
                block_ref[row : row + 32] = both[vd]
                place = (depth_brick * 4 + vd) * 16
                if row_brick == 0:
                    low_ref[place : place + 16] = both[vd, :16]
                if row_brick == 3:
                    high_ref[place : place + 16] = both[vd, 16:]
    for row_brick, ref in ((0, low_ref), (3, high_ref)):
        flags = [slot_flags(source_ref, slot_index(d, row_brick)) for d in range(4)]
        ref[256:288] = jnp.concatenate(flags, axis=0).astype(jnp.bfloat16)
    face_out(base_ref[0], low_ref, high_ref, even_ref, odd_ref)
    for depth_brick, ref in ((0, under_ref), (3, over_ref)):
        first = 0 if depth_brick == 0 else (SIDE - 2) * 128
        ref[0:256] = block_ref[first : first + 256]
        flags = [slot_flags(source_ref, slot_index(depth_brick, r)) for r in range(4)]
        ref[256:288] = jnp.concatenate(flags, axis=0).astype(jnp.bfloat16)
    face_out(base_ref[1], under_ref, over_ref, gz_even_ref, gz_odd_ref)


def face_out(index, low_ref, high_ref, even_ref, odd_ref):
    is_even = index % 2 == 0
    even_ref[...] = jnp.where(is_even, high_ref[...], low_ref[...])
    odd_ref[...] = jnp.where(is_even, low_ref[...], high_ref[...])


def face_in(index, count, even_ref, odd_ref, low_ref, high_ref):
    is_even = index % 2 == 0
    empty = jnp.zeros(low_ref.shape, low_ref.dtype)
    low = jnp.where(is_even, odd_ref[...], even_ref[...])
    high = jnp.where(is_even, even_ref[...], odd_ref[...])
    low_ref[...] = jnp.where(index == 0, empty, low)
    high_ref[...] = jnp.where(index == count - 1, empty, high)


def place_call(base, source, arrived):
    mid = arrived[0].shape[1]
    smem = pl.BlockSpec(memory_space=pltpu.SMEM)
    vmem = pl.BlockSpec(memory_space=pltpu.VMEM)
    return pl.pallas_call(
        place_kernel,
        in_specs=[smem, smem] + [vmem] * K,
        out_specs=[vmem] * 5,
        out_shape=[
            jax.ShapeDtypeStruct((rows, mid), jnp.bfloat16)
            for rows in (SIDE * SIDE * COLS, 288, 288, 288, 288)
        ],
        scratch_shapes=[
            pltpu.VMEM((288, mid), jnp.bfloat16),
            pltpu.VMEM((288, mid), jnp.bfloat16),
            pltpu.VMEM((288, mid), jnp.bfloat16),
            pltpu.VMEM((288, mid), jnp.bfloat16),
            pltpu.VMEM((K * CAP * CELLS, mid), jnp.bfloat16),
        ],
        compiler_params=pltpu.CompilerParams(vmem_limit_bytes=VMEM_LIMIT),
        name="place",
    )(base, source, *arrived)


def corner_kernel(counts, base_ref, *refs):
    faces = refs[:4]
    before_ref, after_ref, under_ref, over_ref, even_out, odd_out, low_ref, high_ref = refs[4:]
    face_in(base_ref[0], counts[1], faces[0], faces[1], before_ref, after_ref)
    face_in(base_ref[1], counts[0], faces[2], faces[3], under_ref, over_ref)
    flags_before = as_rows(before_ref[256:288])
    flags_after = as_rows(after_ref[256:288])
    for ref, first, brick in ((low_ref, 0, 0), (high_ref, (SIDE - 2) * 16, 3)):
        ref[0:32] = before_ref[first : first + 32]
        ref[32:64] = after_ref[first : first + 32]
        ref[64:80] = as_tiles(jnp.stack([flags_before[brick], flags_after[brick]], axis=0))
    face_out(base_ref[1], low_ref, high_ref, even_out, odd_out)


def corner_call(counts, base, faces):
    smem = pl.BlockSpec(memory_space=pltpu.SMEM)
    vmem = pl.BlockSpec(memory_space=pltpu.VMEM)
    mid = faces[0].shape[1]
    return pl.pallas_call(
        functools.partial(corner_kernel, counts),
        in_specs=[smem] + [vmem] * 4,
        out_specs=[vmem] * 6,
        out_shape=[
            jax.ShapeDtypeStruct((rows, mid), jnp.bfloat16) for rows in (288, 288, 288, 288, 80, 80)
        ],
        scratch_shapes=[pltpu.VMEM((80, mid), jnp.bfloat16)] * 2,
        compiler_params=pltpu.CompilerParams(vmem_limit_bytes=VMEM_LIMIT),
        name="corner",
    )(base, *faces)


def gather_weights(w_ref, wide_ref):
    width = w_ref.shape[2]
    for tap in range(9):
        for column in range(3):
            wide_ref[tap * width : (tap + 1) * width, column * width : (column + 1) * width] = (
                w_ref[tap * 3 + column]
            )


def as_rows(value):
    value = value.astype(jnp.float32)
    return value.reshape(value.shape[0] // COLS, COLS, value.shape[1])


def moved_rows(rows):
    empty = jnp.zeros((1,) + rows.shape[1:], jnp.float32)
    return jnp.concatenate([rows[1:], empty], axis=0)


def as_tiles(rows):
    return rows.reshape(rows.shape[0] * COLS, rows.shape[2]).astype(jnp.bfloat16)


def multiply_taps(lhs, wide_ref):
    width = wide_ref.shape[1] // 3
    wide = jnp.dot(lhs, wide_ref[...], preferred_element_type=jnp.float32)
    wide = wide.reshape(lhs.shape[0] // COLS, COLS, 3 * width)
    column = lax.broadcasted_iota(jnp.int32, (lhs.shape[0] // COLS, COLS, width), 1)
    left = jnp.where(column == 0, 0.0, pltpu.roll(wide[:, :, :width], 1, 1))
    right = jnp.where(column == COLS - 1, 0.0, pltpu.roll(wide[:, :, 2 * width :], COLS - 1, 1))
    return left + wide[:, :, width : 2 * width] + right


def plane_taps(here_ref, next_ref, first, planes, rows):
    taps = []
    for dd in range(3):
        span = slice(first + dd, first + dd + planes)
        taps += [
            here_ref[span, 0:rows, :],
            next_ref[span, 0:rows, :],
            here_ref[span, 16 : rows + 16, :],
        ]
    lhs = jnp.concatenate(taps, axis=2)
    return lhs.reshape(planes * rows, lhs.shape[2])


def conv_planes(here_ref, next_ref, wide_ref, first, planes, rows):
    return multiply_taps(plane_taps(here_ref, next_ref, first, planes, rows), wide_ref)


def activate(value, flags):
    return value / (1.0 + jnp.exp(-value)) * flags


def spread_flags(flags, repeats):
    return jnp.concatenate(
        [jnp.broadcast_to(flag[None], (count,) + flag.shape) for flag, count in zip(flags, repeats)],
        axis=0,
    )


def inner_planes(source_ref, block_ref, wide1_ref, hidden_ref, here, moved, groups):
    width = block_ref.shape[1]
    base = groups[0][0] - 1
    for d in range(base, groups[-1][0] + groups[-1][1] + 1):
        plane = block_ref[d * 128 : (d + 1) * 128]
        here[d - base] = plane
        moved[d - base] = as_tiles(moved_rows(as_rows(plane)))
    inner = SIDE - 2
    rows = inner * COLS
    for first, planes in groups:
        value = conv_planes(here, moved, wide1_ref, first - 1 - base, planes, rows)
        value = value.reshape(planes, inner, COLS, width)
        flags = [slot_flags(source_ref, slot_index(first // 4, r)) for r in range(4)]
        value = activate(value, spread_flags(flags, (3, 4, 4, 3))[None])
        hidden_ref[first - 1 - base : first - 1 - base + planes] = value.reshape(
            planes, rows, width
        ).astype(jnp.bfloat16)


def inner_kernel(source_ref, block_ref, wide1_ref, hidden_ref, here, moved):
    inner_planes(source_ref, block_ref, wide1_ref, hidden_ref, here, moved, EARLY)


def conv_cost(rows, width):
    return pl.CostEstimate(
        flops=2 * rows * 27 * width * width, bytes_accessed=27 * width * width * 4, transcendentals=0
    )


def inner_call(source, block, wide1):
    mid = block.shape[1]
    smem = pl.BlockSpec(memory_space=pltpu.SMEM)
    vmem = pl.BlockSpec(memory_space=pltpu.VMEM)
    rows = (SIDE - 2) * COLS
    return pl.pallas_call(
        inner_kernel,
        in_specs=[smem, vmem, vmem],
        out_specs=vmem,
        out_shape=jax.ShapeDtypeStruct((EARLY_PLANES, rows, mid), jnp.bfloat16),
        scratch_shapes=[pltpu.VMEM((EARLY_PLANES + 2, SIDE * COLS, mid), jnp.bfloat16)] * 2,
        compiler_params=pltpu.CompilerParams(vmem_limit_bytes=VMEM_LIMIT),
        cost_estimate=conv_cost(EARLY_PLANES * rows, mid),
        name="inner",
    )(source, block, wide1)


def side_taps(low, high):
    mixed = as_tiles(
        jnp.concatenate(
            [as_rows(low).reshape(-1, 2, COLS, 128)[:, 1:], as_rows(high).reshape(-1, 2, COLS, 128)[:, :1]],
            axis=1,
        ).reshape(-1, COLS, 128)
    )
    return low, mixed, high


def depth_taps(taps, planes):
    parts = [tap[dd * 16 : (dd + planes) * 16] for dd in range(3) for tap in taps]
    return jnp.concatenate(parts, axis=1)


def coarse_rows(source_ref, block_ref, value, depth_brick):
    width = block_ref.shape[1]
    value = value.reshape(4, SIDE, COLS, width)
    rows = slice(depth_brick * 512, (depth_brick + 1) * 512)
    own = block_ref[rows].astype(jnp.float32).reshape(4, SIDE, COLS, width)
    flags = [slot_flags(source_ref, slot_index(depth_brick, r)) for r in range(4)]
    return (value + own) * spread_flags(flags, (4, 4, 4, 4))[None]


def middle_kernel(source_ref, *refs):
    block_ref, before_ref, after_ref, under_ref, over_ref, early_ref, wide1_ref, wide2_ref = refs[:8]
    border_ref, h_here, h_next, coarse_ref, side, late, ends, ends_moved, here, moved = refs[8:]
    width = block_ref.shape[1]
    inner = SIDE - 2
    inner_planes(source_ref, block_ref, wide1_ref, late, here, moved, LATE)

    low = jnp.concatenate([block_ref[d * 128 : d * 128 + 16] for d in range(SIDE)], axis=0)
    high = jnp.concatenate([block_ref[d * 128 + 112 : d * 128 + 128] for d in range(SIDE)], axis=0)
    left = depth_taps(side_taps(before_ref[0:256], low), inner)
    right = depth_taps(side_taps(high, after_ref[0:256]), inner)
    value = multiply_taps(jnp.concatenate([left, right], axis=0), wide1_ref)
    depths = (3, 4, 4, 3)
    edge_flags = (as_rows(before_ref[256:288]), as_rows(after_ref[256:288]))
    flags = []
    for end, row_brick in ((0, 0), (1, 3)):
        own = [slot_flags(source_ref, slot_index(d, row_brick)) for d in range(4)]
        pairs = [jnp.stack([edge_flags[end][d], own[d]][:: 1 - 2 * end], axis=0) for d in range(4)]
        flags.append(spread_flags(pairs, depths))
    value = activate(value.reshape(2, inner, 2, COLS, width), jnp.stack(flags, axis=0))
    side[...] = value.reshape(2, inner, 16, width).astype(jnp.bfloat16)
    for d in range(inner):
        centre = early_ref[d] if d < EARLY_PLANES else late[d - EARLY_PLANES]
        plane = jnp.concatenate([side[0, d], centre, side[1, d]], axis=0)
        h_here[d] = plane
        h_next[d] = as_tiles(moved_rows(as_rows(plane)))

    for k in range(2):
        planes = (
            (k, under_ref[k * 128 : (k + 1) * 128]),
            (2 + k, block_ref[k * 128 : (k + 1) * 128]),
            (4 + k, block_ref[(SIDE - 2 + k) * 128 : (SIDE - 1 + k) * 128]),
            (6 + k, over_ref[k * 128 : (k + 1) * 128]),
        )
        for index, plane in planes:
            ends[index] = plane
            ends_moved[index] = as_tiles(moved_rows(as_rows(plane)))
    lhs = [plane_taps(ends, ends_moved, first, 2, inner * COLS) for first in (0, 4)]
    value = multiply_taps(jnp.concatenate(lhs, axis=0), wide1_ref)
    far = (as_rows(under_ref[256:288]), as_rows(over_ref[256:288]))
    flags = []
    for end, brick in ((0, 0), (1, 3)):
        outer = [far[end][r] for r in range(4)]
        own = [slot_flags(source_ref, slot_index(brick, r)) for r in range(4)]
        for chosen in (outer, own) if end == 0 else (own, outer):
            flags.append(spread_flags(chosen, (3, 4, 4, 3)))
    value = activate(value.reshape(4, inner, COLS, width), jnp.stack(flags, axis=0))
    border_ref[...] = value.reshape(4, inner * COLS, width).astype(jnp.bfloat16)

    for depth_brick in (1, 2):
        value = conv_planes(h_here, h_next, wide2_ref, depth_brick * 4 - 2, 4, SIDE * COLS)
        value = coarse_rows(source_ref, block_ref, value, depth_brick)
        rows = slice((depth_brick - 1) * 512, depth_brick * 512)
        coarse_ref[rows] = value.reshape(512, width).astype(jnp.bfloat16)


def middle_call(source, block, before, after, under, over, early, wide1, wide2):
    mid = block.shape[1]
    smem = pl.BlockSpec(memory_space=pltpu.SMEM)
    vmem = pl.BlockSpec(memory_space=pltpu.VMEM)
    inner = SIDE - 2
    hidden = (inner, HID * COLS, mid)
    return pl.pallas_call(
        middle_kernel,
        in_specs=[smem] + [vmem] * 8,
        out_specs=[vmem] * 4,
        out_shape=[
            jax.ShapeDtypeStruct(shape, jnp.bfloat16)
            for shape in ((4, inner * COLS, mid), hidden, hidden, (1024, mid))
        ],
        scratch_shapes=[
            pltpu.VMEM((2, inner, 16, mid), jnp.bfloat16),
            pltpu.VMEM((LATE_PLANES, inner * COLS, mid), jnp.bfloat16),
            pltpu.VMEM((8, SIDE * COLS, mid), jnp.bfloat16),
            pltpu.VMEM((8, SIDE * COLS, mid), jnp.bfloat16),
            pltpu.VMEM((LATE_PLANES + 2, SIDE * COLS, mid), jnp.bfloat16),
            pltpu.VMEM((LATE_PLANES + 2, SIDE * COLS, mid), jnp.bfloat16),
        ],
        compiler_params=pltpu.CompilerParams(vmem_limit_bytes=VMEM_LIMIT),
        cost_estimate=conv_cost(inner * (8 + LATE_PLANES) * COLS + 1024, mid),
        name="middle",
    )(source, block, before, after, under, over, early, wide1, wide2)


def scatter_bricks(source_ref, stage, value, depth_brick):
    width = value.shape[3]
    half = low_half((4, 2, COLS, width))
    for r in range(4):
        part = value[:, r * 4 : (r + 1) * 4].reshape(4, 2, 2, COLS, width)
        even, odd = part[:, :, 0], part[:, :, 1]
        b0 = jnp.where(half, even, pltpu.roll(odd, 4, 2))
        b1 = jnp.where(half, pltpu.roll(even, 4, 2), odd)
        slot = slot_index(depth_brick, r)
        for k, brick in enumerate((b0, b1)):
            source = source_ref[slot + k]
            row = pl.multiple_of(jnp.where(source >= 0, source, K * CAP) * CELLS, CELLS)
            stage[pl.ds(row, CELLS), :] = brick.reshape(CELLS, width).astype(jnp.bfloat16)


def final_kernel(count, base_ref, source_ref, *refs):
    block_ref, before_ref, after_ref, under_ref, over_ref, even_ref, odd_ref = refs[:7]
    border_ref, mid_here, mid_next, mid_ref, wide1_ref, wide2_ref, coarse_ref = refs[7:14]
    backs = refs[14 : 14 + K]
    h_here, h_next, stage, low_ref, high_ref = refs[14 + K :]
    width = block_ref.shape[1]
    stage[...] = jnp.zeros(stage.shape, jnp.bfloat16)
    face_in(base_ref[1], count, even_ref, odd_ref, low_ref, high_ref)
    flags_before = as_rows(before_ref[256:288])
    flags_after = as_rows(after_ref[256:288])
    lhs = []
    flags = []
    for end, far, corner in ((0, under_ref, low_ref), (1, over_ref, high_ref)):
        first = 0 if end == 0 else SIDE - 2
        brick = 0 if end == 0 else 3
        far_flags = as_rows(far[256:288])
        corner_flags = as_rows(corner[64:80])
        for which, line, lines in ((0, before_ref, flags_before), (1, after_ref, flags_after)):
            row = 0 if which == 0 else 112
            outer = [corner[which * 32 + k * 16 : which * 32 + k * 16 + 16] for k in range(2)]
            outer_own = [line[(first + k) * 16 : (first + k) * 16 + 16] for k in range(2)]
            near = [far[k * 128 + row : k * 128 + row + 16] for k in range(2)]
            near_own = [
                block_ref[(first + k) * 128 + row : (first + k) * 128 + row + 16] for k in range(2)
            ]
            outer = jnp.concatenate(outer + outer_own if end == 0 else outer_own + outer, axis=0)
            near = jnp.concatenate(near + near_own if end == 0 else near_own + near, axis=0)
            taps = side_taps(outer, near) if which == 0 else side_taps(near, outer)
            lhs.append(depth_taps(taps, 2))
            own_flag = slot_flags(source_ref, slot_index(brick, which * 3))
            far_pair = [corner_flags[which], far_flags[which * 3]]
            own_pair = [lines[brick], own_flag]
            for pair in (far_pair, own_pair) if end == 0 else (own_pair, far_pair):
                flags += pair if which == 0 else pair[::-1]
    value = multiply_taps(jnp.concatenate(lhs, axis=0), wide1_ref)
    corners = activate(value, jnp.stack(flags, axis=0))
    corners = corners.reshape(2, 2, 2, 16, width).astype(jnp.bfloat16)
    for end in range(2):
        for k in range(2):
            plane = jnp.concatenate(
                [corners[end, 0, k], border_ref[end * 2 + k], corners[end, 1, k]], axis=0
            )
            index = k if end == 0 else 10 + k
            h_here[index] = plane
            h_next[index] = as_tiles(moved_rows(as_rows(plane)))
    for k in range(4):
        for index, source in ((2 + k, k), (6 + k, SIDE - 6 + k)):
            h_here[index] = mid_here[source]
            h_next[index] = mid_next[source]
    for depth_brick in (1, 2):
        rows = slice((depth_brick - 1) * 512, depth_brick * 512)
        done = mid_ref[rows]
        coarse_ref[depth_brick * 512 : (depth_brick + 1) * 512] = done
        done = done.astype(jnp.float32).reshape(4, SIDE, COLS, width)
        scatter_bricks(source_ref, stage, done, depth_brick)
    for depth_brick in (0, 3):
        value = conv_planes(h_here, h_next, wide2_ref, depth_brick * 2, 4, SIDE * COLS)
        value = coarse_rows(source_ref, block_ref, value, depth_brick)
        rows = slice(depth_brick * 512, (depth_brick + 1) * 512)
        coarse_ref[rows] = value.reshape(512, width).astype(jnp.bfloat16)
        scatter_bricks(source_ref, stage, value, depth_brick)
    for j in range(K):
        backs[j][...] = stage[j * CAP * CELLS : (j + 1) * CAP * CELLS]


def final_call(count, base, source, block, halo, middle, wide1, wide2):
    mid = block.shape[1]
    smem = pl.BlockSpec(memory_space=pltpu.SMEM)
    vmem = pl.BlockSpec(memory_space=pltpu.VMEM)
    return pl.pallas_call(
        functools.partial(final_kernel, count),
        in_specs=[smem, smem] + [vmem] * 13,
        out_specs=[vmem] * (1 + K),
        out_shape=[jax.ShapeDtypeStruct(block.shape, jnp.bfloat16)]
        + [jax.ShapeDtypeStruct((CAP * CELLS, mid), jnp.bfloat16)] * K,
        scratch_shapes=[
            pltpu.VMEM((12, HID * COLS, mid), jnp.bfloat16),
            pltpu.VMEM((12, HID * COLS, mid), jnp.bfloat16),
            pltpu.VMEM(((K * CAP + 1) * CELLS, mid), jnp.bfloat16),
            pltpu.VMEM((80, mid), jnp.bfloat16),
            pltpu.VMEM((80, mid), jnp.bfloat16),
        ],
        compiler_params=pltpu.CompilerParams(vmem_limit_bytes=VMEM_LIMIT),
        cost_estimate=conv_cost(1152, mid),
        name="final",
    )(base, source, block, *halo, *middle, wide1, wide2)


def from_behind(value, axis, steps):
    count = lax.axis_size(axis)
    pairs = [(source, (source + steps) % count) for source in range(count)]
    return lax.ppermute(value, axis, pairs)


def swap_faces(even, odd, axis):
    count = lax.axis_size(axis)
    swapped = []
    for face, first in ((even, 0), (odd, 1)):
        partner = list(range(count))
        for i in range(first, count - 1, 2):
            partner[i], partner[i + 1] = i + 1, i
        swapped.append(lax.ppermute(face, axis, list(enumerate(partner))))
    return swapped


def shards(fine, fine_mask, slot_source, w_down, w_first, w_second, w_up):
    mid = w_down.shape[1]
    base = jnp.stack([lax.axis_index("xy"), lax.axis_index("gz")]).astype(jnp.int32)
    counts = (lax.axis_size("gz"), lax.axis_size("xy"))
    sent = down_call(fine, fine_mask, w_down, SENT)
    arrived = {j: from_behind(sent[j], "xy", j) for j in SENT}
    later = (arrived[SENT[2]], fine, fine_mask, w_down, w_first, w_second)
    arrived[SENT[2]], *later = lax.optimization_barrier(later)
    prepared = lax.optimization_barrier(tuple(prepare_call(*later)))
    arrived[0], mask, wide1, wide2 = prepared
    block, *faces = place_call(base, slot_source, [arrived[j] for j in range(K)])
    gz_even, gz_odd = swap_faces(*faces[2:], "gz")
    even, odd = swap_faces(*faces[:2], "xy")
    early = inner_call(slot_source, block, wide1)
    even, odd, gz_even, gz_odd, early = lax.optimization_barrier((even, odd, gz_even, gz_odd, early))
    *halo, even, odd = corner_call(counts, base, (even, odd, gz_even, gz_odd))
    even, odd = swap_faces(even, odd, "gz")
    middle = middle_call(slot_source, block, *halo, early, wide1, wide2)
    coarse, *back = final_call(
        counts[0], base, slot_source, block, (*halo, even, odd), middle, wide1, wide2
    )
    octant = {j: from_behind(back[j], "xy", -j) for j in SENT}
    octant[0] = back[0]
    fine_out = None
    for group in UP_GROUPS:
        fine_out = up_call(fine, mask, w_up, [octant[j] for j in group], group, fine_out)
    return fine_out, coarse.reshape(SIDE, SIDE, COLS, mid)


def solution(mesh):
    placed = (
        P(("gz", "xy"), None, None),
        P(("gz", "xy"), None),
        P(("gz", "xy")),
        P(),
        P(),
        P(),
        P(),
    )
    return jax.shard_map(
        shards,
        mesh=mesh,
        in_specs=placed,
        out_specs=(P(("gz", "xy"), None, None), P("gz", "xy", None, None)),
        check_vma=False,
    )
```

```python
import functools

import jax
import jax.numpy as jnp
from jax import lax
from jax.experimental import pallas as pl
from jax.experimental.pallas import tpu as pltpu
from jax.sharding import PartitionSpec as P

CAP = 4
K = 8
CELLS = 64
SIDE = 16
COLS = 8
WIDE = SIDE + 4
HID = SIDE + 2
EARLY = ((1, 3), (4, 4))
LATER = ((8, 4),)
LATE = ((12, 3),)
LATE_PLANES = 3
SENT = (4, 3, 5, 2, 6, 1, 7)
UP_OFFSETS = 4
DOWN_LIMIT = 62 * 1024 * 1024
VMEM_LIMIT = 24 * 1024 * 1024


def expand_mask(mask):
    bricks = mask.shape[0]
    values = mask.astype(jnp.float32)
    cell = lax.broadcasted_iota(jnp.int32, (16, 128), 0)
    lane = lax.broadcasted_iota(jnp.int32, (16, 128), 1)
    chosen = (cell == lane // 8).astype(jnp.float32)
    parts = [
        values[:, t * 128 : (t + 1) * 128].reshape(bricks, 1, 128) * chosen[None] for t in range(4)
    ]
    spread = jnp.concatenate(parts, axis=1).reshape(bricks * CELLS, 128).astype(jnp.bfloat16)
    source = lax.broadcasted_iota(jnp.int32, (128, 512), 0)
    target = lax.broadcasted_iota(jnp.int32, (128, 512), 1)
    widen = ((source & 7) == (target >> 6)).astype(jnp.bfloat16)
    return jnp.dot(spread, widen, preferred_element_type=jnp.float32)


def down_kernel(offsets, fine_hbm, mask_hbm, w_hbm, *refs):
    count = len(offsets)
    outs = refs[:count]
    fine_ref, mask_ref, w_ref, wide_ref, sems = refs[count:]
    first = [
        pltpu.make_async_copy(mask_hbm, mask_ref, sems.at[count]),
        pltpu.make_async_copy(w_hbm, w_ref, sems.at[count + 1]),
    ]
    chunks = [
        pltpu.make_async_copy(fine_hbm.at[pl.ds(j * CAP, CAP)], fine_ref.at[k], sems.at[k])
        for k, j in enumerate(offsets)
    ]
    for copy in first + chunks:
        copy.start()
    first[0].wait()
    rows = CAP * CELLS
    for k, j in enumerate(offsets):
        wide_ref[k * rows : (k + 1) * rows] = expand_mask(
            mask_ref[j * CAP : (j + 1) * CAP]
        ).astype(jnp.bfloat16)
    first[1].wait()
    for start in range(0, count, 2):
        group = range(start, min(start + 2, count))
        for k in group:
            chunks[k].wait()
        x = [
            fine_ref[k].reshape(rows, -1) * wide_ref[k * rows : (k + 1) * rows] for k in group
        ]
        y = jnp.dot(jnp.concatenate(x, axis=0), w_ref[...], preferred_element_type=jnp.float32)
        y = y.astype(jnp.bfloat16)
        for part, k in enumerate(group):
            outs[k][...] = y[part * rows : (part + 1) * rows]


def down_call(fine, mask, w, offsets):
    cells, width = fine.shape[1:]
    mid = w.shape[1]
    count = len(offsets)
    rows = count * CAP * cells
    hbm = pl.BlockSpec(memory_space=pltpu.HBM)
    outs = pl.pallas_call(
        functools.partial(down_kernel, offsets),
        in_specs=[hbm, hbm, hbm],
        out_specs=[pl.BlockSpec(memory_space=pltpu.VMEM)] * count,
        out_shape=[jax.ShapeDtypeStruct((CAP * cells, mid), jnp.bfloat16)] * count,
        scratch_shapes=[
            pltpu.VMEM((count, CAP, cells, width), fine.dtype),
            pltpu.VMEM(mask.shape, mask.dtype),
            pltpu.VMEM(w.shape, w.dtype),
            pltpu.VMEM((rows, width), jnp.bfloat16),
            pltpu.SemaphoreType.DMA((count + 2,)),
        ],
        compiler_params=pltpu.CompilerParams(vmem_limit_bytes=DOWN_LIMIT),
        cost_estimate=pl.CostEstimate(
            flops=2 * rows * width * mid, bytes_accessed=rows * width * 2, transcendentals=0
        ),
        name="down",
    )(fine, mask, w)
    return dict(zip(offsets, outs))


def prepare_kernel(
    fine_ref, mask_ref, w_down_ref, w1_ref, w2_ref, own_ref, mask_out, wide1_ref, wide2_ref
):
    gather_weights(w1_ref, wide1_ref)
    gather_weights(w2_ref, wide2_ref)
    step = 8
    for part in range(mask_ref.shape[0] // step):
        rows = slice(part * step * CELLS, (part + 1) * step * CELLS)
        mask_out[rows] = expand_mask(mask_ref[part * step : (part + 1) * step]).astype(jnp.bfloat16)
    rows = CAP * CELLS
    own = fine_ref[...].reshape(rows, -1) * mask_out[:rows]
    own = jnp.dot(own, w_down_ref[...], preferred_element_type=jnp.float32)
    own_ref[...] = own.astype(jnp.bfloat16)


def prepare_call(fine, mask, w_down, w_first, w_second):
    mid = w_first.shape[1]
    vmem = pl.BlockSpec(memory_space=pltpu.VMEM)
    rows = mask.shape[0] * CELLS
    wide = jax.ShapeDtypeStruct((9 * mid, 3 * mid), jnp.bfloat16)
    return pl.pallas_call(
        prepare_kernel,
        grid=(1,),
        in_specs=[pl.BlockSpec((CAP,) + fine.shape[1:], lambda i: (0, 0, 0))] + [vmem] * 4,
        out_specs=[vmem] * 4,
        out_shape=[
            jax.ShapeDtypeStruct((CAP * CELLS, mid), jnp.bfloat16),
            jax.ShapeDtypeStruct((rows, mask.shape[1]), jnp.bfloat16),
            wide,
            wide,
        ],
        compiler_params=pltpu.CompilerParams(vmem_limit_bytes=VMEM_LIMIT),
        cost_estimate=pl.CostEstimate(
            flops=2 * rows * mask.shape[1] * 128, bytes_accessed=rows * mask.shape[1] * 2, transcendentals=0
        ),
        name="prepare",
    )(fine, mask, w_down, w_first, w_second)


def up_kernel(fine_ref, mask_ref, w_ref, *refs):
    out_ref = refs[-1]
    step = pl.program_id(0)
    bricks, cells, width = fine_ref.shape
    count = bricks // CAP
    steps = UP_OFFSETS // count
    for part in range(count):
        octant = refs[part][...]
        for other in range(1, steps):
            octant = jnp.where(step == other, refs[other * count + part][...], octant)
        rows = slice(part * CAP * cells, (part + 1) * CAP * cells)
        up = jnp.dot(octant, w_ref[...], preferred_element_type=jnp.float32)
        fine = fine_ref[part * CAP : (part + 1) * CAP].reshape(CAP * cells, width)
        mask = mask_ref[rows].astype(jnp.float32)
        out = jnp.where(mask > 0.5, fine.astype(jnp.float32) + up, 0.0)
        out_ref[part * CAP : (part + 1) * CAP] = out.astype(jnp.bfloat16).reshape(CAP, cells, width)


def up_call(fine, mask, w, octants, first, partial):
    bricks, cells, width = fine.shape
    mid = w.shape[0]
    step = 8
    blocks = bricks // step

    def place(i):
        return (first + i) % blocks

    partials = [] if partial is None else [partial]
    return pl.pallas_call(
        up_kernel,
        grid=(UP_OFFSETS * CAP // step,),
        in_specs=[
            pl.BlockSpec((step, cells, width), lambda i: (place(i), 0, 0)),
            pl.BlockSpec((step * cells, width), lambda i: (place(i), 0)),
            pl.BlockSpec((mid, width), lambda i: (0, 0)),
        ]
        + [pl.BlockSpec((CAP * cells, mid), lambda i: (0, 0))] * UP_OFFSETS
        + [pl.BlockSpec(memory_space=pl.ANY)] * len(partials),
        out_specs=pl.BlockSpec((step, cells, width), lambda i: (place(i), 0, 0)),
        out_shape=jax.ShapeDtypeStruct(fine.shape, jnp.bfloat16),
        input_output_aliases={3 + UP_OFFSETS: 0} if partials else {},
        compiler_params=pltpu.CompilerParams(vmem_limit_bytes=VMEM_LIMIT),
        cost_estimate=pl.CostEstimate(
            flops=bricks * cells * width * mid, bytes_accessed=bricks * cells * width * 2, transcendentals=0
        ),
        name="up",
    )(fine, mask, w, *octants, *partials)


def low_half(shape):
    return lax.broadcasted_iota(jnp.int32, shape, len(shape) - 2) < 4


def slot_flags(source_ref, first):
    pair = [jnp.where(source_ref[first + k] >= 0, 1.0, 0.0).astype(jnp.float32) for k in range(2)]
    return jnp.where(low_half((8, 128)), pair[0], pair[1])


def slot_index(depth_brick, row_brick):
    pd, qd = divmod(depth_brick, 2)
    pr, qr = divmod(row_brick, 2)
    return (pd * 2 + pr) * 8 + qd * 4 + qr * 2


def take_brick(source_ref, arrived, slot):
    value = source_ref[slot]
    first = pl.multiple_of(jnp.maximum(value, 0) * CELLS, CELLS)
    brick = arrived[pl.ds(first, CELLS), :].astype(jnp.float32)
    return jnp.where(value >= 0, brick, 0.0).reshape(8, 8, 128)


def place_kernel(base_ref, source_ref, *refs):
    block_ref, even_ref, odd_ref, low_ref, high_ref, arrived = refs[K:]
    for j in range(K):
        arrived[j * CAP * CELLS : (j + 1) * CAP * CELLS] = refs[j][...]
    half = low_half((8, 8, 128))
    for depth_brick in range(4):
        for row_brick in range(4):
            slot = slot_index(depth_brick, row_brick)
            b0 = take_brick(source_ref, arrived, slot)
            b1 = take_brick(source_ref, arrived, slot + 1)
            even = jnp.where(half, b0, pltpu.roll(b1, 4, 1))
            odd = jnp.where(half, pltpu.roll(b0, 4, 1), b1)
            both = jnp.stack([even, odd], axis=1).reshape(4, 32, 128).astype(jnp.bfloat16)
            for vd in range(4):
                row = ((depth_brick * 4 + vd) * SIDE + row_brick * 4) * COLS
                block_ref[row : row + 32] = both[vd]
                place = (depth_brick * 4 + vd) * 16
                if row_brick == 0:
                    low_ref[place : place + 16] = both[vd, :16]
                if row_brick == 3:
                    high_ref[place : place + 16] = both[vd, 16:]
    for row_brick, ref in ((0, low_ref), (3, high_ref)):
        flags = [slot_flags(source_ref, slot_index(d, row_brick)) for d in range(4)]
        ref[256:288] = jnp.concatenate(flags, axis=0).astype(jnp.bfloat16)
    face_out(base_ref[0], low_ref, high_ref, even_ref, odd_ref)


def face_out(index, low_ref, high_ref, even_ref, odd_ref):
    is_even = index % 2 == 0
    even_ref[...] = jnp.where(is_even, high_ref[...], low_ref[...])
    odd_ref[...] = jnp.where(is_even, low_ref[...], high_ref[...])


def face_in(index, count, even_ref, odd_ref, low_ref, high_ref):
    is_even = index % 2 == 0
    empty = jnp.zeros(low_ref.shape, low_ref.dtype)
    low = jnp.where(is_even, odd_ref[...], even_ref[...])
    high = jnp.where(is_even, even_ref[...], odd_ref[...])
    low_ref[...] = jnp.where(index == 0, empty, low)
    high_ref[...] = jnp.where(index == count - 1, empty, high)


def place_call(base, source, arrived):
    mid = arrived[0].shape[1]
    smem = pl.BlockSpec(memory_space=pltpu.SMEM)
    vmem = pl.BlockSpec(memory_space=pltpu.VMEM)
    return pl.pallas_call(
        place_kernel,
        in_specs=[smem, smem] + [vmem] * K,
        out_specs=[vmem] * 3,
        out_shape=[
            jax.ShapeDtypeStruct((rows, mid), jnp.bfloat16)
            for rows in (SIDE * SIDE * COLS, 288, 288)
        ],
        scratch_shapes=[
            pltpu.VMEM((288, mid), jnp.bfloat16),
            pltpu.VMEM((288, mid), jnp.bfloat16),
            pltpu.VMEM((K * CAP * CELLS, mid), jnp.bfloat16),
        ],
        compiler_params=pltpu.CompilerParams(vmem_limit_bytes=VMEM_LIMIT),
        name="place",
    )(base, source, *arrived)


def edge_kernel(
    counts,
    base_ref,
    source_ref,
    block_ref,
    even_ref,
    odd_ref,
    before_ref,
    after_ref,
    even_out,
    odd_out,
    low_ref,
    high_ref,
):
    face_in(base_ref[0], counts[1], even_ref, odd_ref, before_ref, after_ref)
    for ref, planes, brick in ((low_ref, (0, 1), 0), (high_ref, (SIDE - 2, SIDE - 1), 3)):
        for k, plane in enumerate(planes):
            start = k * WIDE * COLS
            ref[start : start + 16] = before_ref[plane * 16 : plane * 16 + 16]
            ref[start + 16 : start + 144] = block_ref[plane * 128 : plane * 128 + 128]
            ref[start + 144 : start + 160] = after_ref[plane * 16 : plane * 16 + 16]
        flags = [before_ref[256:288].astype(jnp.float32)[brick * 8 : brick * 8 + 8]]
        flags += [slot_flags(source_ref, slot_index(brick, r)) for r in range(4)]
        flags += [after_ref[256:288].astype(jnp.float32)[brick * 8 : brick * 8 + 8]]
        ref[320:368] = jnp.concatenate(flags, axis=0).astype(jnp.bfloat16)
    face_out(base_ref[1], low_ref, high_ref, even_out, odd_out)


def edge_call(counts, base, source, block, even, odd):
    smem = pl.BlockSpec(memory_space=pltpu.SMEM)
    vmem = pl.BlockSpec(memory_space=pltpu.VMEM)
    mid = block.shape[1]
    return pl.pallas_call(
        functools.partial(edge_kernel, counts),
        in_specs=[smem, smem, vmem, vmem, vmem],
        out_specs=[vmem] * 4,
        out_shape=[
            jax.ShapeDtypeStruct((rows, mid), jnp.bfloat16) for rows in (288, 288, 368, 368)
        ],
        scratch_shapes=[pltpu.VMEM((368, mid), jnp.bfloat16)] * 2,
        compiler_params=pltpu.CompilerParams(vmem_limit_bytes=VMEM_LIMIT),
        name="edge",
    )(base, source, block, even, odd)


def gather_weights(w_ref, wide_ref):
    width = w_ref.shape[2]
    for tap in range(9):
        for column in range(3):
            wide_ref[tap * width : (tap + 1) * width, column * width : (column + 1) * width] = (
                w_ref[tap * 3 + column]
            )


def as_rows(value):
    value = value.astype(jnp.float32)
    return value.reshape(value.shape[0] // COLS, COLS, value.shape[1])


def moved_rows(rows):
    empty = jnp.zeros((1,) + rows.shape[1:], jnp.float32)
    return jnp.concatenate([rows[1:], empty], axis=0)


def as_tiles(rows):
    return rows.reshape(rows.shape[0] * COLS, rows.shape[2]).astype(jnp.bfloat16)


def multiply_taps(lhs, wide_ref):
    width = wide_ref.shape[1] // 3
    wide = jnp.dot(lhs, wide_ref[...], preferred_element_type=jnp.float32)
    wide = wide.reshape(lhs.shape[0] // COLS, COLS, 3 * width)
    column = lax.broadcasted_iota(jnp.int32, (lhs.shape[0] // COLS, COLS, width), 1)
    left = jnp.where(column == 0, 0.0, pltpu.roll(wide[:, :, :width], 1, 1))
    right = jnp.where(column == COLS - 1, 0.0, pltpu.roll(wide[:, :, 2 * width :], COLS - 1, 1))
    return left + wide[:, :, width : 2 * width] + right


def plane_taps(here_ref, next_ref, first, planes, rows):
    taps = []
    for dd in range(3):
        span = slice(first + dd, first + dd + planes)
        taps += [
            here_ref[span, 0:rows, :],
            next_ref[span, 0:rows, :],
            here_ref[span, 16 : rows + 16, :],
        ]
    lhs = jnp.concatenate(taps, axis=2)
    return lhs.reshape(planes * rows, lhs.shape[2])


def conv_planes(here_ref, next_ref, wide_ref, first, planes, rows):
    return multiply_taps(plane_taps(here_ref, next_ref, first, planes, rows), wide_ref)


def activate(value, flags):
    return value / (1.0 + jnp.exp(-value)) * flags


def spread_flags(flags, repeats):
    return jnp.concatenate(
        [jnp.broadcast_to(flag[None], (count,) + flag.shape) for flag, count in zip(flags, repeats)],
        axis=0,
    )


def inner_planes(source_ref, block_ref, wide1_ref, hidden_ref, here, moved, groups):
    width = block_ref.shape[1]
    base = groups[0][0] - 1
    for d in range(base, groups[-1][0] + groups[-1][1] + 1):
        plane = block_ref[d * 128 : (d + 1) * 128]
        here[d - base] = plane
        moved[d - base] = as_tiles(moved_rows(as_rows(plane)))
    inner = SIDE - 2
    rows = inner * COLS
    for first, planes in groups:
        value = conv_planes(here, moved, wide1_ref, first - 1 - base, planes, rows)
        value = value.reshape(planes, inner, COLS, width)
        flags = [slot_flags(source_ref, slot_index(first // 4, r)) for r in range(4)]
        value = activate(value, spread_flags(flags, (3, 4, 4, 3))[None])
        hidden_ref[first - 1 - base : first - 1 - base + planes] = value.reshape(
            planes, rows, width
        ).astype(jnp.bfloat16)


def inner_kernel(groups, source_ref, block_ref, wide1_ref, hidden_ref, here, moved):
    inner_planes(source_ref, block_ref, wide1_ref, hidden_ref, here, moved, groups)


def conv_cost(rows, width):
    return pl.CostEstimate(
        flops=2 * rows * 27 * width * width, bytes_accessed=27 * width * width * 4, transcendentals=0
    )


def inner_call(source, block, wide1, groups):
    mid = block.shape[1]
    smem = pl.BlockSpec(memory_space=pltpu.SMEM)
    vmem = pl.BlockSpec(memory_space=pltpu.VMEM)
    rows = (SIDE - 2) * COLS
    planes = sum(count for _, count in groups)
    return pl.pallas_call(
        functools.partial(inner_kernel, groups),
        in_specs=[smem, vmem, vmem],
        out_specs=vmem,
        out_shape=jax.ShapeDtypeStruct((planes, rows, mid), jnp.bfloat16),
        scratch_shapes=[pltpu.VMEM((planes + 2, SIDE * COLS, mid), jnp.bfloat16)] * 2,
        compiler_params=pltpu.CompilerParams(vmem_limit_bytes=VMEM_LIMIT),
        cost_estimate=conv_cost(planes * rows, mid),
        name="inner",
    )(source, block, wide1)


def side_taps(low, high):
    mixed = as_tiles(
        jnp.concatenate(
            [as_rows(low).reshape(-1, 2, COLS, 128)[:, 1:], as_rows(high).reshape(-1, 2, COLS, 128)[:, :1]],
            axis=1,
        ).reshape(-1, COLS, 128)
    )
    return low, mixed, high


def depth_taps(taps, planes):
    parts = [tap[dd * 16 : (dd + planes) * 16] for dd in range(3) for tap in taps]
    return jnp.concatenate(parts, axis=1)


def coarse_rows(source_ref, block_ref, value, depth_brick):
    width = block_ref.shape[1]
    value = value.reshape(4, SIDE, COLS, width)
    rows = slice(depth_brick * 512, (depth_brick + 1) * 512)
    own = block_ref[rows].astype(jnp.float32).reshape(4, SIDE, COLS, width)
    flags = [slot_flags(source_ref, slot_index(depth_brick, r)) for r in range(4)]
    return (value + own) * spread_flags(flags, (4, 4, 4, 4))[None]


def middle_kernel(source_ref, *refs):
    block_ref, before_ref, after_ref, early_ref, later_ref, wide1_ref, wide2_ref = refs[:7]
    h_here, h_next, coarse_ref, side, late, here, moved = refs[7:]
    width = block_ref.shape[1]
    inner = SIDE - 2
    inner_planes(source_ref, block_ref, wide1_ref, late, here, moved, LATE)

    low = jnp.concatenate([block_ref[d * 128 : d * 128 + 16] for d in range(SIDE)], axis=0)
    high = jnp.concatenate([block_ref[d * 128 + 112 : d * 128 + 128] for d in range(SIDE)], axis=0)
    left = depth_taps(side_taps(before_ref[0:256], low), inner)
    right = depth_taps(side_taps(high, after_ref[0:256]), inner)
    value = multiply_taps(jnp.concatenate([left, right], axis=0), wide1_ref)
    depths = (3, 4, 4, 3)
    edge_flags = (as_rows(before_ref[256:288]), as_rows(after_ref[256:288]))
    flags = []
    for end, row_brick in ((0, 0), (1, 3)):
        own = [slot_flags(source_ref, slot_index(d, row_brick)) for d in range(4)]
        pairs = [jnp.stack([edge_flags[end][d], own[d]][:: 1 - 2 * end], axis=0) for d in range(4)]
        flags.append(spread_flags(pairs, depths))
    value = activate(value.reshape(2, inner, 2, COLS, width), jnp.stack(flags, axis=0))
    side[...] = value.reshape(2, inner, 16, width).astype(jnp.bfloat16)
    centres = [ref[k] for ref in (early_ref, later_ref, late) for k in range(ref.shape[0])]
    for d in range(inner):
        plane = jnp.concatenate([side[0, d], centres[d], side[1, d]], axis=0)
        h_here[d] = plane
        h_next[d] = as_tiles(moved_rows(as_rows(plane)))

    for depth_brick in (1, 2):
        value = conv_planes(h_here, h_next, wide2_ref, depth_brick * 4 - 2, 4, SIDE * COLS)
        value = coarse_rows(source_ref, block_ref, value, depth_brick)
        rows = slice((depth_brick - 1) * 512, depth_brick * 512)
        coarse_ref[rows] = value.reshape(512, width).astype(jnp.bfloat16)


def middle_call(source, block, before, after, early, later, wide1, wide2):
    mid = block.shape[1]
    smem = pl.BlockSpec(memory_space=pltpu.SMEM)
    vmem = pl.BlockSpec(memory_space=pltpu.VMEM)
    inner = SIDE - 2
    hidden = (inner, HID * COLS, mid)
    return pl.pallas_call(
        middle_kernel,
        in_specs=[smem] + [vmem] * 7,
        out_specs=[vmem] * 3,
        out_shape=[
            jax.ShapeDtypeStruct(shape, jnp.bfloat16) for shape in (hidden, hidden, (1024, mid))
        ],
        scratch_shapes=[
            pltpu.VMEM((2, inner, 16, mid), jnp.bfloat16),
            pltpu.VMEM((LATE_PLANES, inner * COLS, mid), jnp.bfloat16),
            pltpu.VMEM((LATE_PLANES + 2, SIDE * COLS, mid), jnp.bfloat16),
            pltpu.VMEM((LATE_PLANES + 2, SIDE * COLS, mid), jnp.bfloat16),
        ],
        compiler_params=pltpu.CompilerParams(vmem_limit_bytes=VMEM_LIMIT),
        cost_estimate=conv_cost(inner * (4 + LATE_PLANES) * COLS + 1024, mid),
        name="middle",
    )(source, block, before, after, early, later, wide1, wide2)


def scatter_bricks(source_ref, stage, value, depth_brick):
    width = value.shape[3]
    half = low_half((4, 2, COLS, width))
    for r in range(4):
        part = value[:, r * 4 : (r + 1) * 4].reshape(4, 2, 2, COLS, width)
        even, odd = part[:, :, 0], part[:, :, 1]
        b0 = jnp.where(half, even, pltpu.roll(odd, 4, 2))
        b1 = jnp.where(half, pltpu.roll(even, 4, 2), odd)
        slot = slot_index(depth_brick, r)
        for k, brick in enumerate((b0, b1)):
            source = source_ref[slot + k]
            row = pl.multiple_of(jnp.where(source >= 0, source, K * CAP) * CELLS, CELLS)
            stage[pl.ds(row, CELLS), :] = brick.reshape(CELLS, width).astype(jnp.bfloat16)


def final_kernel(count, base_ref, source_ref, *refs):
    block_ref, before_ref, after_ref, even_ref, odd_ref = refs[:5]
    mid_here, mid_next, mid_ref, wide1_ref, wide2_ref, coarse_ref = refs[5:11]
    backs = refs[11 : 11 + K]
    x_here, x_next, h_here, h_next, stage, under_ref, over_ref = refs[11 + K :]
    width = block_ref.shape[1]
    stage[...] = jnp.zeros(stage.shape, jnp.bfloat16)
    face_in(base_ref[1], count, even_ref, odd_ref, under_ref, over_ref)
    flags_before = as_rows(before_ref[256:288])
    flags_after = as_rows(after_ref[256:288])
    spread = []
    for end, ref in ((0, under_ref), (1, over_ref)):
        own = []
        for d in (0, 1) if end == 0 else (SIDE - 2, SIDE - 1):
            edge = slice(d * 16, (d + 1) * 16)
            own.append(
                jnp.concatenate(
                    [before_ref[edge], block_ref[d * 128 : (d + 1) * 128], after_ref[edge]], axis=0
                )
            )
        far = [ref[k * 160 : (k + 1) * 160] for k in range(2)]
        for index, plane in enumerate(far + own if end == 0 else own + far):
            x_here[end * 4 + index] = plane
            x_next[end * 4 + index] = as_tiles(moved_rows(as_rows(plane)))
        far_flags = as_rows(ref[320:368])
        brick = 0 if end == 0 else 3
        own_flags = [flags_before[brick]]
        own_flags += [slot_flags(source_ref, slot_index(brick, r)) for r in range(4)]
        own_flags += [flags_after[brick]]
        pair = [
            spread_flags([far_flags[r] for r in range(6)], (1, 4, 4, 4, 4, 1)),
            spread_flags(own_flags, (1, 4, 4, 4, 4, 1)),
        ]
        spread += pair if end == 0 else pair[::-1]
    lhs = [plane_taps(x_here, x_next, first, 2, HID * COLS) for first in (0, 4)]
    value = multiply_taps(jnp.concatenate(lhs, axis=0), wide1_ref)
    value = activate(value.reshape(4, HID, COLS, width), jnp.stack(spread, axis=0))
    for k, index in enumerate((0, 1, 10, 11)):
        h_here[index] = as_tiles(value[k])
        h_next[index] = as_tiles(moved_rows(value[k]))
    for k in range(4):
        for index, source in ((2 + k, k), (6 + k, SIDE - 6 + k)):
            h_here[index] = mid_here[source]
            h_next[index] = mid_next[source]
    for depth_brick in (1, 2):
        rows = slice((depth_brick - 1) * 512, depth_brick * 512)
        done = mid_ref[rows]
        coarse_ref[depth_brick * 512 : (depth_brick + 1) * 512] = done
        done = done.astype(jnp.float32).reshape(4, SIDE, COLS, width)
        scatter_bricks(source_ref, stage, done, depth_brick)
    for depth_brick in (0, 3):
        value = conv_planes(h_here, h_next, wide2_ref, depth_brick * 2, 4, SIDE * COLS)
        value = coarse_rows(source_ref, block_ref, value, depth_brick)
        rows = slice(depth_brick * 512, (depth_brick + 1) * 512)
        coarse_ref[rows] = value.reshape(512, width).astype(jnp.bfloat16)
        scatter_bricks(source_ref, stage, value, depth_brick)
    for j in range(K):
        backs[j][...] = stage[j * CAP * CELLS : (j + 1) * CAP * CELLS]


def final_call(count, base, source, block, halo, middle, wide1, wide2):
    mid = block.shape[1]
    smem = pl.BlockSpec(memory_space=pltpu.SMEM)
    vmem = pl.BlockSpec(memory_space=pltpu.VMEM)
    return pl.pallas_call(
        functools.partial(final_kernel, count),
        in_specs=[smem, smem] + [vmem] * 10,
        out_specs=[vmem] * (1 + K),
        out_shape=[jax.ShapeDtypeStruct(block.shape, jnp.bfloat16)]
        + [jax.ShapeDtypeStruct((CAP * CELLS, mid), jnp.bfloat16)] * K,
        scratch_shapes=[
            pltpu.VMEM((8, WIDE * COLS, mid), jnp.bfloat16),
            pltpu.VMEM((8, WIDE * COLS, mid), jnp.bfloat16),
            pltpu.VMEM((12, HID * COLS, mid), jnp.bfloat16),
            pltpu.VMEM((12, HID * COLS, mid), jnp.bfloat16),
            pltpu.VMEM(((K * CAP + 1) * CELLS, mid), jnp.bfloat16),
            pltpu.VMEM((368, mid), jnp.bfloat16),
            pltpu.VMEM((368, mid), jnp.bfloat16),
        ],
        compiler_params=pltpu.CompilerParams(vmem_limit_bytes=VMEM_LIMIT),
        cost_estimate=conv_cost(1600, mid),
        name="final",
    )(base, source, block, *halo, *middle, wide1, wide2)


def from_behind(value, axis, steps):
    count = lax.axis_size(axis)
    pairs = [(source, (source + steps) % count) for source in range(count)]
    return lax.ppermute(value, axis, pairs)


def swap_face(face, axis, first):
    count = lax.axis_size(axis)
    partner = list(range(count))
    for i in range(first, count - 1, 2):
        partner[i], partner[i + 1] = i + 1, i
    return lax.ppermute(face, axis, list(enumerate(partner)))


def shards(fine, fine_mask, slot_source, w_down, w_first, w_second, w_up):
    mid = w_down.shape[1]
    base = jnp.stack([lax.axis_index("xy"), lax.axis_index("gz")]).astype(jnp.int32)
    counts = (lax.axis_size("gz"), lax.axis_size("xy"))
    sent = down_call(fine, fine_mask, w_down, SENT)
    arrived = {j: from_behind(sent[j], "xy", j) for j in SENT}
    later = (arrived[SENT[2]], fine, fine_mask, w_down, w_first, w_second)
    arrived[SENT[2]], *later = lax.optimization_barrier(later)
    prepared = lax.optimization_barrier(tuple(prepare_call(*later)))
    arrived[0], mask, wide1, wide2 = prepared
    block, even, odd = place_call(base, slot_source, [arrived[j] for j in range(K)])
    odd = swap_face(odd, "xy", 1)
    early = inner_call(slot_source, block, wide1, EARLY)
    even, early = lax.optimization_barrier((even, early))
    even = swap_face(even, "xy", 0)
    later = inner_call(slot_source, block, wide1, LATER)
    even, odd, later = lax.optimization_barrier((even, odd, later))
    before, after, even, odd = edge_call(counts, base, slot_source, block, even, odd)
    even = swap_face(even, "gz", 0)
    odd = swap_face(odd, "gz", 1)
    middle = middle_call(slot_source, block, before, after, early, later, wide1, wide2)
    coarse, *back = final_call(
        counts[0], base, slot_source, block, (before, after, even, odd), middle, wide1, wide2
    )
    octant = {j: from_behind(back[j], "xy", -j) for j in SENT}
    octant[0] = back[0]
    fine_out = up_call(fine, mask, w_up, [octant[j] for j in (2, 3, 4, 5)], 1, None)
    fine_out = up_call(fine, mask, w_up, [octant[j] for j in (6, 7, 0, 1)], 3, fine_out)
    return fine_out, coarse.reshape(SIDE, SIDE, COLS, mid)


def solution(mesh):
    placed = (
        P(("gz", "xy"), None, None),
        P(("gz", "xy"), None),
        P(("gz", "xy")),
        P(),
        P(),
        P(),
        P(),
    )
    return jax.shard_map(
        shards,
        mesh=mesh,
        in_specs=placed,
        out_specs=(P(("gz", "xy"), None, None), P("gz", "xy", None, None)),
        check_vma=False,
    )
```

```python
import functools

import jax
import jax.numpy as jnp
from jax import lax
from jax.experimental import pallas as pl
from jax.experimental.pallas import tpu as pltpu
from jax.sharding import PartitionSpec as P

CAP = 4
K = 8
CELLS = 64
SIDE = 16
COLS = 8
WIDE = SIDE + 4
HID = SIDE + 2
EARLY = ((1, 3),)
LATER = ((4, 4), (8, 4))
LATE = ((12, 3),)
LATE_PLANES = 3
SENT = (4, 3, 5, 2, 6, 1, 7)
UP_OFFSETS = 4
DOWN_LIMIT = 62 * 1024 * 1024
VMEM_LIMIT = 24 * 1024 * 1024


def expand_mask(mask):
    bricks = mask.shape[0]
    values = mask.astype(jnp.float32)
    cell = lax.broadcasted_iota(jnp.int32, (16, 128), 0)
    lane = lax.broadcasted_iota(jnp.int32, (16, 128), 1)
    chosen = (cell == lane // 8).astype(jnp.float32)
    parts = [
        values[:, t * 128 : (t + 1) * 128].reshape(bricks, 1, 128) * chosen[None] for t in range(4)
    ]
    spread = jnp.concatenate(parts, axis=1).reshape(bricks * CELLS, 128).astype(jnp.bfloat16)
    source = lax.broadcasted_iota(jnp.int32, (128, 512), 0)
    target = lax.broadcasted_iota(jnp.int32, (128, 512), 1)
    widen = ((source & 7) == (target >> 6)).astype(jnp.bfloat16)
    return jnp.dot(spread, widen, preferred_element_type=jnp.float32)


def down_kernel(offsets, fine_hbm, mask_hbm, w_hbm, *refs):
    count = len(offsets)
    outs = refs[:count]
    fine_ref, mask_ref, w_ref, wide_ref, sems = refs[count:]
    first = [
        pltpu.make_async_copy(mask_hbm, mask_ref, sems.at[count]),
        pltpu.make_async_copy(w_hbm, w_ref, sems.at[count + 1]),
    ]
    chunks = [
        pltpu.make_async_copy(fine_hbm.at[pl.ds(j * CAP, CAP)], fine_ref.at[k], sems.at[k])
        for k, j in enumerate(offsets)
    ]
    for copy in first + chunks:
        copy.start()
    first[0].wait()
    rows = CAP * CELLS
    for k, j in enumerate(offsets):
        wide_ref[k * rows : (k + 1) * rows] = expand_mask(
            mask_ref[j * CAP : (j + 1) * CAP]
        ).astype(jnp.bfloat16)
    first[1].wait()
    for start in range(0, count, 2):
        group = range(start, min(start + 2, count))
        for k in group:
            chunks[k].wait()
        x = [
            fine_ref[k].reshape(rows, -1) * wide_ref[k * rows : (k + 1) * rows] for k in group
        ]
        y = jnp.dot(jnp.concatenate(x, axis=0), w_ref[...], preferred_element_type=jnp.float32)
        y = y.astype(jnp.bfloat16)
        for part, k in enumerate(group):
            outs[k][...] = y[part * rows : (part + 1) * rows]


def down_call(fine, mask, w, offsets):
    cells, width = fine.shape[1:]
    mid = w.shape[1]
    count = len(offsets)
    rows = count * CAP * cells
    hbm = pl.BlockSpec(memory_space=pltpu.HBM)
    outs = pl.pallas_call(
        functools.partial(down_kernel, offsets),
        in_specs=[hbm, hbm, hbm],
        out_specs=[pl.BlockSpec(memory_space=pltpu.VMEM)] * count,
        out_shape=[jax.ShapeDtypeStruct((CAP * cells, mid), jnp.bfloat16)] * count,
        scratch_shapes=[
            pltpu.VMEM((count, CAP, cells, width), fine.dtype),
            pltpu.VMEM(mask.shape, mask.dtype),
            pltpu.VMEM(w.shape, w.dtype),
            pltpu.VMEM((rows, width), jnp.bfloat16),
            pltpu.SemaphoreType.DMA((count + 2,)),
        ],
        compiler_params=pltpu.CompilerParams(vmem_limit_bytes=DOWN_LIMIT),
        cost_estimate=pl.CostEstimate(
            flops=2 * rows * width * mid, bytes_accessed=rows * width * 2, transcendentals=0
        ),
        name="down",
    )(fine, mask, w)
    return dict(zip(offsets, outs))


def prepare_kernel(
    fine_ref, mask_ref, w_down_ref, w1_ref, w2_ref, own_ref, mask_out, wide1_ref, wide2_ref
):
    gather_weights(w1_ref, wide1_ref)
    gather_weights(w2_ref, wide2_ref)
    step = 8
    for part in range(mask_ref.shape[0] // step):
        rows = slice(part * step * CELLS, (part + 1) * step * CELLS)
        mask_out[rows] = expand_mask(mask_ref[part * step : (part + 1) * step]).astype(jnp.bfloat16)
    rows = CAP * CELLS
    own = fine_ref[...].reshape(rows, -1) * mask_out[:rows]
    own = jnp.dot(own, w_down_ref[...], preferred_element_type=jnp.float32)
    own_ref[...] = own.astype(jnp.bfloat16)


def prepare_call(fine, mask, w_down, w_first, w_second):
    mid = w_first.shape[1]
    vmem = pl.BlockSpec(memory_space=pltpu.VMEM)
    rows = mask.shape[0] * CELLS
    wide = jax.ShapeDtypeStruct((9 * mid, 3 * mid), jnp.bfloat16)
    return pl.pallas_call(
        prepare_kernel,
        grid=(1,),
        in_specs=[pl.BlockSpec((CAP,) + fine.shape[1:], lambda i: (0, 0, 0))] + [vmem] * 4,
        out_specs=[vmem] * 4,
        out_shape=[
            jax.ShapeDtypeStruct((CAP * CELLS, mid), jnp.bfloat16),
            jax.ShapeDtypeStruct((rows, mask.shape[1]), jnp.bfloat16),
            wide,
            wide,
        ],
        compiler_params=pltpu.CompilerParams(vmem_limit_bytes=VMEM_LIMIT),
        cost_estimate=pl.CostEstimate(
            flops=2 * rows * mask.shape[1] * 128, bytes_accessed=rows * mask.shape[1] * 2, transcendentals=0
        ),
        name="prepare",
    )(fine, mask, w_down, w_first, w_second)


def up_kernel(fine_ref, mask_ref, w_ref, *refs):
    out_ref = refs[-1]
    step = pl.program_id(0)
    bricks, cells, width = fine_ref.shape
    count = bricks // CAP
    steps = UP_OFFSETS // count
    for part in range(count):
        octant = refs[part][...]
        for other in range(1, steps):
            octant = jnp.where(step == other, refs[other * count + part][...], octant)
        rows = slice(part * CAP * cells, (part + 1) * CAP * cells)
        up = jnp.dot(octant, w_ref[...], preferred_element_type=jnp.float32)
        fine = fine_ref[part * CAP : (part + 1) * CAP].reshape(CAP * cells, width)
        mask = mask_ref[rows].astype(jnp.float32)
        out = jnp.where(mask > 0.5, fine.astype(jnp.float32) + up, 0.0)
        out_ref[part * CAP : (part + 1) * CAP] = out.astype(jnp.bfloat16).reshape(CAP, cells, width)


def up_call(fine, mask, w, octants, first, partial):
    bricks, cells, width = fine.shape
    mid = w.shape[0]
    step = 8
    blocks = bricks // step

    def place(i):
        return (first + i) % blocks

    partials = [] if partial is None else [partial]
    return pl.pallas_call(
        up_kernel,
        grid=(UP_OFFSETS * CAP // step,),
        in_specs=[
            pl.BlockSpec((step, cells, width), lambda i: (place(i), 0, 0)),
            pl.BlockSpec((step * cells, width), lambda i: (place(i), 0)),
            pl.BlockSpec((mid, width), lambda i: (0, 0)),
        ]
        + [pl.BlockSpec((CAP * cells, mid), lambda i: (0, 0))] * UP_OFFSETS
        + [pl.BlockSpec(memory_space=pl.ANY)] * len(partials),
        out_specs=pl.BlockSpec((step, cells, width), lambda i: (place(i), 0, 0)),
        out_shape=jax.ShapeDtypeStruct(fine.shape, jnp.bfloat16),
        input_output_aliases={3 + UP_OFFSETS: 0} if partials else {},
        compiler_params=pltpu.CompilerParams(vmem_limit_bytes=VMEM_LIMIT),
        cost_estimate=pl.CostEstimate(
            flops=bricks * cells * width * mid, bytes_accessed=bricks * cells * width * 2, transcendentals=0
        ),
        name="up",
    )(fine, mask, w, *octants, *partials)


def low_half(shape):
    return lax.broadcasted_iota(jnp.int32, shape, len(shape) - 2) < 4


def slot_flags(source_ref, first):
    pair = [jnp.where(source_ref[first + k] >= 0, 1.0, 0.0).astype(jnp.float32) for k in range(2)]
    return jnp.where(low_half((8, 128)), pair[0], pair[1])


def slot_index(depth_brick, row_brick):
    pd, qd = divmod(depth_brick, 2)
    pr, qr = divmod(row_brick, 2)
    return (pd * 2 + pr) * 8 + qd * 4 + qr * 2


def take_brick(source_ref, arrived, slot):
    value = source_ref[slot]
    first = pl.multiple_of(jnp.maximum(value, 0) * CELLS, CELLS)
    brick = arrived[pl.ds(first, CELLS), :].astype(jnp.float32)
    return jnp.where(value >= 0, brick, 0.0).reshape(8, 8, 128)


def place_kernel(base_ref, source_ref, *refs):
    block_ref, even_ref, odd_ref, low_ref, high_ref, arrived = refs[K:]
    for j in range(K):
        arrived[j * CAP * CELLS : (j + 1) * CAP * CELLS] = refs[j][...]
    half = low_half((8, 8, 128))
    for depth_brick in range(4):
        for row_brick in range(4):
            slot = slot_index(depth_brick, row_brick)
            b0 = take_brick(source_ref, arrived, slot)
            b1 = take_brick(source_ref, arrived, slot + 1)
            even = jnp.where(half, b0, pltpu.roll(b1, 4, 1))
            odd = jnp.where(half, pltpu.roll(b0, 4, 1), b1)
            both = jnp.stack([even, odd], axis=1).reshape(4, 32, 128).astype(jnp.bfloat16)
            for vd in range(4):
                row = ((depth_brick * 4 + vd) * SIDE + row_brick * 4) * COLS
                block_ref[row : row + 32] = both[vd]
                place = (depth_brick * 4 + vd) * 16
                if row_brick == 0:
                    low_ref[place : place + 16] = both[vd, :16]
                if row_brick == 3:
                    high_ref[place : place + 16] = both[vd, 16:]
    for row_brick, ref in ((0, low_ref), (3, high_ref)):
        flags = [slot_flags(source_ref, slot_index(d, row_brick)) for d in range(4)]
        ref[256:288] = jnp.concatenate(flags, axis=0).astype(jnp.bfloat16)
    face_out(base_ref[0], low_ref, high_ref, even_ref, odd_ref)


def face_out(index, low_ref, high_ref, even_ref, odd_ref):
    is_even = index % 2 == 0
    even_ref[...] = jnp.where(is_even, high_ref[...], low_ref[...])
    odd_ref[...] = jnp.where(is_even, low_ref[...], high_ref[...])


def face_in(index, count, even_ref, odd_ref, low_ref, high_ref):
    is_even = index % 2 == 0
    empty = jnp.zeros(low_ref.shape, low_ref.dtype)
    low = jnp.where(is_even, odd_ref[...], even_ref[...])
    high = jnp.where(is_even, even_ref[...], odd_ref[...])
    low_ref[...] = jnp.where(index == 0, empty, low)
    high_ref[...] = jnp.where(index == count - 1, empty, high)


def place_call(base, source, arrived):
    mid = arrived[0].shape[1]
    smem = pl.BlockSpec(memory_space=pltpu.SMEM)
    vmem = pl.BlockSpec(memory_space=pltpu.VMEM)
    return pl.pallas_call(
        place_kernel,
        in_specs=[smem, smem] + [vmem] * K,
        out_specs=[vmem] * 3,
        out_shape=[
            jax.ShapeDtypeStruct((rows, mid), jnp.bfloat16)
            for rows in (SIDE * SIDE * COLS, 288, 288)
        ],
        scratch_shapes=[
            pltpu.VMEM((288, mid), jnp.bfloat16),
            pltpu.VMEM((288, mid), jnp.bfloat16),
            pltpu.VMEM((K * CAP * CELLS, mid), jnp.bfloat16),
        ],
        compiler_params=pltpu.CompilerParams(vmem_limit_bytes=VMEM_LIMIT),
        name="place",
    )(base, source, *arrived)


def edge_kernel(
    counts,
    base_ref,
    source_ref,
    block_ref,
    even_ref,
    odd_ref,
    before_ref,
    after_ref,
    even_out,
    odd_out,
    low_ref,
    high_ref,
):
    face_in(base_ref[0], counts[1], even_ref, odd_ref, before_ref, after_ref)
    for ref, planes, brick in ((low_ref, (0, 1), 0), (high_ref, (SIDE - 2, SIDE - 1), 3)):
        for k, plane in enumerate(planes):
            start = k * WIDE * COLS
            ref[start : start + 16] = before_ref[plane * 16 : plane * 16 + 16]
            ref[start + 16 : start + 144] = block_ref[plane * 128 : plane * 128 + 128]
            ref[start + 144 : start + 160] = after_ref[plane * 16 : plane * 16 + 16]
        flags = [before_ref[256:288].astype(jnp.float32)[brick * 8 : brick * 8 + 8]]
        flags += [slot_flags(source_ref, slot_index(brick, r)) for r in range(4)]
        flags += [after_ref[256:288].astype(jnp.float32)[brick * 8 : brick * 8 + 8]]
        ref[320:368] = jnp.concatenate(flags, axis=0).astype(jnp.bfloat16)
    face_out(base_ref[1], low_ref, high_ref, even_out, odd_out)


def edge_call(counts, base, source, block, even, odd):
    smem = pl.BlockSpec(memory_space=pltpu.SMEM)
    vmem = pl.BlockSpec(memory_space=pltpu.VMEM)
    mid = block.shape[1]
    return pl.pallas_call(
        functools.partial(edge_kernel, counts),
        in_specs=[smem, smem, vmem, vmem, vmem],
        out_specs=[vmem] * 4,
        out_shape=[
            jax.ShapeDtypeStruct((rows, mid), jnp.bfloat16) for rows in (288, 288, 368, 368)
        ],
        scratch_shapes=[pltpu.VMEM((368, mid), jnp.bfloat16)] * 2,
        compiler_params=pltpu.CompilerParams(vmem_limit_bytes=VMEM_LIMIT),
        name="edge",
    )(base, source, block, even, odd)


def gather_weights(w_ref, wide_ref):
    width = w_ref.shape[2]
    for tap in range(9):
        for column in range(3):
            wide_ref[tap * width : (tap + 1) * width, column * width : (column + 1) * width] = (
                w_ref[tap * 3 + column]
            )


def as_rows(value):
    value = value.astype(jnp.float32)
    return value.reshape(value.shape[0] // COLS, COLS, value.shape[1])


def moved_rows(rows):
    empty = jnp.zeros((1,) + rows.shape[1:], jnp.float32)
    return jnp.concatenate([rows[1:], empty], axis=0)


def as_tiles(rows):
    return rows.reshape(rows.shape[0] * COLS, rows.shape[2]).astype(jnp.bfloat16)


def multiply_taps(lhs, wide_ref):
    width = wide_ref.shape[1] // 3
    wide = jnp.dot(lhs, wide_ref[...], preferred_element_type=jnp.float32)
    wide = wide.reshape(lhs.shape[0] // COLS, COLS, 3 * width)
    column = lax.broadcasted_iota(jnp.int32, (lhs.shape[0] // COLS, COLS, width), 1)
    left = jnp.where(column == 0, 0.0, pltpu.roll(wide[:, :, :width], 1, 1))
    right = jnp.where(column == COLS - 1, 0.0, pltpu.roll(wide[:, :, 2 * width :], COLS - 1, 1))
    return left + wide[:, :, width : 2 * width] + right


def plane_taps(here_ref, next_ref, first, planes, rows):
    taps = []
    for dd in range(3):
        span = slice(first + dd, first + dd + planes)
        taps += [
            here_ref[span, 0:rows, :],
            next_ref[span, 0:rows, :],
            here_ref[span, 16 : rows + 16, :],
        ]
    lhs = jnp.concatenate(taps, axis=2)
    return lhs.reshape(planes * rows, lhs.shape[2])


def conv_planes(here_ref, next_ref, wide_ref, first, planes, rows):
    return multiply_taps(plane_taps(here_ref, next_ref, first, planes, rows), wide_ref)


def activate(value, flags):
    return value / (1.0 + jnp.exp(-value)) * flags


def spread_flags(flags, repeats):
    return jnp.concatenate(
        [jnp.broadcast_to(flag[None], (count,) + flag.shape) for flag, count in zip(flags, repeats)],
        axis=0,
    )


def inner_planes(source_ref, block_ref, wide1_ref, hidden_ref, here, moved, groups):
    width = block_ref.shape[1]
    base = groups[0][0] - 1
    for d in range(base, groups[-1][0] + groups[-1][1] + 1):
        plane = block_ref[d * 128 : (d + 1) * 128]
        here[d - base] = plane
        moved[d - base] = as_tiles(moved_rows(as_rows(plane)))
    inner = SIDE - 2
    rows = inner * COLS
    for first, planes in groups:
        value = conv_planes(here, moved, wide1_ref, first - 1 - base, planes, rows)
        value = value.reshape(planes, inner, COLS, width)
        flags = [slot_flags(source_ref, slot_index(first // 4, r)) for r in range(4)]
        value = activate(value, spread_flags(flags, (3, 4, 4, 3))[None])
        hidden_ref[first - 1 - base : first - 1 - base + planes] = value.reshape(
            planes, rows, width
        ).astype(jnp.bfloat16)


def inner_kernel(groups, source_ref, block_ref, wide1_ref, hidden_ref, here, moved):
    inner_planes(source_ref, block_ref, wide1_ref, hidden_ref, here, moved, groups)


def conv_cost(rows, width):
    return pl.CostEstimate(
        flops=2 * rows * 27 * width * width, bytes_accessed=27 * width * width * 4, transcendentals=0
    )


def inner_call(source, block, wide1, groups):
    mid = block.shape[1]
    smem = pl.BlockSpec(memory_space=pltpu.SMEM)
    vmem = pl.BlockSpec(memory_space=pltpu.VMEM)
    rows = (SIDE - 2) * COLS
    planes = sum(count for _, count in groups)
    return pl.pallas_call(
        functools.partial(inner_kernel, groups),
        in_specs=[smem, vmem, vmem],
        out_specs=vmem,
        out_shape=jax.ShapeDtypeStruct((planes, rows, mid), jnp.bfloat16),
        scratch_shapes=[pltpu.VMEM((planes + 2, SIDE * COLS, mid), jnp.bfloat16)] * 2,
        compiler_params=pltpu.CompilerParams(vmem_limit_bytes=VMEM_LIMIT),
        cost_estimate=conv_cost(planes * rows, mid),
        name="inner",
    )(source, block, wide1)


def side_taps(low, high):
    mixed = as_tiles(
        jnp.concatenate(
            [as_rows(low).reshape(-1, 2, COLS, 128)[:, 1:], as_rows(high).reshape(-1, 2, COLS, 128)[:, :1]],
            axis=1,
        ).reshape(-1, COLS, 128)
    )
    return low, mixed, high


def depth_taps(taps, planes):
    parts = [tap[dd * 16 : (dd + planes) * 16] for dd in range(3) for tap in taps]
    return jnp.concatenate(parts, axis=1)


def coarse_rows(source_ref, block_ref, value, depth_brick):
    width = block_ref.shape[1]
    value = value.reshape(4, SIDE, COLS, width)
    rows = slice(depth_brick * 512, (depth_brick + 1) * 512)
    own = block_ref[rows].astype(jnp.float32).reshape(4, SIDE, COLS, width)
    flags = [slot_flags(source_ref, slot_index(depth_brick, r)) for r in range(4)]
    return (value + own) * spread_flags(flags, (4, 4, 4, 4))[None]


def side_kernel(source_ref, *refs):
    block_ref, before_ref, after_ref, early_ref, later_ref, wide1_ref = refs[:6]
    h_here, h_next, side, late, here, moved = refs[6:]
    width = block_ref.shape[1]
    inner = SIDE - 2
    inner_planes(source_ref, block_ref, wide1_ref, late, here, moved, LATE)

    low = jnp.concatenate([block_ref[d * 128 : d * 128 + 16] for d in range(SIDE)], axis=0)
    high = jnp.concatenate([block_ref[d * 128 + 112 : d * 128 + 128] for d in range(SIDE)], axis=0)
    left = depth_taps(side_taps(before_ref[0:256], low), inner)
    right = depth_taps(side_taps(high, after_ref[0:256]), inner)
    value = multiply_taps(jnp.concatenate([left, right], axis=0), wide1_ref)
    depths = (3, 4, 4, 3)
    edge_flags = (as_rows(before_ref[256:288]), as_rows(after_ref[256:288]))
    flags = []
    for end, row_brick in ((0, 0), (1, 3)):
        own = [slot_flags(source_ref, slot_index(d, row_brick)) for d in range(4)]
        pairs = [jnp.stack([edge_flags[end][d], own[d]][:: 1 - 2 * end], axis=0) for d in range(4)]
        flags.append(spread_flags(pairs, depths))
    value = activate(value.reshape(2, inner, 2, COLS, width), jnp.stack(flags, axis=0))
    side[...] = value.reshape(2, inner, 16, width).astype(jnp.bfloat16)
    centres = [ref[k] for ref in (early_ref, later_ref, late) for k in range(ref.shape[0])]
    for d in range(inner):
        plane = jnp.concatenate([side[0, d], centres[d], side[1, d]], axis=0)
        h_here[d] = plane
        h_next[d] = as_tiles(moved_rows(as_rows(plane)))


def half_kernel(source_ref, block_ref, h_here, h_next, wide2_ref, coarse_ref):
    width = block_ref.shape[1]
    for depth_brick in (1, 2):
        value = conv_planes(h_here, h_next, wide2_ref, depth_brick * 4 - 2, 4, SIDE * COLS)
        value = coarse_rows(source_ref, block_ref, value, depth_brick)
        rows = slice((depth_brick - 1) * 512, depth_brick * 512)
        coarse_ref[rows] = value.reshape(512, width).astype(jnp.bfloat16)


def side_call(source, block, before, after, early, later, wide1):
    mid = block.shape[1]
    smem = pl.BlockSpec(memory_space=pltpu.SMEM)
    vmem = pl.BlockSpec(memory_space=pltpu.VMEM)
    inner = SIDE - 2
    hidden = (inner, HID * COLS, mid)
    return pl.pallas_call(
        side_kernel,
        in_specs=[smem] + [vmem] * 6,
        out_specs=[vmem] * 2,
        out_shape=[jax.ShapeDtypeStruct(hidden, jnp.bfloat16)] * 2,
        scratch_shapes=[
            pltpu.VMEM((2, inner, 16, mid), jnp.bfloat16),
            pltpu.VMEM((LATE_PLANES, inner * COLS, mid), jnp.bfloat16),
            pltpu.VMEM((LATE_PLANES + 2, SIDE * COLS, mid), jnp.bfloat16),
            pltpu.VMEM((LATE_PLANES + 2, SIDE * COLS, mid), jnp.bfloat16),
        ],
        compiler_params=pltpu.CompilerParams(vmem_limit_bytes=VMEM_LIMIT),
        cost_estimate=conv_cost(inner * (4 + LATE_PLANES) * COLS, mid),
        name="side",
    )(source, block, before, after, early, later, wide1)


def half_call(source, block, here, moved, wide2):
    mid = block.shape[1]
    vmem = pl.BlockSpec(memory_space=pltpu.VMEM)
    return pl.pallas_call(
        half_kernel,
        in_specs=[pl.BlockSpec(memory_space=pltpu.SMEM)] + [vmem] * 4,
        out_specs=vmem,
        out_shape=jax.ShapeDtypeStruct((1024, mid), jnp.bfloat16),
        compiler_params=pltpu.CompilerParams(vmem_limit_bytes=VMEM_LIMIT),
        cost_estimate=conv_cost(1024, mid),
        name="half",
    )(source, block, here, moved, wide2)


def scatter_bricks(source_ref, stage, value, depth_brick):
    width = value.shape[3]
    half = low_half((4, 2, COLS, width))
    for r in range(4):
        part = value[:, r * 4 : (r + 1) * 4].reshape(4, 2, 2, COLS, width)
        even, odd = part[:, :, 0], part[:, :, 1]
        b0 = jnp.where(half, even, pltpu.roll(odd, 4, 2))
        b1 = jnp.where(half, pltpu.roll(even, 4, 2), odd)
        slot = slot_index(depth_brick, r)
        for k, brick in enumerate((b0, b1)):
            source = source_ref[slot + k]
            row = pl.multiple_of(jnp.where(source >= 0, source, K * CAP) * CELLS, CELLS)
            stage[pl.ds(row, CELLS), :] = brick.reshape(CELLS, width).astype(jnp.bfloat16)


def final_kernel(count, base_ref, source_ref, *refs):
    block_ref, before_ref, after_ref, even_ref, odd_ref = refs[:5]
    mid_here, mid_next, mid_ref, wide1_ref, wide2_ref, coarse_ref = refs[5:11]
    backs = refs[11 : 11 + K]
    x_here, x_next, h_here, h_next, stage, under_ref, over_ref = refs[11 + K :]
    width = block_ref.shape[1]
    stage[...] = jnp.zeros(stage.shape, jnp.bfloat16)
    face_in(base_ref[1], count, even_ref, odd_ref, under_ref, over_ref)
    flags_before = as_rows(before_ref[256:288])
    flags_after = as_rows(after_ref[256:288])
    spread = []
    for end, ref in ((0, under_ref), (1, over_ref)):
        own = []
        for d in (0, 1) if end == 0 else (SIDE - 2, SIDE - 1):
            edge = slice(d * 16, (d + 1) * 16)
            own.append(
                jnp.concatenate(
                    [before_ref[edge], block_ref[d * 128 : (d + 1) * 128], after_ref[edge]], axis=0
                )
            )
        far = [ref[k * 160 : (k + 1) * 160] for k in range(2)]
        for index, plane in enumerate(far + own if end == 0 else own + far):
            x_here[end * 4 + index] = plane
            x_next[end * 4 + index] = as_tiles(moved_rows(as_rows(plane)))
        far_flags = as_rows(ref[320:368])
        brick = 0 if end == 0 else 3
        own_flags = [flags_before[brick]]
        own_flags += [slot_flags(source_ref, slot_index(brick, r)) for r in range(4)]
        own_flags += [flags_after[brick]]
        pair = [
            spread_flags([far_flags[r] for r in range(6)], (1, 4, 4, 4, 4, 1)),
            spread_flags(own_flags, (1, 4, 4, 4, 4, 1)),
        ]
        spread += pair if end == 0 else pair[::-1]
    lhs = [plane_taps(x_here, x_next, first, 2, HID * COLS) for first in (0, 4)]
    value = multiply_taps(jnp.concatenate(lhs, axis=0), wide1_ref)
    value = activate(value.reshape(4, HID, COLS, width), jnp.stack(spread, axis=0))
    for k, index in enumerate((0, 1, 10, 11)):
        h_here[index] = as_tiles(value[k])
        h_next[index] = as_tiles(moved_rows(value[k]))
    for k in range(4):
        for index, source in ((2 + k, k), (6 + k, SIDE - 6 + k)):
            h_here[index] = mid_here[source]
            h_next[index] = mid_next[source]
    for depth_brick in (1, 2):
        rows = slice((depth_brick - 1) * 512, depth_brick * 512)
        done = mid_ref[rows]
        coarse_ref[depth_brick * 512 : (depth_brick + 1) * 512] = done
        done = done.astype(jnp.float32).reshape(4, SIDE, COLS, width)
        scatter_bricks(source_ref, stage, done, depth_brick)
    for depth_brick in (0, 3):
        value = conv_planes(h_here, h_next, wide2_ref, depth_brick * 2, 4, SIDE * COLS)
        value = coarse_rows(source_ref, block_ref, value, depth_brick)
        rows = slice(depth_brick * 512, (depth_brick + 1) * 512)
        coarse_ref[rows] = value.reshape(512, width).astype(jnp.bfloat16)
        scatter_bricks(source_ref, stage, value, depth_brick)
    for j in range(K):
        backs[j][...] = stage[j * CAP * CELLS : (j + 1) * CAP * CELLS]


def final_call(count, base, source, block, halo, middle, wide1, wide2):
    mid = block.shape[1]
    smem = pl.BlockSpec(memory_space=pltpu.SMEM)
    vmem = pl.BlockSpec(memory_space=pltpu.VMEM)
    return pl.pallas_call(
        functools.partial(final_kernel, count),
        in_specs=[smem, smem] + [vmem] * 10,
        out_specs=[vmem] * (1 + K),
        out_shape=[jax.ShapeDtypeStruct(block.shape, jnp.bfloat16)]
        + [jax.ShapeDtypeStruct((CAP * CELLS, mid), jnp.bfloat16)] * K,
        scratch_shapes=[
            pltpu.VMEM((8, WIDE * COLS, mid), jnp.bfloat16),
            pltpu.VMEM((8, WIDE * COLS, mid), jnp.bfloat16),
            pltpu.VMEM((12, HID * COLS, mid), jnp.bfloat16),
            pltpu.VMEM((12, HID * COLS, mid), jnp.bfloat16),
            pltpu.VMEM(((K * CAP + 1) * CELLS, mid), jnp.bfloat16),
            pltpu.VMEM((368, mid), jnp.bfloat16),
            pltpu.VMEM((368, mid), jnp.bfloat16),
        ],
        compiler_params=pltpu.CompilerParams(vmem_limit_bytes=VMEM_LIMIT),
        cost_estimate=conv_cost(1600, mid),
        name="final",
    )(base, source, block, *halo, *middle, wide1, wide2)


def from_behind(value, axis, steps):
    count = lax.axis_size(axis)
    pairs = [(source, (source + steps) % count) for source in range(count)]
    return lax.ppermute(value, axis, pairs)


def swap_face(face, axis, first):
    count = lax.axis_size(axis)
    partner = list(range(count))
    for i in range(first, count - 1, 2):
        partner[i], partner[i + 1] = i + 1, i
    return lax.ppermute(face, axis, list(enumerate(partner)))


def shards(fine, fine_mask, slot_source, w_down, w_first, w_second, w_up):
    mid = w_down.shape[1]
    base = jnp.stack([lax.axis_index("xy"), lax.axis_index("gz")]).astype(jnp.int32)
    counts = (lax.axis_size("gz"), lax.axis_size("xy"))
    sent = down_call(fine, fine_mask, w_down, SENT)
    arrived = {j: from_behind(sent[j], "xy", j) for j in SENT}
    later = (arrived[SENT[2]], fine, fine_mask, w_down, w_first, w_second)
    arrived[SENT[2]], *later = lax.optimization_barrier(later)
    prepared = lax.optimization_barrier(tuple(prepare_call(*later)))
    arrived[0], mask, wide1, wide2 = prepared
    block, even, odd = place_call(base, slot_source, [arrived[j] for j in range(K)])
    odd = swap_face(odd, "xy", 1)
    early = inner_call(slot_source, block, wide1, EARLY)
    even, early = lax.optimization_barrier((even, early))
    even = swap_face(even, "xy", 0)
    later = inner_call(slot_source, block, wide1, LATER)
    even, odd, later = lax.optimization_barrier((even, odd, later))
    before, after, even, odd = edge_call(counts, base, slot_source, block, even, odd)
    odd = swap_face(odd, "gz", 1)
    here, moved = side_call(slot_source, block, before, after, early, later, wide1)
    even, here, moved = lax.optimization_barrier((even, here, moved))
    even = swap_face(even, "gz", 0)
    middle = (here, moved, half_call(slot_source, block, here, moved, wide2))
    coarse, *back = final_call(
        counts[0], base, slot_source, block, (before, after, even, odd), middle, wide1, wide2
    )
    octant = {j: from_behind(back[j], "xy", -j) for j in SENT}
    octant[0] = back[0]
    fine_out = up_call(fine, mask, w_up, [octant[j] for j in (2, 3, 4, 5)], 1, None)
    fine_out = up_call(fine, mask, w_up, [octant[j] for j in (6, 7, 0, 1)], 3, fine_out)
    return fine_out, coarse.reshape(SIDE, SIDE, COLS, mid)


def solution(mesh):
    placed = (
        P(("gz", "xy"), None, None),
        P(("gz", "xy"), None),
        P(("gz", "xy")),
        P(),
        P(),
        P(),
        P(),
    )
    return jax.shard_map(
        shards,
        mesh=mesh,
        in_specs=placed,
        out_specs=(P(("gz", "xy"), None, None), P("gz", "xy", None, None)),
        check_vma=False,
    )
```

```python
import functools

import jax
import jax.numpy as jnp
from jax import lax
from jax.experimental import pallas as pl
from jax.experimental.pallas import tpu as pltpu
from jax.sharding import PartitionSpec as P

CAP = 4
K = 8
CELLS = 64
SIDE = 16
COLS = 8
WIDE = SIDE + 4
HID = SIDE + 2
EARLY = ((1, 3), (4, 4), (8, 4))
LATE = ((12, 3),)
LATE_PLANES = 3
SENT = (4, 3, 5, 2, 6, 1, 7)
RETURNED = (1, 7, 6, 4, 2, 3, 5)
UP_OFFSETS = 4
DOWN_LIMIT = 62 * 1024 * 1024
VMEM_LIMIT = 24 * 1024 * 1024


def expand_mask(mask):
    bricks = mask.shape[0]
    values = mask.astype(jnp.float32)
    cell = lax.broadcasted_iota(jnp.int32, (16, 128), 0)
    lane = lax.broadcasted_iota(jnp.int32, (16, 128), 1)
    chosen = (cell == lane // 8).astype(jnp.float32)
    parts = [
        values[:, t * 128 : (t + 1) * 128].reshape(bricks, 1, 128) * chosen[None] for t in range(4)
    ]
    spread = jnp.concatenate(parts, axis=1).reshape(bricks * CELLS, 128).astype(jnp.bfloat16)
    source = lax.broadcasted_iota(jnp.int32, (128, 512), 0)
    target = lax.broadcasted_iota(jnp.int32, (128, 512), 1)
    widen = ((source & 7) == (target >> 6)).astype(jnp.bfloat16)
    return jnp.dot(spread, widen, preferred_element_type=jnp.float32)


def down_kernel(offsets, fine_hbm, mask_hbm, w_hbm, *refs):
    count = len(offsets)
    outs = refs[:count]
    fine_ref, mask_ref, w_ref, wide_ref, sems = refs[count:]
    first = [
        pltpu.make_async_copy(mask_hbm, mask_ref, sems.at[count]),
        pltpu.make_async_copy(w_hbm, w_ref, sems.at[count + 1]),
    ]
    chunks = [
        pltpu.make_async_copy(fine_hbm.at[pl.ds(j * CAP, CAP)], fine_ref.at[k], sems.at[k])
        for k, j in enumerate(offsets)
    ]
    for copy in first + chunks:
        copy.start()
    first[0].wait()
    rows = CAP * CELLS
    for k, j in enumerate(offsets):
        wide_ref[k * rows : (k + 1) * rows] = expand_mask(
            mask_ref[j * CAP : (j + 1) * CAP]
        ).astype(jnp.bfloat16)
    first[1].wait()
    for start in range(0, count, 2):
        group = range(start, min(start + 2, count))
        for k in group:
            chunks[k].wait()
        x = [
            fine_ref[k].reshape(rows, -1) * wide_ref[k * rows : (k + 1) * rows] for k in group
        ]
        y = jnp.dot(jnp.concatenate(x, axis=0), w_ref[...], preferred_element_type=jnp.float32)
        y = y.astype(jnp.bfloat16)
        for part, k in enumerate(group):
            outs[k][...] = y[part * rows : (part + 1) * rows]


def down_call(fine, mask, w, offsets):
    cells, width = fine.shape[1:]
    mid = w.shape[1]
    count = len(offsets)
    rows = count * CAP * cells
    hbm = pl.BlockSpec(memory_space=pltpu.HBM)
    outs = pl.pallas_call(
        functools.partial(down_kernel, offsets),
        in_specs=[hbm, hbm, hbm],
        out_specs=[pl.BlockSpec(memory_space=pltpu.VMEM)] * count,
        out_shape=[jax.ShapeDtypeStruct((CAP * cells, mid), jnp.bfloat16)] * count,
        scratch_shapes=[
            pltpu.VMEM((count, CAP, cells, width), fine.dtype),
            pltpu.VMEM(mask.shape, mask.dtype),
            pltpu.VMEM(w.shape, w.dtype),
            pltpu.VMEM((rows, width), jnp.bfloat16),
            pltpu.SemaphoreType.DMA((count + 2,)),
        ],
        compiler_params=pltpu.CompilerParams(vmem_limit_bytes=DOWN_LIMIT),
        cost_estimate=pl.CostEstimate(
            flops=2 * rows * width * mid, bytes_accessed=rows * width * 2, transcendentals=0
        ),
        name="down",
    )(fine, mask, w)
    return dict(zip(offsets, outs))


def prepare_kernel(
    fine_ref, mask_ref, w_down_ref, w1_ref, w2_ref, own_ref, mask_out, wide1_ref, wide2_ref
):
    gather_weights(w1_ref, wide1_ref)
    gather_weights(w2_ref, wide2_ref)
    step = 8
    for part in range(mask_ref.shape[0] // step):
        rows = slice(part * step * CELLS, (part + 1) * step * CELLS)
        mask_out[rows] = expand_mask(mask_ref[part * step : (part + 1) * step]).astype(jnp.bfloat16)
    rows = CAP * CELLS
    own = fine_ref[...].reshape(rows, -1) * mask_out[:rows]
    own = jnp.dot(own, w_down_ref[...], preferred_element_type=jnp.float32)
    own_ref[...] = own.astype(jnp.bfloat16)


def prepare_call(fine, mask, w_down, w_first, w_second):
    mid = w_first.shape[1]
    vmem = pl.BlockSpec(memory_space=pltpu.VMEM)
    rows = mask.shape[0] * CELLS
    wide = jax.ShapeDtypeStruct((9 * mid, 3 * mid), jnp.bfloat16)
    return pl.pallas_call(
        prepare_kernel,
        grid=(1,),
        in_specs=[pl.BlockSpec((CAP,) + fine.shape[1:], lambda i: (0, 0, 0))] + [vmem] * 4,
        out_specs=[vmem] * 4,
        out_shape=[
            jax.ShapeDtypeStruct((CAP * CELLS, mid), jnp.bfloat16),
            jax.ShapeDtypeStruct((rows, mask.shape[1]), jnp.bfloat16),
            wide,
            wide,
        ],
        compiler_params=pltpu.CompilerParams(vmem_limit_bytes=VMEM_LIMIT),
        cost_estimate=pl.CostEstimate(
            flops=2 * rows * mask.shape[1] * 128, bytes_accessed=rows * mask.shape[1] * 2, transcendentals=0
        ),
        name="prepare",
    )(fine, mask, w_down, w_first, w_second)


def up_kernel(fine_ref, mask_ref, w_ref, *refs):
    out_ref = refs[-1]
    step = pl.program_id(0)
    bricks, cells, width = fine_ref.shape
    count = bricks // CAP
    steps = UP_OFFSETS // count
    for part in range(count):
        octant = refs[part][...]
        for other in range(1, steps):
            octant = jnp.where(step == other, refs[other * count + part][...], octant)
        rows = slice(part * CAP * cells, (part + 1) * CAP * cells)
        up = jnp.dot(octant, w_ref[...], preferred_element_type=jnp.float32)
        fine = fine_ref[part * CAP : (part + 1) * CAP].reshape(CAP * cells, width)
        mask = mask_ref[rows].astype(jnp.float32)
        out = jnp.where(mask > 0.5, fine.astype(jnp.float32) + up, 0.0)
        out_ref[part * CAP : (part + 1) * CAP] = out.astype(jnp.bfloat16).reshape(CAP, cells, width)


def up_call(fine, mask, w, octants, first, partial):
    bricks, cells, width = fine.shape
    mid = w.shape[0]
    step = 8
    blocks = bricks // step

    def place(i):
        return (first + i) % blocks

    partials = [] if partial is None else [partial]
    return pl.pallas_call(
        up_kernel,
        grid=(UP_OFFSETS * CAP // step,),
        in_specs=[
            pl.BlockSpec((step, cells, width), lambda i: (place(i), 0, 0)),
            pl.BlockSpec((step * cells, width), lambda i: (place(i), 0)),
            pl.BlockSpec((mid, width), lambda i: (0, 0)),
        ]
        + [pl.BlockSpec((CAP * cells, mid), lambda i: (0, 0))] * UP_OFFSETS
        + [pl.BlockSpec(memory_space=pl.ANY)] * len(partials),
        out_specs=pl.BlockSpec((step, cells, width), lambda i: (place(i), 0, 0)),
        out_shape=jax.ShapeDtypeStruct(fine.shape, jnp.bfloat16),
        input_output_aliases={3 + UP_OFFSETS: 0} if partials else {},
        compiler_params=pltpu.CompilerParams(vmem_limit_bytes=VMEM_LIMIT),
        cost_estimate=pl.CostEstimate(
            flops=bricks * cells * width * mid, bytes_accessed=bricks * cells * width * 2, transcendentals=0
        ),
        name="up",
    )(fine, mask, w, *octants, *partials)


def low_half(shape):
    return lax.broadcasted_iota(jnp.int32, shape, len(shape) - 2) < 4


def slot_flags(source_ref, first):
    pair = [jnp.where(source_ref[first + k] >= 0, 1.0, 0.0).astype(jnp.float32) for k in range(2)]
    return jnp.where(low_half((8, 128)), pair[0], pair[1])


def slot_index(depth_brick, row_brick):
    pd, qd = divmod(depth_brick, 2)
    pr, qr = divmod(row_brick, 2)
    return (pd * 2 + pr) * 8 + qd * 4 + qr * 2


def take_brick(source_ref, arrived, slot):
    value = source_ref[slot]
    first = pl.multiple_of(jnp.maximum(value, 0) * CELLS, CELLS)
    brick = arrived[pl.ds(first, CELLS), :].astype(jnp.float32)
    return jnp.where(value >= 0, brick, 0.0).reshape(8, 8, 128)


def place_kernel(base_ref, source_ref, *refs):
    block_ref, even_ref, odd_ref, low_ref, high_ref, arrived = refs[K:]
    for j in range(K):
        arrived[j * CAP * CELLS : (j + 1) * CAP * CELLS] = refs[j][...]
    half = low_half((8, 8, 128))
    for depth_brick in range(4):
        for row_brick in range(4):
            slot = slot_index(depth_brick, row_brick)
            b0 = take_brick(source_ref, arrived, slot)
            b1 = take_brick(source_ref, arrived, slot + 1)
            even = jnp.where(half, b0, pltpu.roll(b1, 4, 1))
            odd = jnp.where(half, pltpu.roll(b0, 4, 1), b1)
            both = jnp.stack([even, odd], axis=1).reshape(4, 32, 128).astype(jnp.bfloat16)
            for vd in range(4):
                row = ((depth_brick * 4 + vd) * SIDE + row_brick * 4) * COLS
                block_ref[row : row + 32] = both[vd]
                place = (depth_brick * 4 + vd) * 16
                if row_brick == 0:
                    low_ref[place : place + 16] = both[vd, :16]
                if row_brick == 3:
                    high_ref[place : place + 16] = both[vd, 16:]
    for row_brick, ref in ((0, low_ref), (3, high_ref)):
        flags = [slot_flags(source_ref, slot_index(d, row_brick)) for d in range(4)]
        ref[256:288] = jnp.concatenate(flags, axis=0).astype(jnp.bfloat16)
    face_out(base_ref[0], low_ref, high_ref, even_ref, odd_ref)


def face_out(index, low_ref, high_ref, even_ref, odd_ref):
    is_even = index % 2 == 0
    even_ref[...] = jnp.where(is_even, high_ref[...], low_ref[...])
    odd_ref[...] = jnp.where(is_even, low_ref[...], high_ref[...])


def face_in(index, count, even_ref, odd_ref, low_ref, high_ref):
    is_even = index % 2 == 0
    empty = jnp.zeros(low_ref.shape, low_ref.dtype)
    low = jnp.where(is_even, odd_ref[...], even_ref[...])
    high = jnp.where(is_even, even_ref[...], odd_ref[...])
    low_ref[...] = jnp.where(index == 0, empty, low)
    high_ref[...] = jnp.where(index == count - 1, empty, high)


def place_call(base, source, arrived):
    mid = arrived[0].shape[1]
    smem = pl.BlockSpec(memory_space=pltpu.SMEM)
    vmem = pl.BlockSpec(memory_space=pltpu.VMEM)
    return pl.pallas_call(
        place_kernel,
        in_specs=[smem, smem] + [vmem] * K,
        out_specs=[vmem] * 3,
        out_shape=[
            jax.ShapeDtypeStruct((rows, mid), jnp.bfloat16)
            for rows in (SIDE * SIDE * COLS, 288, 288)
        ],
        scratch_shapes=[
            pltpu.VMEM((288, mid), jnp.bfloat16),
            pltpu.VMEM((288, mid), jnp.bfloat16),
            pltpu.VMEM((K * CAP * CELLS, mid), jnp.bfloat16),
        ],
        compiler_params=pltpu.CompilerParams(vmem_limit_bytes=VMEM_LIMIT),
        name="place",
    )(base, source, *arrived)


def edge_kernel(
    counts,
    base_ref,
    source_ref,
    block_ref,
    even_ref,
    odd_ref,
    before_ref,
    after_ref,
    even_out,
    odd_out,
    low_ref,
    high_ref,
):
    face_in(base_ref[0], counts[1], even_ref, odd_ref, before_ref, after_ref)
    for ref, planes, brick in ((low_ref, (0, 1), 0), (high_ref, (SIDE - 2, SIDE - 1), 3)):
        for k, plane in enumerate(planes):
            start = k * WIDE * COLS
            ref[start : start + 16] = before_ref[plane * 16 : plane * 16 + 16]
            ref[start + 16 : start + 144] = block_ref[plane * 128 : plane * 128 + 128]
            ref[start + 144 : start + 160] = after_ref[plane * 16 : plane * 16 + 16]
        flags = [before_ref[256:288].astype(jnp.float32)[brick * 8 : brick * 8 + 8]]
        flags += [slot_flags(source_ref, slot_index(brick, r)) for r in range(4)]
        flags += [after_ref[256:288].astype(jnp.float32)[brick * 8 : brick * 8 + 8]]
        ref[320:368] = jnp.concatenate(flags, axis=0).astype(jnp.bfloat16)
    face_out(base_ref[1], low_ref, high_ref, even_out, odd_out)


def edge_call(counts, base, source, block, even, odd):
    smem = pl.BlockSpec(memory_space=pltpu.SMEM)
    vmem = pl.BlockSpec(memory_space=pltpu.VMEM)
    mid = block.shape[1]
    return pl.pallas_call(
        functools.partial(edge_kernel, counts),
        in_specs=[smem, smem, vmem, vmem, vmem],
        out_specs=[vmem] * 4,
        out_shape=[
            jax.ShapeDtypeStruct((rows, mid), jnp.bfloat16) for rows in (288, 288, 368, 368)
        ],
        scratch_shapes=[pltpu.VMEM((368, mid), jnp.bfloat16)] * 2,
        compiler_params=pltpu.CompilerParams(vmem_limit_bytes=VMEM_LIMIT),
        name="edge",
    )(base, source, block, even, odd)


def gather_weights(w_ref, wide_ref):
    width = w_ref.shape[2]
    for tap in range(9):
        for column in range(3):
            wide_ref[tap * width : (tap + 1) * width, column * width : (column + 1) * width] = (
                w_ref[tap * 3 + column]
            )


def as_rows(value):
    value = value.astype(jnp.float32)
    return value.reshape(value.shape[0] // COLS, COLS, value.shape[1])


def moved_rows(rows):
    empty = jnp.zeros((1,) + rows.shape[1:], jnp.float32)
    return jnp.concatenate([rows[1:], empty], axis=0)


def as_tiles(rows):
    return rows.reshape(rows.shape[0] * COLS, rows.shape[2]).astype(jnp.bfloat16)


def multiply_taps(lhs, wide_ref):
    width = wide_ref.shape[1] // 3
    wide = jnp.dot(lhs, wide_ref[...], preferred_element_type=jnp.float32)
    wide = wide.reshape(lhs.shape[0] // COLS, COLS, 3 * width)
    column = lax.broadcasted_iota(jnp.int32, (lhs.shape[0] // COLS, COLS, width), 1)
    left = jnp.where(column == 0, 0.0, pltpu.roll(wide[:, :, :width], 1, 1))
    right = jnp.where(column == COLS - 1, 0.0, pltpu.roll(wide[:, :, 2 * width :], COLS - 1, 1))
    return left + wide[:, :, width : 2 * width] + right


def plane_taps(here_ref, next_ref, first, planes, rows):
    taps = []
    for dd in range(3):
        span = slice(first + dd, first + dd + planes)
        taps += [
            here_ref[span, 0:rows, :],
            next_ref[span, 0:rows, :],
            here_ref[span, 16 : rows + 16, :],
        ]
    lhs = jnp.concatenate(taps, axis=2)
    return lhs.reshape(planes * rows, lhs.shape[2])


def conv_planes(here_ref, next_ref, wide_ref, first, planes, rows):
    return multiply_taps(plane_taps(here_ref, next_ref, first, planes, rows), wide_ref)


def activate(value, flags):
    return value / (1.0 + jnp.exp(-value)) * flags


def spread_flags(flags, repeats):
    return jnp.concatenate(
        [jnp.broadcast_to(flag[None], (count,) + flag.shape) for flag, count in zip(flags, repeats)],
        axis=0,
    )


def inner_planes(source_ref, block_ref, wide1_ref, hidden_ref, here, moved, groups):
    width = block_ref.shape[1]
    base = groups[0][0] - 1
    for d in range(base, groups[-1][0] + groups[-1][1] + 1):
        plane = block_ref[d * 128 : (d + 1) * 128]
        here[d - base] = plane
        moved[d - base] = as_tiles(moved_rows(as_rows(plane)))
    inner = SIDE - 2
    rows = inner * COLS
    for first, planes in groups:
        value = conv_planes(here, moved, wide1_ref, first - 1 - base, planes, rows)
        value = value.reshape(planes, inner, COLS, width)
        flags = [slot_flags(source_ref, slot_index(first // 4, r)) for r in range(4)]
        value = activate(value, spread_flags(flags, (3, 4, 4, 3))[None])
        hidden_ref[first - 1 - base : first - 1 - base + planes] = value.reshape(
            planes, rows, width
        ).astype(jnp.bfloat16)


def inner_kernel(groups, source_ref, block_ref, wide1_ref, hidden_ref, here, moved):
    inner_planes(source_ref, block_ref, wide1_ref, hidden_ref, here, moved, groups)


def conv_cost(rows, width):
    return pl.CostEstimate(
        flops=2 * rows * 27 * width * width, bytes_accessed=27 * width * width * 4, transcendentals=0
    )


def inner_call(source, block, wide1, groups):
    mid = block.shape[1]
    smem = pl.BlockSpec(memory_space=pltpu.SMEM)
    vmem = pl.BlockSpec(memory_space=pltpu.VMEM)
    rows = (SIDE - 2) * COLS
    planes = sum(count for _, count in groups)
    return pl.pallas_call(
        functools.partial(inner_kernel, groups),
        in_specs=[smem, vmem, vmem],
        out_specs=vmem,
        out_shape=jax.ShapeDtypeStruct((planes, rows, mid), jnp.bfloat16),
        scratch_shapes=[pltpu.VMEM((planes + 2, SIDE * COLS, mid), jnp.bfloat16)] * 2,
        compiler_params=pltpu.CompilerParams(vmem_limit_bytes=VMEM_LIMIT),
        cost_estimate=conv_cost(planes * rows, mid),
        name="inner",
    )(source, block, wide1)


def side_taps(low, high):
    mixed = as_tiles(
        jnp.concatenate(
            [as_rows(low).reshape(-1, 2, COLS, 128)[:, 1:], as_rows(high).reshape(-1, 2, COLS, 128)[:, :1]],
            axis=1,
        ).reshape(-1, COLS, 128)
    )
    return low, mixed, high


def depth_taps(taps, planes):
    parts = [tap[dd * 16 : (dd + planes) * 16] for dd in range(3) for tap in taps]
    return jnp.concatenate(parts, axis=1)


def coarse_rows(source_ref, block_ref, value, depth_brick):
    width = block_ref.shape[1]
    value = value.reshape(4, SIDE, COLS, width)
    rows = slice(depth_brick * 512, (depth_brick + 1) * 512)
    own = block_ref[rows].astype(jnp.float32).reshape(4, SIDE, COLS, width)
    flags = [slot_flags(source_ref, slot_index(depth_brick, r)) for r in range(4)]
    return (value + own) * spread_flags(flags, (4, 4, 4, 4))[None]


def middle_kernel(source_ref, *refs):
    block_ref, before_ref, after_ref, early_ref, wide1_ref, wide2_ref = refs[:6]
    h_here, h_next, coarse_ref, side, late, here, moved = refs[6:]
    width = block_ref.shape[1]
    inner = SIDE - 2
    inner_planes(source_ref, block_ref, wide1_ref, late, here, moved, LATE)

    low = jnp.concatenate([block_ref[d * 128 : d * 128 + 16] for d in range(SIDE)], axis=0)
    high = jnp.concatenate([block_ref[d * 128 + 112 : d * 128 + 128] for d in range(SIDE)], axis=0)
    left = depth_taps(side_taps(before_ref[0:256], low), inner)
    right = depth_taps(side_taps(high, after_ref[0:256]), inner)
    value = multiply_taps(jnp.concatenate([left, right], axis=0), wide1_ref)
    depths = (3, 4, 4, 3)
    edge_flags = (as_rows(before_ref[256:288]), as_rows(after_ref[256:288]))
    flags = []
    for end, row_brick in ((0, 0), (1, 3)):
        own = [slot_flags(source_ref, slot_index(d, row_brick)) for d in range(4)]
        pairs = [jnp.stack([edge_flags[end][d], own[d]][:: 1 - 2 * end], axis=0) for d in range(4)]
        flags.append(spread_flags(pairs, depths))
    value = activate(value.reshape(2, inner, 2, COLS, width), jnp.stack(flags, axis=0))
    side[...] = value.reshape(2, inner, 16, width).astype(jnp.bfloat16)
    centres = [ref[k] for ref in (early_ref, late) for k in range(ref.shape[0])]
    for d in range(inner):
        plane = jnp.concatenate([side[0, d], centres[d], side[1, d]], axis=0)
        h_here[d] = plane
        h_next[d] = as_tiles(moved_rows(as_rows(plane)))

    for depth_brick in (1, 2):
        value = conv_planes(h_here, h_next, wide2_ref, depth_brick * 4 - 2, 4, SIDE * COLS)
        value = coarse_rows(source_ref, block_ref, value, depth_brick)
        rows = slice((depth_brick - 1) * 512, depth_brick * 512)
        coarse_ref[rows] = value.reshape(512, width).astype(jnp.bfloat16)


def middle_call(source, block, before, after, early, wide1, wide2):
    mid = block.shape[1]
    smem = pl.BlockSpec(memory_space=pltpu.SMEM)
    vmem = pl.BlockSpec(memory_space=pltpu.VMEM)
    inner = SIDE - 2
    hidden = (inner, HID * COLS, mid)
    return pl.pallas_call(
        middle_kernel,
        in_specs=[smem] + [vmem] * 6,
        out_specs=[vmem] * 3,
        out_shape=[
            jax.ShapeDtypeStruct(shape, jnp.bfloat16) for shape in (hidden, hidden, (1024, mid))
        ],
        scratch_shapes=[
            pltpu.VMEM((2, inner, 16, mid), jnp.bfloat16),
            pltpu.VMEM((LATE_PLANES, inner * COLS, mid), jnp.bfloat16),
            pltpu.VMEM((LATE_PLANES + 2, SIDE * COLS, mid), jnp.bfloat16),
            pltpu.VMEM((LATE_PLANES + 2, SIDE * COLS, mid), jnp.bfloat16),
        ],
        compiler_params=pltpu.CompilerParams(vmem_limit_bytes=VMEM_LIMIT),
        cost_estimate=conv_cost(inner * (4 + LATE_PLANES) * COLS + 1024, mid),
        name="middle",
    )(source, block, before, after, early, wide1, wide2)


def scatter_bricks(source_ref, stage, value, depth_brick):
    width = value.shape[3]
    half = low_half((4, 2, COLS, width))
    for r in range(4):
        part = value[:, r * 4 : (r + 1) * 4].reshape(4, 2, 2, COLS, width)
        even, odd = part[:, :, 0], part[:, :, 1]
        b0 = jnp.where(half, even, pltpu.roll(odd, 4, 2))
        b1 = jnp.where(half, pltpu.roll(even, 4, 2), odd)
        slot = slot_index(depth_brick, r)
        for k, brick in enumerate((b0, b1)):
            source = source_ref[slot + k]
            row = pl.multiple_of(jnp.where(source >= 0, source, K * CAP) * CELLS, CELLS)
            stage[pl.ds(row, CELLS), :] = brick.reshape(CELLS, width).astype(jnp.bfloat16)


def final_kernel(count, base_ref, source_ref, *refs):
    block_ref, before_ref, after_ref, even_ref, odd_ref = refs[:5]
    mid_here, mid_next, mid_ref, wide1_ref, wide2_ref, coarse_ref = refs[5:11]
    backs = refs[11 : 11 + K]
    x_here, x_next, h_here, h_next, stage, under_ref, over_ref = refs[11 + K :]
    width = block_ref.shape[1]
    stage[...] = jnp.zeros(stage.shape, jnp.bfloat16)
    face_in(base_ref[1], count, even_ref, odd_ref, under_ref, over_ref)
    flags_before = as_rows(before_ref[256:288])
    flags_after = as_rows(after_ref[256:288])
    spread = []
    for end, ref in ((0, under_ref), (1, over_ref)):
        own = []
        for d in (0, 1) if end == 0 else (SIDE - 2, SIDE - 1):
            edge = slice(d * 16, (d + 1) * 16)
            own.append(
                jnp.concatenate(
                    [before_ref[edge], block_ref[d * 128 : (d + 1) * 128], after_ref[edge]], axis=0
                )
            )
        far = [ref[k * 160 : (k + 1) * 160] for k in range(2)]
        for index, plane in enumerate(far + own if end == 0 else own + far):
            x_here[end * 4 + index] = plane
            x_next[end * 4 + index] = as_tiles(moved_rows(as_rows(plane)))
        far_flags = as_rows(ref[320:368])
        brick = 0 if end == 0 else 3
        own_flags = [flags_before[brick]]
        own_flags += [slot_flags(source_ref, slot_index(brick, r)) for r in range(4)]
        own_flags += [flags_after[brick]]
        pair = [
            spread_flags([far_flags[r] for r in range(6)], (1, 4, 4, 4, 4, 1)),
            spread_flags(own_flags, (1, 4, 4, 4, 4, 1)),
        ]
        spread += pair if end == 0 else pair[::-1]
    lhs = [plane_taps(x_here, x_next, first, 2, HID * COLS) for first in (0, 4)]
    value = multiply_taps(jnp.concatenate(lhs, axis=0), wide1_ref)
    value = activate(value.reshape(4, HID, COLS, width), jnp.stack(spread, axis=0))
    for k, index in enumerate((0, 1, 10, 11)):
        h_here[index] = as_tiles(value[k])
        h_next[index] = as_tiles(moved_rows(value[k]))
    for k in range(4):
        for index, source in ((2 + k, k), (6 + k, SIDE - 6 + k)):
            h_here[index] = mid_here[source]
            h_next[index] = mid_next[source]
    for depth_brick in (1, 2):
        rows = slice((depth_brick - 1) * 512, depth_brick * 512)
        done = mid_ref[rows]
        coarse_ref[depth_brick * 512 : (depth_brick + 1) * 512] = done
        done = done.astype(jnp.float32).reshape(4, SIDE, COLS, width)
        scatter_bricks(source_ref, stage, done, depth_brick)
    for depth_brick in (0, 3):
        value = conv_planes(h_here, h_next, wide2_ref, depth_brick * 2, 4, SIDE * COLS)
        value = coarse_rows(source_ref, block_ref, value, depth_brick)
        rows = slice(depth_brick * 512, (depth_brick + 1) * 512)
        coarse_ref[rows] = value.reshape(512, width).astype(jnp.bfloat16)
        scatter_bricks(source_ref, stage, value, depth_brick)
    for j in range(K):
        backs[j][...] = stage[j * CAP * CELLS : (j + 1) * CAP * CELLS]


def final_call(count, base, source, block, halo, middle, wide1, wide2):
    mid = block.shape[1]
    smem = pl.BlockSpec(memory_space=pltpu.SMEM)
    vmem = pl.BlockSpec(memory_space=pltpu.VMEM)
    return pl.pallas_call(
        functools.partial(final_kernel, count),
        in_specs=[smem, smem] + [vmem] * 10,
        out_specs=[vmem] * (1 + K),
        out_shape=[jax.ShapeDtypeStruct(block.shape, jnp.bfloat16)]
        + [jax.ShapeDtypeStruct((CAP * CELLS, mid), jnp.bfloat16)] * K,
        scratch_shapes=[
            pltpu.VMEM((8, WIDE * COLS, mid), jnp.bfloat16),
            pltpu.VMEM((8, WIDE * COLS, mid), jnp.bfloat16),
            pltpu.VMEM((12, HID * COLS, mid), jnp.bfloat16),
            pltpu.VMEM((12, HID * COLS, mid), jnp.bfloat16),
            pltpu.VMEM(((K * CAP + 1) * CELLS, mid), jnp.bfloat16),
            pltpu.VMEM((368, mid), jnp.bfloat16),
            pltpu.VMEM((368, mid), jnp.bfloat16),
        ],
        compiler_params=pltpu.CompilerParams(vmem_limit_bytes=VMEM_LIMIT),
        cost_estimate=conv_cost(1600, mid),
        name="final",
    )(base, source, block, *halo, *middle, wide1, wide2)


def from_behind(value, axis, steps):
    count = lax.axis_size(axis)
    pairs = [(source, (source + steps) % count) for source in range(count)]
    return lax.ppermute(value, axis, pairs)


def swap_face(face, axis, first):
    count = lax.axis_size(axis)
    partner = list(range(count))
    for i in range(first, count - 1, 2):
        partner[i], partner[i + 1] = i + 1, i
    return lax.ppermute(face, axis, list(enumerate(partner)))


def shards(fine, fine_mask, slot_source, w_down, w_first, w_second, w_up):
    mid = w_down.shape[1]
    base = jnp.stack([lax.axis_index("xy"), lax.axis_index("gz")]).astype(jnp.int32)
    counts = (lax.axis_size("gz"), lax.axis_size("xy"))
    sent = down_call(fine, fine_mask, w_down, SENT)
    arrived = {j: from_behind(sent[j], "xy", j) for j in SENT}
    later = (arrived[SENT[2]], fine, fine_mask, w_down, w_first, w_second)
    arrived[SENT[2]], *later = lax.optimization_barrier(later)
    prepared = lax.optimization_barrier(tuple(prepare_call(*later)))
    arrived[0], mask, wide1, wide2 = prepared
    block, even, odd = place_call(base, slot_source, [arrived[j] for j in range(K)])
    even = swap_face(even, "xy", 0)
    odd = swap_face(odd, "xy", 1)
    early = inner_call(slot_source, block, wide1, EARLY)
    even, odd, early = lax.optimization_barrier((even, odd, early))
    before, after, even, odd = edge_call(counts, base, slot_source, block, even, odd)
    even = swap_face(even, "gz", 0)
    odd = swap_face(odd, "gz", 1)
    middle = middle_call(slot_source, block, before, after, early, wide1, wide2)
    coarse, *back = final_call(
        counts[0], base, slot_source, block, (before, after, even, odd), middle, wide1, wide2
    )
    octant = {j: from_behind(back[j], "xy", -j) for j in RETURNED}
    octant[0] = back[0]
    fine_out = up_call(fine, mask, w_up, [octant[j] for j in (6, 7, 0, 1)], 3, None)
    fine_out = up_call(fine, mask, w_up, [octant[j] for j in (2, 3, 4, 5)], 1, fine_out)
    return fine_out, coarse.reshape(SIDE, SIDE, COLS, mid)


def solution(mesh):
    placed = (
        P(("gz", "xy"), None, None),
        P(("gz", "xy"), None),
        P(("gz", "xy")),
        P(),
        P(),
        P(),
        P(),
    )
    return jax.shard_map(
        shards,
        mesh=mesh,
        in_specs=placed,
        out_specs=(P(("gz", "xy"), None, None), P("gz", "xy", None, None)),
        check_vma=False,
    )
```

```python
import functools

import jax
import jax.numpy as jnp
from jax import lax
from jax.experimental import pallas as pl
from jax.experimental.pallas import tpu as pltpu
from jax.sharding import PartitionSpec as P

CAP = 4
K = 8
CELLS = 64
SIDE = 16
COLS = 8
WIDE = SIDE + 4
HID = SIDE + 2
EARLY = ((1, 3), (4, 4), (8, 4))
LATE = ((12, 3),)
LATE_PLANES = 3
SENT = (4, 3, 5, 2, 6, 1, 7)
RETURNED = (1, 7, 6, 4, 2, 3, 5)
DOWN_LIMIT = 62 * 1024 * 1024
VMEM_LIMIT = 24 * 1024 * 1024


def expand_mask(mask):
    bricks = mask.shape[0]
    values = mask.astype(jnp.float32)
    cell = lax.broadcasted_iota(jnp.int32, (16, 128), 0)
    lane = lax.broadcasted_iota(jnp.int32, (16, 128), 1)
    chosen = (cell == lane // 8).astype(jnp.float32)
    parts = [
        values[:, t * 128 : (t + 1) * 128].reshape(bricks, 1, 128) * chosen[None] for t in range(4)
    ]
    spread = jnp.concatenate(parts, axis=1).reshape(bricks * CELLS, 128).astype(jnp.bfloat16)
    source = lax.broadcasted_iota(jnp.int32, (128, 512), 0)
    target = lax.broadcasted_iota(jnp.int32, (128, 512), 1)
    widen = ((source & 7) == (target >> 6)).astype(jnp.bfloat16)
    return jnp.dot(spread, widen, preferred_element_type=jnp.float32)


def down_kernel(offsets, fine_hbm, mask_hbm, w_hbm, *refs):
    count = len(offsets)
    outs = refs[:count]
    fine_ref, mask_ref, w_ref, wide_ref, result_ref, sems, out_sems = refs[count:]
    first = [
        pltpu.make_async_copy(mask_hbm, mask_ref, sems.at[count]),
        pltpu.make_async_copy(w_hbm, w_ref, sems.at[count + 1]),
    ]
    chunks = [
        pltpu.make_async_copy(fine_hbm.at[pl.ds(j * CAP, CAP)], fine_ref.at[k], sems.at[k])
        for k, j in enumerate(offsets)
    ]
    for copy in first + chunks:
        copy.start()
    first[0].wait()
    rows = CAP * CELLS
    for k, j in enumerate(offsets):
        wide_ref[k * rows : (k + 1) * rows] = expand_mask(
            mask_ref[j * CAP : (j + 1) * CAP]
        ).astype(jnp.bfloat16)
    first[1].wait()
    for start in range(0, count, 2):
        group = range(start, min(start + 2, count))
        for k in group:
            chunks[k].wait()
        x = [
            fine_ref[k].reshape(rows, -1) * wide_ref[k * rows : (k + 1) * rows] for k in group
        ]
        y = jnp.dot(jnp.concatenate(x, axis=0), w_ref[...], preferred_element_type=jnp.float32)
        y = y.astype(jnp.bfloat16)
        for part, k in enumerate(group):
            result_ref[k] = y[part * rows : (part + 1) * rows]
            pltpu.make_async_copy(result_ref.at[k], outs[k], out_sems.at[k]).start()
    for k in range(count):
        pltpu.make_async_copy(result_ref.at[k], outs[k], out_sems.at[k]).wait()


def down_call(fine, mask, w, offsets):
    cells, width = fine.shape[1:]
    mid = w.shape[1]
    count = len(offsets)
    rows = count * CAP * cells
    hbm = pl.BlockSpec(memory_space=pltpu.HBM)
    outs = pl.pallas_call(
        functools.partial(down_kernel, offsets),
        in_specs=[hbm, hbm, hbm],
        out_specs=[pl.BlockSpec(memory_space=pl.ANY)] * count,
        out_shape=[jax.ShapeDtypeStruct((CAP * cells, mid), jnp.bfloat16)] * count,
        scratch_shapes=[
            pltpu.VMEM((count, CAP, cells, width), fine.dtype),
            pltpu.VMEM(mask.shape, mask.dtype),
            pltpu.VMEM(w.shape, w.dtype),
            pltpu.VMEM((rows, width), jnp.bfloat16),
            pltpu.VMEM((count, CAP * cells, mid), jnp.bfloat16),
            pltpu.SemaphoreType.DMA((count + 2,)),
            pltpu.SemaphoreType.DMA((count,)),
        ],
        compiler_params=pltpu.CompilerParams(vmem_limit_bytes=DOWN_LIMIT),
        cost_estimate=pl.CostEstimate(
            flops=2 * rows * width * mid, bytes_accessed=rows * width * 2, transcendentals=0
        ),
        name="down",
    )(fine, mask, w)
    return dict(zip(offsets, outs))


def prepare_kernel(
    fine_ref, mask_ref, w_down_ref, w1_ref, w2_ref, own_ref, mask_out, wide1_ref, wide2_ref
):
    gather_weights(w1_ref, wide1_ref)
    gather_weights(w2_ref, wide2_ref)
    step = 8
    for part in range(mask_ref.shape[0] // step):
        rows = slice(part * step * CELLS, (part + 1) * step * CELLS)
        mask_out[rows] = expand_mask(mask_ref[part * step : (part + 1) * step]).astype(jnp.bfloat16)
    rows = CAP * CELLS
    own = fine_ref[...].reshape(rows, -1) * mask_out[:rows]
    own = jnp.dot(own, w_down_ref[...], preferred_element_type=jnp.float32)
    own_ref[...] = own.astype(jnp.bfloat16)


def prepare_call(fine, mask, w_down, w_first, w_second):
    mid = w_first.shape[1]
    vmem = pl.BlockSpec(memory_space=pltpu.VMEM)
    rows = mask.shape[0] * CELLS
    wide = jax.ShapeDtypeStruct((9 * mid, 3 * mid), jnp.bfloat16)
    return pl.pallas_call(
        prepare_kernel,
        grid=(1,),
        in_specs=[pl.BlockSpec((CAP,) + fine.shape[1:], lambda i: (0, 0, 0))] + [vmem] * 4,
        out_specs=[vmem] * 4,
        out_shape=[
            jax.ShapeDtypeStruct((CAP * CELLS, mid), jnp.bfloat16),
            jax.ShapeDtypeStruct((rows, mask.shape[1]), jnp.bfloat16),
            wide,
            wide,
        ],
        compiler_params=pltpu.CompilerParams(vmem_limit_bytes=VMEM_LIMIT),
        cost_estimate=pl.CostEstimate(
            flops=2 * rows * mask.shape[1] * 128, bytes_accessed=rows * mask.shape[1] * 2, transcendentals=0
        ),
        name="prepare",
    )(fine, mask, w_down, w_first, w_second)


def up_kernel(offsets, fine_ref, mask_ref, w_ref, *refs):
    out_ref = refs[-1]
    step = pl.program_id(0)
    bricks, cells, width = fine_ref.shape
    count = bricks // CAP
    steps = offsets // count
    for part in range(count):
        octant = refs[part][...]
        for other in range(1, steps):
            octant = jnp.where(step == other, refs[other * count + part][...], octant)
        rows = slice(part * CAP * cells, (part + 1) * CAP * cells)
        up = jnp.dot(octant, w_ref[...], preferred_element_type=jnp.float32)
        fine = fine_ref[part * CAP : (part + 1) * CAP].reshape(CAP * cells, width)
        mask = mask_ref[rows].astype(jnp.float32)
        out = jnp.where(mask > 0.5, fine.astype(jnp.float32) + up, 0.0)
        out_ref[part * CAP : (part + 1) * CAP] = out.astype(jnp.bfloat16).reshape(CAP, cells, width)


def up_call(fine, mask, w, octants, first, partial):
    bricks, cells, width = fine.shape
    mid = w.shape[0]
    step = 8
    blocks = bricks // step

    def place(i):
        return (first + i) % blocks

    count = len(octants)
    partials = [] if partial is None else [partial]
    return pl.pallas_call(
        functools.partial(up_kernel, count),
        grid=(count * CAP // step,),
        in_specs=[
            pl.BlockSpec((step, cells, width), lambda i: (place(i), 0, 0)),
            pl.BlockSpec((step * cells, width), lambda i: (place(i), 0)),
            pl.BlockSpec((mid, width), lambda i: (0, 0)),
        ]
        + [pl.BlockSpec((CAP * cells, mid), lambda i: (0, 0))] * count
        + [pl.BlockSpec(memory_space=pl.ANY)] * len(partials),
        out_specs=pl.BlockSpec((step, cells, width), lambda i: (place(i), 0, 0)),
        out_shape=jax.ShapeDtypeStruct(fine.shape, jnp.bfloat16),
        input_output_aliases={3 + count: 0} if partials else {},
        compiler_params=pltpu.CompilerParams(vmem_limit_bytes=VMEM_LIMIT),
        cost_estimate=pl.CostEstimate(
            flops=bricks * cells * width * mid, bytes_accessed=bricks * cells * width * 2, transcendentals=0
        ),
        name="up",
    )(fine, mask, w, *octants, *partials)


def low_half(shape):
    return lax.broadcasted_iota(jnp.int32, shape, len(shape) - 2) < 4


def slot_flags(source_ref, first):
    pair = [jnp.where(source_ref[first + k] >= 0, 1.0, 0.0).astype(jnp.float32) for k in range(2)]
    return jnp.where(low_half((8, 128)), pair[0], pair[1])


def slot_index(depth_brick, row_brick):
    pd, qd = divmod(depth_brick, 2)
    pr, qr = divmod(row_brick, 2)
    return (pd * 2 + pr) * 8 + qd * 4 + qr * 2


def take_brick(source_ref, arrived, slot):
    value = source_ref[slot]
    first = pl.multiple_of(jnp.maximum(value, 0) * CELLS, CELLS)
    brick = arrived[pl.ds(first, CELLS), :].astype(jnp.float32)
    return jnp.where(value >= 0, brick, 0.0).reshape(8, 8, 128)


def place_kernel(base_ref, source_ref, *refs):
    block_ref, even_ref, odd_ref, low_ref, high_ref, arrived = refs[K:]
    for j in range(K):
        arrived[j * CAP * CELLS : (j + 1) * CAP * CELLS] = refs[j][...]
    half = low_half((8, 8, 128))
    for depth_brick in range(4):
        for row_brick in range(4):
            slot = slot_index(depth_brick, row_brick)
            b0 = take_brick(source_ref, arrived, slot)
            b1 = take_brick(source_ref, arrived, slot + 1)
            even = jnp.where(half, b0, pltpu.roll(b1, 4, 1))
            odd = jnp.where(half, pltpu.roll(b0, 4, 1), b1)
            both = jnp.stack([even, odd], axis=1).reshape(4, 32, 128).astype(jnp.bfloat16)
            for vd in range(4):
                row = ((depth_brick * 4 + vd) * SIDE + row_brick * 4) * COLS
                block_ref[row : row + 32] = both[vd]
                place = (depth_brick * 4 + vd) * 16
                if row_brick == 0:
                    low_ref[place : place + 16] = both[vd, :16]
                if row_brick == 3:
                    high_ref[place : place + 16] = both[vd, 16:]
    for row_brick, ref in ((0, low_ref), (3, high_ref)):
        flags = [slot_flags(source_ref, slot_index(d, row_brick)) for d in range(4)]
        ref[256:288] = jnp.concatenate(flags, axis=0).astype(jnp.bfloat16)
    face_out(base_ref[0], low_ref, high_ref, even_ref, odd_ref)


def face_out(index, low_ref, high_ref, even_ref, odd_ref):
    is_even = index % 2 == 0
    even_ref[...] = jnp.where(is_even, high_ref[...], low_ref[...])
    odd_ref[...] = jnp.where(is_even, low_ref[...], high_ref[...])


def face_in(index, count, even_ref, odd_ref, low_ref, high_ref):
    is_even = index % 2 == 0
    empty = jnp.zeros(low_ref.shape, low_ref.dtype)
    low = jnp.where(is_even, odd_ref[...], even_ref[...])
    high = jnp.where(is_even, even_ref[...], odd_ref[...])
    low_ref[...] = jnp.where(index == 0, empty, low)
    high_ref[...] = jnp.where(index == count - 1, empty, high)


def place_call(base, source, arrived):
    mid = arrived[0].shape[1]
    smem = pl.BlockSpec(memory_space=pltpu.SMEM)
    vmem = pl.BlockSpec(memory_space=pltpu.VMEM)
    return pl.pallas_call(
        place_kernel,
        in_specs=[smem, smem] + [vmem] * K,
        out_specs=[vmem] * 3,
        out_shape=[
            jax.ShapeDtypeStruct((rows, mid), jnp.bfloat16)
            for rows in (SIDE * SIDE * COLS, 288, 288)
        ],
        scratch_shapes=[
            pltpu.VMEM((288, mid), jnp.bfloat16),
            pltpu.VMEM((288, mid), jnp.bfloat16),
            pltpu.VMEM((K * CAP * CELLS, mid), jnp.bfloat16),
        ],
        compiler_params=pltpu.CompilerParams(vmem_limit_bytes=VMEM_LIMIT),
        name="place",
    )(base, source, *arrived)


def edge_kernel(
    counts,
    base_ref,
    source_ref,
    block_ref,
    even_ref,
    odd_ref,
    before_ref,
    after_ref,
    even_out,
    odd_out,
    low_ref,
    high_ref,
):
    face_in(base_ref[0], counts[1], even_ref, odd_ref, before_ref, after_ref)
    for ref, planes, brick in ((low_ref, (0, 1), 0), (high_ref, (SIDE - 2, SIDE - 1), 3)):
        for k, plane in enumerate(planes):
            start = k * WIDE * COLS
            ref[start : start + 16] = before_ref[plane * 16 : plane * 16 + 16]
            ref[start + 16 : start + 144] = block_ref[plane * 128 : plane * 128 + 128]
            ref[start + 144 : start + 160] = after_ref[plane * 16 : plane * 16 + 16]
        flags = [before_ref[256:288].astype(jnp.float32)[brick * 8 : brick * 8 + 8]]
        flags += [slot_flags(source_ref, slot_index(brick, r)) for r in range(4)]
        flags += [after_ref[256:288].astype(jnp.float32)[brick * 8 : brick * 8 + 8]]
        ref[320:368] = jnp.concatenate(flags, axis=0).astype(jnp.bfloat16)
    face_out(base_ref[1], low_ref, high_ref, even_out, odd_out)


def edge_call(counts, base, source, block, even, odd):
    smem = pl.BlockSpec(memory_space=pltpu.SMEM)
    vmem = pl.BlockSpec(memory_space=pltpu.VMEM)
    mid = block.shape[1]
    return pl.pallas_call(
        functools.partial(edge_kernel, counts),
        in_specs=[smem, smem, vmem, vmem, vmem],
        out_specs=[vmem] * 4,
        out_shape=[
            jax.ShapeDtypeStruct((rows, mid), jnp.bfloat16) for rows in (288, 288, 368, 368)
        ],
        scratch_shapes=[pltpu.VMEM((368, mid), jnp.bfloat16)] * 2,
        compiler_params=pltpu.CompilerParams(vmem_limit_bytes=VMEM_LIMIT),
        name="edge",
    )(base, source, block, even, odd)


def gather_weights(w_ref, wide_ref):
    width = w_ref.shape[2]
    for tap in range(9):
        for column in range(3):
            wide_ref[tap * width : (tap + 1) * width, column * width : (column + 1) * width] = (
                w_ref[tap * 3 + column]
            )


def as_rows(value):
    value = value.astype(jnp.float32)
    return value.reshape(value.shape[0] // COLS, COLS, value.shape[1])


def moved_rows(rows):
    empty = jnp.zeros((1,) + rows.shape[1:], jnp.float32)
    return jnp.concatenate([rows[1:], empty], axis=0)


def as_tiles(rows):
    return rows.reshape(rows.shape[0] * COLS, rows.shape[2]).astype(jnp.bfloat16)


def multiply_taps(lhs, wide_ref):
    width = wide_ref.shape[1] // 3
    wide = jnp.dot(lhs, wide_ref[...], preferred_element_type=jnp.float32)
    wide = wide.reshape(lhs.shape[0] // COLS, COLS, 3 * width)
    column = lax.broadcasted_iota(jnp.int32, (lhs.shape[0] // COLS, COLS, width), 1)
    left = jnp.where(column == 0, 0.0, pltpu.roll(wide[:, :, :width], 1, 1))
    right = jnp.where(column == COLS - 1, 0.0, pltpu.roll(wide[:, :, 2 * width :], COLS - 1, 1))
    return left + wide[:, :, width : 2 * width] + right


def plane_taps(here_ref, next_ref, first, planes, rows):
    taps = []
    for dd in range(3):
        span = slice(first + dd, first + dd + planes)
        taps += [
            here_ref[span, 0:rows, :],
            next_ref[span, 0:rows, :],
            here_ref[span, 16 : rows + 16, :],
        ]
    lhs = jnp.concatenate(taps, axis=2)
    return lhs.reshape(planes * rows, lhs.shape[2])


def conv_planes(here_ref, next_ref, wide_ref, first, planes, rows):
    return multiply_taps(plane_taps(here_ref, next_ref, first, planes, rows), wide_ref)


def activate(value, flags):
    return value / (1.0 + jnp.exp(-value)) * flags


def spread_flags(flags, repeats):
    return jnp.concatenate(
        [jnp.broadcast_to(flag[None], (count,) + flag.shape) for flag, count in zip(flags, repeats)],
        axis=0,
    )


def inner_planes(source_ref, block_ref, wide1_ref, hidden_ref, here, moved, groups):
    width = block_ref.shape[1]
    base = groups[0][0] - 1
    for d in range(base, groups[-1][0] + groups[-1][1] + 1):
        plane = block_ref[d * 128 : (d + 1) * 128]
        here[d - base] = plane
        moved[d - base] = as_tiles(moved_rows(as_rows(plane)))
    inner = SIDE - 2
    rows = inner * COLS
    for first, planes in groups:
        value = conv_planes(here, moved, wide1_ref, first - 1 - base, planes, rows)
        value = value.reshape(planes, inner, COLS, width)
        flags = [slot_flags(source_ref, slot_index(first // 4, r)) for r in range(4)]
        value = activate(value, spread_flags(flags, (3, 4, 4, 3))[None])
        hidden_ref[first - 1 - base : first - 1 - base + planes] = value.reshape(
            planes, rows, width
        ).astype(jnp.bfloat16)


def inner_kernel(groups, source_ref, block_ref, wide1_ref, hidden_ref, here, moved):
    inner_planes(source_ref, block_ref, wide1_ref, hidden_ref, here, moved, groups)


def conv_cost(rows, width):
    return pl.CostEstimate(
        flops=2 * rows * 27 * width * width, bytes_accessed=27 * width * width * 4, transcendentals=0
    )


def inner_call(source, block, wide1, groups):
    mid = block.shape[1]
    smem = pl.BlockSpec(memory_space=pltpu.SMEM)
    vmem = pl.BlockSpec(memory_space=pltpu.VMEM)
    rows = (SIDE - 2) * COLS
    planes = sum(count for _, count in groups)
    return pl.pallas_call(
        functools.partial(inner_kernel, groups),
        in_specs=[smem, vmem, vmem],
        out_specs=vmem,
        out_shape=jax.ShapeDtypeStruct((planes, rows, mid), jnp.bfloat16),
        scratch_shapes=[pltpu.VMEM((planes + 2, SIDE * COLS, mid), jnp.bfloat16)] * 2,
        compiler_params=pltpu.CompilerParams(vmem_limit_bytes=VMEM_LIMIT),
        cost_estimate=conv_cost(planes * rows, mid),
        name="inner",
    )(source, block, wide1)


def side_taps(low, high):
    mixed = as_tiles(
        jnp.concatenate(
            [as_rows(low).reshape(-1, 2, COLS, 128)[:, 1:], as_rows(high).reshape(-1, 2, COLS, 128)[:, :1]],
            axis=1,
        ).reshape(-1, COLS, 128)
    )
    return low, mixed, high


def depth_taps(taps, planes):
    parts = [tap[dd * 16 : (dd + planes) * 16] for dd in range(3) for tap in taps]
    return jnp.concatenate(parts, axis=1)


def coarse_rows(source_ref, block_ref, value, depth_brick):
    width = block_ref.shape[1]
    value = value.reshape(4, SIDE, COLS, width)
    rows = slice(depth_brick * 512, (depth_brick + 1) * 512)
    own = block_ref[rows].astype(jnp.float32).reshape(4, SIDE, COLS, width)
    flags = [slot_flags(source_ref, slot_index(depth_brick, r)) for r in range(4)]
    return (value + own) * spread_flags(flags, (4, 4, 4, 4))[None]


def middle_kernel(source_ref, *refs):
    block_ref, before_ref, after_ref, early_ref, wide1_ref, wide2_ref = refs[:6]
    h_here, h_next, coarse_ref, side, late, here, moved = refs[6:]
    width = block_ref.shape[1]
    inner = SIDE - 2
    inner_planes(source_ref, block_ref, wide1_ref, late, here, moved, LATE)

    low = jnp.concatenate([block_ref[d * 128 : d * 128 + 16] for d in range(SIDE)], axis=0)
    high = jnp.concatenate([block_ref[d * 128 + 112 : d * 128 + 128] for d in range(SIDE)], axis=0)
    left = depth_taps(side_taps(before_ref[0:256], low), inner)
    right = depth_taps(side_taps(high, after_ref[0:256]), inner)
    value = multiply_taps(jnp.concatenate([left, right], axis=0), wide1_ref)
    depths = (3, 4, 4, 3)
    edge_flags = (as_rows(before_ref[256:288]), as_rows(after_ref[256:288]))
    flags = []
    for end, row_brick in ((0, 0), (1, 3)):
        own = [slot_flags(source_ref, slot_index(d, row_brick)) for d in range(4)]
        pairs = [jnp.stack([edge_flags[end][d], own[d]][:: 1 - 2 * end], axis=0) for d in range(4)]
        flags.append(spread_flags(pairs, depths))
    value = activate(value.reshape(2, inner, 2, COLS, width), jnp.stack(flags, axis=0))
    side[...] = value.reshape(2, inner, 16, width).astype(jnp.bfloat16)
    centres = [ref[k] for ref in (early_ref, late) for k in range(ref.shape[0])]
    for d in range(inner):
        plane = jnp.concatenate([side[0, d], centres[d], side[1, d]], axis=0)
        h_here[d] = plane
        h_next[d] = as_tiles(moved_rows(as_rows(plane)))

    for depth_brick in (1, 2):
        value = conv_planes(h_here, h_next, wide2_ref, depth_brick * 4 - 2, 4, SIDE * COLS)
        value = coarse_rows(source_ref, block_ref, value, depth_brick)
        rows = slice((depth_brick - 1) * 512, depth_brick * 512)
        coarse_ref[rows] = value.reshape(512, width).astype(jnp.bfloat16)


def middle_call(source, block, before, after, early, wide1, wide2):
    mid = block.shape[1]
    smem = pl.BlockSpec(memory_space=pltpu.SMEM)
    vmem = pl.BlockSpec(memory_space=pltpu.VMEM)
    inner = SIDE - 2
    hidden = (inner, HID * COLS, mid)
    return pl.pallas_call(
        middle_kernel,
        in_specs=[smem] + [vmem] * 6,
        out_specs=[vmem] * 3,
        out_shape=[
            jax.ShapeDtypeStruct(shape, jnp.bfloat16) for shape in (hidden, hidden, (1024, mid))
        ],
        scratch_shapes=[
            pltpu.VMEM((2, inner, 16, mid), jnp.bfloat16),
            pltpu.VMEM((LATE_PLANES, inner * COLS, mid), jnp.bfloat16),
            pltpu.VMEM((LATE_PLANES + 2, SIDE * COLS, mid), jnp.bfloat16),
            pltpu.VMEM((LATE_PLANES + 2, SIDE * COLS, mid), jnp.bfloat16),
        ],
        compiler_params=pltpu.CompilerParams(vmem_limit_bytes=VMEM_LIMIT),
        cost_estimate=conv_cost(inner * (4 + LATE_PLANES) * COLS + 1024, mid),
        name="middle",
    )(source, block, before, after, early, wide1, wide2)


def scatter_bricks(source_ref, stage, value, depth_brick):
    width = value.shape[3]
    half = low_half((4, 2, COLS, width))
    for r in range(4):
        part = value[:, r * 4 : (r + 1) * 4].reshape(4, 2, 2, COLS, width)
        even, odd = part[:, :, 0], part[:, :, 1]
        b0 = jnp.where(half, even, pltpu.roll(odd, 4, 2))
        b1 = jnp.where(half, pltpu.roll(even, 4, 2), odd)
        slot = slot_index(depth_brick, r)
        for k, brick in enumerate((b0, b1)):
            source = source_ref[slot + k]
            row = pl.multiple_of(jnp.where(source >= 0, source, K * CAP) * CELLS, CELLS)
            stage[pl.ds(row, CELLS), :] = brick.reshape(CELLS, width).astype(jnp.bfloat16)


def final_kernel(count, base_ref, source_ref, *refs):
    block_ref, before_ref, after_ref, even_ref, odd_ref = refs[:5]
    mid_here, mid_next, mid_ref, wide1_ref, wide2_ref, first_ref, last_ref = refs[5:12]
    backs = refs[12 : 12 + K]
    x_here, x_next, h_here, h_next, stage, under_ref, over_ref = refs[12 + K :]
    width = block_ref.shape[1]
    stage[...] = jnp.zeros(stage.shape, jnp.bfloat16)
    face_in(base_ref[1], count, even_ref, odd_ref, under_ref, over_ref)
    flags_before = as_rows(before_ref[256:288])
    flags_after = as_rows(after_ref[256:288])
    spread = []
    for end, ref in ((0, under_ref), (1, over_ref)):
        own = []
        for d in (0, 1) if end == 0 else (SIDE - 2, SIDE - 1):
            edge = slice(d * 16, (d + 1) * 16)
            own.append(
                jnp.concatenate(
                    [before_ref[edge], block_ref[d * 128 : (d + 1) * 128], after_ref[edge]], axis=0
                )
            )
        far = [ref[k * 160 : (k + 1) * 160] for k in range(2)]
        for index, plane in enumerate(far + own if end == 0 else own + far):
            x_here[end * 4 + index] = plane
            x_next[end * 4 + index] = as_tiles(moved_rows(as_rows(plane)))
        far_flags = as_rows(ref[320:368])
        brick = 0 if end == 0 else 3
        own_flags = [flags_before[brick]]
        own_flags += [slot_flags(source_ref, slot_index(brick, r)) for r in range(4)]
        own_flags += [flags_after[brick]]
        pair = [
            spread_flags([far_flags[r] for r in range(6)], (1, 4, 4, 4, 4, 1)),
            spread_flags(own_flags, (1, 4, 4, 4, 4, 1)),
        ]
        spread += pair if end == 0 else pair[::-1]
    lhs = [plane_taps(x_here, x_next, first, 2, HID * COLS) for first in (0, 4)]
    value = multiply_taps(jnp.concatenate(lhs, axis=0), wide1_ref)
    value = activate(value.reshape(4, HID, COLS, width), jnp.stack(spread, axis=0))
    for k, index in enumerate((0, 1, 10, 11)):
        h_here[index] = as_tiles(value[k])
        h_next[index] = as_tiles(moved_rows(value[k]))
    for k in range(4):
        for index, source in ((2 + k, k), (6 + k, SIDE - 6 + k)):
            h_here[index] = mid_here[source]
            h_next[index] = mid_next[source]
    for depth_brick in (1, 2):
        rows = slice((depth_brick - 1) * 512, depth_brick * 512)
        done = mid_ref[rows].astype(jnp.float32).reshape(4, SIDE, COLS, width)
        scatter_bricks(source_ref, stage, done, depth_brick)
    for depth_brick, ref in ((0, first_ref), (3, last_ref)):
        value = conv_planes(h_here, h_next, wide2_ref, depth_brick * 2, 4, SIDE * COLS)
        value = coarse_rows(source_ref, block_ref, value, depth_brick)
        ref[...] = value.reshape(512, width).astype(jnp.bfloat16)
        scatter_bricks(source_ref, stage, value, depth_brick)
    for j in range(K):
        backs[j][...] = stage[j * CAP * CELLS : (j + 1) * CAP * CELLS]


def final_call(count, base, source, block, halo, middle, wide1, wide2):
    mid = block.shape[1]
    smem = pl.BlockSpec(memory_space=pltpu.SMEM)
    vmem = pl.BlockSpec(memory_space=pltpu.VMEM)
    return pl.pallas_call(
        functools.partial(final_kernel, count),
        in_specs=[smem, smem] + [vmem] * 10,
        out_specs=[vmem] * (2 + K),
        out_shape=[jax.ShapeDtypeStruct((512, mid), jnp.bfloat16)] * 2
        + [jax.ShapeDtypeStruct((CAP * CELLS, mid), jnp.bfloat16)] * K,
        scratch_shapes=[
            pltpu.VMEM((8, WIDE * COLS, mid), jnp.bfloat16),
            pltpu.VMEM((8, WIDE * COLS, mid), jnp.bfloat16),
            pltpu.VMEM((12, HID * COLS, mid), jnp.bfloat16),
            pltpu.VMEM((12, HID * COLS, mid), jnp.bfloat16),
            pltpu.VMEM(((K * CAP + 1) * CELLS, mid), jnp.bfloat16),
            pltpu.VMEM((368, mid), jnp.bfloat16),
            pltpu.VMEM((368, mid), jnp.bfloat16),
        ],
        compiler_params=pltpu.CompilerParams(vmem_limit_bytes=VMEM_LIMIT),
        cost_estimate=conv_cost(1600, mid),
        name="final",
    )(base, source, block, *halo, *middle, wide1, wide2)


def from_behind(value, axis, steps):
    count = lax.axis_size(axis)
    pairs = [(source, (source + steps) % count) for source in range(count)]
    return lax.ppermute(value, axis, pairs)


def swap_face(face, axis, first):
    count = lax.axis_size(axis)
    partner = list(range(count))
    for i in range(first, count - 1, 2):
        partner[i], partner[i + 1] = i + 1, i
    return lax.ppermute(face, axis, list(enumerate(partner)))


def shards(fine, fine_mask, slot_source, w_down, w_first, w_second, w_up):
    mid = w_down.shape[1]
    base = jnp.stack([lax.axis_index("xy"), lax.axis_index("gz")]).astype(jnp.int32)
    counts = (lax.axis_size("gz"), lax.axis_size("xy"))
    sent = down_call(fine, fine_mask, w_down, SENT)
    arrived = {j: from_behind(sent[j], "xy", j) for j in SENT}
    later = (arrived[SENT[2]], fine, fine_mask, w_down, w_first, w_second)
    arrived[SENT[2]], *later = lax.optimization_barrier(later)
    prepared = lax.optimization_barrier(tuple(prepare_call(*later)))
    arrived[0], mask, wide1, wide2 = prepared
    block, even, odd = place_call(base, slot_source, [arrived[j] for j in range(K)])
    even = swap_face(even, "xy", 0)
    odd = swap_face(odd, "xy", 1)
    early = inner_call(slot_source, block, wide1, EARLY)
    even, odd, early = lax.optimization_barrier((even, odd, early))
    before, after, even, odd = edge_call(counts, base, slot_source, block, even, odd)
    even = swap_face(even, "gz", 0)
    odd = swap_face(odd, "gz", 1)
    middle = middle_call(slot_source, block, before, after, early, wide1, wide2)
    first, last, *back = final_call(
        counts[0], base, slot_source, block, (before, after, even, odd), middle, wide1, wide2
    )
    octant = {j: from_behind(back[j], "xy", -j) for j in RETURNED}
    octant[0] = back[0]
    octant[6], *pieces = lax.optimization_barrier((octant[6], first, middle[2], last))
    coarse = jnp.concatenate(pieces, axis=0)
    fine_out = None
    for group, block_index in (((6, 7, 0, 1), 3), ((2, 3), 1), ((4, 5), 2)):
        octants = [octant[j] for j in group]
        fine_out = up_call(fine, mask, w_up, octants, block_index, fine_out)
    return fine_out, coarse.reshape(SIDE, SIDE, COLS, mid)


def solution(mesh):
    placed = (
        P(("gz", "xy"), None, None),
        P(("gz", "xy"), None),
        P(("gz", "xy")),
        P(),
        P(),
        P(),
        P(),
    )
    return jax.shard_map(
        shards,
        mesh=mesh,
        in_specs=placed,
        out_specs=(P(("gz", "xy"), None, None), P("gz", "xy", None, None)),
        check_vma=False,
    )
```

```python
import functools

import jax
import jax.numpy as jnp
from jax import lax
from jax.experimental import pallas as pl
from jax.experimental.pallas import tpu as pltpu
from jax.sharding import PartitionSpec as P

CAP = 4
K = 8
CELLS = 64
SIDE = 16
COLS = 8
WIDE = SIDE + 4
HID = SIDE + 2
EARLY = ((1, 3), (4, 4), (8, 4))
LATE = ((12, 3),)
LATE_PLANES = 3
SENT = (4, 3, 5, 2, 6, 1, 7)
RETURNED = (6, 7, 4, 5, 2, 3, 1)
DOWN_LIMIT = 62 * 1024 * 1024
VMEM_LIMIT = 24 * 1024 * 1024


def expand_mask(mask):
    bricks = mask.shape[0]
    values = mask.astype(jnp.float32)
    cell = lax.broadcasted_iota(jnp.int32, (16, 128), 0)
    lane = lax.broadcasted_iota(jnp.int32, (16, 128), 1)
    chosen = (cell == lane // 8).astype(jnp.float32)
    parts = [
        values[:, t * 128 : (t + 1) * 128].reshape(bricks, 1, 128) * chosen[None] for t in range(4)
    ]
    spread = jnp.concatenate(parts, axis=1).reshape(bricks * CELLS, 128).astype(jnp.bfloat16)
    source = lax.broadcasted_iota(jnp.int32, (128, 512), 0)
    target = lax.broadcasted_iota(jnp.int32, (128, 512), 1)
    widen = ((source & 7) == (target >> 6)).astype(jnp.bfloat16)
    return jnp.dot(spread, widen, preferred_element_type=jnp.float32)


def down_kernel(offsets, fine_hbm, mask_hbm, w_hbm, *refs):
    count = len(offsets)
    outs = refs[:count]
    fine_ref, mask_ref, w_ref, wide_ref, result_ref, sems, out_sems = refs[count:]
    first = [
        pltpu.make_async_copy(mask_hbm, mask_ref, sems.at[count]),
        pltpu.make_async_copy(w_hbm, w_ref, sems.at[count + 1]),
    ]
    chunks = [
        pltpu.make_async_copy(fine_hbm.at[pl.ds(j * CAP, CAP)], fine_ref.at[k], sems.at[k])
        for k, j in enumerate(offsets)
    ]
    for copy in first + chunks:
        copy.start()
    first[0].wait()
    rows = CAP * CELLS
    for k, j in enumerate(offsets):
        wide_ref[k * rows : (k + 1) * rows] = expand_mask(
            mask_ref[j * CAP : (j + 1) * CAP]
        ).astype(jnp.bfloat16)
    first[1].wait()
    for start in range(0, count, 2):
        group = range(start, min(start + 2, count))
        for k in group:
            chunks[k].wait()
        x = [
            fine_ref[k].reshape(rows, -1) * wide_ref[k * rows : (k + 1) * rows] for k in group
        ]
        y = jnp.dot(jnp.concatenate(x, axis=0), w_ref[...], preferred_element_type=jnp.float32)
        y = y.astype(jnp.bfloat16)
        for part, k in enumerate(group):
            result_ref[k] = y[part * rows : (part + 1) * rows]
            pltpu.make_async_copy(result_ref.at[k], outs[k], out_sems.at[k]).start()
    for k in range(count):
        pltpu.make_async_copy(result_ref.at[k], outs[k], out_sems.at[k]).wait()


def down_call(fine, mask, w, offsets):
    cells, width = fine.shape[1:]
    mid = w.shape[1]
    count = len(offsets)
    rows = count * CAP * cells
    hbm = pl.BlockSpec(memory_space=pltpu.HBM)
    outs = pl.pallas_call(
        functools.partial(down_kernel, offsets),
        in_specs=[hbm, hbm, hbm],
        out_specs=[pl.BlockSpec(memory_space=pl.ANY)] * count,
        out_shape=[jax.ShapeDtypeStruct((CAP * cells, mid), jnp.bfloat16)] * count,
        scratch_shapes=[
            pltpu.VMEM((count, CAP, cells, width), fine.dtype),
            pltpu.VMEM(mask.shape, mask.dtype),
            pltpu.VMEM(w.shape, w.dtype),
            pltpu.VMEM((rows, width), jnp.bfloat16),
            pltpu.VMEM((count, CAP * cells, mid), jnp.bfloat16),
            pltpu.SemaphoreType.DMA((count + 2,)),
            pltpu.SemaphoreType.DMA((count,)),
        ],
        compiler_params=pltpu.CompilerParams(vmem_limit_bytes=DOWN_LIMIT),
        cost_estimate=pl.CostEstimate(
            flops=2 * rows * width * mid, bytes_accessed=rows * width * 2, transcendentals=0
        ),
        name="down",
    )(fine, mask, w)
    return dict(zip(offsets, outs))


def prepare_kernel(
    fine_ref, mask_ref, w_down_ref, w1_ref, w2_ref, own_ref, mask_out, wide1_ref, wide2_ref
):
    gather_weights(w1_ref, wide1_ref)
    gather_weights(w2_ref, wide2_ref)
    step = 8
    for part in range(mask_ref.shape[0] // step):
        rows = slice(part * step * CELLS, (part + 1) * step * CELLS)
        mask_out[rows] = expand_mask(mask_ref[part * step : (part + 1) * step]).astype(jnp.bfloat16)
    rows = CAP * CELLS
    own = fine_ref[...].reshape(rows, -1) * mask_out[:rows]
    own = jnp.dot(own, w_down_ref[...], preferred_element_type=jnp.float32)
    own_ref[...] = own.astype(jnp.bfloat16)


def prepare_call(fine, mask, w_down, w_first, w_second):
    mid = w_first.shape[1]
    vmem = pl.BlockSpec(memory_space=pltpu.VMEM)
    rows = mask.shape[0] * CELLS
    wide = jax.ShapeDtypeStruct((9 * mid, 3 * mid), jnp.bfloat16)
    return pl.pallas_call(
        prepare_kernel,
        grid=(1,),
        in_specs=[pl.BlockSpec((CAP,) + fine.shape[1:], lambda i: (0, 0, 0))] + [vmem] * 4,
        out_specs=[vmem] * 4,
        out_shape=[
            jax.ShapeDtypeStruct((CAP * CELLS, mid), jnp.bfloat16),
            jax.ShapeDtypeStruct((rows, mask.shape[1]), jnp.bfloat16),
            wide,
            wide,
        ],
        compiler_params=pltpu.CompilerParams(vmem_limit_bytes=VMEM_LIMIT),
        cost_estimate=pl.CostEstimate(
            flops=2 * rows * mask.shape[1] * 128, bytes_accessed=rows * mask.shape[1] * 2, transcendentals=0
        ),
        name="prepare",
    )(fine, mask, w_down, w_first, w_second)


def up_kernel(offsets, fine_ref, mask_ref, w_ref, *refs):
    out_ref = refs[-1]
    step = pl.program_id(0)
    bricks, cells, width = fine_ref.shape
    count = bricks // CAP
    steps = offsets // count
    for part in range(count):
        octant = refs[part][...]
        for other in range(1, steps):
            octant = jnp.where(step == other, refs[other * count + part][...], octant)
        rows = slice(part * CAP * cells, (part + 1) * CAP * cells)
        up = jnp.dot(octant, w_ref[...], preferred_element_type=jnp.float32)
        fine = fine_ref[part * CAP : (part + 1) * CAP].reshape(CAP * cells, width)
        mask = mask_ref[rows].astype(jnp.float32)
        out = jnp.where(mask > 0.5, fine.astype(jnp.float32) + up, 0.0)
        out_ref[part * CAP : (part + 1) * CAP] = out.astype(jnp.bfloat16).reshape(CAP, cells, width)


def up_call(fine, mask, w, octants, first, partial):
    bricks, cells, width = fine.shape
    mid = w.shape[0]
    step = 8
    blocks = bricks // step

    def place(i):
        return (first + i) % blocks

    count = len(octants)
    partials = [] if partial is None else [partial]
    return pl.pallas_call(
        functools.partial(up_kernel, count),
        grid=(count * CAP // step,),
        in_specs=[
            pl.BlockSpec((step, cells, width), lambda i: (place(i), 0, 0)),
            pl.BlockSpec((step * cells, width), lambda i: (place(i), 0)),
            pl.BlockSpec((mid, width), lambda i: (0, 0)),
        ]
        + [pl.BlockSpec((CAP * cells, mid), lambda i: (0, 0))] * count
        + [pl.BlockSpec(memory_space=pl.ANY)] * len(partials),
        out_specs=pl.BlockSpec((step, cells, width), lambda i: (place(i), 0, 0)),
        out_shape=jax.ShapeDtypeStruct(fine.shape, jnp.bfloat16),
        input_output_aliases={3 + count: 0} if partials else {},
        compiler_params=pltpu.CompilerParams(vmem_limit_bytes=VMEM_LIMIT),
        cost_estimate=pl.CostEstimate(
            flops=bricks * cells * width * mid, bytes_accessed=bricks * cells * width * 2, transcendentals=0
        ),
        name="up",
    )(fine, mask, w, *octants, *partials)


def low_half(shape):
    return lax.broadcasted_iota(jnp.int32, shape, len(shape) - 2) < 4


def slot_flags(source_ref, first):
    pair = [jnp.where(source_ref[first + k] >= 0, 1.0, 0.0).astype(jnp.float32) for k in range(2)]
    return jnp.where(low_half((8, 128)), pair[0], pair[1])


def slot_index(depth_brick, row_brick):
    pd, qd = divmod(depth_brick, 2)
    pr, qr = divmod(row_brick, 2)
    return (pd * 2 + pr) * 8 + qd * 4 + qr * 2


def take_brick(source_ref, arrived, slot):
    value = source_ref[slot]
    first = pl.multiple_of(jnp.maximum(value, 0) * CELLS, CELLS)
    brick = arrived[pl.ds(first, CELLS), :].astype(jnp.float32)
    return jnp.where(value >= 0, brick, 0.0).reshape(8, 8, 128)


def place_kernel(base_ref, source_ref, *refs):
    block_ref, even_ref, odd_ref, low_ref, high_ref, arrived = refs[K:]
    for j in range(K):
        arrived[j * CAP * CELLS : (j + 1) * CAP * CELLS] = refs[j][...]
    half = low_half((8, 8, 128))
    for depth_brick in range(4):
        for row_brick in range(4):
            slot = slot_index(depth_brick, row_brick)
            b0 = take_brick(source_ref, arrived, slot)
            b1 = take_brick(source_ref, arrived, slot + 1)
            even = jnp.where(half, b0, pltpu.roll(b1, 4, 1))
            odd = jnp.where(half, pltpu.roll(b0, 4, 1), b1)
            both = jnp.stack([even, odd], axis=1).reshape(4, 32, 128).astype(jnp.bfloat16)
            for vd in range(4):
                row = ((depth_brick * 4 + vd) * SIDE + row_brick * 4) * COLS
                block_ref[row : row + 32] = both[vd]
                place = (depth_brick * 4 + vd) * 16
                if row_brick == 0:
                    low_ref[place : place + 16] = both[vd, :16]
                if row_brick == 3:
                    high_ref[place : place + 16] = both[vd, 16:]
    for row_brick, ref in ((0, low_ref), (3, high_ref)):
        flags = [slot_flags(source_ref, slot_index(d, row_brick)) for d in range(4)]
        ref[256:288] = jnp.concatenate(flags, axis=0).astype(jnp.bfloat16)
    face_out(base_ref[0], low_ref, high_ref, even_ref, odd_ref)


def face_out(index, low_ref, high_ref, even_ref, odd_ref):
    is_even = index % 2 == 0
    even_ref[...] = jnp.where(is_even, high_ref[...], low_ref[...])
    odd_ref[...] = jnp.where(is_even, low_ref[...], high_ref[...])


def face_in(index, count, even_ref, odd_ref, low_ref, high_ref):
    is_even = index % 2 == 0
    empty = jnp.zeros(low_ref.shape, low_ref.dtype)
    low = jnp.where(is_even, odd_ref[...], even_ref[...])
    high = jnp.where(is_even, even_ref[...], odd_ref[...])
    low_ref[...] = jnp.where(index == 0, empty, low)
    high_ref[...] = jnp.where(index == count - 1, empty, high)


def place_call(base, source, arrived):
    mid = arrived[0].shape[1]
    smem = pl.BlockSpec(memory_space=pltpu.SMEM)
    vmem = pl.BlockSpec(memory_space=pltpu.VMEM)
    return pl.pallas_call(
        place_kernel,
        in_specs=[smem, smem] + [vmem] * K,
        out_specs=[vmem] * 3,
        out_shape=[
            jax.ShapeDtypeStruct((rows, mid), jnp.bfloat16)
            for rows in (SIDE * SIDE * COLS, 288, 288)
        ],
        scratch_shapes=[
            pltpu.VMEM((288, mid), jnp.bfloat16),
            pltpu.VMEM((288, mid), jnp.bfloat16),
            pltpu.VMEM((K * CAP * CELLS, mid), jnp.bfloat16),
        ],
        compiler_params=pltpu.CompilerParams(vmem_limit_bytes=VMEM_LIMIT),
        name="place",
    )(base, source, *arrived)


def edge_kernel(
    counts,
    base_ref,
    source_ref,
    block_ref,
    even_ref,
    odd_ref,
    before_ref,
    after_ref,
    even_out,
    odd_out,
    low_ref,
    high_ref,
):
    face_in(base_ref[0], counts[1], even_ref, odd_ref, before_ref, after_ref)
    for ref, planes, brick in ((low_ref, (0, 1), 0), (high_ref, (SIDE - 2, SIDE - 1), 3)):
        for k, plane in enumerate(planes):
            start = k * WIDE * COLS
            ref[start : start + 16] = before_ref[plane * 16 : plane * 16 + 16]
            ref[start + 16 : start + 144] = block_ref[plane * 128 : plane * 128 + 128]
            ref[start + 144 : start + 160] = after_ref[plane * 16 : plane * 16 + 16]
        flags = [before_ref[256:288].astype(jnp.float32)[brick * 8 : brick * 8 + 8]]
        flags += [slot_flags(source_ref, slot_index(brick, r)) for r in range(4)]
        flags += [after_ref[256:288].astype(jnp.float32)[brick * 8 : brick * 8 + 8]]
        ref[320:368] = jnp.concatenate(flags, axis=0).astype(jnp.bfloat16)
    face_out(base_ref[1], low_ref, high_ref, even_out, odd_out)


def edge_call(counts, base, source, block, even, odd):
    smem = pl.BlockSpec(memory_space=pltpu.SMEM)
    vmem = pl.BlockSpec(memory_space=pltpu.VMEM)
    mid = block.shape[1]
    return pl.pallas_call(
        functools.partial(edge_kernel, counts),
        in_specs=[smem, smem, vmem, vmem, vmem],
        out_specs=[vmem] * 4,
        out_shape=[
            jax.ShapeDtypeStruct((rows, mid), jnp.bfloat16) for rows in (288, 288, 368, 368)
        ],
        scratch_shapes=[pltpu.VMEM((368, mid), jnp.bfloat16)] * 2,
        compiler_params=pltpu.CompilerParams(vmem_limit_bytes=VMEM_LIMIT),
        name="edge",
    )(base, source, block, even, odd)


def gather_weights(w_ref, wide_ref):
    width = w_ref.shape[2]
    for tap in range(9):
        for column in range(3):
            wide_ref[tap * width : (tap + 1) * width, column * width : (column + 1) * width] = (
                w_ref[tap * 3 + column]
            )


def as_rows(value):
    value = value.astype(jnp.float32)
    return value.reshape(value.shape[0] // COLS, COLS, value.shape[1])


def moved_rows(rows):
    empty = jnp.zeros((1,) + rows.shape[1:], jnp.float32)
    return jnp.concatenate([rows[1:], empty], axis=0)


def as_tiles(rows):
    return rows.reshape(rows.shape[0] * COLS, rows.shape[2]).astype(jnp.bfloat16)


def multiply_taps(lhs, wide_ref):
    width = wide_ref.shape[1] // 3
    wide = jnp.dot(lhs, wide_ref[...], preferred_element_type=jnp.float32)
    wide = wide.reshape(lhs.shape[0] // COLS, COLS, 3 * width)
    column = lax.broadcasted_iota(jnp.int32, (lhs.shape[0] // COLS, COLS, width), 1)
    left = jnp.where(column == 0, 0.0, pltpu.roll(wide[:, :, :width], 1, 1))
    right = jnp.where(column == COLS - 1, 0.0, pltpu.roll(wide[:, :, 2 * width :], COLS - 1, 1))
    return left + wide[:, :, width : 2 * width] + right


def plane_taps(here_ref, next_ref, first, planes, rows):
    taps = []
    for dd in range(3):
        span = slice(first + dd, first + dd + planes)
        taps += [
            here_ref[span, 0:rows, :],
            next_ref[span, 0:rows, :],
            here_ref[span, 16 : rows + 16, :],
        ]
    lhs = jnp.concatenate(taps, axis=2)
    return lhs.reshape(planes * rows, lhs.shape[2])


def conv_planes(here_ref, next_ref, wide_ref, first, planes, rows):
    return multiply_taps(plane_taps(here_ref, next_ref, first, planes, rows), wide_ref)


def activate(value, flags):
    return value / (1.0 + jnp.exp(-value)) * flags


def spread_flags(flags, repeats):
    return jnp.concatenate(
        [jnp.broadcast_to(flag[None], (count,) + flag.shape) for flag, count in zip(flags, repeats)],
        axis=0,
    )


def inner_planes(source_ref, block_ref, wide1_ref, hidden_ref, here, moved, groups):
    width = block_ref.shape[1]
    base = groups[0][0] - 1
    for d in range(base, groups[-1][0] + groups[-1][1] + 1):
        plane = block_ref[d * 128 : (d + 1) * 128]
        here[d - base] = plane
        moved[d - base] = as_tiles(moved_rows(as_rows(plane)))
    inner = SIDE - 2
    rows = inner * COLS
    for first, planes in groups:
        value = conv_planes(here, moved, wide1_ref, first - 1 - base, planes, rows)
        value = value.reshape(planes, inner, COLS, width)
        flags = [slot_flags(source_ref, slot_index(first // 4, r)) for r in range(4)]
        value = activate(value, spread_flags(flags, (3, 4, 4, 3))[None])
        hidden_ref[first - 1 - base : first - 1 - base + planes] = value.reshape(
            planes, rows, width
        ).astype(jnp.bfloat16)


def inner_kernel(groups, source_ref, block_ref, wide1_ref, hidden_ref, here, moved):
    inner_planes(source_ref, block_ref, wide1_ref, hidden_ref, here, moved, groups)


def conv_cost(rows, width):
    return pl.CostEstimate(
        flops=2 * rows * 27 * width * width, bytes_accessed=27 * width * width * 4, transcendentals=0
    )


def inner_call(source, block, wide1, groups):
    mid = block.shape[1]
    smem = pl.BlockSpec(memory_space=pltpu.SMEM)
    vmem = pl.BlockSpec(memory_space=pltpu.VMEM)
    rows = (SIDE - 2) * COLS
    planes = sum(count for _, count in groups)
    return pl.pallas_call(
        functools.partial(inner_kernel, groups),
        in_specs=[smem, vmem, vmem],
        out_specs=vmem,
        out_shape=jax.ShapeDtypeStruct((planes, rows, mid), jnp.bfloat16),
        scratch_shapes=[pltpu.VMEM((planes + 2, SIDE * COLS, mid), jnp.bfloat16)] * 2,
        compiler_params=pltpu.CompilerParams(vmem_limit_bytes=VMEM_LIMIT),
        cost_estimate=conv_cost(planes * rows, mid),
        name="inner",
    )(source, block, wide1)


def side_taps(low, high):
    mixed = as_tiles(
        jnp.concatenate(
            [as_rows(low).reshape(-1, 2, COLS, 128)[:, 1:], as_rows(high).reshape(-1, 2, COLS, 128)[:, :1]],
            axis=1,
        ).reshape(-1, COLS, 128)
    )
    return low, mixed, high


def depth_taps(taps, planes):
    parts = [tap[dd * 16 : (dd + planes) * 16] for dd in range(3) for tap in taps]
    return jnp.concatenate(parts, axis=1)


def coarse_rows(source_ref, block_ref, value, depth_brick):
    width = block_ref.shape[1]
    value = value.reshape(4, SIDE, COLS, width)
    rows = slice(depth_brick * 512, (depth_brick + 1) * 512)
    own = block_ref[rows].astype(jnp.float32).reshape(4, SIDE, COLS, width)
    flags = [slot_flags(source_ref, slot_index(depth_brick, r)) for r in range(4)]
    return (value + own) * spread_flags(flags, (4, 4, 4, 4))[None]


def middle_kernel(source_ref, *refs):
    block_ref, before_ref, after_ref, early_ref, wide1_ref, wide2_ref = refs[:6]
    h_here, h_next, coarse_ref, side, late, here, moved = refs[6:]
    width = block_ref.shape[1]
    inner = SIDE - 2
    inner_planes(source_ref, block_ref, wide1_ref, late, here, moved, LATE)

    low = jnp.concatenate([block_ref[d * 128 : d * 128 + 16] for d in range(SIDE)], axis=0)
    high = jnp.concatenate([block_ref[d * 128 + 112 : d * 128 + 128] for d in range(SIDE)], axis=0)
    left = depth_taps(side_taps(before_ref[0:256], low), inner)
    right = depth_taps(side_taps(high, after_ref[0:256]), inner)
    value = multiply_taps(jnp.concatenate([left, right], axis=0), wide1_ref)
    depths = (3, 4, 4, 3)
    edge_flags = (as_rows(before_ref[256:288]), as_rows(after_ref[256:288]))
    flags = []
    for end, row_brick in ((0, 0), (1, 3)):
        own = [slot_flags(source_ref, slot_index(d, row_brick)) for d in range(4)]
        pairs = [jnp.stack([edge_flags[end][d], own[d]][:: 1 - 2 * end], axis=0) for d in range(4)]
        flags.append(spread_flags(pairs, depths))
    value = activate(value.reshape(2, inner, 2, COLS, width), jnp.stack(flags, axis=0))
    side[...] = value.reshape(2, inner, 16, width).astype(jnp.bfloat16)
    centres = [ref[k] for ref in (early_ref, late) for k in range(ref.shape[0])]
    for d in range(inner):
        plane = jnp.concatenate([side[0, d], centres[d], side[1, d]], axis=0)
        h_here[d] = plane
        h_next[d] = as_tiles(moved_rows(as_rows(plane)))

    for depth_brick in (1, 2):
        value = conv_planes(h_here, h_next, wide2_ref, depth_brick * 4 - 2, 4, SIDE * COLS)
        value = coarse_rows(source_ref, block_ref, value, depth_brick)
        rows = slice((depth_brick - 1) * 512, depth_brick * 512)
        coarse_ref[rows] = value.reshape(512, width).astype(jnp.bfloat16)


def middle_call(source, block, before, after, early, wide1, wide2):
    mid = block.shape[1]
    smem = pl.BlockSpec(memory_space=pltpu.SMEM)
    vmem = pl.BlockSpec(memory_space=pltpu.VMEM)
    inner = SIDE - 2
    hidden = (inner, HID * COLS, mid)
    return pl.pallas_call(
        middle_kernel,
        in_specs=[smem] + [vmem] * 6,
        out_specs=[vmem] * 3,
        out_shape=[
            jax.ShapeDtypeStruct(shape, jnp.bfloat16) for shape in (hidden, hidden, (1024, mid))
        ],
        scratch_shapes=[
            pltpu.VMEM((2, inner, 16, mid), jnp.bfloat16),
            pltpu.VMEM((LATE_PLANES, inner * COLS, mid), jnp.bfloat16),
            pltpu.VMEM((LATE_PLANES + 2, SIDE * COLS, mid), jnp.bfloat16),
            pltpu.VMEM((LATE_PLANES + 2, SIDE * COLS, mid), jnp.bfloat16),
        ],
        compiler_params=pltpu.CompilerParams(vmem_limit_bytes=VMEM_LIMIT),
        cost_estimate=conv_cost(inner * (4 + LATE_PLANES) * COLS + 1024, mid),
        name="middle",
    )(source, block, before, after, early, wide1, wide2)


def scatter_bricks(source_ref, stage, value, depth_brick):
    width = value.shape[3]
    half = low_half((4, 2, COLS, width))
    for r in range(4):
        part = value[:, r * 4 : (r + 1) * 4].reshape(4, 2, 2, COLS, width)
        even, odd = part[:, :, 0], part[:, :, 1]
        b0 = jnp.where(half, even, pltpu.roll(odd, 4, 2))
        b1 = jnp.where(half, pltpu.roll(even, 4, 2), odd)
        slot = slot_index(depth_brick, r)
        for k, brick in enumerate((b0, b1)):
            source = source_ref[slot + k]
            row = pl.multiple_of(jnp.where(source >= 0, source, K * CAP) * CELLS, CELLS)
            stage[pl.ds(row, CELLS), :] = brick.reshape(CELLS, width).astype(jnp.bfloat16)


def final_kernel(count, base_ref, source_ref, *refs):
    block_ref, before_ref, after_ref, even_ref, odd_ref = refs[:5]
    mid_here, mid_next, mid_ref, wide1_ref, wide2_ref, first_ref, last_ref = refs[5:12]
    backs = refs[12 : 12 + K]
    x_here, x_next, h_here, h_next, stage, under_ref, over_ref = refs[12 + K :]
    width = block_ref.shape[1]
    stage[...] = jnp.zeros(stage.shape, jnp.bfloat16)
    face_in(base_ref[1], count, even_ref, odd_ref, under_ref, over_ref)
    flags_before = as_rows(before_ref[256:288])
    flags_after = as_rows(after_ref[256:288])
    spread = []
    for end, ref in ((0, under_ref), (1, over_ref)):
        own = []
        for d in (0, 1) if end == 0 else (SIDE - 2, SIDE - 1):
            edge = slice(d * 16, (d + 1) * 16)
            own.append(
                jnp.concatenate(
                    [before_ref[edge], block_ref[d * 128 : (d + 1) * 128], after_ref[edge]], axis=0
                )
            )
        far = [ref[k * 160 : (k + 1) * 160] for k in range(2)]
        for index, plane in enumerate(far + own if end == 0 else own + far):
            x_here[end * 4 + index] = plane
            x_next[end * 4 + index] = as_tiles(moved_rows(as_rows(plane)))
        far_flags = as_rows(ref[320:368])
        brick = 0 if end == 0 else 3
        own_flags = [flags_before[brick]]
        own_flags += [slot_flags(source_ref, slot_index(brick, r)) for r in range(4)]
        own_flags += [flags_after[brick]]
        pair = [
            spread_flags([far_flags[r] for r in range(6)], (1, 4, 4, 4, 4, 1)),
            spread_flags(own_flags, (1, 4, 4, 4, 4, 1)),
        ]
        spread += pair if end == 0 else pair[::-1]
    lhs = [plane_taps(x_here, x_next, first, 2, HID * COLS) for first in (0, 4)]
    value = multiply_taps(jnp.concatenate(lhs, axis=0), wide1_ref)
    value = activate(value.reshape(4, HID, COLS, width), jnp.stack(spread, axis=0))
    for k, index in enumerate((0, 1, 10, 11)):
        h_here[index] = as_tiles(value[k])
        h_next[index] = as_tiles(moved_rows(value[k]))
    for k in range(4):
        for index, source in ((2 + k, k), (6 + k, SIDE - 6 + k)):
            h_here[index] = mid_here[source]
            h_next[index] = mid_next[source]
    for depth_brick in (1, 2):
        rows = slice((depth_brick - 1) * 512, depth_brick * 512)
        done = mid_ref[rows].astype(jnp.float32).reshape(4, SIDE, COLS, width)
        scatter_bricks(source_ref, stage, done, depth_brick)
    for depth_brick, ref in ((0, first_ref), (3, last_ref)):
        value = conv_planes(h_here, h_next, wide2_ref, depth_brick * 2, 4, SIDE * COLS)
        value = coarse_rows(source_ref, block_ref, value, depth_brick)
        ref[...] = value.reshape(512, width).astype(jnp.bfloat16)
        scatter_bricks(source_ref, stage, value, depth_brick)
    for j in range(K):
        backs[j][...] = stage[j * CAP * CELLS : (j + 1) * CAP * CELLS]


def final_call(count, base, source, block, halo, middle, wide1, wide2):
    mid = block.shape[1]
    smem = pl.BlockSpec(memory_space=pltpu.SMEM)
    vmem = pl.BlockSpec(memory_space=pltpu.VMEM)
    return pl.pallas_call(
        functools.partial(final_kernel, count),
        in_specs=[smem, smem] + [vmem] * 10,
        out_specs=[vmem] * (2 + K),
        out_shape=[jax.ShapeDtypeStruct((512, mid), jnp.bfloat16)] * 2
        + [jax.ShapeDtypeStruct((CAP * CELLS, mid), jnp.bfloat16)] * K,
        scratch_shapes=[
            pltpu.VMEM((8, WIDE * COLS, mid), jnp.bfloat16),
            pltpu.VMEM((8, WIDE * COLS, mid), jnp.bfloat16),
            pltpu.VMEM((12, HID * COLS, mid), jnp.bfloat16),
            pltpu.VMEM((12, HID * COLS, mid), jnp.bfloat16),
            pltpu.VMEM(((K * CAP + 1) * CELLS, mid), jnp.bfloat16),
            pltpu.VMEM((368, mid), jnp.bfloat16),
            pltpu.VMEM((368, mid), jnp.bfloat16),
        ],
        compiler_params=pltpu.CompilerParams(vmem_limit_bytes=VMEM_LIMIT),
        cost_estimate=conv_cost(1600, mid),
        name="final",
    )(base, source, block, *halo, *middle, wide1, wide2)


def from_behind(value, axis, steps):
    count = lax.axis_size(axis)
    pairs = [(source, (source + steps) % count) for source in range(count)]
    return lax.ppermute(value, axis, pairs)


def swap_face(face, axis, first):
    count = lax.axis_size(axis)
    partner = list(range(count))
    for i in range(first, count - 1, 2):
        partner[i], partner[i + 1] = i + 1, i
    return lax.ppermute(face, axis, list(enumerate(partner)))


def shards(fine, fine_mask, slot_source, w_down, w_first, w_second, w_up):
    mid = w_down.shape[1]
    base = jnp.stack([lax.axis_index("xy"), lax.axis_index("gz")]).astype(jnp.int32)
    counts = (lax.axis_size("gz"), lax.axis_size("xy"))
    sent = down_call(fine, fine_mask, w_down, SENT)
    arrived = {j: from_behind(sent[j], "xy", j) for j in SENT}
    later = (arrived[SENT[2]], fine, fine_mask, w_down, w_first, w_second)
    arrived[SENT[2]], *later = lax.optimization_barrier(later)
    prepared = lax.optimization_barrier(tuple(prepare_call(*later)))
    arrived[0], mask, wide1, wide2 = prepared
    block, even, odd = place_call(base, slot_source, [arrived[j] for j in range(K)])
    even = swap_face(even, "xy", 0)
    odd = swap_face(odd, "xy", 1)
    early = inner_call(slot_source, block, wide1, EARLY)
    even, odd, early = lax.optimization_barrier((even, odd, early))
    before, after, even, odd = edge_call(counts, base, slot_source, block, even, odd)
    even = swap_face(even, "gz", 0)
    odd = swap_face(odd, "gz", 1)
    middle = middle_call(slot_source, block, before, after, early, wide1, wide2)
    first, last, *back = final_call(
        counts[0], base, slot_source, block, (before, after, even, odd), middle, wide1, wide2
    )
    octant = {j: from_behind(back[j], "xy", -j) for j in RETURNED[:5]}
    for done, j in zip(RETURNED, RETURNED[5:]):
        octant[done], value = lax.optimization_barrier((octant[done], back[j]))
        octant[j] = from_behind(value, "xy", -j)
    octant[0] = back[0]
    octant[7], *pieces = lax.optimization_barrier((octant[7], first, middle[2], last))
    coarse = jnp.concatenate(pieces, axis=0)
    fine_out = None
    for block_index in (3, 2, 1, 0):
        octants = [octant[2 * block_index], octant[2 * block_index + 1]]
        fine_out = up_call(fine, mask, w_up, octants, block_index, fine_out)
    return fine_out, coarse.reshape(SIDE, SIDE, COLS, mid)


def solution(mesh):
    placed = (
        P(("gz", "xy"), None, None),
        P(("gz", "xy"), None),
        P(("gz", "xy")),
        P(),
        P(),
        P(),
        P(),
    )
    return jax.shard_map(
        shards,
        mesh=mesh,
        in_specs=placed,
        out_specs=(P(("gz", "xy"), None, None), P("gz", "xy", None, None)),
        check_vma=False,
    )
```

```python
import functools

import jax
import jax.numpy as jnp
from jax import lax
from jax.experimental import pallas as pl
from jax.experimental.pallas import tpu as pltpu
from jax.sharding import PartitionSpec as P

CAP = 4
K = 8
CELLS = 64
SIDE = 16
COLS = 8
WIDE = SIDE + 4
HID = SIDE + 2
EARLY = ((1, 3), (4, 4), (8, 4))
LATE = ((12, 3),)
LATE_PLANES = 3
SENT = (4, 3, 5, 2, 6, 1, 7)
RETURNED = (6, 7, 4, 5, 2, 3, 1)
DOWN_LIMIT = 62 * 1024 * 1024
VMEM_LIMIT = 24 * 1024 * 1024


def expand_mask(mask):
    bricks = mask.shape[0]
    values = mask.astype(jnp.float32)
    cell = lax.broadcasted_iota(jnp.int32, (16, 128), 0)
    lane = lax.broadcasted_iota(jnp.int32, (16, 128), 1)
    chosen = (cell == lane // 8).astype(jnp.float32)
    parts = [
        values[:, t * 128 : (t + 1) * 128].reshape(bricks, 1, 128) * chosen[None] for t in range(4)
    ]
    spread = jnp.concatenate(parts, axis=1).reshape(bricks * CELLS, 128).astype(jnp.bfloat16)
    source = lax.broadcasted_iota(jnp.int32, (128, 512), 0)
    target = lax.broadcasted_iota(jnp.int32, (128, 512), 1)
    widen = ((source & 7) == (target >> 6)).astype(jnp.bfloat16)
    return jnp.dot(spread, widen, preferred_element_type=jnp.float32)


def down_kernel(offsets, fine_hbm, mask_hbm, w_hbm, *refs):
    count = len(offsets)
    outs = refs[:count]
    fine_ref, mask_ref, w_ref, wide_ref, result_ref, sems, out_sems = refs[count:]
    first = [
        pltpu.make_async_copy(mask_hbm, mask_ref, sems.at[count]),
        pltpu.make_async_copy(w_hbm, w_ref, sems.at[count + 1]),
    ]
    chunks = [
        pltpu.make_async_copy(fine_hbm.at[pl.ds(j * CAP, CAP)], fine_ref.at[k], sems.at[k])
        for k, j in enumerate(offsets)
    ]
    for copy in first + chunks:
        copy.start()
    first[0].wait()
    rows = CAP * CELLS
    for k, j in enumerate(offsets):
        wide_ref[k * rows : (k + 1) * rows] = expand_mask(
            mask_ref[j * CAP : (j + 1) * CAP]
        ).astype(jnp.bfloat16)
    first[1].wait()
    for start in range(0, count, 2):
        group = range(start, min(start + 2, count))
        for k in group:
            chunks[k].wait()
        x = [
            fine_ref[k].reshape(rows, -1) * wide_ref[k * rows : (k + 1) * rows] for k in group
        ]
        y = jnp.dot(jnp.concatenate(x, axis=0), w_ref[...], preferred_element_type=jnp.float32)
        y = y.astype(jnp.bfloat16)
        for part, k in enumerate(group):
            result_ref[k] = y[part * rows : (part + 1) * rows]
            pltpu.make_async_copy(result_ref.at[k], outs[k], out_sems.at[k]).start()
    for k in range(count):
        pltpu.make_async_copy(result_ref.at[k], outs[k], out_sems.at[k]).wait()


def down_call(fine, mask, w, offsets):
    cells, width = fine.shape[1:]
    mid = w.shape[1]
    count = len(offsets)
    rows = count * CAP * cells
    hbm = pl.BlockSpec(memory_space=pltpu.HBM)
    outs = pl.pallas_call(
        functools.partial(down_kernel, offsets),
        in_specs=[hbm, hbm, hbm],
        out_specs=[pl.BlockSpec(memory_space=pl.ANY)] * count,
        out_shape=[jax.ShapeDtypeStruct((CAP * cells, mid), jnp.bfloat16)] * count,
        scratch_shapes=[
            pltpu.VMEM((count, CAP, cells, width), fine.dtype),
            pltpu.VMEM(mask.shape, mask.dtype),
            pltpu.VMEM(w.shape, w.dtype),
            pltpu.VMEM((rows, width), jnp.bfloat16),
            pltpu.VMEM((count, CAP * cells, mid), jnp.bfloat16),
            pltpu.SemaphoreType.DMA((count + 2,)),
            pltpu.SemaphoreType.DMA((count,)),
        ],
        compiler_params=pltpu.CompilerParams(vmem_limit_bytes=DOWN_LIMIT),
        cost_estimate=pl.CostEstimate(
            flops=2 * rows * width * mid, bytes_accessed=rows * width * 2, transcendentals=0
        ),
        name="down",
    )(fine, mask, w)
    return dict(zip(offsets, outs))


def prepare_kernel(
    fine_ref, mask_ref, w_down_ref, w1_ref, w2_ref, own_ref, mask_out, wide1_ref, wide2_ref
):
    gather_weights(w1_ref, wide1_ref)
    gather_weights(w2_ref, wide2_ref)
    step = 8
    for part in range(mask_ref.shape[0] // step):
        rows = slice(part * step * CELLS, (part + 1) * step * CELLS)
        mask_out[rows] = expand_mask(mask_ref[part * step : (part + 1) * step]).astype(jnp.bfloat16)
    rows = CAP * CELLS
    own = fine_ref[...].reshape(rows, -1) * mask_out[:rows]
    own = jnp.dot(own, w_down_ref[...], preferred_element_type=jnp.float32)
    own_ref[...] = own.astype(jnp.bfloat16)


def prepare_call(fine, mask, w_down, w_first, w_second):
    mid = w_first.shape[1]
    vmem = pl.BlockSpec(memory_space=pltpu.VMEM)
    rows = mask.shape[0] * CELLS
    wide = jax.ShapeDtypeStruct((9 * mid, 3 * mid), jnp.bfloat16)
    return pl.pallas_call(
        prepare_kernel,
        grid=(1,),
        in_specs=[pl.BlockSpec((CAP,) + fine.shape[1:], lambda i: (0, 0, 0))] + [vmem] * 4,
        out_specs=[vmem] * 4,
        out_shape=[
            jax.ShapeDtypeStruct((CAP * CELLS, mid), jnp.bfloat16),
            jax.ShapeDtypeStruct((rows, mask.shape[1]), jnp.bfloat16),
            wide,
            wide,
        ],
        compiler_params=pltpu.CompilerParams(vmem_limit_bytes=VMEM_LIMIT),
        cost_estimate=pl.CostEstimate(
            flops=2 * rows * mask.shape[1] * 128, bytes_accessed=rows * mask.shape[1] * 2, transcendentals=0
        ),
        name="prepare",
    )(fine, mask, w_down, w_first, w_second)


def up_kernel(offsets, fine_ref, mask_ref, w_ref, *refs):
    out_ref = refs[-1]
    step = pl.program_id(0)
    bricks, cells, width = fine_ref.shape
    count = bricks // CAP
    steps = offsets // count
    for part in range(count):
        octant = refs[part][...]
        for other in range(1, steps):
            octant = jnp.where(step == other, refs[other * count + part][...], octant)
        rows = slice(part * CAP * cells, (part + 1) * CAP * cells)
        up = jnp.dot(octant, w_ref[...], preferred_element_type=jnp.float32)
        fine = fine_ref[part * CAP : (part + 1) * CAP].reshape(CAP * cells, width)
        mask = mask_ref[rows].astype(jnp.float32)
        out = jnp.where(mask > 0.5, fine.astype(jnp.float32) + up, 0.0)
        out_ref[part * CAP : (part + 1) * CAP] = out.astype(jnp.bfloat16).reshape(CAP, cells, width)


def up_call(fine, mask, w, octants, first, partial):
    bricks, cells, width = fine.shape
    mid = w.shape[0]
    step = 8

    def place(i):
        return first - i

    count = len(octants)
    partials = [] if partial is None else [partial]
    return pl.pallas_call(
        functools.partial(up_kernel, count),
        grid=(count * CAP // step,),
        in_specs=[
            pl.BlockSpec((step, cells, width), lambda i: (place(i), 0, 0)),
            pl.BlockSpec((step * cells, width), lambda i: (place(i), 0)),
            pl.BlockSpec((mid, width), lambda i: (0, 0)),
        ]
        + [pl.BlockSpec((CAP * cells, mid), lambda i: (0, 0))] * count
        + [pl.BlockSpec(memory_space=pl.ANY)] * len(partials),
        out_specs=pl.BlockSpec((step, cells, width), lambda i: (place(i), 0, 0)),
        out_shape=jax.ShapeDtypeStruct(fine.shape, jnp.bfloat16),
        input_output_aliases={3 + count: 0} if partials else {},
        compiler_params=pltpu.CompilerParams(vmem_limit_bytes=VMEM_LIMIT),
        cost_estimate=pl.CostEstimate(
            flops=bricks * cells * width * mid, bytes_accessed=bricks * cells * width * 2, transcendentals=0
        ),
        name="up",
    )(fine, mask, w, *octants, *partials)


def low_half(shape):
    return lax.broadcasted_iota(jnp.int32, shape, len(shape) - 2) < 4


def slot_flags(source_ref, first):
    pair = [jnp.where(source_ref[first + k] >= 0, 1.0, 0.0).astype(jnp.float32) for k in range(2)]
    return jnp.where(low_half((8, 128)), pair[0], pair[1])


def slot_index(depth_brick, row_brick):
    pd, qd = divmod(depth_brick, 2)
    pr, qr = divmod(row_brick, 2)
    return (pd * 2 + pr) * 8 + qd * 4 + qr * 2


def take_brick(source_ref, arrived, slot):
    value = source_ref[slot]
    first = pl.multiple_of(jnp.maximum(value, 0) * CELLS, CELLS)
    brick = arrived[pl.ds(first, CELLS), :].astype(jnp.float32)
    return jnp.where(value >= 0, brick, 0.0).reshape(8, 8, 128)


def place_kernel(base_ref, source_ref, *refs):
    block_ref, even_ref, odd_ref, low_ref, high_ref, arrived = refs[K:]
    for j in range(K):
        arrived[j * CAP * CELLS : (j + 1) * CAP * CELLS] = refs[j][...]
    half = low_half((8, 8, 128))
    for depth_brick in range(4):
        for row_brick in range(4):
            slot = slot_index(depth_brick, row_brick)
            b0 = take_brick(source_ref, arrived, slot)
            b1 = take_brick(source_ref, arrived, slot + 1)
            even = jnp.where(half, b0, pltpu.roll(b1, 4, 1))
            odd = jnp.where(half, pltpu.roll(b0, 4, 1), b1)
            both = jnp.stack([even, odd], axis=1).reshape(4, 32, 128).astype(jnp.bfloat16)
            for vd in range(4):
                row = ((depth_brick * 4 + vd) * SIDE + row_brick * 4) * COLS
                block_ref[row : row + 32] = both[vd]
                place = (depth_brick * 4 + vd) * 16
                if row_brick == 0:
                    low_ref[place : place + 16] = both[vd, :16]
                if row_brick == 3:
                    high_ref[place : place + 16] = both[vd, 16:]
    for row_brick, ref in ((0, low_ref), (3, high_ref)):
        flags = [slot_flags(source_ref, slot_index(d, row_brick)) for d in range(4)]
        ref[256:288] = jnp.concatenate(flags, axis=0).astype(jnp.bfloat16)
    face_out(base_ref[0], low_ref, high_ref, even_ref, odd_ref)


def face_out(index, low_ref, high_ref, even_ref, odd_ref):
    is_even = index % 2 == 0
    even_ref[...] = jnp.where(is_even, high_ref[...], low_ref[...])
    odd_ref[...] = jnp.where(is_even, low_ref[...], high_ref[...])


def face_in(index, count, even_ref, odd_ref, low_ref, high_ref):
    is_even = index % 2 == 0
    empty = jnp.zeros(low_ref.shape, low_ref.dtype)
    low = jnp.where(is_even, odd_ref[...], even_ref[...])
    high = jnp.where(is_even, even_ref[...], odd_ref[...])
    low_ref[...] = jnp.where(index == 0, empty, low)
    high_ref[...] = jnp.where(index == count - 1, empty, high)


def place_call(base, source, arrived):
    mid = arrived[0].shape[1]
    smem = pl.BlockSpec(memory_space=pltpu.SMEM)
    vmem = pl.BlockSpec(memory_space=pltpu.VMEM)
    return pl.pallas_call(
        place_kernel,
        in_specs=[smem, smem] + [vmem] * K,
        out_specs=[vmem] * 3,
        out_shape=[
            jax.ShapeDtypeStruct((rows, mid), jnp.bfloat16)
            for rows in (SIDE * SIDE * COLS, 288, 288)
        ],
        scratch_shapes=[
            pltpu.VMEM((288, mid), jnp.bfloat16),
            pltpu.VMEM((288, mid), jnp.bfloat16),
            pltpu.VMEM((K * CAP * CELLS, mid), jnp.bfloat16),
        ],
        compiler_params=pltpu.CompilerParams(vmem_limit_bytes=VMEM_LIMIT),
        name="place",
    )(base, source, *arrived)


def edge_kernel(
    counts,
    base_ref,
    source_ref,
    block_ref,
    even_ref,
    odd_ref,
    before_ref,
    after_ref,
    even_out,
    odd_out,
    low_ref,
    high_ref,
):
    face_in(base_ref[0], counts[1], even_ref, odd_ref, before_ref, after_ref)
    for ref, planes, brick in ((low_ref, (0, 1), 0), (high_ref, (SIDE - 2, SIDE - 1), 3)):
        for k, plane in enumerate(planes):
            start = k * WIDE * COLS
            ref[start : start + 16] = before_ref[plane * 16 : plane * 16 + 16]
            ref[start + 16 : start + 144] = block_ref[plane * 128 : plane * 128 + 128]
            ref[start + 144 : start + 160] = after_ref[plane * 16 : plane * 16 + 16]
        flags = [before_ref[256:288].astype(jnp.float32)[brick * 8 : brick * 8 + 8]]
        flags += [slot_flags(source_ref, slot_index(brick, r)) for r in range(4)]
        flags += [after_ref[256:288].astype(jnp.float32)[brick * 8 : brick * 8 + 8]]
        ref[320:368] = jnp.concatenate(flags, axis=0).astype(jnp.bfloat16)
    face_out(base_ref[1], low_ref, high_ref, even_out, odd_out)


def edge_call(counts, base, source, block, even, odd):
    smem = pl.BlockSpec(memory_space=pltpu.SMEM)
    vmem = pl.BlockSpec(memory_space=pltpu.VMEM)
    mid = block.shape[1]
    return pl.pallas_call(
        functools.partial(edge_kernel, counts),
        in_specs=[smem, smem, vmem, vmem, vmem],
        out_specs=[vmem] * 4,
        out_shape=[
            jax.ShapeDtypeStruct((rows, mid), jnp.bfloat16) for rows in (288, 288, 368, 368)
        ],
        scratch_shapes=[pltpu.VMEM((368, mid), jnp.bfloat16)] * 2,
        compiler_params=pltpu.CompilerParams(vmem_limit_bytes=VMEM_LIMIT),
        name="edge",
    )(base, source, block, even, odd)


def gather_weights(w_ref, wide_ref):
    width = w_ref.shape[2]
    for tap in range(9):
        for column in range(3):
            wide_ref[tap * width : (tap + 1) * width, column * width : (column + 1) * width] = (
                w_ref[tap * 3 + column]
            )


def as_rows(value):
    value = value.astype(jnp.float32)
    return value.reshape(value.shape[0] // COLS, COLS, value.shape[1])


def moved_rows(rows):
    empty = jnp.zeros((1,) + rows.shape[1:], jnp.float32)
    return jnp.concatenate([rows[1:], empty], axis=0)


def as_tiles(rows):
    return rows.reshape(rows.shape[0] * COLS, rows.shape[2]).astype(jnp.bfloat16)


def multiply_taps(lhs, wide_ref):
    width = wide_ref.shape[1] // 3
    wide = jnp.dot(lhs, wide_ref[...], preferred_element_type=jnp.float32)
    wide = wide.reshape(lhs.shape[0] // COLS, COLS, 3 * width)
    column = lax.broadcasted_iota(jnp.int32, (lhs.shape[0] // COLS, COLS, width), 1)
    left = jnp.where(column == 0, 0.0, pltpu.roll(wide[:, :, :width], 1, 1))
    right = jnp.where(column == COLS - 1, 0.0, pltpu.roll(wide[:, :, 2 * width :], COLS - 1, 1))
    return left + wide[:, :, width : 2 * width] + right


def plane_taps(here_ref, next_ref, first, planes, rows):
    taps = []
    for dd in range(3):
        span = slice(first + dd, first + dd + planes)
        taps += [
            here_ref[span, 0:rows, :],
            next_ref[span, 0:rows, :],
            here_ref[span, 16 : rows + 16, :],
        ]
    lhs = jnp.concatenate(taps, axis=2)
    return lhs.reshape(planes * rows, lhs.shape[2])


def conv_planes(here_ref, next_ref, wide_ref, first, planes, rows):
    return multiply_taps(plane_taps(here_ref, next_ref, first, planes, rows), wide_ref)


def activate(value, flags):
    return value / (1.0 + jnp.exp(-value)) * flags


def spread_flags(flags, repeats):
    return jnp.concatenate(
        [jnp.broadcast_to(flag[None], (count,) + flag.shape) for flag, count in zip(flags, repeats)],
        axis=0,
    )


def inner_planes(source_ref, block_ref, wide1_ref, hidden_ref, here, moved, groups):
    width = block_ref.shape[1]
    base = groups[0][0] - 1
    for d in range(base, groups[-1][0] + groups[-1][1] + 1):
        plane = block_ref[d * 128 : (d + 1) * 128]
        here[d - base] = plane
        moved[d - base] = as_tiles(moved_rows(as_rows(plane)))
    inner = SIDE - 2
    rows = inner * COLS
    for first, planes in groups:
        value = conv_planes(here, moved, wide1_ref, first - 1 - base, planes, rows)
        value = value.reshape(planes, inner, COLS, width)
        flags = [slot_flags(source_ref, slot_index(first // 4, r)) for r in range(4)]
        value = activate(value, spread_flags(flags, (3, 4, 4, 3))[None])
        hidden_ref[first - 1 - base : first - 1 - base + planes] = value.reshape(
            planes, rows, width
        ).astype(jnp.bfloat16)


def inner_kernel(groups, source_ref, block_ref, wide1_ref, hidden_ref, here, moved):
    inner_planes(source_ref, block_ref, wide1_ref, hidden_ref, here, moved, groups)


def conv_cost(rows, width):
    return pl.CostEstimate(
        flops=2 * rows * 27 * width * width, bytes_accessed=27 * width * width * 4, transcendentals=0
    )


def inner_call(source, block, wide1, groups):
    mid = block.shape[1]
    smem = pl.BlockSpec(memory_space=pltpu.SMEM)
    vmem = pl.BlockSpec(memory_space=pltpu.VMEM)
    rows = (SIDE - 2) * COLS
    planes = sum(count for _, count in groups)
    return pl.pallas_call(
        functools.partial(inner_kernel, groups),
        in_specs=[smem, vmem, vmem],
        out_specs=vmem,
        out_shape=jax.ShapeDtypeStruct((planes, rows, mid), jnp.bfloat16),
        scratch_shapes=[pltpu.VMEM((planes + 2, SIDE * COLS, mid), jnp.bfloat16)] * 2,
        compiler_params=pltpu.CompilerParams(vmem_limit_bytes=VMEM_LIMIT),
        cost_estimate=conv_cost(planes * rows, mid),
        name="inner",
    )(source, block, wide1)


def side_taps(low, high):
    mixed = as_tiles(
        jnp.concatenate(
            [as_rows(low).reshape(-1, 2, COLS, 128)[:, 1:], as_rows(high).reshape(-1, 2, COLS, 128)[:, :1]],
            axis=1,
        ).reshape(-1, COLS, 128)
    )
    return low, mixed, high


def depth_taps(taps, planes):
    parts = [tap[dd * 16 : (dd + planes) * 16] for dd in range(3) for tap in taps]
    return jnp.concatenate(parts, axis=1)


def coarse_rows(source_ref, block_ref, value, depth_brick):
    width = block_ref.shape[1]
    value = value.reshape(4, SIDE, COLS, width)
    rows = slice(depth_brick * 512, (depth_brick + 1) * 512)
    own = block_ref[rows].astype(jnp.float32).reshape(4, SIDE, COLS, width)
    flags = [slot_flags(source_ref, slot_index(depth_brick, r)) for r in range(4)]
    return (value + own) * spread_flags(flags, (4, 4, 4, 4))[None]


def middle_kernel(source_ref, *refs):
    block_ref, before_ref, after_ref, early_ref, wide1_ref, wide2_ref = refs[:6]
    h_here, h_next, coarse_ref, side, late, here, moved = refs[6:]
    width = block_ref.shape[1]
    inner = SIDE - 2
    inner_planes(source_ref, block_ref, wide1_ref, late, here, moved, LATE)

    low = jnp.concatenate([block_ref[d * 128 : d * 128 + 16] for d in range(SIDE)], axis=0)
    high = jnp.concatenate([block_ref[d * 128 + 112 : d * 128 + 128] for d in range(SIDE)], axis=0)
    left = depth_taps(side_taps(before_ref[0:256], low), inner)
    right = depth_taps(side_taps(high, after_ref[0:256]), inner)
    value = multiply_taps(jnp.concatenate([left, right], axis=0), wide1_ref)
    depths = (3, 4, 4, 3)
    edge_flags = (as_rows(before_ref[256:288]), as_rows(after_ref[256:288]))
    flags = []
    for end, row_brick in ((0, 0), (1, 3)):
        own = [slot_flags(source_ref, slot_index(d, row_brick)) for d in range(4)]
        pairs = [jnp.stack([edge_flags[end][d], own[d]][:: 1 - 2 * end], axis=0) for d in range(4)]
        flags.append(spread_flags(pairs, depths))
    value = activate(value.reshape(2, inner, 2, COLS, width), jnp.stack(flags, axis=0))
    side[...] = value.reshape(2, inner, 16, width).astype(jnp.bfloat16)
    centres = [ref[k] for ref in (early_ref, late) for k in range(ref.shape[0])]
    for d in range(inner):
        plane = jnp.concatenate([side[0, d], centres[d], side[1, d]], axis=0)
        h_here[d] = plane
        h_next[d] = as_tiles(moved_rows(as_rows(plane)))

    for depth_brick in (1, 2):
        value = conv_planes(h_here, h_next, wide2_ref, depth_brick * 4 - 2, 4, SIDE * COLS)
        value = coarse_rows(source_ref, block_ref, value, depth_brick)
        rows = slice((depth_brick - 1) * 512, depth_brick * 512)
        coarse_ref[rows] = value.reshape(512, width).astype(jnp.bfloat16)


def middle_call(source, block, before, after, early, wide1, wide2):
    mid = block.shape[1]
    smem = pl.BlockSpec(memory_space=pltpu.SMEM)
    vmem = pl.BlockSpec(memory_space=pltpu.VMEM)
    inner = SIDE - 2
    hidden = (inner, HID * COLS, mid)
    return pl.pallas_call(
        middle_kernel,
        in_specs=[smem] + [vmem] * 6,
        out_specs=[vmem] * 3,
        out_shape=[
            jax.ShapeDtypeStruct(shape, jnp.bfloat16) for shape in (hidden, hidden, (1024, mid))
        ],
        scratch_shapes=[
            pltpu.VMEM((2, inner, 16, mid), jnp.bfloat16),
            pltpu.VMEM((LATE_PLANES, inner * COLS, mid), jnp.bfloat16),
            pltpu.VMEM((LATE_PLANES + 2, SIDE * COLS, mid), jnp.bfloat16),
            pltpu.VMEM((LATE_PLANES + 2, SIDE * COLS, mid), jnp.bfloat16),
        ],
        compiler_params=pltpu.CompilerParams(vmem_limit_bytes=VMEM_LIMIT),
        cost_estimate=conv_cost(inner * (4 + LATE_PLANES) * COLS + 1024, mid),
        name="middle",
    )(source, block, before, after, early, wide1, wide2)


def scatter_bricks(source_ref, stage, value, depth_brick):
    width = value.shape[3]
    half = low_half((4, 2, COLS, width))
    for r in range(4):
        part = value[:, r * 4 : (r + 1) * 4].reshape(4, 2, 2, COLS, width)
        even, odd = part[:, :, 0], part[:, :, 1]
        b0 = jnp.where(half, even, pltpu.roll(odd, 4, 2))
        b1 = jnp.where(half, pltpu.roll(even, 4, 2), odd)
        slot = slot_index(depth_brick, r)
        for k, brick in enumerate((b0, b1)):
            source = source_ref[slot + k]
            row = pl.multiple_of(jnp.where(source >= 0, source, K * CAP) * CELLS, CELLS)
            stage[pl.ds(row, CELLS), :] = brick.reshape(CELLS, width).astype(jnp.bfloat16)


def final_kernel(count, base_ref, source_ref, *refs):
    block_ref, before_ref, after_ref, even_ref, odd_ref = refs[:5]
    mid_here, mid_next, mid_ref, wide1_ref, wide2_ref, first_ref, last_ref = refs[5:12]
    backs = refs[12 : 12 + K]
    x_here, x_next, h_here, h_next, stage, under_ref, over_ref = refs[12 + K :]
    width = block_ref.shape[1]
    stage[...] = jnp.zeros(stage.shape, jnp.bfloat16)
    face_in(base_ref[1], count, even_ref, odd_ref, under_ref, over_ref)
    flags_before = as_rows(before_ref[256:288])
    flags_after = as_rows(after_ref[256:288])
    spread = []
    for end, ref in ((0, under_ref), (1, over_ref)):
        own = []
        for d in (0, 1) if end == 0 else (SIDE - 2, SIDE - 1):
            edge = slice(d * 16, (d + 1) * 16)
            own.append(
                jnp.concatenate(
                    [before_ref[edge], block_ref[d * 128 : (d + 1) * 128], after_ref[edge]], axis=0
                )
            )
        far = [ref[k * 160 : (k + 1) * 160] for k in range(2)]
        for index, plane in enumerate(far + own if end == 0 else own + far):
            x_here[end * 4 + index] = plane
            x_next[end * 4 + index] = as_tiles(moved_rows(as_rows(plane)))
        far_flags = as_rows(ref[320:368])
        brick = 0 if end == 0 else 3
        own_flags = [flags_before[brick]]
        own_flags += [slot_flags(source_ref, slot_index(brick, r)) for r in range(4)]
        own_flags += [flags_after[brick]]
        pair = [
            spread_flags([far_flags[r] for r in range(6)], (1, 4, 4, 4, 4, 1)),
            spread_flags(own_flags, (1, 4, 4, 4, 4, 1)),
        ]
        spread += pair if end == 0 else pair[::-1]
    lhs = [plane_taps(x_here, x_next, first, 2, HID * COLS) for first in (0, 4)]
    value = multiply_taps(jnp.concatenate(lhs, axis=0), wide1_ref)
    value = activate(value.reshape(4, HID, COLS, width), jnp.stack(spread, axis=0))
    for k, index in enumerate((0, 1, 10, 11)):
        h_here[index] = as_tiles(value[k])
        h_next[index] = as_tiles(moved_rows(value[k]))
    for k in range(4):
        for index, source in ((2 + k, k), (6 + k, SIDE - 6 + k)):
            h_here[index] = mid_here[source]
            h_next[index] = mid_next[source]
    for depth_brick in (1, 2):
        rows = slice((depth_brick - 1) * 512, depth_brick * 512)
        done = mid_ref[rows].astype(jnp.float32).reshape(4, SIDE, COLS, width)
        scatter_bricks(source_ref, stage, done, depth_brick)
    for depth_brick, ref in ((0, first_ref), (3, last_ref)):
        value = conv_planes(h_here, h_next, wide2_ref, depth_brick * 2, 4, SIDE * COLS)
        value = coarse_rows(source_ref, block_ref, value, depth_brick)
        ref[...] = value.reshape(512, width).astype(jnp.bfloat16)
        scatter_bricks(source_ref, stage, value, depth_brick)
    for j in range(K):
        backs[j][...] = stage[j * CAP * CELLS : (j + 1) * CAP * CELLS]


def final_call(count, base, source, block, halo, middle, wide1, wide2):
    mid = block.shape[1]
    smem = pl.BlockSpec(memory_space=pltpu.SMEM)
    vmem = pl.BlockSpec(memory_space=pltpu.VMEM)
    return pl.pallas_call(
        functools.partial(final_kernel, count),
        in_specs=[smem, smem] + [vmem] * 10,
        out_specs=[vmem] * (2 + K),
        out_shape=[jax.ShapeDtypeStruct((512, mid), jnp.bfloat16)] * 2
        + [jax.ShapeDtypeStruct((CAP * CELLS, mid), jnp.bfloat16)] * K,
        scratch_shapes=[
            pltpu.VMEM((8, WIDE * COLS, mid), jnp.bfloat16),
            pltpu.VMEM((8, WIDE * COLS, mid), jnp.bfloat16),
            pltpu.VMEM((12, HID * COLS, mid), jnp.bfloat16),
            pltpu.VMEM((12, HID * COLS, mid), jnp.bfloat16),
            pltpu.VMEM(((K * CAP + 1) * CELLS, mid), jnp.bfloat16),
            pltpu.VMEM((368, mid), jnp.bfloat16),
            pltpu.VMEM((368, mid), jnp.bfloat16),
        ],
        compiler_params=pltpu.CompilerParams(vmem_limit_bytes=VMEM_LIMIT),
        cost_estimate=conv_cost(1600, mid),
        name="final",
    )(base, source, block, *halo, *middle, wide1, wide2)


def from_behind(value, axis, steps):
    count = lax.axis_size(axis)
    pairs = [(source, (source + steps) % count) for source in range(count)]
    return lax.ppermute(value, axis, pairs)


def swap_face(face, axis, first):
    count = lax.axis_size(axis)
    partner = list(range(count))
    for i in range(first, count - 1, 2):
        partner[i], partner[i + 1] = i + 1, i
    return lax.ppermute(face, axis, list(enumerate(partner)))


def shards(fine, fine_mask, slot_source, w_down, w_first, w_second, w_up):
    mid = w_down.shape[1]
    base = jnp.stack([lax.axis_index("xy"), lax.axis_index("gz")]).astype(jnp.int32)
    counts = (lax.axis_size("gz"), lax.axis_size("xy"))
    sent = down_call(fine, fine_mask, w_down, SENT)
    arrived = {j: from_behind(sent[j], "xy", j) for j in SENT}
    later = (arrived[SENT[2]], fine, fine_mask, w_down, w_first, w_second)
    arrived[SENT[2]], *later = lax.optimization_barrier(later)
    prepared = lax.optimization_barrier(tuple(prepare_call(*later)))
    arrived[0], mask, wide1, wide2 = prepared
    block, even, odd = place_call(base, slot_source, [arrived[j] for j in range(K)])
    even = swap_face(even, "xy", 0)
    odd = swap_face(odd, "xy", 1)
    early = inner_call(slot_source, block, wide1, EARLY)
    even, odd, early = lax.optimization_barrier((even, odd, early))
    before, after, even, odd = edge_call(counts, base, slot_source, block, even, odd)
    even = swap_face(even, "gz", 0)
    odd = swap_face(odd, "gz", 1)
    middle = middle_call(slot_source, block, before, after, early, wide1, wide2)
    first, last, *back = final_call(
        counts[0], base, slot_source, block, (before, after, even, odd), middle, wide1, wide2
    )
    octant = {j: from_behind(back[j], "xy", -j) for j in RETURNED[:5]}
    for done, j in zip(RETURNED, RETURNED[5:]):
        octant[done], value = lax.optimization_barrier((octant[done], back[j]))
        octant[j] = from_behind(value, "xy", -j)
    octant[0] = back[0]
    octant[7], *pieces = lax.optimization_barrier((octant[7], first, middle[2], last))
    coarse = jnp.concatenate(pieces, axis=0)
    fine_out = None
    for block_indices in ((3,), (2, 1, 0)):
        octants = [octant[2 * k + part] for k in block_indices for part in range(2)]
        fine_out = up_call(fine, mask, w_up, octants, block_indices[0], fine_out)
    return fine_out, coarse.reshape(SIDE, SIDE, COLS, mid)


def solution(mesh):
    placed = (
        P(("gz", "xy"), None, None),
        P(("gz", "xy"), None),
        P(("gz", "xy")),
        P(),
        P(),
        P(),
        P(),
    )
    return jax.shard_map(
        shards,
        mesh=mesh,
        in_specs=placed,
        out_specs=(P(("gz", "xy"), None, None), P("gz", "xy", None, None)),
        check_vma=False,
    )
```

```python
import functools

import jax
import jax.numpy as jnp
from jax import lax
from jax.experimental import pallas as pl
from jax.experimental.pallas import tpu as pltpu
from jax.sharding import PartitionSpec as P

CAP = 4
K = 8
CELLS = 64
SIDE = 16
COLS = 8
WIDE = SIDE + 4
HID = SIDE + 2
EARLY = ((1, 3), (4, 4), (8, 4))
LATE = ((12, 3),)
LATE_PLANES = 3
SENT = (4, 3, 5, 2, 6, 1, 7)
RETURNED = (7, 6, 4, 5, 2, 3, 1)
DOWN_LIMIT = 62 * 1024 * 1024
VMEM_LIMIT = 24 * 1024 * 1024


def expand_mask(mask):
    bricks = mask.shape[0]
    values = mask.astype(jnp.float32)
    cell = lax.broadcasted_iota(jnp.int32, (16, 128), 0)
    lane = lax.broadcasted_iota(jnp.int32, (16, 128), 1)
    chosen = (cell == lane // 8).astype(jnp.float32)
    parts = [
        values[:, t * 128 : (t + 1) * 128].reshape(bricks, 1, 128) * chosen[None] for t in range(4)
    ]
    spread = jnp.concatenate(parts, axis=1).reshape(bricks * CELLS, 128).astype(jnp.bfloat16)
    source = lax.broadcasted_iota(jnp.int32, (128, 512), 0)
    target = lax.broadcasted_iota(jnp.int32, (128, 512), 1)
    widen = ((source & 7) == (target >> 6)).astype(jnp.bfloat16)
    return jnp.dot(spread, widen, preferred_element_type=jnp.float32)


def down_kernel(offsets, fine_hbm, mask_hbm, w_hbm, *refs):
    count = len(offsets)
    outs = refs[:count]
    fine_ref, mask_ref, w_ref, wide_ref, result_ref, sems, out_sems = refs[count:]
    first = [
        pltpu.make_async_copy(mask_hbm, mask_ref, sems.at[count]),
        pltpu.make_async_copy(w_hbm, w_ref, sems.at[count + 1]),
    ]
    chunks = [
        pltpu.make_async_copy(fine_hbm.at[pl.ds(j * CAP, CAP)], fine_ref.at[k], sems.at[k])
        for k, j in enumerate(offsets)
    ]
    for copy in first + chunks:
        copy.start()
    first[0].wait()
    rows = CAP * CELLS
    for k, j in enumerate(offsets):
        wide_ref[k * rows : (k + 1) * rows] = expand_mask(
            mask_ref[j * CAP : (j + 1) * CAP]
        ).astype(jnp.bfloat16)
    first[1].wait()
    for start in range(0, count, 2):
        group = range(start, min(start + 2, count))
        for k in group:
            chunks[k].wait()
        x = [
            fine_ref[k].reshape(rows, -1) * wide_ref[k * rows : (k + 1) * rows] for k in group
        ]
        y = jnp.dot(jnp.concatenate(x, axis=0), w_ref[...], preferred_element_type=jnp.float32)
        y = y.astype(jnp.bfloat16)
        for part, k in enumerate(group):
            result_ref[k] = y[part * rows : (part + 1) * rows]
            pltpu.make_async_copy(result_ref.at[k], outs[k], out_sems.at[k]).start()
    for k in range(count):
        pltpu.make_async_copy(result_ref.at[k], outs[k], out_sems.at[k]).wait()


def down_call(fine, mask, w, offsets):
    cells, width = fine.shape[1:]
    mid = w.shape[1]
    count = len(offsets)
    rows = count * CAP * cells
    hbm = pl.BlockSpec(memory_space=pltpu.HBM)
    outs = pl.pallas_call(
        functools.partial(down_kernel, offsets),
        in_specs=[hbm, hbm, hbm],
        out_specs=[pl.BlockSpec(memory_space=pl.ANY)] * count,
        out_shape=[jax.ShapeDtypeStruct((CAP * cells, mid), jnp.bfloat16)] * count,
        scratch_shapes=[
            pltpu.VMEM((count, CAP, cells, width), fine.dtype),
            pltpu.VMEM(mask.shape, mask.dtype),
            pltpu.VMEM(w.shape, w.dtype),
            pltpu.VMEM((rows, width), jnp.bfloat16),
            pltpu.VMEM((count, CAP * cells, mid), jnp.bfloat16),
            pltpu.SemaphoreType.DMA((count + 2,)),
            pltpu.SemaphoreType.DMA((count,)),
        ],
        compiler_params=pltpu.CompilerParams(vmem_limit_bytes=DOWN_LIMIT),
        cost_estimate=pl.CostEstimate(
            flops=2 * rows * width * mid, bytes_accessed=rows * width * 2, transcendentals=0
        ),
        name="down",
    )(fine, mask, w)
    return dict(zip(offsets, outs))


def prepare_kernel(
    fine_ref, mask_ref, w_down_ref, w1_ref, w2_ref, own_ref, mask_out, wide1_ref, wide2_ref
):
    gather_weights(w1_ref, wide1_ref)
    gather_weights(w2_ref, wide2_ref)
    step = 8
    for part in range(mask_ref.shape[0] // step):
        rows = slice(part * step * CELLS, (part + 1) * step * CELLS)
        mask_out[rows] = expand_mask(mask_ref[part * step : (part + 1) * step]).astype(jnp.bfloat16)
    rows = CAP * CELLS
    own = fine_ref[...].reshape(rows, -1) * mask_out[:rows]
    own = jnp.dot(own, w_down_ref[...], preferred_element_type=jnp.float32)
    own_ref[...] = own.astype(jnp.bfloat16)


def prepare_call(fine, mask, w_down, w_first, w_second):
    mid = w_first.shape[1]
    vmem = pl.BlockSpec(memory_space=pltpu.VMEM)
    rows = mask.shape[0] * CELLS
    wide = jax.ShapeDtypeStruct((9 * mid, 3 * mid), jnp.bfloat16)
    return pl.pallas_call(
        prepare_kernel,
        grid=(1,),
        in_specs=[pl.BlockSpec((CAP,) + fine.shape[1:], lambda i: (0, 0, 0))] + [vmem] * 4,
        out_specs=[vmem] * 4,
        out_shape=[
            jax.ShapeDtypeStruct((CAP * CELLS, mid), jnp.bfloat16),
            jax.ShapeDtypeStruct((rows, mask.shape[1]), jnp.bfloat16),
            wide,
            wide,
        ],
        compiler_params=pltpu.CompilerParams(vmem_limit_bytes=VMEM_LIMIT),
        cost_estimate=pl.CostEstimate(
            flops=2 * rows * mask.shape[1] * 128, bytes_accessed=rows * mask.shape[1] * 2, transcendentals=0
        ),
        name="prepare",
    )(fine, mask, w_down, w_first, w_second)


def up_kernel(offsets, fine_ref, mask_ref, w_ref, *refs):
    out_ref = refs[-1]
    step = pl.program_id(0)
    bricks, cells, width = fine_ref.shape
    count = bricks // CAP
    steps = offsets // count
    for part in range(count):
        octant = refs[part][...]
        for other in range(1, steps):
            octant = jnp.where(step == other, refs[other * count + part][...], octant)
        rows = slice(part * CAP * cells, (part + 1) * CAP * cells)
        up = jnp.dot(octant, w_ref[...], preferred_element_type=jnp.float32)
        fine = fine_ref[part * CAP : (part + 1) * CAP].reshape(CAP * cells, width)
        mask = mask_ref[rows].astype(jnp.float32)
        out = jnp.where(mask > 0.5, fine.astype(jnp.float32) + up, 0.0)
        out_ref[part * CAP : (part + 1) * CAP] = out.astype(jnp.bfloat16).reshape(CAP, cells, width)


def up_call(fine, mask, w, octants, first, partial):
    bricks, cells, width = fine.shape
    mid = w.shape[0]
    step = 8

    def place(i):
        return first - i

    count = len(octants)
    partials = [] if partial is None else [partial]
    return pl.pallas_call(
        functools.partial(up_kernel, count),
        grid=(count * CAP // step,),
        in_specs=[
            pl.BlockSpec((step, cells, width), lambda i: (place(i), 0, 0)),
            pl.BlockSpec((step * cells, width), lambda i: (place(i), 0)),
            pl.BlockSpec((mid, width), lambda i: (0, 0)),
        ]
        + [pl.BlockSpec((CAP * cells, mid), lambda i: (0, 0))] * count
        + [pl.BlockSpec(memory_space=pl.ANY)] * len(partials),
        out_specs=pl.BlockSpec((step, cells, width), lambda i: (place(i), 0, 0)),
        out_shape=jax.ShapeDtypeStruct(fine.shape, jnp.bfloat16),
        input_output_aliases={3 + count: 0} if partials else {},
        compiler_params=pltpu.CompilerParams(vmem_limit_bytes=VMEM_LIMIT),
        cost_estimate=pl.CostEstimate(
            flops=bricks * cells * width * mid, bytes_accessed=bricks * cells * width * 2, transcendentals=0
        ),
        name="up",
    )(fine, mask, w, *octants, *partials)


def low_half(shape):
    return lax.broadcasted_iota(jnp.int32, shape, len(shape) - 2) < 4


def slot_flags(source_ref, first):
    pair = [jnp.where(source_ref[first + k] >= 0, 1.0, 0.0).astype(jnp.float32) for k in range(2)]
    return jnp.where(low_half((8, 128)), pair[0], pair[1])


def slot_index(depth_brick, row_brick):
    pd, qd = divmod(depth_brick, 2)
    pr, qr = divmod(row_brick, 2)
    return (pd * 2 + pr) * 8 + qd * 4 + qr * 2


def take_brick(source_ref, arrived, slot):
    value = source_ref[slot]
    first = pl.multiple_of(jnp.maximum(value, 0) * CELLS, CELLS)
    brick = arrived[pl.ds(first, CELLS), :].astype(jnp.float32)
    return jnp.where(value >= 0, brick, 0.0).reshape(8, 8, 128)


def place_kernel(base_ref, source_ref, *refs):
    block_ref, even_ref, odd_ref, low_ref, high_ref, arrived = refs[K:]
    for j in range(K):
        arrived[j * CAP * CELLS : (j + 1) * CAP * CELLS] = refs[j][...]
    half = low_half((8, 8, 128))
    for depth_brick in range(4):
        for row_brick in range(4):
            slot = slot_index(depth_brick, row_brick)
            b0 = take_brick(source_ref, arrived, slot)
            b1 = take_brick(source_ref, arrived, slot + 1)
            even = jnp.where(half, b0, pltpu.roll(b1, 4, 1))
            odd = jnp.where(half, pltpu.roll(b0, 4, 1), b1)
            both = jnp.stack([even, odd], axis=1).reshape(4, 32, 128).astype(jnp.bfloat16)
            for vd in range(4):
                row = ((depth_brick * 4 + vd) * SIDE + row_brick * 4) * COLS
                block_ref[row : row + 32] = both[vd]
                place = (depth_brick * 4 + vd) * 16
                if row_brick == 0:
                    low_ref[place : place + 16] = both[vd, :16]
                if row_brick == 3:
                    high_ref[place : place + 16] = both[vd, 16:]
    for row_brick, ref in ((0, low_ref), (3, high_ref)):
        flags = [slot_flags(source_ref, slot_index(d, row_brick)) for d in range(4)]
        ref[256:288] = jnp.concatenate(flags, axis=0).astype(jnp.bfloat16)
    face_out(base_ref[0], low_ref, high_ref, even_ref, odd_ref)


def face_out(index, low_ref, high_ref, even_ref, odd_ref):
    is_even = index % 2 == 0
    even_ref[...] = jnp.where(is_even, high_ref[...], low_ref[...])
    odd_ref[...] = jnp.where(is_even, low_ref[...], high_ref[...])


def face_in(index, count, even_ref, odd_ref, low_ref, high_ref):
    is_even = index % 2 == 0
    empty = jnp.zeros(low_ref.shape, low_ref.dtype)
    low = jnp.where(is_even, odd_ref[...], even_ref[...])
    high = jnp.where(is_even, even_ref[...], odd_ref[...])
    low_ref[...] = jnp.where(index == 0, empty, low)
    high_ref[...] = jnp.where(index == count - 1, empty, high)


def place_call(base, source, arrived):
    mid = arrived[0].shape[1]
    smem = pl.BlockSpec(memory_space=pltpu.SMEM)
    vmem = pl.BlockSpec(memory_space=pltpu.VMEM)
    return pl.pallas_call(
        place_kernel,
        in_specs=[smem, smem] + [vmem] * K,
        out_specs=[vmem] * 3,
        out_shape=[
            jax.ShapeDtypeStruct((rows, mid), jnp.bfloat16)
            for rows in (SIDE * SIDE * COLS, 288, 288)
        ],
        scratch_shapes=[
            pltpu.VMEM((288, mid), jnp.bfloat16),
            pltpu.VMEM((288, mid), jnp.bfloat16),
            pltpu.VMEM((K * CAP * CELLS, mid), jnp.bfloat16),
        ],
        compiler_params=pltpu.CompilerParams(vmem_limit_bytes=VMEM_LIMIT),
        name="place",
    )(base, source, *arrived)


def edge_kernel(
    counts,
    base_ref,
    source_ref,
    block_ref,
    even_ref,
    odd_ref,
    before_ref,
    after_ref,
    even_out,
    odd_out,
    low_ref,
    high_ref,
):
    face_in(base_ref[0], counts[1], even_ref, odd_ref, before_ref, after_ref)
    for ref, planes, brick in ((low_ref, (0, 1), 0), (high_ref, (SIDE - 2, SIDE - 1), 3)):
        for k, plane in enumerate(planes):
            start = k * WIDE * COLS
            ref[start : start + 16] = before_ref[plane * 16 : plane * 16 + 16]
            ref[start + 16 : start + 144] = block_ref[plane * 128 : plane * 128 + 128]
            ref[start + 144 : start + 160] = after_ref[plane * 16 : plane * 16 + 16]
        flags = [before_ref[256:288].astype(jnp.float32)[brick * 8 : brick * 8 + 8]]
        flags += [slot_flags(source_ref, slot_index(brick, r)) for r in range(4)]
        flags += [after_ref[256:288].astype(jnp.float32)[brick * 8 : brick * 8 + 8]]
        ref[320:368] = jnp.concatenate(flags, axis=0).astype(jnp.bfloat16)
    face_out(base_ref[1], low_ref, high_ref, even_out, odd_out)


def edge_call(counts, base, source, block, even, odd):
    smem = pl.BlockSpec(memory_space=pltpu.SMEM)
    vmem = pl.BlockSpec(memory_space=pltpu.VMEM)
    mid = block.shape[1]
    return pl.pallas_call(
        functools.partial(edge_kernel, counts),
        in_specs=[smem, smem, vmem, vmem, vmem],
        out_specs=[vmem] * 4,
        out_shape=[
            jax.ShapeDtypeStruct((rows, mid), jnp.bfloat16) for rows in (288, 288, 368, 368)
        ],
        scratch_shapes=[pltpu.VMEM((368, mid), jnp.bfloat16)] * 2,
        compiler_params=pltpu.CompilerParams(vmem_limit_bytes=VMEM_LIMIT),
        name="edge",
    )(base, source, block, even, odd)


def gather_weights(w_ref, wide_ref):
    width = w_ref.shape[2]
    for tap in range(9):
        for column in range(3):
            wide_ref[tap * width : (tap + 1) * width, column * width : (column + 1) * width] = (
                w_ref[tap * 3 + column]
            )


def as_rows(value):
    value = value.astype(jnp.float32)
    return value.reshape(value.shape[0] // COLS, COLS, value.shape[1])


def moved_rows(rows):
    empty = jnp.zeros((1,) + rows.shape[1:], jnp.float32)
    return jnp.concatenate([rows[1:], empty], axis=0)


def as_tiles(rows):
    return rows.reshape(rows.shape[0] * COLS, rows.shape[2]).astype(jnp.bfloat16)


def multiply_taps(lhs, wide_ref):
    width = wide_ref.shape[1] // 3
    wide = jnp.dot(lhs, wide_ref[...], preferred_element_type=jnp.float32)
    wide = wide.reshape(lhs.shape[0] // COLS, COLS, 3 * width)
    column = lax.broadcasted_iota(jnp.int32, (lhs.shape[0] // COLS, COLS, width), 1)
    left = jnp.where(column == 0, 0.0, pltpu.roll(wide[:, :, :width], 1, 1))
    right = jnp.where(column == COLS - 1, 0.0, pltpu.roll(wide[:, :, 2 * width :], COLS - 1, 1))
    return left + wide[:, :, width : 2 * width] + right


def plane_taps(here_ref, next_ref, first, planes, rows):
    taps = []
    for dd in range(3):
        span = slice(first + dd, first + dd + planes)
        taps += [
            here_ref[span, 0:rows, :],
            next_ref[span, 0:rows, :],
            here_ref[span, 16 : rows + 16, :],
        ]
    lhs = jnp.concatenate(taps, axis=2)
    return lhs.reshape(planes * rows, lhs.shape[2])


def conv_planes(here_ref, next_ref, wide_ref, first, planes, rows):
    return multiply_taps(plane_taps(here_ref, next_ref, first, planes, rows), wide_ref)


def activate(value, flags):
    return value / (1.0 + jnp.exp(-value)) * flags


def spread_flags(flags, repeats):
    return jnp.concatenate(
        [jnp.broadcast_to(flag[None], (count,) + flag.shape) for flag, count in zip(flags, repeats)],
        axis=0,
    )


def inner_planes(source_ref, block_ref, wide1_ref, hidden_ref, here, moved, groups):
    width = block_ref.shape[1]
    base = groups[0][0] - 1
    for d in range(base, groups[-1][0] + groups[-1][1] + 1):
        plane = block_ref[d * 128 : (d + 1) * 128]
        here[d - base] = plane
        moved[d - base] = as_tiles(moved_rows(as_rows(plane)))
    inner = SIDE - 2
    rows = inner * COLS
    for first, planes in groups:
        value = conv_planes(here, moved, wide1_ref, first - 1 - base, planes, rows)
        value = value.reshape(planes, inner, COLS, width)
        flags = [slot_flags(source_ref, slot_index(first // 4, r)) for r in range(4)]
        value = activate(value, spread_flags(flags, (3, 4, 4, 3))[None])
        hidden_ref[first - 1 - base : first - 1 - base + planes] = value.reshape(
            planes, rows, width
        ).astype(jnp.bfloat16)


def inner_kernel(groups, source_ref, block_ref, wide1_ref, hidden_ref, here, moved):
    inner_planes(source_ref, block_ref, wide1_ref, hidden_ref, here, moved, groups)


def conv_cost(rows, width):
    return pl.CostEstimate(
        flops=2 * rows * 27 * width * width, bytes_accessed=27 * width * width * 4, transcendentals=0
    )


def inner_call(source, block, wide1, groups):
    mid = block.shape[1]
    smem = pl.BlockSpec(memory_space=pltpu.SMEM)
    vmem = pl.BlockSpec(memory_space=pltpu.VMEM)
    rows = (SIDE - 2) * COLS
    planes = sum(count for _, count in groups)
    return pl.pallas_call(
        functools.partial(inner_kernel, groups),
        in_specs=[smem, vmem, vmem],
        out_specs=vmem,
        out_shape=jax.ShapeDtypeStruct((planes, rows, mid), jnp.bfloat16),
        scratch_shapes=[pltpu.VMEM((planes + 2, SIDE * COLS, mid), jnp.bfloat16)] * 2,
        compiler_params=pltpu.CompilerParams(vmem_limit_bytes=VMEM_LIMIT),
        cost_estimate=conv_cost(planes * rows, mid),
        name="inner",
    )(source, block, wide1)


def side_taps(low, high):
    mixed = as_tiles(
        jnp.concatenate(
            [as_rows(low).reshape(-1, 2, COLS, 128)[:, 1:], as_rows(high).reshape(-1, 2, COLS, 128)[:, :1]],
            axis=1,
        ).reshape(-1, COLS, 128)
    )
    return low, mixed, high


def depth_taps(taps, planes):
    parts = [tap[dd * 16 : (dd + planes) * 16] for dd in range(3) for tap in taps]
    return jnp.concatenate(parts, axis=1)


def coarse_rows(source_ref, block_ref, value, depth_brick):
    width = block_ref.shape[1]
    value = value.reshape(4, SIDE, COLS, width)
    rows = slice(depth_brick * 512, (depth_brick + 1) * 512)
    own = block_ref[rows].astype(jnp.float32).reshape(4, SIDE, COLS, width)
    flags = [slot_flags(source_ref, slot_index(depth_brick, r)) for r in range(4)]
    return (value + own) * spread_flags(flags, (4, 4, 4, 4))[None]


def middle_kernel(source_ref, *refs):
    block_ref, before_ref, after_ref, early_ref, wide1_ref, wide2_ref = refs[:6]
    h_here, h_next, coarse_ref, side, late, here, moved = refs[6:]
    width = block_ref.shape[1]
    inner = SIDE - 2
    inner_planes(source_ref, block_ref, wide1_ref, late, here, moved, LATE)

    low = jnp.concatenate([block_ref[d * 128 : d * 128 + 16] for d in range(SIDE)], axis=0)
    high = jnp.concatenate([block_ref[d * 128 + 112 : d * 128 + 128] for d in range(SIDE)], axis=0)
    left = depth_taps(side_taps(before_ref[0:256], low), inner)
    right = depth_taps(side_taps(high, after_ref[0:256]), inner)
    value = multiply_taps(jnp.concatenate([left, right], axis=0), wide1_ref)
    depths = (3, 4, 4, 3)
    edge_flags = (as_rows(before_ref[256:288]), as_rows(after_ref[256:288]))
    flags = []
    for end, row_brick in ((0, 0), (1, 3)):
        own = [slot_flags(source_ref, slot_index(d, row_brick)) for d in range(4)]
        pairs = [jnp.stack([edge_flags[end][d], own[d]][:: 1 - 2 * end], axis=0) for d in range(4)]
        flags.append(spread_flags(pairs, depths))
    value = activate(value.reshape(2, inner, 2, COLS, width), jnp.stack(flags, axis=0))
    side[...] = value.reshape(2, inner, 16, width).astype(jnp.bfloat16)
    centres = [ref[k] for ref in (early_ref, late) for k in range(ref.shape[0])]
    for d in range(inner):
        plane = jnp.concatenate([side[0, d], centres[d], side[1, d]], axis=0)
        h_here[d] = plane
        h_next[d] = as_tiles(moved_rows(as_rows(plane)))

    for depth_brick in (1, 2):
        value = conv_planes(h_here, h_next, wide2_ref, depth_brick * 4 - 2, 4, SIDE * COLS)
        value = coarse_rows(source_ref, block_ref, value, depth_brick)
        rows = slice((depth_brick - 1) * 512, depth_brick * 512)
        coarse_ref[rows] = value.reshape(512, width).astype(jnp.bfloat16)


def middle_call(source, block, before, after, early, wide1, wide2):
    mid = block.shape[1]
    smem = pl.BlockSpec(memory_space=pltpu.SMEM)
    vmem = pl.BlockSpec(memory_space=pltpu.VMEM)
    inner = SIDE - 2
    hidden = (inner, HID * COLS, mid)
    return pl.pallas_call(
        middle_kernel,
        in_specs=[smem] + [vmem] * 6,
        out_specs=[vmem] * 3,
        out_shape=[
            jax.ShapeDtypeStruct(shape, jnp.bfloat16) for shape in (hidden, hidden, (1024, mid))
        ],
        scratch_shapes=[
            pltpu.VMEM((2, inner, 16, mid), jnp.bfloat16),
            pltpu.VMEM((LATE_PLANES, inner * COLS, mid), jnp.bfloat16),
            pltpu.VMEM((LATE_PLANES + 2, SIDE * COLS, mid), jnp.bfloat16),
            pltpu.VMEM((LATE_PLANES + 2, SIDE * COLS, mid), jnp.bfloat16),
        ],
        compiler_params=pltpu.CompilerParams(vmem_limit_bytes=VMEM_LIMIT),
        cost_estimate=conv_cost(inner * (4 + LATE_PLANES) * COLS + 1024, mid),
        name="middle",
    )(source, block, before, after, early, wide1, wide2)


def scatter_bricks(source_ref, stage, value, depth_brick):
    width = value.shape[3]
    half = low_half((4, 2, COLS, width))
    for r in range(4):
        part = value[:, r * 4 : (r + 1) * 4].reshape(4, 2, 2, COLS, width)
        even, odd = part[:, :, 0], part[:, :, 1]
        b0 = jnp.where(half, even, pltpu.roll(odd, 4, 2))
        b1 = jnp.where(half, pltpu.roll(even, 4, 2), odd)
        slot = slot_index(depth_brick, r)
        for k, brick in enumerate((b0, b1)):
            source = source_ref[slot + k]
            row = pl.multiple_of(jnp.where(source >= 0, source, K * CAP) * CELLS, CELLS)
            stage[pl.ds(row, CELLS), :] = brick.reshape(CELLS, width).astype(jnp.bfloat16)


def final_kernel(count, base_ref, source_ref, *refs):
    block_ref, before_ref, after_ref, even_ref, odd_ref = refs[:5]
    mid_here, mid_next, mid_ref, wide1_ref, wide2_ref, first_ref, last_ref = refs[5:12]
    backs = refs[12 : 12 + K]
    x_here, x_next, h_here, h_next, stage, under_ref, over_ref = refs[12 + K :]
    width = block_ref.shape[1]
    stage[...] = jnp.zeros(stage.shape, jnp.bfloat16)
    face_in(base_ref[1], count, even_ref, odd_ref, under_ref, over_ref)
    flags_before = as_rows(before_ref[256:288])
    flags_after = as_rows(after_ref[256:288])
    spread = []
    for end, ref in ((0, under_ref), (1, over_ref)):
        own = []
        for d in (0, 1) if end == 0 else (SIDE - 2, SIDE - 1):
            edge = slice(d * 16, (d + 1) * 16)
            own.append(
                jnp.concatenate(
                    [before_ref[edge], block_ref[d * 128 : (d + 1) * 128], after_ref[edge]], axis=0
                )
            )
        far = [ref[k * 160 : (k + 1) * 160] for k in range(2)]
        for index, plane in enumerate(far + own if end == 0 else own + far):
            x_here[end * 4 + index] = plane
            x_next[end * 4 + index] = as_tiles(moved_rows(as_rows(plane)))
        far_flags = as_rows(ref[320:368])
        brick = 0 if end == 0 else 3
        own_flags = [flags_before[brick]]
        own_flags += [slot_flags(source_ref, slot_index(brick, r)) for r in range(4)]
        own_flags += [flags_after[brick]]
        pair = [
            spread_flags([far_flags[r] for r in range(6)], (1, 4, 4, 4, 4, 1)),
            spread_flags(own_flags, (1, 4, 4, 4, 4, 1)),
        ]
        spread += pair if end == 0 else pair[::-1]
    lhs = [plane_taps(x_here, x_next, first, 2, HID * COLS) for first in (0, 4)]
    value = multiply_taps(jnp.concatenate(lhs, axis=0), wide1_ref)
    value = activate(value.reshape(4, HID, COLS, width), jnp.stack(spread, axis=0))
    for k, index in enumerate((0, 1, 10, 11)):
        h_here[index] = as_tiles(value[k])
        h_next[index] = as_tiles(moved_rows(value[k]))
    for k in range(4):
        for index, source in ((2 + k, k), (6 + k, SIDE - 6 + k)):
            h_here[index] = mid_here[source]
            h_next[index] = mid_next[source]
    for depth_brick in (1, 2):
        rows = slice((depth_brick - 1) * 512, depth_brick * 512)
        done = mid_ref[rows].astype(jnp.float32).reshape(4, SIDE, COLS, width)
        scatter_bricks(source_ref, stage, done, depth_brick)
    for depth_brick, ref in ((0, first_ref), (3, last_ref)):
        value = conv_planes(h_here, h_next, wide2_ref, depth_brick * 2, 4, SIDE * COLS)
        value = coarse_rows(source_ref, block_ref, value, depth_brick)
        ref[...] = value.reshape(512, width).astype(jnp.bfloat16)
        scatter_bricks(source_ref, stage, value, depth_brick)
    for j in range(K):
        backs[j][...] = stage[j * CAP * CELLS : (j + 1) * CAP * CELLS]


def final_call(count, base, source, block, halo, middle, wide1, wide2):
    mid = block.shape[1]
    smem = pl.BlockSpec(memory_space=pltpu.SMEM)
    vmem = pl.BlockSpec(memory_space=pltpu.VMEM)
    return pl.pallas_call(
        functools.partial(final_kernel, count),
        in_specs=[smem, smem] + [vmem] * 10,
        out_specs=[vmem] * (2 + K),
        out_shape=[jax.ShapeDtypeStruct((512, mid), jnp.bfloat16)] * 2
        + [jax.ShapeDtypeStruct((CAP * CELLS, mid), jnp.bfloat16)] * K,
        scratch_shapes=[
            pltpu.VMEM((8, WIDE * COLS, mid), jnp.bfloat16),
            pltpu.VMEM((8, WIDE * COLS, mid), jnp.bfloat16),
            pltpu.VMEM((12, HID * COLS, mid), jnp.bfloat16),
            pltpu.VMEM((12, HID * COLS, mid), jnp.bfloat16),
            pltpu.VMEM(((K * CAP + 1) * CELLS, mid), jnp.bfloat16),
            pltpu.VMEM((368, mid), jnp.bfloat16),
            pltpu.VMEM((368, mid), jnp.bfloat16),
        ],
        compiler_params=pltpu.CompilerParams(vmem_limit_bytes=VMEM_LIMIT),
        cost_estimate=conv_cost(1600, mid),
        name="final",
    )(base, source, block, *halo, *middle, wide1, wide2)


def from_behind(value, axis, steps):
    count = lax.axis_size(axis)
    pairs = [(source, (source + steps) % count) for source in range(count)]
    return lax.ppermute(value, axis, pairs)


def swap_face(face, axis, first):
    count = lax.axis_size(axis)
    partner = list(range(count))
    for i in range(first, count - 1, 2):
        partner[i], partner[i + 1] = i + 1, i
    return lax.ppermute(face, axis, list(enumerate(partner)))


def shards(fine, fine_mask, slot_source, w_down, w_first, w_second, w_up):
    mid = w_down.shape[1]
    base = jnp.stack([lax.axis_index("xy"), lax.axis_index("gz")]).astype(jnp.int32)
    counts = (lax.axis_size("gz"), lax.axis_size("xy"))
    sent = down_call(fine, fine_mask, w_down, SENT)
    arrived = {j: from_behind(sent[j], "xy", j) for j in SENT}
    later = (arrived[SENT[2]], fine, fine_mask, w_down, w_first, w_second)
    arrived[SENT[2]], *later = lax.optimization_barrier(later)
    prepared = lax.optimization_barrier(tuple(prepare_call(*later)))
    arrived[0], mask, wide1, wide2 = prepared
    block, even, odd = place_call(base, slot_source, [arrived[j] for j in range(K)])
    even = swap_face(even, "xy", 0)
    odd = swap_face(odd, "xy", 1)
    early = inner_call(slot_source, block, wide1, EARLY)
    even, odd, early = lax.optimization_barrier((even, odd, early))
    before, after, even, odd = edge_call(counts, base, slot_source, block, even, odd)
    even = swap_face(even, "gz", 0)
    odd = swap_face(odd, "gz", 1)
    middle = middle_call(slot_source, block, before, after, early, wide1, wide2)
    first, last, *back = final_call(
        counts[0], base, slot_source, block, (before, after, even, odd), middle, wide1, wide2
    )
    octant = {j: from_behind(back[j], "xy", -j) for j in RETURNED[:5]}
    for done, j in zip(RETURNED, RETURNED[5:]):
        octant[done], value = lax.optimization_barrier((octant[done], back[j]))
        octant[j] = from_behind(value, "xy", -j)
    octant[0] = back[0]
    octant[7], *pieces = lax.optimization_barrier((octant[7], first, middle[2], last))
    coarse = jnp.concatenate(pieces, axis=0)
    fine_out = None
    for block_indices in ((3,), (2, 1), (0,)):
        octants = [octant[2 * k + part] for k in block_indices for part in range(2)]
        fine_out = up_call(fine, mask, w_up, octants, block_indices[0], fine_out)
    return fine_out, coarse.reshape(SIDE, SIDE, COLS, mid)


def solution(mesh):
    placed = (
        P(("gz", "xy"), None, None),
        P(("gz", "xy"), None),
        P(("gz", "xy")),
        P(),
        P(),
        P(),
        P(),
    )
    return jax.shard_map(
        shards,
        mesh=mesh,
        in_specs=placed,
        out_specs=(P(("gz", "xy"), None, None), P("gz", "xy", None, None)),
        check_vma=False,
    )
```

```python
import functools

import jax
import jax.numpy as jnp
from jax import lax
from jax.experimental import pallas as pl
from jax.experimental.pallas import tpu as pltpu
from jax.sharding import PartitionSpec as P

CAP = 4
K = 8
CELLS = 64
SIDE = 16
COLS = 8
WIDE = SIDE + 4
HID = SIDE + 2
EARLY = ((1, 3), (4, 4), (8, 4))
LATE = ((12, 3),)
LATE_PLANES = 3
SENT = (2, 1, 4, 3, 6, 5, 7)
RETURNED = (6, 7, 4, 5, 2, 3, 1)
DOWN_LIMIT = 62 * 1024 * 1024
VMEM_LIMIT = 24 * 1024 * 1024


def expand_mask(mask):
    bricks = mask.shape[0]
    values = mask.astype(jnp.float32)
    cell = lax.broadcasted_iota(jnp.int32, (16, 128), 0)
    lane = lax.broadcasted_iota(jnp.int32, (16, 128), 1)
    chosen = (cell == lane // 8).astype(jnp.float32)
    parts = [
        values[:, t * 128 : (t + 1) * 128].reshape(bricks, 1, 128) * chosen[None] for t in range(4)
    ]
    spread = jnp.concatenate(parts, axis=1).reshape(bricks * CELLS, 128).astype(jnp.bfloat16)
    source = lax.broadcasted_iota(jnp.int32, (128, 512), 0)
    target = lax.broadcasted_iota(jnp.int32, (128, 512), 1)
    widen = ((source & 7) == (target >> 6)).astype(jnp.bfloat16)
    return jnp.dot(spread, widen, preferred_element_type=jnp.float32)


def down_kernel(offsets, fine_hbm, mask_hbm, w_hbm, *refs):
    count = len(offsets)
    outs = refs[:count]
    fine_ref, mask_ref, w_ref, wide_ref, result_ref, sems, out_sems = refs[count:]
    first = [
        pltpu.make_async_copy(mask_hbm, mask_ref, sems.at[count]),
        pltpu.make_async_copy(w_hbm, w_ref, sems.at[count + 1]),
    ]
    chunks = [
        pltpu.make_async_copy(fine_hbm.at[pl.ds(j * CAP, CAP)], fine_ref.at[k], sems.at[k])
        for k, j in enumerate(offsets)
    ]
    for copy in first + chunks:
        copy.start()
    first[0].wait()
    rows = CAP * CELLS
    for k, j in enumerate(offsets):
        wide_ref[k * rows : (k + 1) * rows] = expand_mask(
            mask_ref[j * CAP : (j + 1) * CAP]
        ).astype(jnp.bfloat16)
    first[1].wait()
    for start in range(0, count, 2):
        group = range(start, min(start + 2, count))
        for k in group:
            chunks[k].wait()
        x = [
            fine_ref[k].reshape(rows, -1) * wide_ref[k * rows : (k + 1) * rows] for k in group
        ]
        y = jnp.dot(jnp.concatenate(x, axis=0), w_ref[...], preferred_element_type=jnp.float32)
        y = y.astype(jnp.bfloat16)
        for part, k in enumerate(group):
            result_ref[k] = y[part * rows : (part + 1) * rows]
            pltpu.make_async_copy(result_ref.at[k], outs[k], out_sems.at[k]).start()
    for k in range(count):
        pltpu.make_async_copy(result_ref.at[k], outs[k], out_sems.at[k]).wait()


def down_call(fine, mask, w, offsets):
    cells, width = fine.shape[1:]
    mid = w.shape[1]
    count = len(offsets)
    rows = count * CAP * cells
    hbm = pl.BlockSpec(memory_space=pltpu.HBM)
    outs = pl.pallas_call(
        functools.partial(down_kernel, offsets),
        in_specs=[hbm, hbm, hbm],
        out_specs=[pl.BlockSpec(memory_space=pl.ANY)] * count,
        out_shape=[jax.ShapeDtypeStruct((CAP * cells, mid), jnp.bfloat16)] * count,
        scratch_shapes=[
            pltpu.VMEM((count, CAP, cells, width), fine.dtype),
            pltpu.VMEM(mask.shape, mask.dtype),
            pltpu.VMEM(w.shape, w.dtype),
            pltpu.VMEM((rows, width), jnp.bfloat16),
            pltpu.VMEM((count, CAP * cells, mid), jnp.bfloat16),
            pltpu.SemaphoreType.DMA((count + 2,)),
            pltpu.SemaphoreType.DMA((count,)),
        ],
        compiler_params=pltpu.CompilerParams(vmem_limit_bytes=DOWN_LIMIT),
        cost_estimate=pl.CostEstimate(
            flops=2 * rows * width * mid, bytes_accessed=rows * width * 2, transcendentals=0
        ),
        name="down",
    )(fine, mask, w)
    return dict(zip(offsets, outs))


def prepare_kernel(
    fine_ref, mask_ref, w_down_ref, w1_ref, w2_ref, own_ref, mask_out, wide1_ref, wide2_ref
):
    gather_weights(w1_ref, wide1_ref)
    gather_weights(w2_ref, wide2_ref)
    step = 8
    for part in range(mask_ref.shape[0] // step):
        rows = slice(part * step * CELLS, (part + 1) * step * CELLS)
        mask_out[rows] = expand_mask(mask_ref[part * step : (part + 1) * step]).astype(jnp.bfloat16)
    rows = CAP * CELLS
    own = fine_ref[...].reshape(rows, -1) * mask_out[:rows]
    own = jnp.dot(own, w_down_ref[...], preferred_element_type=jnp.float32)
    own_ref[...] = own.astype(jnp.bfloat16)


def prepare_call(fine, mask, w_down, w_first, w_second):
    mid = w_first.shape[1]
    vmem = pl.BlockSpec(memory_space=pltpu.VMEM)
    rows = mask.shape[0] * CELLS
    wide = jax.ShapeDtypeStruct((9 * mid, 3 * mid), jnp.bfloat16)
    return pl.pallas_call(
        prepare_kernel,
        grid=(1,),
        in_specs=[pl.BlockSpec((CAP,) + fine.shape[1:], lambda i: (0, 0, 0))] + [vmem] * 4,
        out_specs=[vmem] * 4,
        out_shape=[
            jax.ShapeDtypeStruct((CAP * CELLS, mid), jnp.bfloat16),
            jax.ShapeDtypeStruct((rows, mask.shape[1]), jnp.bfloat16),
            wide,
            wide,
        ],
        compiler_params=pltpu.CompilerParams(vmem_limit_bytes=VMEM_LIMIT),
        cost_estimate=pl.CostEstimate(
            flops=2 * rows * mask.shape[1] * 128, bytes_accessed=rows * mask.shape[1] * 2, transcendentals=0
        ),
        name="prepare",
    )(fine, mask, w_down, w_first, w_second)


def up_kernel(offsets, fine_ref, mask_ref, w_ref, *refs):
    out_ref = refs[-1]
    step = pl.program_id(0)
    bricks, cells, width = fine_ref.shape
    count = bricks // CAP
    steps = offsets // count
    for part in range(count):
        octant = refs[part][...]
        for other in range(1, steps):
            octant = jnp.where(step == other, refs[other * count + part][...], octant)
        rows = slice(part * CAP * cells, (part + 1) * CAP * cells)
        up = jnp.dot(octant, w_ref[...], preferred_element_type=jnp.float32)
        fine = fine_ref[part * CAP : (part + 1) * CAP].reshape(CAP * cells, width)
        mask = mask_ref[rows].astype(jnp.float32)
        out = jnp.where(mask > 0.5, fine.astype(jnp.float32) + up, 0.0)
        out_ref[part * CAP : (part + 1) * CAP] = out.astype(jnp.bfloat16).reshape(CAP, cells, width)


def up_call(fine, mask, w, octants, first, partial):
    bricks, cells, width = fine.shape
    mid = w.shape[0]
    step = 8

    def place(i):
        return first - i

    count = len(octants)
    partials = [] if partial is None else [partial]
    return pl.pallas_call(
        functools.partial(up_kernel, count),
        grid=(count * CAP // step,),
        in_specs=[
            pl.BlockSpec((step, cells, width), lambda i: (place(i), 0, 0)),
            pl.BlockSpec((step * cells, width), lambda i: (place(i), 0)),
            pl.BlockSpec((mid, width), lambda i: (0, 0)),
        ]
        + [pl.BlockSpec((CAP * cells, mid), lambda i: (0, 0))] * count
        + [pl.BlockSpec(memory_space=pl.ANY)] * len(partials),
        out_specs=pl.BlockSpec((step, cells, width), lambda i: (place(i), 0, 0)),
        out_shape=jax.ShapeDtypeStruct(fine.shape, jnp.bfloat16),
        input_output_aliases={3 + count: 0} if partials else {},
        compiler_params=pltpu.CompilerParams(vmem_limit_bytes=VMEM_LIMIT),
        cost_estimate=pl.CostEstimate(
            flops=bricks * cells * width * mid, bytes_accessed=bricks * cells * width * 2, transcendentals=0
        ),
        name="up",
    )(fine, mask, w, *octants, *partials)


def low_half(shape):
    return lax.broadcasted_iota(jnp.int32, shape, len(shape) - 2) < 4


def slot_flags(source_ref, first):
    pair = [jnp.where(source_ref[first + k] >= 0, 1.0, 0.0).astype(jnp.float32) for k in range(2)]
    return jnp.where(low_half((8, 128)), pair[0], pair[1])


def slot_index(depth_brick, row_brick):
    pd, qd = divmod(depth_brick, 2)
    pr, qr = divmod(row_brick, 2)
    return (pd * 2 + pr) * 8 + qd * 4 + qr * 2


def take_brick(source_ref, arrived, slot):
    value = source_ref[slot]
    first = pl.multiple_of(jnp.maximum(value, 0) * CELLS, CELLS)
    brick = arrived[pl.ds(first, CELLS), :].astype(jnp.float32)
    return jnp.where(value >= 0, brick, 0.0).reshape(8, 8, 128)


def place_kernel(base_ref, source_ref, *refs):
    block_ref, even_ref, odd_ref, low_ref, high_ref, arrived = refs[K:]
    for k, j in enumerate(SENT + (0,)):
        arrived[j * CAP * CELLS : (j + 1) * CAP * CELLS] = refs[k][...]
    half = low_half((8, 8, 128))
    for depth_brick in range(4):
        for row_brick in range(4):
            slot = slot_index(depth_brick, row_brick)
            b0 = take_brick(source_ref, arrived, slot)
            b1 = take_brick(source_ref, arrived, slot + 1)
            even = jnp.where(half, b0, pltpu.roll(b1, 4, 1))
            odd = jnp.where(half, pltpu.roll(b0, 4, 1), b1)
            both = jnp.stack([even, odd], axis=1).reshape(4, 32, 128).astype(jnp.bfloat16)
            for vd in range(4):
                row = ((depth_brick * 4 + vd) * SIDE + row_brick * 4) * COLS
                block_ref[row : row + 32] = both[vd]
                place = (depth_brick * 4 + vd) * 16
                if row_brick == 0:
                    low_ref[place : place + 16] = both[vd, :16]
                if row_brick == 3:
                    high_ref[place : place + 16] = both[vd, 16:]
    for row_brick, ref in ((0, low_ref), (3, high_ref)):
        flags = [slot_flags(source_ref, slot_index(d, row_brick)) for d in range(4)]
        ref[256:288] = jnp.concatenate(flags, axis=0).astype(jnp.bfloat16)
    face_out(base_ref[0], low_ref, high_ref, even_ref, odd_ref)


def face_out(index, low_ref, high_ref, even_ref, odd_ref):
    is_even = index % 2 == 0
    even_ref[...] = jnp.where(is_even, high_ref[...], low_ref[...])
    odd_ref[...] = jnp.where(is_even, low_ref[...], high_ref[...])


def face_in(index, count, even_ref, odd_ref, low_ref, high_ref):
    is_even = index % 2 == 0
    empty = jnp.zeros(low_ref.shape, low_ref.dtype)
    low = jnp.where(is_even, odd_ref[...], even_ref[...])
    high = jnp.where(is_even, even_ref[...], odd_ref[...])
    low_ref[...] = jnp.where(index == 0, empty, low)
    high_ref[...] = jnp.where(index == count - 1, empty, high)


def place_call(base, source, arrived):
    mid = arrived[0].shape[1]
    smem = pl.BlockSpec(memory_space=pltpu.SMEM)
    vmem = pl.BlockSpec(memory_space=pltpu.VMEM)
    return pl.pallas_call(
        place_kernel,
        in_specs=[smem, smem] + [vmem] * K,
        out_specs=[vmem] * 3,
        out_shape=[
            jax.ShapeDtypeStruct((rows, mid), jnp.bfloat16)
            for rows in (SIDE * SIDE * COLS, 288, 288)
        ],
        scratch_shapes=[
            pltpu.VMEM((288, mid), jnp.bfloat16),
            pltpu.VMEM((288, mid), jnp.bfloat16),
            pltpu.VMEM((K * CAP * CELLS, mid), jnp.bfloat16),
        ],
        compiler_params=pltpu.CompilerParams(vmem_limit_bytes=VMEM_LIMIT),
        name="place",
    )(base, source, *arrived)


def edge_kernel(
    counts,
    base_ref,
    source_ref,
    block_ref,
    even_ref,
    odd_ref,
    before_ref,
    after_ref,
    even_out,
    odd_out,
    low_ref,
    high_ref,
):
    face_in(base_ref[0], counts[1], even_ref, odd_ref, before_ref, after_ref)
    for ref, planes, brick in ((low_ref, (0, 1), 0), (high_ref, (SIDE - 2, SIDE - 1), 3)):
        for k, plane in enumerate(planes):
            start = k * WIDE * COLS
            ref[start : start + 16] = before_ref[plane * 16 : plane * 16 + 16]
            ref[start + 16 : start + 144] = block_ref[plane * 128 : plane * 128 + 128]
            ref[start + 144 : start + 160] = after_ref[plane * 16 : plane * 16 + 16]
        flags = [before_ref[256:288].astype(jnp.float32)[brick * 8 : brick * 8 + 8]]
        flags += [slot_flags(source_ref, slot_index(brick, r)) for r in range(4)]
        flags += [after_ref[256:288].astype(jnp.float32)[brick * 8 : brick * 8 + 8]]
        ref[320:368] = jnp.concatenate(flags, axis=0).astype(jnp.bfloat16)
    face_out(base_ref[1], low_ref, high_ref, even_out, odd_out)


def edge_call(counts, base, source, block, even, odd):
    smem = pl.BlockSpec(memory_space=pltpu.SMEM)
    vmem = pl.BlockSpec(memory_space=pltpu.VMEM)
    mid = block.shape[1]
    return pl.pallas_call(
        functools.partial(edge_kernel, counts),
        in_specs=[smem, smem, vmem, vmem, vmem],
        out_specs=[vmem] * 4,
        out_shape=[
            jax.ShapeDtypeStruct((rows, mid), jnp.bfloat16) for rows in (288, 288, 368, 368)
        ],
        scratch_shapes=[pltpu.VMEM((368, mid), jnp.bfloat16)] * 2,
        compiler_params=pltpu.CompilerParams(vmem_limit_bytes=VMEM_LIMIT),
        name="edge",
    )(base, source, block, even, odd)


def gather_weights(w_ref, wide_ref):
    width = w_ref.shape[2]
    for tap in range(9):
        for column in range(3):
            wide_ref[tap * width : (tap + 1) * width, column * width : (column + 1) * width] = (
                w_ref[tap * 3 + column]
            )


def as_rows(value):
    value = value.astype(jnp.float32)
    return value.reshape(value.shape[0] // COLS, COLS, value.shape[1])


def moved_rows(rows):
    empty = jnp.zeros((1,) + rows.shape[1:], jnp.float32)
    return jnp.concatenate([rows[1:], empty], axis=0)


def as_tiles(rows):
    return rows.reshape(rows.shape[0] * COLS, rows.shape[2]).astype(jnp.bfloat16)


def multiply_taps(lhs, wide_ref):
    width = wide_ref.shape[1] // 3
    wide = jnp.dot(lhs, wide_ref[...], preferred_element_type=jnp.float32)
    wide = wide.reshape(lhs.shape[0] // COLS, COLS, 3 * width)
    column = lax.broadcasted_iota(jnp.int32, (lhs.shape[0] // COLS, COLS, width), 1)
    left = jnp.where(column == 0, 0.0, pltpu.roll(wide[:, :, :width], 1, 1))
    right = jnp.where(column == COLS - 1, 0.0, pltpu.roll(wide[:, :, 2 * width :], COLS - 1, 1))
    return left + wide[:, :, width : 2 * width] + right


def plane_taps(here_ref, next_ref, first, planes, rows):
    taps = []
    for dd in range(3):
        span = slice(first + dd, first + dd + planes)
        taps += [
            here_ref[span, 0:rows, :],
            next_ref[span, 0:rows, :],
            here_ref[span, 16 : rows + 16, :],
        ]
    lhs = jnp.concatenate(taps, axis=2)
    return lhs.reshape(planes * rows, lhs.shape[2])


def conv_planes(here_ref, next_ref, wide_ref, first, planes, rows):
    return multiply_taps(plane_taps(here_ref, next_ref, first, planes, rows), wide_ref)


def activate(value, flags):
    return value / (1.0 + jnp.exp(-value)) * flags


def spread_flags(flags, repeats):
    return jnp.concatenate(
        [jnp.broadcast_to(flag[None], (count,) + flag.shape) for flag, count in zip(flags, repeats)],
        axis=0,
    )


def inner_planes(source_ref, block_ref, wide1_ref, hidden_ref, here, moved, groups):
    width = block_ref.shape[1]
    base = groups[0][0] - 1
    for d in range(base, groups[-1][0] + groups[-1][1] + 1):
        plane = block_ref[d * 128 : (d + 1) * 128]
        here[d - base] = plane
        moved[d - base] = as_tiles(moved_rows(as_rows(plane)))
    inner = SIDE - 2
    rows = inner * COLS
    for first, planes in groups:
        value = conv_planes(here, moved, wide1_ref, first - 1 - base, planes, rows)
        value = value.reshape(planes, inner, COLS, width)
        flags = [slot_flags(source_ref, slot_index(first // 4, r)) for r in range(4)]
        value = activate(value, spread_flags(flags, (3, 4, 4, 3))[None])
        hidden_ref[first - 1 - base : first - 1 - base + planes] = value.reshape(
            planes, rows, width
        ).astype(jnp.bfloat16)


def inner_kernel(groups, source_ref, block_ref, wide1_ref, hidden_ref, here, moved):
    inner_planes(source_ref, block_ref, wide1_ref, hidden_ref, here, moved, groups)


def conv_cost(rows, width):
    return pl.CostEstimate(
        flops=2 * rows * 27 * width * width, bytes_accessed=27 * width * width * 4, transcendentals=0
    )


def inner_call(source, block, wide1, groups):
    mid = block.shape[1]
    smem = pl.BlockSpec(memory_space=pltpu.SMEM)
    vmem = pl.BlockSpec(memory_space=pltpu.VMEM)
    rows = (SIDE - 2) * COLS
    planes = sum(count for _, count in groups)
    return pl.pallas_call(
        functools.partial(inner_kernel, groups),
        in_specs=[smem, vmem, vmem],
        out_specs=vmem,
        out_shape=jax.ShapeDtypeStruct((planes, rows, mid), jnp.bfloat16),
        scratch_shapes=[pltpu.VMEM((planes + 2, SIDE * COLS, mid), jnp.bfloat16)] * 2,
        compiler_params=pltpu.CompilerParams(vmem_limit_bytes=VMEM_LIMIT),
        cost_estimate=conv_cost(planes * rows, mid),
        name="inner",
    )(source, block, wide1)


def side_taps(low, high):
    mixed = as_tiles(
        jnp.concatenate(
            [as_rows(low).reshape(-1, 2, COLS, 128)[:, 1:], as_rows(high).reshape(-1, 2, COLS, 128)[:, :1]],
            axis=1,
        ).reshape(-1, COLS, 128)
    )
    return low, mixed, high


def depth_taps(taps, planes):
    parts = [tap[dd * 16 : (dd + planes) * 16] for dd in range(3) for tap in taps]
    return jnp.concatenate(parts, axis=1)


def coarse_rows(source_ref, block_ref, value, depth_brick):
    width = block_ref.shape[1]
    value = value.reshape(4, SIDE, COLS, width)
    rows = slice(depth_brick * 512, (depth_brick + 1) * 512)
    own = block_ref[rows].astype(jnp.float32).reshape(4, SIDE, COLS, width)
    flags = [slot_flags(source_ref, slot_index(depth_brick, r)) for r in range(4)]
    return (value + own) * spread_flags(flags, (4, 4, 4, 4))[None]


def middle_kernel(source_ref, *refs):
    block_ref, before_ref, after_ref, early_ref, wide1_ref, wide2_ref = refs[:6]
    h_here, h_next, coarse_ref, side, late, here, moved = refs[6:]
    width = block_ref.shape[1]
    inner = SIDE - 2
    inner_planes(source_ref, block_ref, wide1_ref, late, here, moved, LATE)

    low = jnp.concatenate([block_ref[d * 128 : d * 128 + 16] for d in range(SIDE)], axis=0)
    high = jnp.concatenate([block_ref[d * 128 + 112 : d * 128 + 128] for d in range(SIDE)], axis=0)
    left = depth_taps(side_taps(before_ref[0:256], low), inner)
    right = depth_taps(side_taps(high, after_ref[0:256]), inner)
    value = multiply_taps(jnp.concatenate([left, right], axis=0), wide1_ref)
    depths = (3, 4, 4, 3)
    edge_flags = (as_rows(before_ref[256:288]), as_rows(after_ref[256:288]))
    flags = []
    for end, row_brick in ((0, 0), (1, 3)):
        own = [slot_flags(source_ref, slot_index(d, row_brick)) for d in range(4)]
        pairs = [jnp.stack([edge_flags[end][d], own[d]][:: 1 - 2 * end], axis=0) for d in range(4)]
        flags.append(spread_flags(pairs, depths))
    value = activate(value.reshape(2, inner, 2, COLS, width), jnp.stack(flags, axis=0))
    side[...] = value.reshape(2, inner, 16, width).astype(jnp.bfloat16)
    centres = [ref[k] for ref in (early_ref, late) for k in range(ref.shape[0])]
    for d in range(inner):
        plane = jnp.concatenate([side[0, d], centres[d], side[1, d]], axis=0)
        h_here[d] = plane
        h_next[d] = as_tiles(moved_rows(as_rows(plane)))

    for depth_brick in (1, 2):
        value = conv_planes(h_here, h_next, wide2_ref, depth_brick * 4 - 2, 4, SIDE * COLS)
        value = coarse_rows(source_ref, block_ref, value, depth_brick)
        rows = slice((depth_brick - 1) * 512, depth_brick * 512)
        coarse_ref[rows] = value.reshape(512, width).astype(jnp.bfloat16)


def middle_call(source, block, before, after, early, wide1, wide2):
    mid = block.shape[1]
    smem = pl.BlockSpec(memory_space=pltpu.SMEM)
    vmem = pl.BlockSpec(memory_space=pltpu.VMEM)
    inner = SIDE - 2
    hidden = (inner, HID * COLS, mid)
    return pl.pallas_call(
        middle_kernel,
        in_specs=[smem] + [vmem] * 6,
        out_specs=[vmem] * 3,
        out_shape=[
            jax.ShapeDtypeStruct(shape, jnp.bfloat16) for shape in (hidden, hidden, (1024, mid))
        ],
        scratch_shapes=[
            pltpu.VMEM((2, inner, 16, mid), jnp.bfloat16),
            pltpu.VMEM((LATE_PLANES, inner * COLS, mid), jnp.bfloat16),
            pltpu.VMEM((LATE_PLANES + 2, SIDE * COLS, mid), jnp.bfloat16),
            pltpu.VMEM((LATE_PLANES + 2, SIDE * COLS, mid), jnp.bfloat16),
        ],
        compiler_params=pltpu.CompilerParams(vmem_limit_bytes=VMEM_LIMIT),
        cost_estimate=conv_cost(inner * (4 + LATE_PLANES) * COLS + 1024, mid),
        name="middle",
    )(source, block, before, after, early, wide1, wide2)


def scatter_bricks(source_ref, stage, value, depth_brick):
    width = value.shape[3]
    half = low_half((4, 2, COLS, width))
    for r in range(4):
        part = value[:, r * 4 : (r + 1) * 4].reshape(4, 2, 2, COLS, width)
        even, odd = part[:, :, 0], part[:, :, 1]
        b0 = jnp.where(half, even, pltpu.roll(odd, 4, 2))
        b1 = jnp.where(half, pltpu.roll(even, 4, 2), odd)
        slot = slot_index(depth_brick, r)
        for k, brick in enumerate((b0, b1)):
            source = source_ref[slot + k]
            row = pl.multiple_of(jnp.where(source >= 0, source, K * CAP) * CELLS, CELLS)
            stage[pl.ds(row, CELLS), :] = brick.reshape(CELLS, width).astype(jnp.bfloat16)


def final_kernel(count, base_ref, source_ref, *refs):
    block_ref, before_ref, after_ref, even_ref, odd_ref = refs[:5]
    mid_here, mid_next, mid_ref, wide1_ref, wide2_ref, first_ref, last_ref = refs[5:12]
    backs = refs[12 : 12 + K]
    x_here, x_next, h_here, h_next, stage, under_ref, over_ref = refs[12 + K :]
    width = block_ref.shape[1]
    stage[...] = jnp.zeros(stage.shape, jnp.bfloat16)
    face_in(base_ref[1], count, even_ref, odd_ref, under_ref, over_ref)
    flags_before = as_rows(before_ref[256:288])
    flags_after = as_rows(after_ref[256:288])
    spread = []
    for end, ref in ((0, under_ref), (1, over_ref)):
        own = []
        for d in (0, 1) if end == 0 else (SIDE - 2, SIDE - 1):
            edge = slice(d * 16, (d + 1) * 16)
            own.append(
                jnp.concatenate(
                    [before_ref[edge], block_ref[d * 128 : (d + 1) * 128], after_ref[edge]], axis=0
                )
            )
        far = [ref[k * 160 : (k + 1) * 160] for k in range(2)]
        for index, plane in enumerate(far + own if end == 0 else own + far):
            x_here[end * 4 + index] = plane
            x_next[end * 4 + index] = as_tiles(moved_rows(as_rows(plane)))
        far_flags = as_rows(ref[320:368])
        brick = 0 if end == 0 else 3
        own_flags = [flags_before[brick]]
        own_flags += [slot_flags(source_ref, slot_index(brick, r)) for r in range(4)]
        own_flags += [flags_after[brick]]
        pair = [
            spread_flags([far_flags[r] for r in range(6)], (1, 4, 4, 4, 4, 1)),
            spread_flags(own_flags, (1, 4, 4, 4, 4, 1)),
        ]
        spread += pair if end == 0 else pair[::-1]
    lhs = [plane_taps(x_here, x_next, first, 2, HID * COLS) for first in (0, 4)]
    value = multiply_taps(jnp.concatenate(lhs, axis=0), wide1_ref)
    value = activate(value.reshape(4, HID, COLS, width), jnp.stack(spread, axis=0))
    for k, index in enumerate((0, 1, 10, 11)):
        h_here[index] = as_tiles(value[k])
        h_next[index] = as_tiles(moved_rows(value[k]))
    for k in range(4):
        for index, source in ((2 + k, k), (6 + k, SIDE - 6 + k)):
            h_here[index] = mid_here[source]
            h_next[index] = mid_next[source]
    for depth_brick in (1, 2):
        rows = slice((depth_brick - 1) * 512, depth_brick * 512)
        done = mid_ref[rows].astype(jnp.float32).reshape(4, SIDE, COLS, width)
        scatter_bricks(source_ref, stage, done, depth_brick)
    for depth_brick, ref in ((0, first_ref), (3, last_ref)):
        value = conv_planes(h_here, h_next, wide2_ref, depth_brick * 2, 4, SIDE * COLS)
        value = coarse_rows(source_ref, block_ref, value, depth_brick)
        ref[...] = value.reshape(512, width).astype(jnp.bfloat16)
        scatter_bricks(source_ref, stage, value, depth_brick)
    for j in range(K):
        backs[j][...] = stage[j * CAP * CELLS : (j + 1) * CAP * CELLS]


def final_call(count, base, source, block, halo, middle, wide1, wide2):
    mid = block.shape[1]
    smem = pl.BlockSpec(memory_space=pltpu.SMEM)
    vmem = pl.BlockSpec(memory_space=pltpu.VMEM)
    return pl.pallas_call(
        functools.partial(final_kernel, count),
        in_specs=[smem, smem] + [vmem] * 10,
        out_specs=[vmem] * (2 + K),
        out_shape=[jax.ShapeDtypeStruct((512, mid), jnp.bfloat16)] * 2
        + [jax.ShapeDtypeStruct((CAP * CELLS, mid), jnp.bfloat16)] * K,
        scratch_shapes=[
            pltpu.VMEM((8, WIDE * COLS, mid), jnp.bfloat16),
            pltpu.VMEM((8, WIDE * COLS, mid), jnp.bfloat16),
            pltpu.VMEM((12, HID * COLS, mid), jnp.bfloat16),
            pltpu.VMEM((12, HID * COLS, mid), jnp.bfloat16),
            pltpu.VMEM(((K * CAP + 1) * CELLS, mid), jnp.bfloat16),
            pltpu.VMEM((368, mid), jnp.bfloat16),
            pltpu.VMEM((368, mid), jnp.bfloat16),
        ],
        compiler_params=pltpu.CompilerParams(vmem_limit_bytes=VMEM_LIMIT),
        cost_estimate=conv_cost(1600, mid),
        name="final",
    )(base, source, block, *halo, *middle, wide1, wide2)


def from_behind(value, axis, steps):
    count = lax.axis_size(axis)
    pairs = [(source, (source + steps) % count) for source in range(count)]
    return lax.ppermute(value, axis, pairs)


def swap_face(face, axis, first):
    count = lax.axis_size(axis)
    partner = list(range(count))
    for i in range(first, count - 1, 2):
        partner[i], partner[i + 1] = i + 1, i
    return lax.ppermute(face, axis, list(enumerate(partner)))


def shards(fine, fine_mask, slot_source, w_down, w_first, w_second, w_up):
    mid = w_down.shape[1]
    base = jnp.stack([lax.axis_index("xy"), lax.axis_index("gz")]).astype(jnp.int32)
    counts = (lax.axis_size("gz"), lax.axis_size("xy"))
    sent = down_call(fine, fine_mask, w_down, SENT)
    arrived = {j: from_behind(sent[j], "xy", j) for j in SENT}
    later = (arrived[SENT[0]], fine, fine_mask, w_down, w_first, w_second)
    arrived[SENT[0]], *later = lax.optimization_barrier(later)
    prepared = lax.optimization_barrier(tuple(prepare_call(*later)))
    arrived[0], mask, wide1, wide2 = prepared
    block, even, odd = place_call(base, slot_source, [arrived[j] for j in SENT + (0,)])
    even = swap_face(even, "xy", 0)
    odd = swap_face(odd, "xy", 1)
    early = inner_call(slot_source, block, wide1, EARLY)
    even, odd, early = lax.optimization_barrier((even, odd, early))
    before, after, even, odd = edge_call(counts, base, slot_source, block, even, odd)
    even = swap_face(even, "gz", 0)
    odd = swap_face(odd, "gz", 1)
    middle = middle_call(slot_source, block, before, after, early, wide1, wide2)
    first, last, *back = final_call(
        counts[0], base, slot_source, block, (before, after, even, odd), middle, wide1, wide2
    )
    octant = {j: from_behind(back[j], "xy", -j) for j in RETURNED[:5]}
    for done, j in zip(RETURNED, RETURNED[5:]):
        octant[done], value = lax.optimization_barrier((octant[done], back[j]))
        octant[j] = from_behind(value, "xy", -j)
    octant[0] = back[0]
    octant[7], *pieces = lax.optimization_barrier((octant[7], first, middle[2], last))
    coarse = jnp.concatenate(pieces, axis=0)
    fine_out = None
    for block_indices in ((3,), (2, 1, 0)):
        octants = [octant[2 * k + part] for k in block_indices for part in range(2)]
        fine_out = up_call(fine, mask, w_up, octants, block_indices[0], fine_out)
    return fine_out, coarse.reshape(SIDE, SIDE, COLS, mid)


def solution(mesh):
    placed = (
        P(("gz", "xy"), None, None),
        P(("gz", "xy"), None),
        P(("gz", "xy")),
        P(),
        P(),
        P(),
        P(),
    )
    return jax.shard_map(
        shards,
        mesh=mesh,
        in_specs=placed,
        out_specs=(P(("gz", "xy"), None, None), P("gz", "xy", None, None)),
        check_vma=False,
    )
```

```python
import functools

import jax
import jax.numpy as jnp
from jax import lax
from jax.experimental import pallas as pl
from jax.experimental.pallas import tpu as pltpu
from jax.sharding import PartitionSpec as P

CAP = 4
K = 8
CELLS = 64
SIDE = 16
COLS = 8
WIDE = SIDE + 4
HID = SIDE + 2
EARLY = ((1, 3), (4, 4), (8, 4))
LATE = ((12, 3),)
LATE_PLANES = 3
SENT = (4, 3, 5, 2, 6, 1, 7)
RETURNED = (6, 7, 4, 5, 2, 3, 1)
DOWN_LIMIT = 62 * 1024 * 1024
VMEM_LIMIT = 24 * 1024 * 1024


def expand_mask(mask):
    bricks = mask.shape[0]
    values = mask.astype(jnp.float32)
    cell = lax.broadcasted_iota(jnp.int32, (16, 128), 0)
    lane = lax.broadcasted_iota(jnp.int32, (16, 128), 1)
    chosen = (cell == lane // 8).astype(jnp.float32)
    parts = [
        values[:, t * 128 : (t + 1) * 128].reshape(bricks, 1, 128) * chosen[None] for t in range(4)
    ]
    spread = jnp.concatenate(parts, axis=1).reshape(bricks * CELLS, 128).astype(jnp.bfloat16)
    source = lax.broadcasted_iota(jnp.int32, (128, 512), 0)
    target = lax.broadcasted_iota(jnp.int32, (128, 512), 1)
    widen = ((source & 7) == (target >> 6)).astype(jnp.bfloat16)
    return jnp.dot(spread, widen, preferred_element_type=jnp.float32)


def down_kernel(offsets, fine_hbm, mask_hbm, w_hbm, *refs):
    count = len(offsets)
    outs = refs[:count]
    fine_ref, mask_ref, w_ref, wide_ref, result_ref, sems, out_sems = refs[count:]
    first = [
        pltpu.make_async_copy(mask_hbm, mask_ref, sems.at[count]),
        pltpu.make_async_copy(w_hbm, w_ref, sems.at[count + 1]),
    ]
    chunks = [
        pltpu.make_async_copy(fine_hbm.at[pl.ds(j * CAP, CAP)], fine_ref.at[k], sems.at[k])
        for k, j in enumerate(offsets)
    ]
    for copy in first + chunks:
        copy.start()
    first[0].wait()
    rows = CAP * CELLS
    for k, j in enumerate(offsets):
        wide_ref[k * rows : (k + 1) * rows] = expand_mask(
            mask_ref[j * CAP : (j + 1) * CAP]
        ).astype(jnp.bfloat16)
    first[1].wait()
    for start in range(0, count, 2):
        group = range(start, min(start + 2, count))
        for k in group:
            chunks[k].wait()
        x = [
            fine_ref[k].reshape(rows, -1) * wide_ref[k * rows : (k + 1) * rows] for k in group
        ]
        y = jnp.dot(jnp.concatenate(x, axis=0), w_ref[...], preferred_element_type=jnp.float32)
        y = y.astype(jnp.bfloat16)
        for part, k in enumerate(group):
            result_ref[k] = y[part * rows : (part + 1) * rows]
            pltpu.make_async_copy(result_ref.at[k], outs[k], out_sems.at[k]).start()
    for k in range(count):
        pltpu.make_async_copy(result_ref.at[k], outs[k], out_sems.at[k]).wait()


def down_call(fine, mask, w, offsets):
    cells, width = fine.shape[1:]
    mid = w.shape[1]
    count = len(offsets)
    rows = count * CAP * cells
    hbm = pl.BlockSpec(memory_space=pltpu.HBM)
    outs = pl.pallas_call(
        functools.partial(down_kernel, offsets),
        in_specs=[hbm, hbm, hbm],
        out_specs=[pl.BlockSpec(memory_space=pl.ANY)] * count,
        out_shape=[jax.ShapeDtypeStruct((CAP * cells, mid), jnp.bfloat16)] * count,
        scratch_shapes=[
            pltpu.VMEM((count, CAP, cells, width), fine.dtype),
            pltpu.VMEM(mask.shape, mask.dtype),
            pltpu.VMEM(w.shape, w.dtype),
            pltpu.VMEM((rows, width), jnp.bfloat16),
            pltpu.VMEM((count, CAP * cells, mid), jnp.bfloat16),
            pltpu.SemaphoreType.DMA((count + 2,)),
            pltpu.SemaphoreType.DMA((count,)),
        ],
        compiler_params=pltpu.CompilerParams(vmem_limit_bytes=DOWN_LIMIT),
        cost_estimate=pl.CostEstimate(
            flops=2 * rows * width * mid, bytes_accessed=rows * width * 2, transcendentals=0
        ),
        name="down",
    )(fine, mask, w)
    return dict(zip(offsets, outs))


def prepare_kernel(
    fine_ref, mask_ref, w_down_ref, w1_ref, w2_ref, own_ref, mask_out, wide1_ref, wide2_ref
):
    gather_weights(w1_ref, wide1_ref)
    gather_weights(w2_ref, wide2_ref)
    step = 8
    for part in range(mask_ref.shape[0] // step):
        rows = slice(part * step * CELLS, (part + 1) * step * CELLS)
        mask_out[rows] = expand_mask(mask_ref[part * step : (part + 1) * step]).astype(jnp.bfloat16)
    rows = CAP * CELLS
    own = fine_ref[...].reshape(rows, -1) * mask_out[:rows]
    own = jnp.dot(own, w_down_ref[...], preferred_element_type=jnp.float32)
    own_ref[...] = own.astype(jnp.bfloat16)


def prepare_call(fine, mask, w_down, w_first, w_second):
    mid = w_first.shape[1]
    vmem = pl.BlockSpec(memory_space=pltpu.VMEM)
    rows = mask.shape[0] * CELLS
    wide = jax.ShapeDtypeStruct((9 * mid, 3 * mid), jnp.bfloat16)
    return pl.pallas_call(
        prepare_kernel,
        grid=(1,),
        in_specs=[pl.BlockSpec((CAP,) + fine.shape[1:], lambda i: (0, 0, 0))] + [vmem] * 4,
        out_specs=[vmem] * 4,
        out_shape=[
            jax.ShapeDtypeStruct((CAP * CELLS, mid), jnp.bfloat16),
            jax.ShapeDtypeStruct((rows, mask.shape[1]), jnp.bfloat16),
            wide,
            wide,
        ],
        compiler_params=pltpu.CompilerParams(vmem_limit_bytes=VMEM_LIMIT),
        cost_estimate=pl.CostEstimate(
            flops=2 * rows * mask.shape[1] * 128, bytes_accessed=rows * mask.shape[1] * 2, transcendentals=0
        ),
        name="prepare",
    )(fine, mask, w_down, w_first, w_second)


def up_kernel(offsets, fine_ref, mask_ref, w_ref, *refs):
    out_ref, octant_ref = refs[-2:]
    step = pl.program_id(0)
    bricks, cells, width = fine_ref.shape
    count = bricks // CAP
    steps = offsets // count
    for part in range(count):
        for k in range(steps):

            @pl.when(step == k)
            def _():
                octant_ref[part] = refs[k * count + part][...]

    for part in range(count):
        rows = slice(part * CAP * cells, (part + 1) * CAP * cells)
        up = jnp.dot(octant_ref[part], w_ref[...], preferred_element_type=jnp.float32)
        fine = fine_ref[part * CAP : (part + 1) * CAP].reshape(CAP * cells, width)
        mask = mask_ref[rows].astype(jnp.float32)
        out = jnp.where(mask > 0.5, fine.astype(jnp.float32) + up, 0.0)
        out_ref[part * CAP : (part + 1) * CAP] = out.astype(jnp.bfloat16).reshape(CAP, cells, width)


def up_call(fine, mask, w, octants, first, partial):
    bricks, cells, width = fine.shape
    mid = w.shape[0]
    step = 8

    def place(i):
        return first - i

    count = len(octants)
    partials = [] if partial is None else [partial]
    return pl.pallas_call(
        functools.partial(up_kernel, count),
        grid=(count * CAP // step,),
        in_specs=[
            pl.BlockSpec((step, cells, width), lambda i: (place(i), 0, 0)),
            pl.BlockSpec((step * cells, width), lambda i: (place(i), 0)),
            pl.BlockSpec((mid, width), lambda i: (0, 0)),
        ]
        + [pl.BlockSpec((CAP * cells, mid), lambda i: (0, 0))] * count
        + [pl.BlockSpec(memory_space=pl.ANY)] * len(partials),
        out_specs=pl.BlockSpec((step, cells, width), lambda i: (place(i), 0, 0)),
        out_shape=jax.ShapeDtypeStruct(fine.shape, jnp.bfloat16),
        input_output_aliases={3 + count: 0} if partials else {},
        scratch_shapes=[pltpu.VMEM((step // CAP, CAP * cells, mid), jnp.bfloat16)],
        compiler_params=pltpu.CompilerParams(vmem_limit_bytes=VMEM_LIMIT),
        cost_estimate=pl.CostEstimate(
            flops=bricks * cells * width * mid, bytes_accessed=bricks * cells * width * 2, transcendentals=0
        ),
        name="up",
    )(fine, mask, w, *octants, *partials)


def low_half(shape):
    return lax.broadcasted_iota(jnp.int32, shape, len(shape) - 2) < 4


def slot_flags(source_ref, first):
    pair = [jnp.where(source_ref[first + k] >= 0, 1.0, 0.0).astype(jnp.float32) for k in range(2)]
    return jnp.where(low_half((8, 128)), pair[0], pair[1])


def slot_index(depth_brick, row_brick):
    pd, qd = divmod(depth_brick, 2)
    pr, qr = divmod(row_brick, 2)
    return (pd * 2 + pr) * 8 + qd * 4 + qr * 2


def take_brick(source_ref, arrived, slot):
    value = source_ref[slot]
    first = pl.multiple_of(jnp.maximum(value, 0) * CELLS, CELLS)
    brick = arrived[pl.ds(first, CELLS), :].astype(jnp.float32)
    return jnp.where(value >= 0, brick, 0.0).reshape(8, 8, 128)


def place_kernel(base_ref, source_ref, *refs):
    block_ref, even_ref, odd_ref, low_ref, high_ref, arrived = refs[K:]
    for j in range(K):
        arrived[j * CAP * CELLS : (j + 1) * CAP * CELLS] = refs[j][...]
    half = low_half((8, 8, 128))
    for depth_brick in range(4):
        for row_brick in range(4):
            slot = slot_index(depth_brick, row_brick)
            b0 = take_brick(source_ref, arrived, slot)
            b1 = take_brick(source_ref, arrived, slot + 1)
            even = jnp.where(half, b0, pltpu.roll(b1, 4, 1))
            odd = jnp.where(half, pltpu.roll(b0, 4, 1), b1)
            both = jnp.stack([even, odd], axis=1).reshape(4, 32, 128).astype(jnp.bfloat16)
            for vd in range(4):
                row = ((depth_brick * 4 + vd) * SIDE + row_brick * 4) * COLS
                block_ref[row : row + 32] = both[vd]
                place = (depth_brick * 4 + vd) * 16
                if row_brick == 0:
                    low_ref[place : place + 16] = both[vd, :16]
                if row_brick == 3:
                    high_ref[place : place + 16] = both[vd, 16:]
    for row_brick, ref in ((0, low_ref), (3, high_ref)):
        flags = [slot_flags(source_ref, slot_index(d, row_brick)) for d in range(4)]
        ref[256:288] = jnp.concatenate(flags, axis=0).astype(jnp.bfloat16)
    face_out(base_ref[0], low_ref, high_ref, even_ref, odd_ref)


def face_out(index, low_ref, high_ref, even_ref, odd_ref):
    is_even = index % 2 == 0
    even_ref[...] = jnp.where(is_even, high_ref[...], low_ref[...])
    odd_ref[...] = jnp.where(is_even, low_ref[...], high_ref[...])


def face_in(index, count, even_ref, odd_ref, low_ref, high_ref):
    is_even = index % 2 == 0
    empty = jnp.zeros(low_ref.shape, low_ref.dtype)
    low = jnp.where(is_even, odd_ref[...], even_ref[...])
    high = jnp.where(is_even, even_ref[...], odd_ref[...])
    low_ref[...] = jnp.where(index == 0, empty, low)
    high_ref[...] = jnp.where(index == count - 1, empty, high)


def place_call(base, source, arrived):
    mid = arrived[0].shape[1]
    smem = pl.BlockSpec(memory_space=pltpu.SMEM)
    vmem = pl.BlockSpec(memory_space=pltpu.VMEM)
    return pl.pallas_call(
        place_kernel,
        in_specs=[smem, smem] + [vmem] * K,
        out_specs=[vmem] * 3,
        out_shape=[
            jax.ShapeDtypeStruct((rows, mid), jnp.bfloat16)
            for rows in (SIDE * SIDE * COLS, 288, 288)
        ],
        scratch_shapes=[
            pltpu.VMEM((288, mid), jnp.bfloat16),
            pltpu.VMEM((288, mid), jnp.bfloat16),
            pltpu.VMEM((K * CAP * CELLS, mid), jnp.bfloat16),
        ],
        compiler_params=pltpu.CompilerParams(vmem_limit_bytes=VMEM_LIMIT),
        name="place",
    )(base, source, *arrived)


def edge_kernel(
    counts,
    base_ref,
    source_ref,
    block_ref,
    even_ref,
    odd_ref,
    before_ref,
    after_ref,
    even_out,
    odd_out,
    low_ref,
    high_ref,
):
    face_in(base_ref[0], counts[1], even_ref, odd_ref, before_ref, after_ref)
    for ref, planes, brick in ((low_ref, (0, 1), 0), (high_ref, (SIDE - 2, SIDE - 1), 3)):
        for k, plane in enumerate(planes):
            start = k * WIDE * COLS
            ref[start : start + 16] = before_ref[plane * 16 : plane * 16 + 16]
            ref[start + 16 : start + 144] = block_ref[plane * 128 : plane * 128 + 128]
            ref[start + 144 : start + 160] = after_ref[plane * 16 : plane * 16 + 16]
        flags = [before_ref[256:288].astype(jnp.float32)[brick * 8 : brick * 8 + 8]]
        flags += [slot_flags(source_ref, slot_index(brick, r)) for r in range(4)]
        flags += [after_ref[256:288].astype(jnp.float32)[brick * 8 : brick * 8 + 8]]
        ref[320:368] = jnp.concatenate(flags, axis=0).astype(jnp.bfloat16)
    face_out(base_ref[1], low_ref, high_ref, even_out, odd_out)


def edge_call(counts, base, source, block, even, odd):
    smem = pl.BlockSpec(memory_space=pltpu.SMEM)
    vmem = pl.BlockSpec(memory_space=pltpu.VMEM)
    mid = block.shape[1]
    return pl.pallas_call(
        functools.partial(edge_kernel, counts),
        in_specs=[smem, smem, vmem, vmem, vmem],
        out_specs=[vmem] * 4,
        out_shape=[
            jax.ShapeDtypeStruct((rows, mid), jnp.bfloat16) for rows in (288, 288, 368, 368)
        ],
        scratch_shapes=[pltpu.VMEM((368, mid), jnp.bfloat16)] * 2,
        compiler_params=pltpu.CompilerParams(vmem_limit_bytes=VMEM_LIMIT),
        name="edge",
    )(base, source, block, even, odd)


def gather_weights(w_ref, wide_ref):
    width = w_ref.shape[2]
    for tap in range(9):
        for column in range(3):
            wide_ref[tap * width : (tap + 1) * width, column * width : (column + 1) * width] = (
                w_ref[tap * 3 + column]
            )


def as_rows(value):
    value = value.astype(jnp.float32)
    return value.reshape(value.shape[0] // COLS, COLS, value.shape[1])


def moved_rows(rows):
    empty = jnp.zeros((1,) + rows.shape[1:], jnp.float32)
    return jnp.concatenate([rows[1:], empty], axis=0)


def as_tiles(rows):
    return rows.reshape(rows.shape[0] * COLS, rows.shape[2]).astype(jnp.bfloat16)


def multiply_taps(lhs, wide_ref):
    width = wide_ref.shape[1] // 3
    wide = jnp.dot(lhs, wide_ref[...], preferred_element_type=jnp.float32)
    wide = wide.reshape(lhs.shape[0] // COLS, COLS, 3 * width)
    column = lax.broadcasted_iota(jnp.int32, (lhs.shape[0] // COLS, COLS, width), 1)
    left = jnp.where(column == 0, 0.0, pltpu.roll(wide[:, :, :width], 1, 1))
    right = jnp.where(column == COLS - 1, 0.0, pltpu.roll(wide[:, :, 2 * width :], COLS - 1, 1))
    return left + wide[:, :, width : 2 * width] + right


def plane_taps(here_ref, next_ref, first, planes, rows):
    taps = []
    for dd in range(3):
        span = slice(first + dd, first + dd + planes)
        taps += [
            here_ref[span, 0:rows, :],
            next_ref[span, 0:rows, :],
            here_ref[span, 16 : rows + 16, :],
        ]
    lhs = jnp.concatenate(taps, axis=2)
    return lhs.reshape(planes * rows, lhs.shape[2])


def conv_planes(here_ref, next_ref, wide_ref, first, planes, rows):
    return multiply_taps(plane_taps(here_ref, next_ref, first, planes, rows), wide_ref)


def activate(value, flags):
    return value / (1.0 + jnp.exp(-value)) * flags


def spread_flags(flags, repeats):
    return jnp.concatenate(
        [jnp.broadcast_to(flag[None], (count,) + flag.shape) for flag, count in zip(flags, repeats)],
        axis=0,
    )


def inner_planes(source_ref, block_ref, wide1_ref, hidden_ref, here, moved, groups):
    width = block_ref.shape[1]
    base = groups[0][0] - 1
    for d in range(base, groups[-1][0] + groups[-1][1] + 1):
        plane = block_ref[d * 128 : (d + 1) * 128]
        here[d - base] = plane
        moved[d - base] = as_tiles(moved_rows(as_rows(plane)))
    inner = SIDE - 2
    rows = inner * COLS
    for first, planes in groups:
        value = conv_planes(here, moved, wide1_ref, first - 1 - base, planes, rows)
        value = value.reshape(planes, inner, COLS, width)
        flags = [slot_flags(source_ref, slot_index(first // 4, r)) for r in range(4)]
        value = activate(value, spread_flags(flags, (3, 4, 4, 3))[None])
        hidden_ref[first - 1 - base : first - 1 - base + planes] = value.reshape(
            planes, rows, width
        ).astype(jnp.bfloat16)


def inner_kernel(groups, source_ref, block_ref, wide1_ref, hidden_ref, here, moved):
    inner_planes(source_ref, block_ref, wide1_ref, hidden_ref, here, moved, groups)


def conv_cost(rows, width):
    return pl.CostEstimate(
        flops=2 * rows * 27 * width * width, bytes_accessed=27 * width * width * 4, transcendentals=0
    )


def inner_call(source, block, wide1, groups):
    mid = block.shape[1]
    smem = pl.BlockSpec(memory_space=pltpu.SMEM)
    vmem = pl.BlockSpec(memory_space=pltpu.VMEM)
    rows = (SIDE - 2) * COLS
    planes = sum(count for _, count in groups)
    return pl.pallas_call(
        functools.partial(inner_kernel, groups),
        in_specs=[smem, vmem, vmem],
        out_specs=vmem,
        out_shape=jax.ShapeDtypeStruct((planes, rows, mid), jnp.bfloat16),
        scratch_shapes=[pltpu.VMEM((planes + 2, SIDE * COLS, mid), jnp.bfloat16)] * 2,
        compiler_params=pltpu.CompilerParams(vmem_limit_bytes=VMEM_LIMIT),
        cost_estimate=conv_cost(planes * rows, mid),
        name="inner",
    )(source, block, wide1)


def side_taps(low, high):
    mixed = as_tiles(
        jnp.concatenate(
            [as_rows(low).reshape(-1, 2, COLS, 128)[:, 1:], as_rows(high).reshape(-1, 2, COLS, 128)[:, :1]],
            axis=1,
        ).reshape(-1, COLS, 128)
    )
    return low, mixed, high


def depth_taps(taps, planes):
    parts = [tap[dd * 16 : (dd + planes) * 16] for dd in range(3) for tap in taps]
    return jnp.concatenate(parts, axis=1)


def coarse_rows(source_ref, block_ref, value, depth_brick):
    width = block_ref.shape[1]
    value = value.reshape(4, SIDE, COLS, width)
    rows = slice(depth_brick * 512, (depth_brick + 1) * 512)
    own = block_ref[rows].astype(jnp.float32).reshape(4, SIDE, COLS, width)
    flags = [slot_flags(source_ref, slot_index(depth_brick, r)) for r in range(4)]
    return (value + own) * spread_flags(flags, (4, 4, 4, 4))[None]


def middle_kernel(source_ref, *refs):
    block_ref, before_ref, after_ref, early_ref, wide1_ref, wide2_ref = refs[:6]
    h_here, h_next, coarse_ref, side, late, here, moved = refs[6:]
    width = block_ref.shape[1]
    inner = SIDE - 2
    inner_planes(source_ref, block_ref, wide1_ref, late, here, moved, LATE)

    low = jnp.concatenate([block_ref[d * 128 : d * 128 + 16] for d in range(SIDE)], axis=0)
    high = jnp.concatenate([block_ref[d * 128 + 112 : d * 128 + 128] for d in range(SIDE)], axis=0)
    left = depth_taps(side_taps(before_ref[0:256], low), inner)
    right = depth_taps(side_taps(high, after_ref[0:256]), inner)
    value = multiply_taps(jnp.concatenate([left, right], axis=0), wide1_ref)
    depths = (3, 4, 4, 3)
    edge_flags = (as_rows(before_ref[256:288]), as_rows(after_ref[256:288]))
    flags = []
    for end, row_brick in ((0, 0), (1, 3)):
        own = [slot_flags(source_ref, slot_index(d, row_brick)) for d in range(4)]
        pairs = [jnp.stack([edge_flags[end][d], own[d]][:: 1 - 2 * end], axis=0) for d in range(4)]
        flags.append(spread_flags(pairs, depths))
    value = activate(value.reshape(2, inner, 2, COLS, width), jnp.stack(flags, axis=0))
    side[...] = value.reshape(2, inner, 16, width).astype(jnp.bfloat16)
    centres = [ref[k] for ref in (early_ref, late) for k in range(ref.shape[0])]
    for d in range(inner):
        plane = jnp.concatenate([side[0, d], centres[d], side[1, d]], axis=0)
        h_here[d] = plane
        h_next[d] = as_tiles(moved_rows(as_rows(plane)))

    for depth_brick in (1, 2):
        value = conv_planes(h_here, h_next, wide2_ref, depth_brick * 4 - 2, 4, SIDE * COLS)
        value = coarse_rows(source_ref, block_ref, value, depth_brick)
        rows = slice((depth_brick - 1) * 512, depth_brick * 512)
        coarse_ref[rows] = value.reshape(512, width).astype(jnp.bfloat16)


def middle_call(source, block, before, after, early, wide1, wide2):
    mid = block.shape[1]
    smem = pl.BlockSpec(memory_space=pltpu.SMEM)
    vmem = pl.BlockSpec(memory_space=pltpu.VMEM)
    inner = SIDE - 2
    hidden = (inner, HID * COLS, mid)
    return pl.pallas_call(
        middle_kernel,
        in_specs=[smem] + [vmem] * 6,
        out_specs=[vmem] * 3,
        out_shape=[
            jax.ShapeDtypeStruct(shape, jnp.bfloat16) for shape in (hidden, hidden, (1024, mid))
        ],
        scratch_shapes=[
            pltpu.VMEM((2, inner, 16, mid), jnp.bfloat16),
            pltpu.VMEM((LATE_PLANES, inner * COLS, mid), jnp.bfloat16),
            pltpu.VMEM((LATE_PLANES + 2, SIDE * COLS, mid), jnp.bfloat16),
            pltpu.VMEM((LATE_PLANES + 2, SIDE * COLS, mid), jnp.bfloat16),
        ],
        compiler_params=pltpu.CompilerParams(vmem_limit_bytes=VMEM_LIMIT),
        cost_estimate=conv_cost(inner * (4 + LATE_PLANES) * COLS + 1024, mid),
        name="middle",
    )(source, block, before, after, early, wide1, wide2)


def scatter_bricks(source_ref, stage, value, depth_brick):
    width = value.shape[3]
    half = low_half((4, 2, COLS, width))
    for r in range(4):
        part = value[:, r * 4 : (r + 1) * 4].reshape(4, 2, 2, COLS, width)
        even, odd = part[:, :, 0], part[:, :, 1]
        b0 = jnp.where(half, even, pltpu.roll(odd, 4, 2))
        b1 = jnp.where(half, pltpu.roll(even, 4, 2), odd)
        slot = slot_index(depth_brick, r)
        for k, brick in enumerate((b0, b1)):
            source = source_ref[slot + k]
            row = pl.multiple_of(jnp.where(source >= 0, source, K * CAP) * CELLS, CELLS)
            stage[pl.ds(row, CELLS), :] = brick.reshape(CELLS, width).astype(jnp.bfloat16)


def final_kernel(count, base_ref, source_ref, *refs):
    block_ref, before_ref, after_ref, even_ref, odd_ref = refs[:5]
    mid_here, mid_next, mid_ref, wide1_ref, wide2_ref, first_ref, last_ref = refs[5:12]
    backs = refs[12 : 12 + K]
    x_here, x_next, h_here, h_next, stage, under_ref, over_ref = refs[12 + K :]
    width = block_ref.shape[1]
    stage[...] = jnp.zeros(stage.shape, jnp.bfloat16)
    face_in(base_ref[1], count, even_ref, odd_ref, under_ref, over_ref)
    flags_before = as_rows(before_ref[256:288])
    flags_after = as_rows(after_ref[256:288])
    spread = []
    for end, ref in ((0, under_ref), (1, over_ref)):
        own = []
        for d in (0, 1) if end == 0 else (SIDE - 2, SIDE - 1):
            edge = slice(d * 16, (d + 1) * 16)
            own.append(
                jnp.concatenate(
                    [before_ref[edge], block_ref[d * 128 : (d + 1) * 128], after_ref[edge]], axis=0
                )
            )
        far = [ref[k * 160 : (k + 1) * 160] for k in range(2)]
        for index, plane in enumerate(far + own if end == 0 else own + far):
            x_here[end * 4 + index] = plane
            x_next[end * 4 + index] = as_tiles(moved_rows(as_rows(plane)))
        far_flags = as_rows(ref[320:368])
        brick = 0 if end == 0 else 3
        own_flags = [flags_before[brick]]
        own_flags += [slot_flags(source_ref, slot_index(brick, r)) for r in range(4)]
        own_flags += [flags_after[brick]]
        pair = [
            spread_flags([far_flags[r] for r in range(6)], (1, 4, 4, 4, 4, 1)),
            spread_flags(own_flags, (1, 4, 4, 4, 4, 1)),
        ]
        spread += pair if end == 0 else pair[::-1]
    lhs = [plane_taps(x_here, x_next, first, 2, HID * COLS) for first in (0, 4)]
    value = multiply_taps(jnp.concatenate(lhs, axis=0), wide1_ref)
    value = activate(value.reshape(4, HID, COLS, width), jnp.stack(spread, axis=0))
    for k, index in enumerate((0, 1, 10, 11)):
        h_here[index] = as_tiles(value[k])
        h_next[index] = as_tiles(moved_rows(value[k]))
    for k in range(4):
        for index, source in ((2 + k, k), (6 + k, SIDE - 6 + k)):
            h_here[index] = mid_here[source]
            h_next[index] = mid_next[source]
    for depth_brick in (1, 2):
        rows = slice((depth_brick - 1) * 512, depth_brick * 512)
        done = mid_ref[rows].astype(jnp.float32).reshape(4, SIDE, COLS, width)
        scatter_bricks(source_ref, stage, done, depth_brick)
    for depth_brick, ref in ((0, first_ref), (3, last_ref)):
        value = conv_planes(h_here, h_next, wide2_ref, depth_brick * 2, 4, SIDE * COLS)
        value = coarse_rows(source_ref, block_ref, value, depth_brick)
        ref[...] = value.reshape(512, width).astype(jnp.bfloat16)
        scatter_bricks(source_ref, stage, value, depth_brick)
    for j in range(K):
        backs[j][...] = stage[j * CAP * CELLS : (j + 1) * CAP * CELLS]


def final_call(count, base, source, block, halo, middle, wide1, wide2):
    mid = block.shape[1]
    smem = pl.BlockSpec(memory_space=pltpu.SMEM)
    vmem = pl.BlockSpec(memory_space=pltpu.VMEM)
    return pl.pallas_call(
        functools.partial(final_kernel, count),
        in_specs=[smem, smem] + [vmem] * 10,
        out_specs=[vmem] * (2 + K),
        out_shape=[jax.ShapeDtypeStruct((512, mid), jnp.bfloat16)] * 2
        + [jax.ShapeDtypeStruct((CAP * CELLS, mid), jnp.bfloat16)] * K,
        scratch_shapes=[
            pltpu.VMEM((8, WIDE * COLS, mid), jnp.bfloat16),
            pltpu.VMEM((8, WIDE * COLS, mid), jnp.bfloat16),
            pltpu.VMEM((12, HID * COLS, mid), jnp.bfloat16),
            pltpu.VMEM((12, HID * COLS, mid), jnp.bfloat16),
            pltpu.VMEM(((K * CAP + 1) * CELLS, mid), jnp.bfloat16),
            pltpu.VMEM((368, mid), jnp.bfloat16),
            pltpu.VMEM((368, mid), jnp.bfloat16),
        ],
        compiler_params=pltpu.CompilerParams(vmem_limit_bytes=VMEM_LIMIT),
        cost_estimate=conv_cost(1600, mid),
        name="final",
    )(base, source, block, *halo, *middle, wide1, wide2)


def from_behind(value, axis, steps):
    count = lax.axis_size(axis)
    pairs = [(source, (source + steps) % count) for source in range(count)]
    return lax.ppermute(value, axis, pairs)


def swap_face(face, axis, first):
    count = lax.axis_size(axis)
    partner = list(range(count))
    for i in range(first, count - 1, 2):
        partner[i], partner[i + 1] = i + 1, i
    return lax.ppermute(face, axis, list(enumerate(partner)))


def shards(fine, fine_mask, slot_source, w_down, w_first, w_second, w_up):
    mid = w_down.shape[1]
    base = jnp.stack([lax.axis_index("xy"), lax.axis_index("gz")]).astype(jnp.int32)
    counts = (lax.axis_size("gz"), lax.axis_size("xy"))
    sent = down_call(fine, fine_mask, w_down, SENT)
    arrived = {j: from_behind(sent[j], "xy", j) for j in SENT}
    later = (arrived[SENT[2]], fine, fine_mask, w_down, w_first, w_second)
    arrived[SENT[2]], *later = lax.optimization_barrier(later)
    prepared = lax.optimization_barrier(tuple(prepare_call(*later)))
    arrived[0], mask, wide1, wide2 = prepared
    block, even, odd = place_call(base, slot_source, [arrived[j] for j in range(K)])
    even = swap_face(even, "xy", 0)
    odd = swap_face(odd, "xy", 1)
    early = inner_call(slot_source, block, wide1, EARLY)
    even, odd, early = lax.optimization_barrier((even, odd, early))
    before, after, even, odd = edge_call(counts, base, slot_source, block, even, odd)
    even = swap_face(even, "gz", 0)
    odd = swap_face(odd, "gz", 1)
    middle = middle_call(slot_source, block, before, after, early, wide1, wide2)
    first, last, *back = final_call(
        counts[0], base, slot_source, block, (before, after, even, odd), middle, wide1, wide2
    )
    octant = {j: from_behind(back[j], "xy", -j) for j in RETURNED[:5]}
    for done, j in zip(RETURNED, RETURNED[5:]):
        octant[done], value = lax.optimization_barrier((octant[done], back[j]))
        octant[j] = from_behind(value, "xy", -j)
    octant[0] = back[0]
    octant[7], *pieces = lax.optimization_barrier((octant[7], first, middle[2], last))
    coarse = jnp.concatenate(pieces, axis=0)
    fine_out = None
    for block_indices in ((3,), (2, 1, 0)):
        octants = [octant[2 * k + part] for k in block_indices for part in range(2)]
        fine_out = up_call(fine, mask, w_up, octants, block_indices[0], fine_out)
    return fine_out, coarse.reshape(SIDE, SIDE, COLS, mid)


def solution(mesh):
    placed = (
        P(("gz", "xy"), None, None),
        P(("gz", "xy"), None),
        P(("gz", "xy")),
        P(),
        P(),
        P(),
        P(),
    )
    return jax.shard_map(
        shards,
        mesh=mesh,
        in_specs=placed,
        out_specs=(P(("gz", "xy"), None, None), P("gz", "xy", None, None)),
        check_vma=False,
    )
```

```python
import functools

import jax
import jax.numpy as jnp
from jax import lax
from jax.experimental import pallas as pl
from jax.experimental.pallas import tpu as pltpu
from jax.sharding import PartitionSpec as P

CAP = 4
K = 8
CELLS = 64
SIDE = 16
COLS = 8
WIDE = SIDE + 4
HID = SIDE + 2
EARLY = ((1, 3), (4, 4), (8, 4))
LATE = ((12, 3),)
LATE_PLANES = 3
SENT = (4, 3, 5, 2, 6, 1, 7)
RETURNED = (6, 7, 4, 5, 2, 3, 1)
DOWN_LIMIT = 66000000
VMEM_LIMIT = 24 * 1024 * 1024


def expand_mask(mask):
    bricks = mask.shape[0]
    values = mask.astype(jnp.float32)
    cell = lax.broadcasted_iota(jnp.int32, (16, 128), 0)
    lane = lax.broadcasted_iota(jnp.int32, (16, 128), 1)
    chosen = (cell == lane // 8).astype(jnp.float32)
    parts = [
        values[:, t * 128 : (t + 1) * 128].reshape(bricks, 1, 128) * chosen[None] for t in range(4)
    ]
    spread = jnp.concatenate(parts, axis=1).reshape(bricks * CELLS, 128).astype(jnp.bfloat16)
    source = lax.broadcasted_iota(jnp.int32, (128, 512), 0)
    target = lax.broadcasted_iota(jnp.int32, (128, 512), 1)
    widen = ((source & 7) == (target >> 6)).astype(jnp.bfloat16)
    return jnp.dot(spread, widen, preferred_element_type=jnp.float32)


def down_kernel(offsets, fine_hbm, mask_hbm, w_hbm, *refs):
    count = len(offsets)
    outs = refs[:count]
    fine_ref, mask_ref, w_ref, wide_ref, result_ref, sems, out_sems = refs[count:]
    first = [
        pltpu.make_async_copy(mask_hbm, mask_ref, sems.at[count]),
        pltpu.make_async_copy(w_hbm, w_ref, sems.at[count + 1]),
    ]
    chunks = [
        pltpu.make_async_copy(fine_hbm.at[pl.ds(j * CAP, CAP)], fine_ref.at[k], sems.at[k])
        for k, j in enumerate(offsets)
    ]
    for copy in first + chunks:
        copy.start()
    first[0].wait()
    rows = CAP * CELLS
    for k, j in enumerate(offsets):
        wide_ref[k * rows : (k + 1) * rows] = expand_mask(
            mask_ref[j * CAP : (j + 1) * CAP]
        ).astype(jnp.bfloat16)
    first[1].wait()
    for start in range(0, count, 2):
        group = range(start, min(start + 2, count))
        for k in group:
            chunks[k].wait()
        x = [
            fine_ref[k].reshape(rows, -1) * wide_ref[k * rows : (k + 1) * rows] for k in group
        ]
        y = jnp.dot(jnp.concatenate(x, axis=0), w_ref[...], preferred_element_type=jnp.float32)
        y = y.astype(jnp.bfloat16)
        for part, k in enumerate(group):
            result_ref[k] = y[part * rows : (part + 1) * rows]
            pltpu.make_async_copy(result_ref.at[k], outs[k], out_sems.at[k]).start()
    for k in range(count):
        pltpu.make_async_copy(result_ref.at[k], outs[k], out_sems.at[k]).wait()


def down_call(fine, mask, w, offsets):
    cells, width = fine.shape[1:]
    mid = w.shape[1]
    count = len(offsets)
    rows = count * CAP * cells
    hbm = pl.BlockSpec(memory_space=pltpu.HBM)
    outs = pl.pallas_call(
        functools.partial(down_kernel, offsets),
        in_specs=[hbm, hbm, hbm],
        out_specs=[pl.BlockSpec(memory_space=pl.ANY)] * count,
        out_shape=[jax.ShapeDtypeStruct((CAP * cells, mid), jnp.bfloat16)] * count,
        scratch_shapes=[
            pltpu.VMEM((count, CAP, cells, width), fine.dtype),
            pltpu.VMEM(mask.shape, mask.dtype),
            pltpu.VMEM(w.shape, w.dtype),
            pltpu.VMEM((rows, width), jnp.bfloat16),
            pltpu.VMEM((count, CAP * cells, mid), jnp.bfloat16),
            pltpu.SemaphoreType.DMA((count + 2,)),
            pltpu.SemaphoreType.DMA((count,)),
        ],
        compiler_params=pltpu.CompilerParams(vmem_limit_bytes=DOWN_LIMIT),
        cost_estimate=pl.CostEstimate(
            flops=2 * rows * width * mid, bytes_accessed=rows * width * 2, transcendentals=0
        ),
        name="down",
    )(fine, mask, w)
    return dict(zip(offsets, outs))


def prepare_kernel(
    fine_ref, mask_ref, w_down_ref, w1_ref, w2_ref, own_ref, mask_out, wide1_ref, wide2_ref
):
    gather_weights(w1_ref, wide1_ref)
    gather_weights(w2_ref, wide2_ref)
    step = 8
    for part in range(mask_ref.shape[0] // step):
        rows = slice(part * step * CELLS, (part + 1) * step * CELLS)
        mask_out[rows] = expand_mask(mask_ref[part * step : (part + 1) * step]).astype(jnp.bfloat16)
    rows = CAP * CELLS
    own = fine_ref[...].reshape(rows, -1) * mask_out[:rows]
    own = jnp.dot(own, w_down_ref[...], preferred_element_type=jnp.float32)
    own_ref[...] = own.astype(jnp.bfloat16)


def prepare_call(fine, mask, w_down, w_first, w_second):
    mid = w_first.shape[1]
    vmem = pl.BlockSpec(memory_space=pltpu.VMEM)
    rows = mask.shape[0] * CELLS
    wide = jax.ShapeDtypeStruct((9 * mid, 3 * mid), jnp.bfloat16)
    return pl.pallas_call(
        prepare_kernel,
        grid=(1,),
        in_specs=[pl.BlockSpec((CAP,) + fine.shape[1:], lambda i: (0, 0, 0))] + [vmem] * 4,
        out_specs=[vmem] * 4,
        out_shape=[
            jax.ShapeDtypeStruct((CAP * CELLS, mid), jnp.bfloat16),
            jax.ShapeDtypeStruct((rows, mask.shape[1]), jnp.bfloat16),
            wide,
            wide,
        ],
        compiler_params=pltpu.CompilerParams(vmem_limit_bytes=VMEM_LIMIT),
        cost_estimate=pl.CostEstimate(
            flops=2 * rows * mask.shape[1] * 128, bytes_accessed=rows * mask.shape[1] * 2, transcendentals=0
        ),
        name="prepare",
    )(fine, mask, w_down, w_first, w_second)


def up_kernel(offsets, fine_ref, mask_ref, w_ref, *refs):
    out_ref, octant_ref = refs[-2:]
    step = pl.program_id(0)
    bricks, cells, width = fine_ref.shape
    count = bricks // CAP
    steps = offsets // count
    for part in range(count):
        for k in range(steps):

            @pl.when(step == k)
            def _():
                octant_ref[part] = refs[k * count + part][...]

    for part in range(count):
        rows = slice(part * CAP * cells, (part + 1) * CAP * cells)
        up = jnp.dot(octant_ref[part], w_ref[...], preferred_element_type=jnp.float32)
        fine = fine_ref[part * CAP : (part + 1) * CAP].reshape(CAP * cells, width)
        mask = mask_ref[rows].astype(jnp.float32)
        out = jnp.where(mask > 0.5, fine.astype(jnp.float32) + up, 0.0)
        out_ref[part * CAP : (part + 1) * CAP] = out.astype(jnp.bfloat16).reshape(CAP, cells, width)


def up_call(fine, mask, w, octants, first, partial):
    bricks, cells, width = fine.shape
    mid = w.shape[0]
    step = 8

    def place(i):
        return first - i

    count = len(octants)
    partials = [] if partial is None else [partial]
    return pl.pallas_call(
        functools.partial(up_kernel, count),
        grid=(count * CAP // step,),
        in_specs=[
            pl.BlockSpec((step, cells, width), lambda i: (place(i), 0, 0)),
            pl.BlockSpec((step * cells, width), lambda i: (place(i), 0)),
            pl.BlockSpec((mid, width), lambda i: (0, 0)),
        ]
        + [pl.BlockSpec((CAP * cells, mid), lambda i: (0, 0))] * count
        + [pl.BlockSpec(memory_space=pl.ANY)] * len(partials),
        out_specs=pl.BlockSpec((step, cells, width), lambda i: (place(i), 0, 0)),
        out_shape=jax.ShapeDtypeStruct(fine.shape, jnp.bfloat16),
        input_output_aliases={3 + count: 0} if partials else {},
        scratch_shapes=[pltpu.VMEM((step // CAP, CAP * cells, mid), jnp.bfloat16)],
        compiler_params=pltpu.CompilerParams(vmem_limit_bytes=VMEM_LIMIT),
        cost_estimate=pl.CostEstimate(
            flops=bricks * cells * width * mid, bytes_accessed=bricks * cells * width * 2, transcendentals=0
        ),
        name="up",
    )(fine, mask, w, *octants, *partials)


def low_half(shape):
    return lax.broadcasted_iota(jnp.int32, shape, len(shape) - 2) < 4


def slot_flags(source_ref, first):
    pair = [jnp.where(source_ref[first + k] >= 0, 1.0, 0.0).astype(jnp.float32) for k in range(2)]
    return jnp.where(low_half((8, 128)), pair[0], pair[1])


def slot_index(depth_brick, row_brick):
    pd, qd = divmod(depth_brick, 2)
    pr, qr = divmod(row_brick, 2)
    return (pd * 2 + pr) * 8 + qd * 4 + qr * 2


def take_brick(source_ref, arrived, slot):
    value = source_ref[slot]
    first = pl.multiple_of(jnp.maximum(value, 0) * CELLS, CELLS)
    brick = arrived[pl.ds(first, CELLS), :].astype(jnp.float32)
    return jnp.where(value >= 0, brick, 0.0).reshape(8, 8, 128)


def place_kernel(base_ref, source_ref, *refs):
    block_ref, even_ref, odd_ref, low_ref, high_ref, arrived = refs[K:]
    for j in range(K):
        arrived[j * CAP * CELLS : (j + 1) * CAP * CELLS] = refs[j][...]
    half = low_half((8, 8, 128))
    for depth_brick in range(4):
        for row_brick in range(4):
            slot = slot_index(depth_brick, row_brick)
            b0 = take_brick(source_ref, arrived, slot)
            b1 = take_brick(source_ref, arrived, slot + 1)
            even = jnp.where(half, b0, pltpu.roll(b1, 4, 1))
            odd = jnp.where(half, pltpu.roll(b0, 4, 1), b1)
            both = jnp.stack([even, odd], axis=1).reshape(4, 32, 128).astype(jnp.bfloat16)
            for vd in range(4):
                row = ((depth_brick * 4 + vd) * SIDE + row_brick * 4) * COLS
                block_ref[row : row + 32] = both[vd]
                place = (depth_brick * 4 + vd) * 16
                if row_brick == 0:
                    low_ref[place : place + 16] = both[vd, :16]
                if row_brick == 3:
                    high_ref[place : place + 16] = both[vd, 16:]
    for row_brick, ref in ((0, low_ref), (3, high_ref)):
        flags = [slot_flags(source_ref, slot_index(d, row_brick)) for d in range(4)]
        ref[256:288] = jnp.concatenate(flags, axis=0).astype(jnp.bfloat16)
    face_out(base_ref[0], low_ref, high_ref, even_ref, odd_ref)


def face_out(index, low_ref, high_ref, even_ref, odd_ref):
    is_even = index % 2 == 0
    even_ref[...] = jnp.where(is_even, high_ref[...], low_ref[...])
    odd_ref[...] = jnp.where(is_even, low_ref[...], high_ref[...])


def face_in(index, count, even_ref, odd_ref, low_ref, high_ref):
    is_even = index % 2 == 0
    empty = jnp.zeros(low_ref.shape, low_ref.dtype)
    low = jnp.where(is_even, odd_ref[...], even_ref[...])
    high = jnp.where(is_even, even_ref[...], odd_ref[...])
    low_ref[...] = jnp.where(index == 0, empty, low)
    high_ref[...] = jnp.where(index == count - 1, empty, high)


def place_call(base, source, arrived):
    mid = arrived[0].shape[1]
    smem = pl.BlockSpec(memory_space=pltpu.SMEM)
    vmem = pl.BlockSpec(memory_space=pltpu.VMEM)
    return pl.pallas_call(
        place_kernel,
        in_specs=[smem, smem] + [vmem] * K,
        out_specs=[vmem] * 3,
        out_shape=[
            jax.ShapeDtypeStruct((rows, mid), jnp.bfloat16)
            for rows in (SIDE * SIDE * COLS, 288, 288)
        ],
        scratch_shapes=[
            pltpu.VMEM((288, mid), jnp.bfloat16),
            pltpu.VMEM((288, mid), jnp.bfloat16),
            pltpu.VMEM((K * CAP * CELLS, mid), jnp.bfloat16),
        ],
        compiler_params=pltpu.CompilerParams(vmem_limit_bytes=VMEM_LIMIT),
        name="place",
    )(base, source, *arrived)


def edge_kernel(
    counts,
    base_ref,
    source_ref,
    block_ref,
    even_ref,
    odd_ref,
    before_ref,
    after_ref,
    even_out,
    odd_out,
    low_ref,
    high_ref,
):
    face_in(base_ref[0], counts[1], even_ref, odd_ref, before_ref, after_ref)
    for ref, planes, brick in ((low_ref, (0, 1), 0), (high_ref, (SIDE - 2, SIDE - 1), 3)):
        for k, plane in enumerate(planes):
            start = k * WIDE * COLS
            ref[start : start + 16] = before_ref[plane * 16 : plane * 16 + 16]
            ref[start + 16 : start + 144] = block_ref[plane * 128 : plane * 128 + 128]
            ref[start + 144 : start + 160] = after_ref[plane * 16 : plane * 16 + 16]
        flags = [before_ref[256:288].astype(jnp.float32)[brick * 8 : brick * 8 + 8]]
        flags += [slot_flags(source_ref, slot_index(brick, r)) for r in range(4)]
        flags += [after_ref[256:288].astype(jnp.float32)[brick * 8 : brick * 8 + 8]]
        ref[320:368] = jnp.concatenate(flags, axis=0).astype(jnp.bfloat16)
    face_out(base_ref[1], low_ref, high_ref, even_out, odd_out)


def edge_call(counts, base, source, block, even, odd):
    smem = pl.BlockSpec(memory_space=pltpu.SMEM)
    vmem = pl.BlockSpec(memory_space=pltpu.VMEM)
    mid = block.shape[1]
    return pl.pallas_call(
        functools.partial(edge_kernel, counts),
        in_specs=[smem, smem, vmem, vmem, vmem],
        out_specs=[vmem] * 4,
        out_shape=[
            jax.ShapeDtypeStruct((rows, mid), jnp.bfloat16) for rows in (288, 288, 368, 368)
        ],
        scratch_shapes=[pltpu.VMEM((368, mid), jnp.bfloat16)] * 2,
        compiler_params=pltpu.CompilerParams(vmem_limit_bytes=VMEM_LIMIT),
        name="edge",
    )(base, source, block, even, odd)


def gather_weights(w_ref, wide_ref):
    width = w_ref.shape[2]
    for tap in range(9):
        for column in range(3):
            wide_ref[tap * width : (tap + 1) * width, column * width : (column + 1) * width] = (
                w_ref[tap * 3 + column]
            )


def as_rows(value):
    value = value.astype(jnp.float32)
    return value.reshape(value.shape[0] // COLS, COLS, value.shape[1])


def moved_rows(rows):
    empty = jnp.zeros((1,) + rows.shape[1:], jnp.float32)
    return jnp.concatenate([rows[1:], empty], axis=0)


def as_tiles(rows):
    return rows.reshape(rows.shape[0] * COLS, rows.shape[2]).astype(jnp.bfloat16)


def multiply_taps(lhs, wide_ref):
    width = wide_ref.shape[1] // 3
    wide = jnp.dot(lhs, wide_ref[...], preferred_element_type=jnp.float32)
    wide = wide.reshape(lhs.shape[0] // COLS, COLS, 3 * width)
    column = lax.broadcasted_iota(jnp.int32, (lhs.shape[0] // COLS, COLS, width), 1)
    left = jnp.where(column == 0, 0.0, pltpu.roll(wide[:, :, :width], 1, 1))
    right = jnp.where(column == COLS - 1, 0.0, pltpu.roll(wide[:, :, 2 * width :], COLS - 1, 1))
    return left + wide[:, :, width : 2 * width] + right


def plane_taps(here_ref, next_ref, first, planes, rows):
    taps = []
    for dd in range(3):
        span = slice(first + dd, first + dd + planes)
        taps += [
            here_ref[span, 0:rows, :],
            next_ref[span, 0:rows, :],
            here_ref[span, 16 : rows + 16, :],
        ]
    lhs = jnp.concatenate(taps, axis=2)
    return lhs.reshape(planes * rows, lhs.shape[2])


def conv_planes(here_ref, next_ref, wide_ref, first, planes, rows):
    return multiply_taps(plane_taps(here_ref, next_ref, first, planes, rows), wide_ref)


def activate(value, flags):
    return value / (1.0 + jnp.exp(-value)) * flags


def spread_flags(flags, repeats):
    return jnp.concatenate(
        [jnp.broadcast_to(flag[None], (count,) + flag.shape) for flag, count in zip(flags, repeats)],
        axis=0,
    )


def inner_planes(source_ref, block_ref, wide1_ref, hidden_ref, here, moved, groups):
    width = block_ref.shape[1]
    base = groups[0][0] - 1
    for d in range(base, groups[-1][0] + groups[-1][1] + 1):
        plane = block_ref[d * 128 : (d + 1) * 128]
        here[d - base] = plane
        moved[d - base] = as_tiles(moved_rows(as_rows(plane)))
    inner = SIDE - 2
    rows = inner * COLS
    for first, planes in groups:
        value = conv_planes(here, moved, wide1_ref, first - 1 - base, planes, rows)
        value = value.reshape(planes, inner, COLS, width)
        flags = [slot_flags(source_ref, slot_index(first // 4, r)) for r in range(4)]
        value = activate(value, spread_flags(flags, (3, 4, 4, 3))[None])
        hidden_ref[first - 1 - base : first - 1 - base + planes] = value.reshape(
            planes, rows, width
        ).astype(jnp.bfloat16)


def inner_kernel(groups, source_ref, block_ref, wide1_ref, hidden_ref, here, moved):
    inner_planes(source_ref, block_ref, wide1_ref, hidden_ref, here, moved, groups)


def conv_cost(rows, width):
    return pl.CostEstimate(
        flops=2 * rows * 27 * width * width, bytes_accessed=27 * width * width * 4, transcendentals=0
    )


def inner_call(source, block, wide1, groups):
    mid = block.shape[1]
    smem = pl.BlockSpec(memory_space=pltpu.SMEM)
    vmem = pl.BlockSpec(memory_space=pltpu.VMEM)
    rows = (SIDE - 2) * COLS
    planes = sum(count for _, count in groups)
    return pl.pallas_call(
        functools.partial(inner_kernel, groups),
        in_specs=[smem, vmem, vmem],
        out_specs=vmem,
        out_shape=jax.ShapeDtypeStruct((planes, rows, mid), jnp.bfloat16),
        scratch_shapes=[pltpu.VMEM((planes + 2, SIDE * COLS, mid), jnp.bfloat16)] * 2,
        compiler_params=pltpu.CompilerParams(vmem_limit_bytes=VMEM_LIMIT),
        cost_estimate=conv_cost(planes * rows, mid),
        name="inner",
    )(source, block, wide1)


def side_taps(low, high):
    mixed = as_tiles(
        jnp.concatenate(
            [as_rows(low).reshape(-1, 2, COLS, 128)[:, 1:], as_rows(high).reshape(-1, 2, COLS, 128)[:, :1]],
            axis=1,
        ).reshape(-1, COLS, 128)
    )
    return low, mixed, high


def depth_taps(taps, planes):
    parts = [tap[dd * 16 : (dd + planes) * 16] for dd in range(3) for tap in taps]
    return jnp.concatenate(parts, axis=1)


def coarse_rows(source_ref, block_ref, value, depth_brick):
    width = block_ref.shape[1]
    value = value.reshape(4, SIDE, COLS, width)
    rows = slice(depth_brick * 512, (depth_brick + 1) * 512)
    own = block_ref[rows].astype(jnp.float32).reshape(4, SIDE, COLS, width)
    flags = [slot_flags(source_ref, slot_index(depth_brick, r)) for r in range(4)]
    return (value + own) * spread_flags(flags, (4, 4, 4, 4))[None]


def middle_kernel(source_ref, *refs):
    block_ref, before_ref, after_ref, early_ref, wide1_ref, wide2_ref = refs[:6]
    h_here, h_next, coarse_ref, side, late, here, moved = refs[6:]
    width = block_ref.shape[1]
    inner = SIDE - 2
    inner_planes(source_ref, block_ref, wide1_ref, late, here, moved, LATE)

    low = jnp.concatenate([block_ref[d * 128 : d * 128 + 16] for d in range(SIDE)], axis=0)
    high = jnp.concatenate([block_ref[d * 128 + 112 : d * 128 + 128] for d in range(SIDE)], axis=0)
    left = depth_taps(side_taps(before_ref[0:256], low), inner)
    right = depth_taps(side_taps(high, after_ref[0:256]), inner)
    value = multiply_taps(jnp.concatenate([left, right], axis=0), wide1_ref)
    depths = (3, 4, 4, 3)
    edge_flags = (as_rows(before_ref[256:288]), as_rows(after_ref[256:288]))
    flags = []
    for end, row_brick in ((0, 0), (1, 3)):
        own = [slot_flags(source_ref, slot_index(d, row_brick)) for d in range(4)]
        pairs = [jnp.stack([edge_flags[end][d], own[d]][:: 1 - 2 * end], axis=0) for d in range(4)]
        flags.append(spread_flags(pairs, depths))
    value = activate(value.reshape(2, inner, 2, COLS, width), jnp.stack(flags, axis=0))
    side[...] = value.reshape(2, inner, 16, width).astype(jnp.bfloat16)
    centres = [ref[k] for ref in (early_ref, late) for k in range(ref.shape[0])]
    for d in range(inner):
        plane = jnp.concatenate([side[0, d], centres[d], side[1, d]], axis=0)
        h_here[d] = plane
        h_next[d] = as_tiles(moved_rows(as_rows(plane)))

    for depth_brick in (1, 2):
        value = conv_planes(h_here, h_next, wide2_ref, depth_brick * 4 - 2, 4, SIDE * COLS)
        value = coarse_rows(source_ref, block_ref, value, depth_brick)
        rows = slice((depth_brick - 1) * 512, depth_brick * 512)
        coarse_ref[rows] = value.reshape(512, width).astype(jnp.bfloat16)


def middle_call(source, block, before, after, early, wide1, wide2):
    mid = block.shape[1]
    smem = pl.BlockSpec(memory_space=pltpu.SMEM)
    vmem = pl.BlockSpec(memory_space=pltpu.VMEM)
    inner = SIDE - 2
    hidden = (inner, HID * COLS, mid)
    return pl.pallas_call(
        middle_kernel,
        in_specs=[smem] + [vmem] * 6,
        out_specs=[vmem] * 3,
        out_shape=[
            jax.ShapeDtypeStruct(shape, jnp.bfloat16) for shape in (hidden, hidden, (1024, mid))
        ],
        scratch_shapes=[
            pltpu.VMEM((2, inner, 16, mid), jnp.bfloat16),
            pltpu.VMEM((LATE_PLANES, inner * COLS, mid), jnp.bfloat16),
            pltpu.VMEM((LATE_PLANES + 2, SIDE * COLS, mid), jnp.bfloat16),
            pltpu.VMEM((LATE_PLANES + 2, SIDE * COLS, mid), jnp.bfloat16),
        ],
        compiler_params=pltpu.CompilerParams(vmem_limit_bytes=VMEM_LIMIT),
        cost_estimate=conv_cost(inner * (4 + LATE_PLANES) * COLS + 1024, mid),
        name="middle",
    )(source, block, before, after, early, wide1, wide2)


def scatter_bricks(source_ref, stage, value, depth_brick):
    width = value.shape[3]
    half = low_half((4, 2, COLS, width))
    for r in range(4):
        part = value[:, r * 4 : (r + 1) * 4].reshape(4, 2, 2, COLS, width)
        even, odd = part[:, :, 0], part[:, :, 1]
        b0 = jnp.where(half, even, pltpu.roll(odd, 4, 2))
        b1 = jnp.where(half, pltpu.roll(even, 4, 2), odd)
        slot = slot_index(depth_brick, r)
        for k, brick in enumerate((b0, b1)):
            source = source_ref[slot + k]
            row = pl.multiple_of(jnp.where(source >= 0, source, K * CAP) * CELLS, CELLS)
            stage[pl.ds(row, CELLS), :] = brick.reshape(CELLS, width).astype(jnp.bfloat16)


def final_kernel(count, base_ref, source_ref, *refs):
    block_ref, before_ref, after_ref, even_ref, odd_ref = refs[:5]
    mid_here, mid_next, mid_ref, wide1_ref, wide2_ref, first_ref, last_ref = refs[5:12]
    backs = refs[12 : 12 + K]
    x_here, x_next, h_here, h_next, stage, under_ref, over_ref = refs[12 + K :]
    width = block_ref.shape[1]
    stage[...] = jnp.zeros(stage.shape, jnp.bfloat16)
    face_in(base_ref[1], count, even_ref, odd_ref, under_ref, over_ref)
    flags_before = as_rows(before_ref[256:288])
    flags_after = as_rows(after_ref[256:288])
    spread = []
    for end, ref in ((0, under_ref), (1, over_ref)):
        own = []
        for d in (0, 1) if end == 0 else (SIDE - 2, SIDE - 1):
            edge = slice(d * 16, (d + 1) * 16)
            own.append(
                jnp.concatenate(
                    [before_ref[edge], block_ref[d * 128 : (d + 1) * 128], after_ref[edge]], axis=0
                )
            )
        far = [ref[k * 160 : (k + 1) * 160] for k in range(2)]
        for index, plane in enumerate(far + own if end == 0 else own + far):
            x_here[end * 4 + index] = plane
            x_next[end * 4 + index] = as_tiles(moved_rows(as_rows(plane)))
        far_flags = as_rows(ref[320:368])
        brick = 0 if end == 0 else 3
        own_flags = [flags_before[brick]]
        own_flags += [slot_flags(source_ref, slot_index(brick, r)) for r in range(4)]
        own_flags += [flags_after[brick]]
        pair = [
            spread_flags([far_flags[r] for r in range(6)], (1, 4, 4, 4, 4, 1)),
            spread_flags(own_flags, (1, 4, 4, 4, 4, 1)),
        ]
        spread += pair if end == 0 else pair[::-1]
    lhs = [plane_taps(x_here, x_next, first, 2, HID * COLS) for first in (0, 4)]
    value = multiply_taps(jnp.concatenate(lhs, axis=0), wide1_ref)
    value = activate(value.reshape(4, HID, COLS, width), jnp.stack(spread, axis=0))
    for k, index in enumerate((0, 1, 10, 11)):
        h_here[index] = as_tiles(value[k])
        h_next[index] = as_tiles(moved_rows(value[k]))
    for k in range(4):
        for index, source in ((2 + k, k), (6 + k, SIDE - 6 + k)):
            h_here[index] = mid_here[source]
            h_next[index] = mid_next[source]
    for depth_brick in (1, 2):
        rows = slice((depth_brick - 1) * 512, depth_brick * 512)
        done = mid_ref[rows].astype(jnp.float32).reshape(4, SIDE, COLS, width)
        scatter_bricks(source_ref, stage, done, depth_brick)
    for depth_brick, ref in ((0, first_ref), (3, last_ref)):
        value = conv_planes(h_here, h_next, wide2_ref, depth_brick * 2, 4, SIDE * COLS)
        value = coarse_rows(source_ref, block_ref, value, depth_brick)
        ref[...] = value.reshape(512, width).astype(jnp.bfloat16)
        scatter_bricks(source_ref, stage, value, depth_brick)
    for j in range(K):
        backs[j][...] = stage[j * CAP * CELLS : (j + 1) * CAP * CELLS]


def final_call(count, base, source, block, halo, middle, wide1, wide2):
    mid = block.shape[1]
    smem = pl.BlockSpec(memory_space=pltpu.SMEM)
    vmem = pl.BlockSpec(memory_space=pltpu.VMEM)
    return pl.pallas_call(
        functools.partial(final_kernel, count),
        in_specs=[smem, smem] + [vmem] * 10,
        out_specs=[vmem] * (2 + K),
        out_shape=[jax.ShapeDtypeStruct((512, mid), jnp.bfloat16)] * 2
        + [jax.ShapeDtypeStruct((CAP * CELLS, mid), jnp.bfloat16)] * K,
        scratch_shapes=[
            pltpu.VMEM((8, WIDE * COLS, mid), jnp.bfloat16),
            pltpu.VMEM((8, WIDE * COLS, mid), jnp.bfloat16),
            pltpu.VMEM((12, HID * COLS, mid), jnp.bfloat16),
            pltpu.VMEM((12, HID * COLS, mid), jnp.bfloat16),
            pltpu.VMEM(((K * CAP + 1) * CELLS, mid), jnp.bfloat16),
            pltpu.VMEM((368, mid), jnp.bfloat16),
            pltpu.VMEM((368, mid), jnp.bfloat16),
        ],
        compiler_params=pltpu.CompilerParams(vmem_limit_bytes=VMEM_LIMIT),
        cost_estimate=conv_cost(1600, mid),
        name="final",
    )(base, source, block, *halo, *middle, wide1, wide2)


def from_behind(value, axis, steps):
    count = lax.axis_size(axis)
    pairs = [(source, (source + steps) % count) for source in range(count)]
    return lax.ppermute(value, axis, pairs)


def swap_face(face, axis, first):
    count = lax.axis_size(axis)
    partner = list(range(count))
    for i in range(first, count - 1, 2):
        partner[i], partner[i + 1] = i + 1, i
    return lax.ppermute(face, axis, list(enumerate(partner)))


def shards(fine, fine_mask, slot_source, w_down, w_first, w_second, w_up):
    mid = w_down.shape[1]
    base = jnp.stack([lax.axis_index("xy"), lax.axis_index("gz")]).astype(jnp.int32)
    counts = (lax.axis_size("gz"), lax.axis_size("xy"))
    sent = down_call(fine, fine_mask, w_down, SENT)
    arrived = {j: from_behind(sent[j], "xy", j) for j in SENT}
    later = (arrived[SENT[2]], fine, fine_mask, w_down, w_first, w_second)
    arrived[SENT[2]], *later = lax.optimization_barrier(later)
    prepared = lax.optimization_barrier(tuple(prepare_call(*later)))
    arrived[0], mask, wide1, wide2 = prepared
    block, even, odd = place_call(base, slot_source, [arrived[j] for j in range(K)])
    even = swap_face(even, "xy", 0)
    odd = swap_face(odd, "xy", 1)
    early = inner_call(slot_source, block, wide1, EARLY)
    even, odd, early = lax.optimization_barrier((even, odd, early))
    before, after, even, odd = edge_call(counts, base, slot_source, block, even, odd)
    even = swap_face(even, "gz", 0)
    odd = swap_face(odd, "gz", 1)
    middle = middle_call(slot_source, block, before, after, early, wide1, wide2)
    first, last, *back = final_call(
        counts[0], base, slot_source, block, (before, after, even, odd), middle, wide1, wide2
    )
    octant = {j: from_behind(back[j], "xy", -j) for j in RETURNED[:5]}
    for done, j in zip(RETURNED, RETURNED[5:]):
        octant[done], value = lax.optimization_barrier((octant[done], back[j]))
        octant[j] = from_behind(value, "xy", -j)
    octant[0] = back[0]
    octant[7], *pieces = lax.optimization_barrier((octant[7], first, middle[2], last))
    coarse = jnp.concatenate(pieces, axis=0)
    fine_out = None
    for block_indices in ((3,), (2, 1, 0)):
        octants = [octant[2 * k + part] for k in block_indices for part in range(2)]
        fine_out = up_call(fine, mask, w_up, octants, block_indices[0], fine_out)
    return fine_out, coarse.reshape(SIDE, SIDE, COLS, mid)


def solution(mesh):
    placed = (
        P(("gz", "xy"), None, None),
        P(("gz", "xy"), None),
        P(("gz", "xy")),
        P(),
        P(),
        P(),
        P(),
    )
    return jax.shard_map(
        shards,
        mesh=mesh,
        in_specs=placed,
        out_specs=(P(("gz", "xy"), None, None), P("gz", "xy", None, None)),
        check_vma=False,
    )
```
